32 devices in a mesh: dp: 16 (over z, x, core), tensor: 2 (over y).
Axes of the slice: x: 2, y: 2, z: 4, core: 2. Of those that a mesh axis runs over, the one named last changes fastest.
Arguments:
- block_in: bfloat16 [4096, 1536], P('dp', 'tensor'), may hold values from -6 to 6
- cotangent: bfloat16 [4096, 1536], P('dp', 'tensor'), may hold values from -6 to 6
- lengths: int32 [16, 1], P('dp'), may hold values from 0 to 256, as said below
- dest_slot: int32 [4096], replicated, may hold values from 0 to 4095, as said below
- return_slot: int32 [4096], replicated, may hold values from 0 to 4095, as said below
- norm_gain: float32 [1536], replicated, may hold values from 0.5 to 1.5
- inner_weight: bfloat16 [1536, 2, 3072], P(None, None, 'tensor'), may hold values from -0.15625 to 0.15625
- state_weight: bfloat16 [1536, 256], replicated, may hold values from -0.15625 to 0.15625
- step_weight: bfloat16 [1536, 48], P(None, 'tensor'), may hold values from -0.15625 to 0.15625
- conv_inner: float32 [4, 3072], P(None, 'tensor'), may hold values from -3 to 3
- conv_inner_bias: float32 [3072], P('tensor'), may hold values from -3 to 3
- conv_state: float32 [4, 256], replicated, may hold values from -3 to 3
- conv_state_bias: float32 [256], replicated, may hold values from -3 to 3
- step_bias: float32 [48], P('tensor'), may hold values from -7 to -2
- log_rate: float32 [48], P('tensor'), may hold values from 0 to 2.77
- skip_gain: float32 [48], P('tensor'), may hold values from 0.5 to 2
- gate_gain: float32 [3072], P('tensor'), may hold values from 0.5 to 1.5
- out_weight: bfloat16 [3072, 1536], P('tensor'), may hold values from -0.109375 to 0.109375
Outputs:
- block_out: bfloat16 [4096, 1536], P('dp', 'tensor')
- input_grad: bfloat16 [4096, 1536], P('dp', 'tensor')
- norm_gain_grad: float32 [1536], P('dp')
- inner_weight_grad: float32 [1536, 2, 3072], P('dp', None, 'tensor')
- state_weight_grad: float32 [1536, 256], P('dp')
- step_weight_grad: float32 [1536, 48], P('dp', 'tensor')
- conv_inner_grad: float32 [4, 3072], P(None, 'tensor')
- conv_inner_bias_grad: float32 [3072], P('tensor')
- conv_state_grad: float32 [4, 256], replicated
- conv_state_bias_grad: float32 [256], replicated
- step_bias_grad: float32 [48], P('tensor')
- log_rate_grad: float32 [48], P('tensor')
- skip_gain_grad: float32 [48], P('tensor')
- gate_gain_grad: float32 [3072], P('tensor')
- out_weight_grad: float32 [3072, 1536], P('tensor', 'dp')
The draws below stay inside these ranges and needn't reach their ends.
Inputs may be any that keep to these rules, and one draw needn't show every extreme that they name: lengths[g, k] > 0 exactly where a sequence begins at stretch k of group g; stretch 0 of every group begins one; a sequence fills lengths[g, k] slots from the first slot of its stretch and ends before the next stretch that begins a sequence, or at the group's end; some group holds one sequence of 256 slots. A permutation of the slots: input row p goes to slot dest_slot[p] % 256 of group dest_slot[p] // 256. Of the 256 rows of one dp device, at most 32 go to one group, and some device sends exactly 32 rows to some group. A permutation of the slots: returned row q takes the output of slot return_slot[q] % 256 of group return_slot[q] // 256. Of the 256 rows of one dp device, at most 32 come from one group, and some device takes exactly 32 rows from some group.
All inputs are finite; a program needn't handle non-finite values.
Results may differ from the reference program's by a relative error of at most 0.0082.
Values may be sent and summed in bfloat16 or wider, within the bound.
A program may use at most 192 MiB of HBM per device.

```python
import jax
import jax.numpy as jnp
from jax import lax

D = 1536
HEADS = 48
HEAD_DIM = 64
STATE = 128
CONV = 4
STRETCH = 256
CAP = 256
INNER = 3072
TOKENS = 4096
N_DP = 16


def route_table(key):
    base = CAP // N_DP
    pairs = N_DP // 2
    keys = jax.random.split(key, 5)
    swing = jax.random.randint(keys[0], (pairs, pairs), -base, base + 1)
    row_pick = jax.random.randint(keys[1], (), 0, pairs)
    col_pick = jax.random.randint(keys[2], (), 0, pairs)
    grid = jnp.arange(pairs, dtype=jnp.int32)
    swing = jnp.where((grid[:, None] == row_pick) & (grid[None, :] == col_pick), base, swing)
    parity = 1 - 2 * (jnp.arange(N_DP, dtype=jnp.int32) % 2)
    counts = base + jnp.repeat(jnp.repeat(swing, 2, axis=0), 2, axis=1) * parity[:, None] * parity[None, :]
    ends = jnp.cumsum(counts, axis=1)
    starts = ends - counts
    ranks = jnp.arange(CAP, dtype=jnp.int32)
    target = jnp.sum((ends[:, None, :] <= ranks[None, :, None]).astype(jnp.int32), axis=2)
    offset_in_pair = ranks[None, :] - jnp.take_along_axis(starts, target, axis=1)
    before = jnp.cumsum(counts, axis=0) - counts
    arrival = jnp.take_along_axis(before, target, axis=1) + offset_in_pair
    slot_perm = jax.vmap(lambda sub: jax.random.permutation(sub, CAP))(jax.random.split(keys[3], N_DP)).astype(jnp.int32)
    slot = slot_perm[target, arrival]
    row_perm = jax.vmap(lambda sub: jax.random.permutation(sub, CAP))(jax.random.split(keys[4], N_DP)).astype(jnp.int32)
    source = jnp.arange(N_DP, dtype=jnp.int32)[:, None]
    flat = jnp.zeros((N_DP * CAP,), jnp.int32)
    return flat.at[(source * CAP + row_perm).reshape(-1)].set((target * CAP + slot).reshape(-1))


def draw_dest_slot(key, part):
    return route_table(jax.random.fold_in(key, 11))


def draw_return_slot(key, part):
    return route_table(jax.random.fold_in(key, 23))


def draw_lengths(key, part):
    keys = jax.random.split(key, 3)
    stretches = CAP // STRETCH
    numbers = jnp.arange(stretches, dtype=jnp.int32)
    begins = jax.random.randint(keys[0], (N_DP, stretches), 0, 2)
    single = jax.random.randint(keys[1], (), 0, N_DP)
    group_ids = jnp.arange(N_DP, dtype=jnp.int32)[:, None]
    begins = jnp.where(numbers[None, :] == 0, 1, jnp.where(group_ids == single, 0, begins))
    following = jnp.where((begins[:, None, :] > 0) & (numbers[None, None, :] > numbers[None, :, None]), numbers[None, None, :], stretches)
    span = jnp.min(following, axis=2) - numbers[None, :]
    upper = span * STRETCH
    lower = jnp.maximum(1, upper - 3 * STRETCH // 2)
    drawn = jax.random.randint(keys[2], (N_DP, stretches), lower, upper + 1)
    drawn = jnp.where(group_ids == single, jnp.where(numbers[None, :] == 0, CAP, 0), drawn)
    return jnp.where(begins > 0, drawn, 0).astype(jnp.int32)


def shard_levels(rng, shape, cuts, smallest, top_value):
    loudness, own = 1.0, jax.random.fold_in(rng, 6)
    for dim, shards_of in cuts:
        steps = jnp.exp(jax.random.uniform(jax.random.fold_in(own, dim), (shards_of,), jnp.float32, smallest / len(cuts), top_value / len(cuts)))
        loudness = loudness * jnp.repeat(steps, shape[dim] // shards_of).reshape([-1 if axis == dim else 1 for axis in range(len(shape))])
    return loudness


def gaussian(stream_key, extent, scale, limit, cuts=(), kind=jnp.bfloat16):
    array = scale * jax.random.normal(stream_key, extent, jnp.float32)
    if cuts:
        array = array * shard_levels(stream_key, extent, cuts, -0.22, 0.18)
    return jnp.clip(array, -limit, limit).astype(kind)


def setup_inputs(seed: int = 0) -> dict:
    key_list = jax.random.split(jax.random.key(seed), 19)
    block_in = gaussian(key_list[0], (TOKENS, D), 1.0, 6.0, ((0, 16), (1, 2)))
    cotangent = gaussian(key_list[1], (TOKENS, D), 1.0, 6.0, ((0, 16), (1, 2)))
    lengths = draw_lengths(jax.random.fold_in(key_list[18], 71), 0)
    dest_slot = draw_dest_slot(jax.random.fold_in(key_list[18], 71), 0)
    return_slot = draw_return_slot(jax.random.fold_in(key_list[18], 71), 0)
    norm_gain = jnp.clip(1.0 + 0.1 * jax.random.normal(key_list[5], (D,), jnp.float32), 0.5, 1.5)
    inner_weight = gaussian(key_list[6], (D, 2, INNER), D ** -0.5, 0.15625, ((2, 2),))
    state_weight = gaussian(key_list[7], (D, 2 * STATE), D ** -0.5, 0.15625)
    step_weight = gaussian(key_list[8], (D, HEADS), D ** -0.5, 0.15625, ((1, 2),))
    conv_inner = gaussian(key_list[9], (CONV, INNER), CONV ** -0.5, 3.0, ((1, 2),), jnp.float32)
    conv_inner_bias = gaussian(key_list[10], (INNER,), 0.5, 3.0, ((0, 2),), jnp.float32)
    conv_state = gaussian(key_list[11], (CONV, 2 * STATE), CONV ** -0.5, 3.0, (), jnp.float32)
    conv_state_bias = gaussian(key_list[12], (2 * STATE,), 0.5, 3.0, (), jnp.float32)
    step_bias = jnp.clip(-7.0 + 5.0 * jax.random.uniform(key_list[13], (HEADS,), jnp.float32) ** shard_levels(key_list[13], (HEADS,), ((0, 2),), -0.2, 0.2), -7.0, -2.0)
    log_rate = jnp.clip(2.77 * jax.random.uniform(key_list[14], (HEADS,), jnp.float32) ** shard_levels(key_list[14], (HEADS,), ((0, 2),), -0.2, 0.2), 0.0, 2.77)
    skip_gain = jnp.clip(0.5 + 1.5 * jax.random.uniform(key_list[15], (HEADS,), jnp.float32) ** shard_levels(key_list[15], (HEADS,), ((0, 2),), -0.2, 0.2), 0.5, 2.0)
    gate_gain = jnp.clip(1.0 + 0.1 * jax.random.normal(key_list[16], (INNER,), jnp.float32), 0.5, 1.5)
    out_weight = gaussian(key_list[17], (INNER, D), INNER ** -0.5, 0.109375, ((0, 2),))
    return {"block_in": block_in, "cotangent": cotangent, "lengths": lengths, "dest_slot": dest_slot, "return_slot": return_slot, "norm_gain": norm_gain, "inner_weight": inner_weight, "state_weight": state_weight, "step_weight": step_weight, "conv_inner": conv_inner, "conv_inner_bias": conv_inner_bias, "conv_state": conv_state, "conv_state_bias": conv_state_bias, "step_bias": step_bias, "log_rate": log_rate, "skip_gain": skip_gain, "gate_gain": gate_gain, "out_weight": out_weight}


PRECISE = lax.Precision.HIGHEST
EPSILON = 1e-05

@jax.custom_vjp
def low(v):
    return lax.optimization_barrier(v.astype(jnp.bfloat16)).astype(jnp.float32)

@jax.custom_vjp
def low_back(v):
    return v

def low_keep(v):
    return (low(v), None)

def low_pass(kept, grad):
    return (grad,)

def back_keep(v):
    return (v, None)

def back_low(kept, grad):
    return (low(grad),)
low.defvjp(low_keep, low_pass)
low_back.defvjp(back_keep, back_low)

def stretch_layout(seq_lengths, stretch_rows):
    total_stretches = seq_lengths.shape[0]
    numbers = jnp.arange(total_stretches, dtype=jnp.int32)
    begins = seq_lengths > 0
    first_stretch = lax.optimization_barrier(jnp.max(jnp.where(begins[None, :] & (numbers[None, :] <= numbers[:, None]), numbers[None, :], 0), axis=1))
    seq_length = lax.optimization_barrier(jnp.sum(jnp.where(numbers[None, :] == first_stretch[:, None], seq_lengths[None, :], 0), axis=1))
    within = jnp.arange(stretch_rows, dtype=jnp.int32)[None, :] + ((numbers - first_stretch) * stretch_rows)[:, None]
    live_mask = (within < seq_length[:, None]).astype(jnp.float32).reshape(-1)
    keep_state = 1.0 - begins.astype(jnp.float32)
    return (within.reshape(-1), live_mask, keep_state)

def shift_down(values, steps):
    return jnp.concatenate([jnp.zeros((steps,) + values.shape[1:], values.dtype), values[:-steps]], axis=0)

def conv_forward(raw_in, tap_weights, tap_bias, seq_pos):
    total = tap_bias[None, :] + tap_weights[0][None, :] * raw_in
    for tap_index in range(1, tap_weights.shape[0]):
        valid = (seq_pos >= tap_index).astype(jnp.float32)[:, None]
        total = total + tap_weights[tap_index][None, :] * shift_down(raw_in, tap_index) * valid
    return total

def state_mix(x_heads, written, readout, step_size, decay_rate, skip_gain, keep_state):
    rows_all, heads, head_dim = x_heads.shape
    stretches = rows_all // STRETCH
    x_blocks = x_heads.reshape(stretches, STRETCH, heads, head_dim)
    w_blocks = written.reshape(stretches, STRETCH, -1)
    r_blocks = readout.reshape(stretches, STRETCH, -1)
    step_blocks = step_size.reshape(stretches, STRETCH, heads)
    log_decay = jnp.cumsum(step_blocks * decay_rate[None, None, :], axis=1)
    causal = (jnp.arange(STRETCH)[:, None] >= jnp.arange(STRETCH)[None, :])[None, :, :, None]
    spread = log_decay[:, :, None, :] - log_decay[:, None, :, :]
    fading = jnp.where(causal, jnp.exp(jnp.where(causal, spread, 0.0)), 0.0)
    intersection = jnp.einsum('cin,cjn->cij', r_blocks, w_blocks, precision=PRECISE)
    mixing = intersection[:, :, :, None] * fading
    driven = step_blocks[..., None] * x_blocks
    result = jnp.einsum('cijh,cjhp->cihp', mixing, driven, precision=PRECISE)
    to_end = jnp.exp(log_decay[:, -1:, :] - log_decay)
    stretch_state = jnp.einsum('cjhp,cjn->chpn', to_end[..., None] * driven, w_blocks, precision=PRECISE)
    end_fade = jnp.exp(log_decay[:, -1, :])
    running = jnp.zeros(stretch_state.shape[1:], jnp.float32)
    entering = []
    for number in range(stretches):
        entering.append(running)
        if number + 1 < stretches:
            running = keep_state[number + 1] * (end_fade[number][:, None, None] * running + stretch_state[number])
    entering = jnp.stack(entering)
    result = result + jnp.exp(log_decay)[..., None] * jnp.einsum('chpn,cin->cihp', entering, r_blocks, precision=PRECISE)
    result = result + skip_gain[None, None, :, None] * x_blocks
    return result.reshape(rows_all, heads * head_dim)

def group_forward(params, hidden, seq_lengths):
    norm_gain, inner_weight, state_weight, step_weight, conv_inner, conv_inner_bias, conv_state, conv_state_bias, step_bias, log_rate, skip_gain, gate_gain, out_weight = params
    seq_pos, live_mask, keep_state = stretch_layout(seq_lengths, STRETCH)
    norm_scale = lax.rsqrt(lax.optimization_barrier(jnp.mean(hidden * hidden, axis=1, keepdims=True)) + EPSILON)
    normed = low(hidden * norm_scale * norm_gain)
    gate_raw = low_back(jnp.dot(normed, inner_weight[:, 0, :], precision=PRECISE, preferred_element_type=jnp.float32))
    conv_in_x = low_back(jnp.dot(normed, inner_weight[:, 1, :], precision=PRECISE, preferred_element_type=jnp.float32))
    conv_in_state = low_back(jnp.dot(normed, state_weight, precision=PRECISE, preferred_element_type=jnp.float32))
    step_raw = low_back(jnp.dot(normed, step_weight, precision=PRECISE, preferred_element_type=jnp.float32))
    x_act = jax.nn.silu(conv_forward(conv_in_x, conv_inner, conv_inner_bias, seq_pos))
    state_act = jax.nn.silu(conv_forward(conv_in_state, conv_state, conv_state_bias, seq_pos))
    step_size = jax.nn.softplus(step_raw + step_bias) * live_mask[:, None]
    decay_rate = -jnp.exp(log_rate)
    mixed = state_mix(x_act.reshape(CAP, HEADS, HEAD_DIM), state_act[:, :STATE], state_act[:, STATE:], step_size, decay_rate, skip_gain, keep_state)
    gated = mixed * jax.nn.silu(gate_raw)
    gate_scale = lax.rsqrt(lax.optimization_barrier(jnp.mean(gated * gated, axis=1, keepdims=True)) + EPSILON)
    gate_normed = low(gated * gate_scale * gate_gain)
    branch = low_back(jnp.dot(gate_normed, out_weight, precision=PRECISE, preferred_element_type=jnp.float32))
    return hidden + live_mask[:, None] * branch

def reference(block_in, cotangent, lengths, dest_slot, return_slot, norm_gain, inner_weight, state_weight, step_weight, conv_inner, conv_inner_bias, conv_state, conv_state_bias, step_bias, log_rate, skip_gain, gate_gain, out_weight):
    params = tuple((member.astype(jnp.float32) for member in (norm_gain, inner_weight, state_weight, step_weight, conv_inner, conv_inner_bias, conv_state, conv_state_bias, step_bias, log_rate, skip_gain, gate_gain, out_weight)))
    owner_rows = jnp.zeros((TOKENS, D), jnp.float32).at[dest_slot].set(block_in.astype(jnp.float32))
    owner_ct = jnp.zeros((TOKENS, D), jnp.float32).at[return_slot].set(cotangent.astype(jnp.float32))

    def forward(weights, placed):

        def one_group(pieces):
            return jax.checkpoint(group_forward)(weights, pieces[0], pieces[1])
        return lax.map(one_group, (placed.reshape(N_DP, CAP, D), lengths)).reshape(TOKENS, D)
    result, pullback = jax.vjp(forward, params, owner_rows)
    weight_grads, row_grads = pullback(owner_ct)
    norm_gain_grad, inner_weight_grad, state_weight_grad, step_weight_grad, conv_inner_grad, conv_inner_bias_grad, conv_state_grad, conv_state_bias_grad, step_bias_grad, log_rate_grad, skip_gain_grad, gate_gain_grad, out_weight_grad = weight_grads
    block_out = result.astype(jnp.bfloat16)[return_slot]
    input_grad = row_grads.astype(jnp.bfloat16)[dest_slot]
    return (block_out, input_grad, norm_gain_grad, inner_weight_grad, state_weight_grad, step_weight_grad, conv_inner_grad, conv_inner_bias_grad, conv_state_grad, conv_state_bias_grad, step_bias_grad, log_rate_grad, skip_gain_grad, gate_gain_grad, out_weight_grad)
```

```python
import jax
import jax.numpy as jnp
from jax import lax
from jax.sharding import PartitionSpec as P

STRETCH = 256


PRECISE = lax.Precision.HIGHEST
EPSILON = 1e-05


def silu_slope(values):
    logistic = jax.nn.sigmoid(values)
    return logistic * (1.0 + values * (1.0 - logistic))


def stretch_layout(seq_lengths, stretch_rows):
    total_stretches = seq_lengths.shape[0]
    numbers = jnp.arange(total_stretches, dtype=jnp.int32)
    begins = seq_lengths > 0
    first_stretch = jnp.max(
        jnp.where(begins[None, :] & (numbers[None, :] <= numbers[:, None]), numbers[None, :], 0),
        axis=1,
    )
    seq_length = jnp.sum(
        jnp.where(numbers[None, :] == first_stretch[:, None], seq_lengths[None, :], 0), axis=1
    )
    within = (
        jnp.arange(stretch_rows, dtype=jnp.int32)[None, :]
        + ((numbers - first_stretch) * stretch_rows)[:, None]
    )
    live_mask = (within < seq_length[:, None]).astype(jnp.float32).reshape(-1)
    keep_state = 1.0 - begins.astype(jnp.float32)
    return (within.reshape(-1), live_mask, keep_state)


def shift_down(values, steps):
    return jnp.concatenate(
        [jnp.zeros((steps,) + values.shape[1:], values.dtype), values[:-steps]], axis=0
    )


def shift_up(values, steps):
    return jnp.concatenate(
        [values[steps:], jnp.zeros((steps,) + values.shape[1:], values.dtype)], axis=0
    )


def conv_forward(raw_in, tap_weights, tap_bias, seq_pos):
    total = tap_bias[None, :] + tap_weights[0][None, :] * raw_in
    for tap_index in range(1, tap_weights.shape[0]):
        valid = (seq_pos >= tap_index).astype(jnp.float32)[:, None]
        total = total + tap_weights[tap_index][None, :] * shift_down(raw_in, tap_index) * valid
    return total


def conv_backward(raw_in, tap_weights, seq_pos, conv_grad):
    tap_grads = [jnp.sum(conv_grad * raw_in, axis=0)]
    raw_grad = tap_weights[0][None, :] * conv_grad
    for tap_index in range(1, tap_weights.shape[0]):
        masked = conv_grad * (seq_pos >= tap_index).astype(jnp.float32)[:, None]
        tap_grads.append(jnp.sum(masked * shift_down(raw_in, tap_index), axis=0))
        raw_grad = raw_grad + tap_weights[tap_index][None, :] * shift_up(masked, tap_index)
    return (raw_grad, jnp.stack(tap_grads, axis=0), jnp.sum(conv_grad, axis=0))


def send_layout(targets, group_rows, capacity, groups):
    owner_group = targets // group_rows
    onehot = (owner_group[:, None] == jnp.arange(groups, dtype=jnp.int32)[None, :]).astype(
        jnp.int32
    )
    arrival = jnp.sum(jnp.cumsum(onehot, axis=0) * onehot, axis=1) - 1
    return owner_group * capacity + arrival


def arrivals(targets, group_rows, capacity, groups, own_group):
    by_source = targets.reshape(groups, group_rows)
    owner_group = by_source // group_rows
    is_mine = (owner_group == own_group).astype(jnp.int32)
    arrival = jnp.cumsum(is_mine, axis=1) - 1
    position = jnp.arange(groups, dtype=jnp.int32)[:, None] * capacity + arrival
    position = jnp.where(is_mine > 0, position, groups * capacity)
    filler = jnp.full((groups * capacity,), group_rows, jnp.int32)
    return filler.at[position.reshape(-1)].set(
        (by_source - owner_group * group_rows).reshape(-1), mode="drop"
    )


def state_forward(x_heads, written, readout, step_size, decay_rate, stretch_rows):
    rows_all, heads, head_dim = x_heads.shape
    stretches = rows_all // stretch_rows
    x_blocks = x_heads.reshape(stretches, stretch_rows, heads, head_dim)
    w_blocks = written.reshape(stretches, stretch_rows, -1)
    r_blocks = readout.reshape(stretches, stretch_rows, -1)
    step_blocks = step_size.reshape(stretches, stretch_rows, heads)
    log_decay = jnp.cumsum(step_blocks * decay_rate[None, None, :], axis=1)
    by_head = jnp.transpose(log_decay, (0, 2, 1))
    causal = jnp.arange(stretch_rows)[:, None] >= jnp.arange(stretch_rows)[None, :]
    spread = by_head[:, :, :, None] - by_head[:, :, None, :]
    fading = jnp.where(causal, jnp.exp(jnp.where(causal, spread, 0.0)), 0.0)
    intersection = jnp.einsum("cin,cjn->cij", r_blocks, w_blocks, precision=PRECISE)
    mixing = intersection[:, None, :, :] * fading
    driven = step_blocks[..., None] * x_blocks
    to_end = jnp.exp(log_decay[:, -1:, :] - log_decay)
    stretch_state = jnp.einsum(
        "cjhp,cjn->chpn", to_end[..., None] * driven, w_blocks, precision=PRECISE
    )
    end_fade = jnp.exp(log_decay[:, -1, :])
    running = jnp.zeros(stretch_state.shape[1:], jnp.float32)
    entering = []
    entering.append(running)
    entering = jnp.stack(entering)
    from_start = jnp.exp(log_decay)
    carried_out = from_start[..., None] * jnp.einsum(
        "chpn,cin->cihp", entering, r_blocks, precision=PRECISE
    )
    inner_out = jnp.einsum("chij,cjhp->cihp", mixing, driven, precision=PRECISE)
    saved = (
        x_blocks,
        w_blocks,
        r_blocks,
        step_blocks,
        causal,
        fading,
        mixing,
        driven,
        to_end,
        entering,
        end_fade,
        from_start,
        carried_out,
    )
    return ((inner_out + carried_out).reshape(rows_all, heads * head_dim), saved)


def state_backward(saved, mixed_grad, decay_rate):
    (
        x_blocks,
        w_blocks,
        r_blocks,
        step_blocks,
        causal,
        fading,
        mixing,
        driven,
        to_end,
        entering,
        end_fade,
        from_start,
        carried_out,
    ) = saved
    stretches = x_blocks.shape[0]
    scaled = from_start[..., None] * mixed_grad
    readout_grad = jnp.einsum("cihp,chpn->cin", scaled, entering, precision=PRECISE)
    from_out = jnp.einsum("cihp,cin->chpn", scaled, r_blocks, precision=PRECISE)
    decay_grad = jnp.sum(carried_out * mixed_grad, axis=3)
    downstream = jnp.zeros(from_out.shape[1:], jnp.float32)
    passed = []
    end_grads = []
    for number in reversed(range(stretches)):
        handed = jnp.zeros_like(downstream)
        passed.append(handed)
        end_grads.append(jnp.sum(handed * entering[number], axis=(1, 2)))
        downstream = from_out[number] + end_fade[number][:, None, None] * handed
    passed = jnp.stack(passed[::-1])
    end_grads = jnp.stack(end_grads[::-1])
    pulled = jnp.einsum("chpn,cjn->cjhp", passed, w_blocks, precision=PRECISE)
    driven_grad = to_end[..., None] * pulled
    written_grad = jnp.einsum(
        "cjhp,chpn->cjn", to_end[..., None] * driven, passed, precision=PRECISE
    )
    tail_grad = jnp.sum(pulled * driven, axis=3) * to_end
    decay_grad = decay_grad - tail_grad
    last_extra = jnp.sum(tail_grad, axis=1) + end_grads * end_fade
    mixing_grad = jnp.where(
        causal, jnp.einsum("cihp,cjhp->chij", mixed_grad, driven, precision=PRECISE), 0.0
    )
    driven_grad = driven_grad + jnp.einsum("chij,cihp->cjhp", mixing, mixed_grad, precision=PRECISE)
    intersection_grad = jnp.sum(mixing_grad * fading, axis=1)
    readout_grad = readout_grad + jnp.einsum(
        "cij,cjn->cin", intersection_grad, w_blocks, precision=PRECISE
    )
    written_grad = written_grad + jnp.einsum(
        "cij,cin->cjn", intersection_grad, r_blocks, precision=PRECISE
    )
    product = mixing_grad * mixing
    decay_grad = decay_grad + jnp.transpose(
        jnp.sum(product, axis=3) - jnp.sum(product, axis=2), (0, 2, 1)
    )
    decay_grad = decay_grad.at[:, -1, :].add(last_extra)
    step_grad = jnp.sum(driven_grad * x_blocks, axis=3)
    x_state_grad = step_blocks[..., None] * driven_grad
    rate_grad = jnp.flip(jnp.cumsum(jnp.flip(decay_grad, axis=1), axis=1), axis=1)
    step_grad = step_grad + rate_grad * decay_rate[None, None, :]
    rate_total = jnp.sum(rate_grad * step_blocks, axis=(0, 1))
    return (x_state_grad, written_grad, readout_grad, step_grad, rate_total)


def on_device(
    block_in,
    cotangent,
    lengths,
    dest_slot,
    return_slot,
    norm_gain,
    inner_weight,
    state_weight,
    step_weight,
    conv_inner,
    conv_inner_bias,
    conv_state,
    conv_state_bias,
    step_bias,
    log_rate,
    skip_gain,
    gate_gain,
    out_weight,
):
    groups = lax.axis_size("dp")
    group_rows = block_in.shape[0]
    half_width = block_in.shape[1]
    capacity = 2 * group_rows // groups
    own_group = lax.axis_index("dp")
    own_dest = lax.dynamic_slice_in_dim(dest_slot, own_group * group_rows, group_rows)
    own_return = lax.dynamic_slice_in_dim(return_slot, own_group * group_rows, group_rows)
    send_spot = send_layout(own_dest, group_rows, capacity, groups)
    back_spot = send_layout(own_return, group_rows, capacity, groups)
    slots_in = arrivals(dest_slot, group_rows, capacity, groups, own_group)
    slots_back = arrivals(return_slot, group_rows, capacity, groups, own_group)
    blank_rows = jnp.zeros((groups * capacity, half_width), jnp.bfloat16)
    packed_rows = blank_rows.at[send_spot].set(block_in).reshape(groups, capacity, half_width)
    packed_grads = blank_rows.at[back_spot].set(cotangent).reshape(groups, capacity, half_width)
    came_rows, came_grads = (
        lax.all_to_all(packed_rows, "dp", split_axis=0, concat_axis=0, tiled=True),
        lax.all_to_all(packed_grads, "dp", split_axis=0, concat_axis=0, tiled=True),
    )
    empty_rows = jnp.zeros((group_rows, half_width), jnp.bfloat16)
    own_rows = empty_rows.at[slots_in].set(came_rows.reshape(-1, half_width), mode="drop")
    own_grads = empty_rows.at[slots_back].set(came_grads.reshape(-1, half_width), mode="drop")
    full_rows, full_grads = (
        lax.all_gather(own_rows, "tensor", axis=1, tiled=True),
        lax.all_gather(own_grads, "tensor", axis=1, tiled=True),
    )
    seq_pos, live_mask, keep_state = stretch_layout(lengths[0], STRETCH)
    live_col = live_mask[:, None]
    hidden = full_rows.astype(jnp.float32)
    norm_scale = lax.rsqrt(jnp.mean(hidden * hidden, axis=1, keepdims=True) + EPSILON)
    normed = (hidden * norm_scale * norm_gain).astype(jnp.bfloat16)
    inner_local = inner_weight.shape[2]
    zx_weight = inner_weight.reshape(inner_weight.shape[0], 2 * inner_local)
    projected = jnp.dot(normed, zx_weight, preferred_element_type=jnp.float32)
    gate_raw = projected[:, :inner_local]
    conv_in_x = projected[:, inner_local:]
    conv_in_state = jnp.dot(normed, state_weight, preferred_element_type=jnp.float32)
    step_raw = jnp.dot(normed, step_weight, preferred_element_type=jnp.float32)
    x_conv = conv_forward(conv_in_x, conv_inner, conv_inner_bias, seq_pos)
    state_conv = conv_forward(conv_in_state, conv_state, conv_state_bias, seq_pos)
    x_act = jax.nn.silu(x_conv)
    state_act = jax.nn.silu(state_conv)
    state_width = state_act.shape[1] // 2
    heads_local = step_weight.shape[1]
    head_dim = inner_local // heads_local
    stretches = group_rows // STRETCH
    step_input = step_raw + step_bias[None, :]
    step_size = jax.nn.softplus(step_input) * live_col
    decay_rate = -jnp.exp(log_rate)
    skip_wide = jnp.repeat(skip_gain, head_dim)[None, :]
    scanned, saved = state_forward(
        x_act.reshape(group_rows, heads_local, head_dim),
        state_act[:, :state_width],
        state_act[:, state_width:],
        step_size,
        decay_rate,
        STRETCH,
    )
    mixed = scanned + skip_wide * x_act
    gate_act = jax.nn.silu(gate_raw)
    gated = mixed * gate_act
    inner_total = inner_local * lax.axis_size("tensor")
    square_sum = lax.psum(jnp.sum(gated * gated, axis=1), "tensor")
    gate_scale = lax.rsqrt(square_sum / inner_total + EPSILON)[:, None]
    gate_normed = (gated * gate_scale * gate_gain).astype(jnp.bfloat16)
    partial_out = jnp.dot(gate_normed, out_weight, preferred_element_type=jnp.float32)
    branch_half = lax.psum_scatter(partial_out, "tensor", scatter_dimension=1, tiled=True)
    half_index = lax.axis_index("tensor")
    out_half = (own_rows.astype(jnp.float32) + live_col * branch_half).astype(jnp.bfloat16)
    zero_row = jnp.zeros((1, half_width), jnp.bfloat16)
    reply_rows = jnp.concatenate([out_half, zero_row], axis=0)[slots_back]
    returned = lax.all_to_all(
        reply_rows.reshape(groups, capacity, half_width),
        "dp",
        split_axis=0,
        concat_axis=0,
        tiled=True,
    )
    block_out = returned.reshape(-1, half_width)[back_spot]
    owner_ct = full_grads.astype(jnp.float32)
    out_grad = (owner_ct * live_col).astype(jnp.bfloat16)
    out_weight_grad = jnp.einsum(
        "ti,td->id", gate_normed, out_grad, preferred_element_type=jnp.float32
    )
    normed_out_grad = jnp.einsum(
        "td,id->ti", out_grad, out_weight, preferred_element_type=jnp.float32
    )
    gate_gain_grad = jnp.sum(normed_out_grad * gated * gate_scale, axis=0)
    scaled_grad = gate_gain * normed_out_grad
    cross = lax.psum(jnp.sum(gated * scaled_grad, axis=1), "tensor")[:, None]
    gated_grad = gate_scale * scaled_grad - gated * gate_scale**3 * cross / inner_total
    mixed_grad = gated_grad * gate_act
    gate_raw_grad = gated_grad * mixed * silu_slope(gate_raw)
    skip_gain_grad = jnp.sum(
        (mixed_grad * x_act).reshape(group_rows, heads_local, head_dim), axis=(0, 2)
    )
    x_state_grad, written_grad, readout_grad, step_grad, rate_total = state_backward(
        saved, mixed_grad.reshape(stretches, STRETCH, heads_local, head_dim), decay_rate
    )
    x_act_grad = x_state_grad.reshape(group_rows, inner_local) + skip_wide * mixed_grad
    state_grad = lax.psum(
        jnp.concatenate(
            [written_grad.reshape(group_rows, -1), readout_grad.reshape(group_rows, -1)], axis=1
        ),
        "tensor",
    )
    state_conv_grad = state_grad * silu_slope(state_conv)
    x_conv_grad = x_act_grad * silu_slope(x_conv)
    state_raw_grad, conv_state_grad, conv_state_bias_grad = conv_backward(
        conv_in_state, conv_state, seq_pos, state_conv_grad
    )
    x_raw_grad, conv_inner_grad, conv_inner_bias_grad = conv_backward(
        conv_in_x, conv_inner, seq_pos, x_conv_grad
    )
    step_raw_grad = (
        step_grad.reshape(group_rows, heads_local) * live_col * jax.nn.sigmoid(step_input)
    )
    step_bias_grad = jnp.sum(step_raw_grad, axis=0)
    log_rate_grad = rate_total * decay_rate
    zx_low = jnp.concatenate([gate_raw_grad, x_raw_grad], axis=1).astype(jnp.bfloat16)
    state_low = state_raw_grad.astype(jnp.bfloat16)
    step_low = step_raw_grad.astype(jnp.bfloat16)
    inner_weight_grad = jnp.einsum(
        "td,tk->dk", normed, zx_low, preferred_element_type=jnp.float32
    )
    state_weight_grad = jnp.einsum(
        "td,tk->dk", normed, state_low, preferred_element_type=jnp.float32
    )
    step_weight_grad = jnp.einsum("td,tk->dk", normed, step_low, preferred_element_type=jnp.float32)
    lead_share = (half_index == 0).astype(jnp.float32)
    normed_grad = jnp.einsum("tk,dk->td", zx_low, zx_weight, preferred_element_type=jnp.float32)
    normed_grad = normed_grad + jnp.einsum(
        "tk,dk->td", step_low, step_weight, preferred_element_type=jnp.float32
    )
    normed_grad = normed_grad + lead_share * jnp.einsum(
        "tk,dk->td", state_low, state_weight, preferred_element_type=jnp.float32
    )
    normed_grad = lax.psum(normed_grad, "tensor")
    norm_gain_grad = jnp.sum(normed_grad * hidden * norm_scale, axis=0)
    input_scaled = norm_gain * normed_grad
    hidden_grad = (
        norm_scale * input_scaled
        - hidden * norm_scale**3 * jnp.mean(hidden * input_scaled, axis=1, keepdims=True)
        + owner_ct
    )
    own_grad = lax.dynamic_slice_in_dim(hidden_grad, half_index * half_width, half_width, 1).astype(
        jnp.bfloat16
    )
    answer_rows = jnp.concatenate([own_grad, zero_row], axis=0)[slots_in]
    gone = lax.all_to_all(
        answer_rows.reshape(groups, capacity, half_width),
        "dp",
        split_axis=0,
        concat_axis=0,
        tiled=True,
    )
    input_grad = gone.reshape(-1, half_width)[send_spot]
    (
        conv_inner_grad,
        conv_inner_bias_grad,
        conv_state_grad,
        conv_state_bias_grad,
        step_bias_grad,
        log_rate_grad,
        skip_gain_grad,
        gate_gain_grad,
    ) = lax.psum(
        (
            conv_inner_grad,
            conv_inner_bias_grad,
            conv_state_grad,
            conv_state_bias_grad,
            step_bias_grad,
            log_rate_grad,
            skip_gain_grad,
            gate_gain_grad,
        ),
        "dp",
    )
    zx_share, state_share, step_share, gain_share, out_share = (
        lax.psum_scatter(inner_weight_grad.astype(jnp.bfloat16), "dp", scatter_dimension=0, tiled=True),
        lax.psum_scatter(state_weight_grad, "dp", scatter_dimension=0, tiled=True),
        lax.psum_scatter(step_weight_grad, "dp", scatter_dimension=0, tiled=True),
        lax.psum_scatter(norm_gain_grad, "dp", scatter_dimension=0, tiled=True),
        lax.psum_scatter(out_weight_grad.astype(jnp.bfloat16), "dp", scatter_dimension=1, tiled=True),
    )
    zx_share = zx_share.astype(jnp.float32).reshape((-1,) + inner_weight.shape[1:])
    out_share = out_share.astype(jnp.float32)
    return (
        block_out,
        input_grad,
        gain_share,
        zx_share,
        state_share,
        step_share,
        conv_inner_grad,
        conv_inner_bias_grad,
        conv_state_grad,
        conv_state_bias_grad,
        step_bias_grad,
        log_rate_grad,
        skip_gain_grad,
        gate_gain_grad,
        out_share,
    )


def solution(mesh):
    placed = (
        P("dp", "tensor"),
        P("dp", "tensor"),
        P("dp", None),
        P(),
        P(),
        P(),
        P(None, None, "tensor"),
        P(),
        P(None, "tensor"),
        P(None, "tensor"),
        P("tensor"),
        P(),
        P(),
        P("tensor"),
        P("tensor"),
        P("tensor"),
        P("tensor"),
        P("tensor", None),
    )
    return jax.shard_map(
        on_device,
        mesh=mesh,
        in_specs=placed,
        out_specs=(
            P("dp", "tensor"),
            P("dp", "tensor"),
            P("dp"),
            P("dp", None, "tensor"),
            P("dp", None),
            P("dp", "tensor"),
            P(None, "tensor"),
            P("tensor"),
            P(),
            P(),
            P("tensor"),
            P("tensor"),
            P("tensor"),
            P("tensor"),
            P("tensor", "dp"),
        ),
        check_vma=False,
    )
```

```python
import functools

import jax
import jax.numpy as jnp
from jax import lax
from jax.experimental import pallas as pl
from jax.experimental.pallas import tpu as pltpu
from jax.sharding import PartitionSpec as P

STRETCH = 256


PRECISE = lax.Precision.HIGHEST
EPSILON = 1e-05


def silu_slope(values):
    logistic = jax.nn.sigmoid(values)
    return logistic * (1.0 + values * (1.0 - logistic))


def stretch_layout(seq_lengths, stretch_rows):
    total_stretches = seq_lengths.shape[0]
    numbers = jnp.arange(total_stretches, dtype=jnp.int32)
    begins = seq_lengths > 0
    first_stretch = jnp.max(
        jnp.where(begins[None, :] & (numbers[None, :] <= numbers[:, None]), numbers[None, :], 0),
        axis=1,
    )
    seq_length = jnp.sum(
        jnp.where(numbers[None, :] == first_stretch[:, None], seq_lengths[None, :], 0), axis=1
    )
    within = (
        jnp.arange(stretch_rows, dtype=jnp.int32)[None, :]
        + ((numbers - first_stretch) * stretch_rows)[:, None]
    )
    live_mask = (within < seq_length[:, None]).astype(jnp.float32).reshape(-1)
    keep_state = 1.0 - begins.astype(jnp.float32)
    return (within.reshape(-1), live_mask, keep_state)


def shift_down(values, steps):
    return jnp.concatenate(
        [jnp.zeros((steps,) + values.shape[1:], values.dtype), values[:-steps]], axis=0
    )


def shift_up(values, steps):
    return jnp.concatenate(
        [values[steps:], jnp.zeros((steps,) + values.shape[1:], values.dtype)], axis=0
    )


def conv_forward(raw_in, tap_weights, tap_bias, seq_pos):
    total = tap_bias[None, :] + tap_weights[0][None, :] * raw_in
    for tap_index in range(1, tap_weights.shape[0]):
        valid = (seq_pos >= tap_index).astype(jnp.float32)[:, None]
        total = total + tap_weights[tap_index][None, :] * shift_down(raw_in, tap_index) * valid
    return total


def conv_backward(raw_in, tap_weights, seq_pos, conv_grad):
    tap_grads = [jnp.sum(conv_grad * raw_in, axis=0)]
    raw_grad = tap_weights[0][None, :] * conv_grad
    for tap_index in range(1, tap_weights.shape[0]):
        masked = conv_grad * (seq_pos >= tap_index).astype(jnp.float32)[:, None]
        tap_grads.append(jnp.sum(masked * shift_down(raw_in, tap_index), axis=0))
        raw_grad = raw_grad + tap_weights[tap_index][None, :] * shift_up(masked, tap_index)
    return (raw_grad, jnp.stack(tap_grads, axis=0), jnp.sum(conv_grad, axis=0))


def send_layout(targets, group_rows, capacity, groups):
    owner_group = targets // group_rows
    onehot = (owner_group[:, None] == jnp.arange(groups, dtype=jnp.int32)[None, :]).astype(
        jnp.int32
    )
    arrival = jnp.sum(jnp.cumsum(onehot, axis=0) * onehot, axis=1) - 1
    return owner_group * capacity + arrival


def arrivals(targets, group_rows, capacity, groups, own_group):
    by_source = targets.reshape(groups, group_rows)
    owner_group = by_source // group_rows
    is_mine = (owner_group == own_group).astype(jnp.int32)
    arrival = jnp.cumsum(is_mine, axis=1) - 1
    position = jnp.arange(groups, dtype=jnp.int32)[:, None] * capacity + arrival
    position = jnp.where(is_mine > 0, position, groups * capacity)
    filler = jnp.full((groups * capacity,), group_rows, jnp.int32)
    return filler.at[position.reshape(-1)].set(
        (by_source - owner_group * group_rows).reshape(-1), mode="drop"
    )


def state_forward(x_heads, written, readout, step_size, decay_rate, stretch_rows):
    rows_all, heads, head_dim = x_heads.shape
    stretches = rows_all // stretch_rows
    x_blocks = x_heads.reshape(stretches, stretch_rows, heads, head_dim)
    w_blocks = written.reshape(stretches, stretch_rows, -1)
    r_blocks = readout.reshape(stretches, stretch_rows, -1)
    step_blocks = step_size.reshape(stretches, stretch_rows, heads)
    log_decay = jnp.cumsum(step_blocks * decay_rate[None, None, :], axis=1)
    by_head = jnp.transpose(log_decay, (0, 2, 1))
    causal = jnp.arange(stretch_rows)[:, None] >= jnp.arange(stretch_rows)[None, :]
    spread = by_head[:, :, :, None] - by_head[:, :, None, :]
    fading = jnp.where(causal, jnp.exp(jnp.where(causal, spread, 0.0)), 0.0)
    intersection = jnp.einsum("cin,cjn->cij", r_blocks, w_blocks, precision=PRECISE)
    mixing = intersection[:, None, :, :] * fading
    driven = step_blocks[..., None] * x_blocks
    to_end = jnp.exp(log_decay[:, -1:, :] - log_decay)
    stretch_state = jnp.einsum(
        "cjhp,cjn->chpn", to_end[..., None] * driven, w_blocks, precision=PRECISE
    )
    end_fade = jnp.exp(log_decay[:, -1, :])
    running = jnp.zeros(stretch_state.shape[1:], jnp.float32)
    entering = []
    entering.append(running)
    entering = jnp.stack(entering)
    from_start = jnp.exp(log_decay)
    carried_out = from_start[..., None] * jnp.einsum(
        "chpn,cin->cihp", entering, r_blocks, precision=PRECISE
    )
    inner_out = jnp.einsum("chij,cjhp->cihp", mixing, driven, precision=PRECISE)
    saved = (
        x_blocks,
        w_blocks,
        r_blocks,
        step_blocks,
        causal,
        fading,
        mixing,
        driven,
        to_end,
        entering,
        end_fade,
        from_start,
        carried_out,
    )
    return ((inner_out + carried_out).reshape(rows_all, heads * head_dim), saved)


def state_backward(saved, mixed_grad, decay_rate):
    (
        x_blocks,
        w_blocks,
        r_blocks,
        step_blocks,
        causal,
        fading,
        mixing,
        driven,
        to_end,
        entering,
        end_fade,
        from_start,
        carried_out,
    ) = saved
    stretches = x_blocks.shape[0]
    scaled = from_start[..., None] * mixed_grad
    readout_grad = jnp.einsum("cihp,chpn->cin", scaled, entering, precision=PRECISE)
    from_out = jnp.einsum("cihp,cin->chpn", scaled, r_blocks, precision=PRECISE)
    decay_grad = jnp.sum(carried_out * mixed_grad, axis=3)
    downstream = jnp.zeros(from_out.shape[1:], jnp.float32)
    passed = []
    end_grads = []
    for number in reversed(range(stretches)):
        handed = jnp.zeros_like(downstream)
        passed.append(handed)
        end_grads.append(jnp.sum(handed * entering[number], axis=(1, 2)))
        downstream = from_out[number] + end_fade[number][:, None, None] * handed
    passed = jnp.stack(passed[::-1])
    end_grads = jnp.stack(end_grads[::-1])
    pulled = jnp.einsum("chpn,cjn->cjhp", passed, w_blocks, precision=PRECISE)
    driven_grad = to_end[..., None] * pulled
    written_grad = jnp.einsum(
        "cjhp,chpn->cjn", to_end[..., None] * driven, passed, precision=PRECISE
    )
    tail_grad = jnp.sum(pulled * driven, axis=3) * to_end
    decay_grad = decay_grad - tail_grad
    last_extra = jnp.sum(tail_grad, axis=1) + end_grads * end_fade
    mixing_grad = jnp.where(
        causal, jnp.einsum("cihp,cjhp->chij", mixed_grad, driven, precision=PRECISE), 0.0
    )
    driven_grad = driven_grad + jnp.einsum("chij,cihp->cjhp", mixing, mixed_grad, precision=PRECISE)
    intersection_grad = jnp.sum(mixing_grad * fading, axis=1)
    readout_grad = readout_grad + jnp.einsum(
        "cij,cjn->cin", intersection_grad, w_blocks, precision=PRECISE
    )
    written_grad = written_grad + jnp.einsum(
        "cij,cin->cjn", intersection_grad, r_blocks, precision=PRECISE
    )
    product = mixing_grad * mixing
    decay_grad = decay_grad + jnp.transpose(
        jnp.sum(product, axis=3) - jnp.sum(product, axis=2), (0, 2, 1)
    )
    decay_grad = decay_grad.at[:, -1, :].add(last_extra)
    step_grad = jnp.sum(driven_grad * x_blocks, axis=3)
    x_state_grad = step_blocks[..., None] * driven_grad
    rate_grad = jnp.flip(jnp.cumsum(jnp.flip(decay_grad, axis=1), axis=1), axis=1)
    step_grad = step_grad + rate_grad * decay_rate[None, None, :]
    rate_total = jnp.sum(rate_grad * step_blocks, axis=(0, 1))
    return (x_state_grad, written_grad, readout_grad, step_grad, rate_total)


MESH = pl.DeviceIdType.MESH
BF = jnp.bfloat16
F32 = jnp.float32
NEG = -1e30


def dot_nn(a, b):
    return lax.dot_general(a, b, (((1,), (0,)), ((), ())), preferred_element_type=F32)


def dot_nt(a, b):
    return lax.dot_general(a, b, (((1,), (1,)), ((), ())), preferred_element_type=F32)


def dot_tn(a, b):
    return lax.dot_general(a, b, (((0,), (0,)), ((), ())), preferred_element_type=F32)


def iota(shape, axis):
    return lax.broadcasted_iota(jnp.int32, shape, axis)


def one_hot(cond):
    return jnp.where(cond, 1.0, 0.0).astype(BF)


def split3(v):
    high = v.astype(BF)
    rest = v - high.astype(F32)
    mid = rest.astype(BF)
    return high, mid, (rest - mid.astype(F32)).astype(BF)


def sigmoid(v):
    return 1.0 / (1.0 + jnp.exp(-v))


def rows_down(v, k):
    return jnp.where(iota(v.shape, 0) >= k, pltpu.roll(v, k, 0), 0.0)


def rows_up(v, k):
    n = v.shape[0]
    return jnp.where(iota(v.shape, 0) < n - k, pltpu.roll(v, n - k, 0), 0.0)


def pick(v, lane, index):
    return jnp.sum(jnp.where(lane == index, v, 0.0), axis=1, keepdims=True)


class Sizes:
    def __init__(self, dp, rows, half, inner, heads, state, capacity):
        self.dp, self.rows, self.half, self.inner = dp, rows, half, inner
        self.heads, self.state, self.cap = heads, state, capacity
        self.width = 2 * half
        self.nz = dp // 4
        self.share = self.width // dp
        self.quarter = self.nz * self.share
        self.slots = dp * capacity
        self.tiles = inner // 128
        self.extra = 2 * state + 128
        self.cols = 3 * inner + self.extra
        n = inner // 2
        self.chunks = [(i * n, n) for i in range(6)] + [(6 * n, self.extra)]
        self.levels = self.nz.bit_length() - 1


def send_table(targets, g, sz):
    strict = one_hot(iota((sz.rows, sz.rows), 0) < iota((sz.rows, sz.rows), 1))
    group = lax.shift_right_logical(targets[pl.ds(g, 1), :], 8)
    hot = jnp.where(iota((sz.dp, sz.rows), 0) == group, 1.0, 0.0)
    before = dot_nn(hot.astype(BF), strict)
    rank = jnp.sum(hot * before, axis=0, keepdims=True)
    spot = group.astype(F32) * sz.cap + rank
    return one_hot(iota((sz.slots, sz.rows), 0).astype(F32) == spot)


def owner_table(targets, g, sz):
    strict = one_hot(iota((sz.rows, sz.rows), 0) < iota((sz.rows, sz.rows), 1))
    every = targets[...]
    mine = jnp.where(lax.shift_right_logical(every, 8) == g, 1.0, 0.0)
    rank = dot_nn(mine.astype(BF), strict)
    slot = mine * ((every & 255) + 1).astype(F32)
    lane = iota((sz.dp, 128), 1)
    found = jnp.zeros((sz.dp, 128), F32)
    for a in range(sz.cap):
        one = jnp.sum(jnp.where(rank == float(a), slot, 0.0), axis=1, keepdims=True)
        found = jnp.where(lane == a, one, found)
    place = iota((128, sz.slots), 1)
    spread = one_hot((place % sz.cap) == iota((128, sz.slots), 0))
    wide = dot_nn(found.astype(BF), spread)
    keep = (iota((sz.dp, sz.slots), 1) // sz.cap) == iota((sz.dp, sz.slots), 0)
    row = jnp.sum(jnp.where(keep, wide, 0.0), axis=0, keepdims=True) - 1.0
    return one_hot(iota((sz.rows, sz.slots), 0).astype(F32) == row)


def block_kernel(sz, *refs):
    (dest, back, length, rows_hbm, ct_hbm, win_hbm, wout_hbm, wst_hbm, wstep_hbm, par,
     out_rows, out_grads, inner_out, proj_out, extra_out, small_out, gain_out,
     win, wout, wst, wstep,
     pk_in, pk_ct, rc_in, rc_ct, ry_in, ry_ct, gn_o, gn_g,
     p_in, p_bk, q_in, q_bk,
     hid, cts, normed, lowct, perm, xA, xE, tA, tE,
     gr, xr, xa, xs, mx, ng,
     yb, pb, r0, rl,
     inter, interT, igrad, ptile,
     sraw, sslope, wr, dtv, lac, lar, sgr, rgr, stepsig, acc1, acc2, scale,
     stat_s, stat_r, half_s, half_r, st_s, st_r,
     sms, smr, gall, gsum,
     a2a_s, a2a_r, fw_s, fw_r, quad_s, quad_r, xq_s, xq_r, z_s, z_r, y_s, y_r, gg_s, gg_r, sm_s, sm_r, w_s, o_s) = refs
    dp, R, H, C = sz.dp, sz.rows, sz.half, sz.inner
    W, NT_ = sz.width, sz.tiles
    g = lax.axis_index("dp")
    t = lax.axis_index("tensor")
    o = 1 - t
    c, x, z = g % 2, (g // 2) % 2, g // 4
    q = g % 4
    sib, xp = g + 1 - 2 * c, g + 2 - 4 * x
    diag = sib + 2 - 4 * x

    def rcopy(src, dst, ss, rs, peer, side=None):
        return pltpu.make_async_remote_copy(
            src_ref=src, dst_ref=dst, send_sem=ss, recv_sem=rs,
            device_id=(peer, t if side is None else side), device_id_type=MESH)

    sent = []

    def go(copy):
        copy.start()
        sent.append(copy)
        return copy

    loads = [pltpu.make_async_copy(a, b, w_s.at[i]) for i, (a, b) in enumerate(
        [(wst_hbm, wst), (wstep_hbm, wstep), (win_hbm, win), (wout_hbm, wout),
         (rows_hbm, cts.at[0]), (ct_hbm, cts.at[1])])]
    loads[4].start()
    loads[5].start()

    barrier = pltpu.get_barrier_semaphore()
    for off in range(1, dp):
        pl.semaphore_signal(barrier, inc=1, device_id=((g + off) % dp, t), device_id_type=MESH)
    pl.semaphore_signal(barrier, inc=1, device_id=(g, o), device_id_type=MESH)

    far = sorted(range(1, dp), key=lambda k: (abs(k - dp // 2), k))

    def exchange(i, source, target):
        copies = []
        for off in far:
            peer = (g + off) % dp
            copies.append(rcopy(source.at[peer], target.at[g], a2a_s.at[i, peer], a2a_r.at[i, g], peer))
            copies[-1].start()
        target[pl.ds(g, 1)] = source[pl.ds(g, 1)]
        return copies

    def settle(copies):
        for copy in copies:
            copy.wait_send()

    def arrived(i, target, src):
        rcopy(target.at[src], target.at[src], a2a_s.at[i, src], a2a_r.at[i, src], src).wait_recv()

    def pack(table, source, target):
        for k in range(2):
            n = sz.slots // 2
            part = dot_nn(table[k * n:(k + 1) * n, :], source[...]).astype(BF)
            target[k * (dp // 2):(k + 1) * (dp // 2)] = part.reshape(dp // 2, sz.cap, H)

    p_in[...] = send_table(dest, g, sz)
    loads[4].wait()
    pack(p_in, cts.at[0], pk_in)
    pl.semaphore_wait(barrier, dp)
    rows_away = exchange(0, pk_in, rc_in)
    for load in loads[:4]:
        load.start()
    p_bk[...] = send_table(back, g, sz)
    loads[5].wait()
    pack(p_bk, cts.at[1], pk_ct)
    grads_away = exchange(1, pk_ct, rc_ct)
    q_in[...] = owner_table(dest, g, sz)
    q_bk[...] = owner_table(back, g, sz)

    near = [k for k in reversed(far)]

    def forward(i, arr, dst, src):
        arrived(i, arr, src)
        return rcopy(arr.at[src], dst.at[src], fw_s.at[i, src], fw_r.at[i, src], g, o)

    go(rcopy(rc_in.at[g], ry_in.at[g], fw_s.at[0, g], fw_r.at[0, g], g, o))
    go(rcopy(rc_ct.at[g], ry_ct.at[g], fw_s.at[1, g], fw_r.at[1, g], g, o))
    for off in near:
        go(forward(0, rc_in, ry_in, (g + off) % dp))
    hid[pl.ds(t, 1)] = dot_nn(q_in[...], rc_in[...].reshape(sz.slots, H)).astype(BF)[None]
    for d in range(dp):
        rcopy(ry_in.at[d], ry_in.at[d], fw_s.at[0, d], fw_r.at[0, d], g, o).wait_recv()
    hid[pl.ds(o, 1)] = dot_nn(q_in[...], ry_in[...].reshape(sz.slots, H)).astype(BF)[None]

    total = jnp.zeros((R, 128), F32)
    for k in range(W // 128):
        v = hid[k // (H // 128), :, (k % (H // 128)) * 128:(k % (H // 128)) * 128 + 128].astype(F32)
        total = total + v * v
    norm_scale = lax.rsqrt(jnp.sum(total, axis=1, keepdims=True) / W + EPSILON)
    scale[...] = jnp.broadcast_to(norm_scale, (R, 128))
    for k in range(W // 128):
        v = hid[k // (H // 128), :, (k % (H // 128)) * 128:(k % (H // 128)) * 128 + 128].astype(F32)
        normed[:, k * 128:(k + 1) * 128] = (v * scale[...] * par[6:7, k * 128:(k + 1) * 128]).astype(BF)

    def quarters(source):
        for qq in range(4):
            perm[qq] = jnp.concatenate(
                [source[:, sz.share * (4 * zz + qq):sz.share * (4 * zz + qq + 1)] for zz in range(sz.nz)], axis=1)

    def send_quarter(i, dst):
        copies = [
            rcopy(perm.at[peer % 4], dst.at[rel], xq_s.at[i, rel - 1], xq_r.at[i, rel - 1], peer)
            for rel, peer in ((2, xp), (3, diag), (1, sib))]
        for copy in copies:
            copy.start()
        dst[0:1] = perm[pl.ds(q, 1)]
        return copies

    def turn_quarter(i, dst, turned):
        for rel, peer in ((1, sib), (2, xp), (3, diag)):
            rcopy(dst.at[rel], dst.at[rel], xq_s.at[i, rel - 1], xq_r.at[i, rel - 1], peer).wait_recv()
        for rel in range(4):
            turned[:, rel * R:(rel + 1) * R] = jnp.transpose(dst[rel].astype(F32)).astype(BF)

    quarters(normed)
    quarter_away = send_quarter(0, xA)

    loads[0].wait()
    loads[1].wait()
    row = iota((R, 128), 0)
    lane = iota((R, 128), 1)
    live = jnp.where(row < length[0, 0], 1.0, 0.0)
    sraw[...] = dot_nn(normed[...], wst[...])
    step_in = dot_nn(normed[...], wstep[...]) + par[9:10, :128]
    S = sz.state
    for k in range(2):
        cut = slice(k * S, (k + 1) * S)
        raw = sraw[:, cut]
        conv = par[8:9, 4 * 2 * S + k * S:4 * 2 * S + (k + 1) * S] + par[8:9, cut] * raw
        for tap in range(1, 4):
            conv = conv + par[8:9, tap * 2 * S + k * S:tap * 2 * S + (k + 1) * S] * rows_down(raw, tap)
        sg = sigmoid(conv)
        sslope[:, cut] = sg * (1.0 + conv * (1.0 - sg))
        wr[:, cut] = (conv * sg).astype(BF)
    written, readout = wr[:, :S], wr[:, S:]
    inter[...] = dot_nt(readout, written)
    interT[...] = dot_nt(written, readout)
    stepsig[...] = sigmoid(step_in) * live
    heads_live = jnp.where(lane < sz.heads, live, 0.0)
    step = (jnp.maximum(step_in, 0.0) + jnp.log1p(jnp.exp(-jnp.abs(step_in)))) * heads_live
    rate = -jnp.exp(par[10:11, :128])
    dtv[...] = step
    lower = one_hot(iota((R, R), 0) >= iota((R, R), 1))
    log_decay = sum(dot_nn(lower, part) for part in split3(step * rate))
    lac[...] = log_decay
    lar[...] = jnp.transpose(log_decay)

    loads[2].wait()

    def project(dst, base):
        def body(n, carry):
            at = pl.multiple_of(n * 256, 256)
            dst[:, pl.ds(at, 256)] = dot_nn(normed[...], win[:, pl.ds(pl.multiple_of(base + n * 256, 256), 256)])
            return carry
        lax.fori_loop(0, C // 256, body, 0)

    project(xr, C)
    project(gr, 0)

    def lanes(p):
        return pl.ds(pl.multiple_of(p * 128, 128), 128)

    B = 64

    def step_columns(p, lane):
        first = lane < 64
        return jnp.where(first, pick(dtv[...], lane, 2 * p), pick(dtv[...], lane, 2 * p + 1))

    def scan(p, carry):
        at = lanes(p)
        row = iota((R, 128), 0)
        lane = iota((R, 128), 1)
        raw = xr[:, at]
        conv = par[4:5, at] + par[0:1, at] * raw
        for tap in range(1, 4):
            conv = conv + par[tap:tap + 1, at] * rows_down(raw, tap)
        sg = sigmoid(conv)
        act = conv * sg
        xa[:, at] = act
        xs[:, at] = (sg * (1.0 + conv * (1.0 - sg))).astype(BF)
        driven = act * step_columns(p, lane)
        parts = [jnp.where(lane < 64, driven, 0.0).astype(BF), jnp.where(lane >= 64, driven, 0.0).astype(BF)]
        cols = [pick(lac[...], lane, 2 * p + k) for k in range(2)]
        for b in range(R // B):
            reach = 128 * ((b * B) // 128 + 1)
            cut = slice(b * B, (b + 1) * B)
            causal = iota((B, reach), 0) + b * B >= iota((B, reach), 1)
            mixed = par[7:8, at] * act[cut]
            for k in range(2):
                spread = cols[k][cut] - lar[pl.ds(2 * p + k, 1), :][:, :reach]
                fading = jnp.exp(jnp.where(causal, spread, NEG))
                mixing = (inter[cut, :reach] * fading).astype(BF)
                mixed = mixed + dot_nn(mixing, parts[k][:reach])
            mx[cut, at] = mixed
        return carry

    def scan_and_forward(p, carry):
        scan(p, carry)
        src = (g + 1 + p) % dp
        forward(1, rc_ct, ry_ct, src).start()
        return carry

    lax.fori_loop(0, NT_, scan_and_forward, 0)
    for k in range(NT_, dp - 1):
        go(forward(1, rc_ct, ry_ct, (g + 1 + k) % dp))
    for k in range(min(NT_, dp - 1)):
        sent.append(rcopy(rc_ct.at[(g + 1 + k) % dp], ry_ct.at[(g + 1 + k) % dp], fw_s.at[1, (g + 1 + k) % dp],
                          fw_r.at[1, (g + 1 + k) % dp], g, o))

    cts[pl.ds(t, 1)] = dot_nn(q_bk[...], rc_ct[...].reshape(sz.slots, H)).astype(BF)[None]
    for d in range(dp):
        rcopy(ry_ct.at[d], ry_ct.at[d], fw_s.at[1, d], fw_r.at[1, d], g, o).wait_recv()
    cts[pl.ds(o, 1)] = dot_nn(q_bk[...], ry_ct[...].reshape(sz.slots, H)).astype(BF)[None]
    for k in range(W // 128):
        v = cts[k // (H // 128), :, (k % (H // 128)) * 128:(k % (H // 128)) * 128 + 128].astype(F32)
        lowct[:, k * 128:(k + 1) * 128] = (v * live).astype(BF)
    settle(quarter_away)
    quarters(lowct)
    sent.extend(send_quarter(1, xE))
    loads[3].wait()

    def back_project(n, carry):
        at = pl.ds(pl.multiple_of(n * 256, 256), 256)
        ng[:, at] = dot_nt(lowct[...], wout[at, :])
        return carry
    lax.fori_loop(0, C // 256, back_project, 0)

    acc1[...] = jnp.zeros_like(acc1)
    acc2[...] = jnp.zeros_like(acc2)

    def stats(p, carry):
        at = lanes(p)
        raw = gr[:, at]
        gated = mx[:, at] * raw * sigmoid(raw)
        acc1[...] += gated * gated
        acc2[...] += gated * (par[5:6, at] * ng[:, at])
        return carry
    lax.fori_loop(0, NT_, stats, 0)
    squares = jnp.sum(acc1[...], axis=1, keepdims=True)
    cross = jnp.sum(acc2[...], axis=1, keepdims=True)
    both = jnp.where(lane == 0, squares, jnp.where(lane == 1, cross, 0.0))
    stat_s[0] = jnp.transpose(both)[:8]
    go(rcopy(stat_s.at[0], stat_r.at[0], y_s.at[0], y_r.at[0], g, o)).wait_recv()
    both = jnp.transpose(jnp.concatenate([stat_s[0] + stat_r[0], jnp.zeros((120, R), F32)], axis=0))
    whole = float(2 * C)
    gate_scale = lax.rsqrt(pick(both, lane, 0) / whole + EPSILON)
    pull = gate_scale * gate_scale * gate_scale * (pick(both, lane, 1) / whole)
    acc1[...] = jnp.broadcast_to(gate_scale, (R, 128))
    acc2[...] = jnp.broadcast_to(pull, (R, 128))

    def gate_back(p, carry):
        at = lanes(p)
        raw, mixed, grad = gr[:, at], mx[:, at], ng[:, at]
        sg = sigmoid(raw)
        act = raw * sg
        gated = mixed * act
        scaled = gated * acc1[...]
        gain = par[5:6, at]
        yb[0, :, at] = (scaled * gain).astype(BF)
        gated_grad = acc1[...] * (gain * grad) - gated * acc2[...]
        sms[0, 5:6, at] = jnp.sum(grad * scaled, axis=0, keepdims=True)
        mixed_grad = gated_grad * act
        ng[:, at] = mixed_grad
        sms[0, 6:7, at] = jnp.sum(mixed_grad * xa[:, at], axis=0, keepdims=True)
        yb[0, :, pl.ds(pl.multiple_of(C + p * 128, 128), 128)] = (
            gated_grad * mixed * (sg * (1.0 + raw * (1.0 - sg)))).astype(BF)
        return carry
    lax.fori_loop(0, NT_, gate_back, 0)

    def cols_of(i):
        return pl.ds(sz.chunks[i][0], sz.chunks[i][1])

    def quad_send(i):
        at = cols_of(i)
        go(rcopy(yb.at[0, :, at], yb.at[2, :, at], quad_s.at[i, 1], quad_r.at[i, 1], xp))
        go(rcopy(yb.at[0, :, at], yb.at[1, :, at], quad_s.at[i, 0], quad_r.at[i, 0], sib))

    def quad_pass(i):
        at = cols_of(i)
        rcopy(yb.at[2, :, at], yb.at[2, :, at], quad_s.at[i, 1], quad_r.at[i, 1], xp).wait_recv()
        go(rcopy(yb.at[2, :, at], yb.at[3, :, at], quad_s.at[i, 2], quad_r.at[i, 2], sib))

    def z_peer(level):
        bit = (z // 2 ** level) % 2
        return bit, g + (1 - 2 * bit) * 4 * 2 ** level

    bases = []
    at0 = 0
    for level in range(sz.levels):
        bases.append(at0)
        at0 += sz.nz // 2 ** (level + 1)
    landing = [r0, rl]

    def z_send(i, level):
        bit, peer = z_peer(level)
        at = cols_of(i)
        for k in range(sz.nz // 2 ** (level + 1)):
            low = z % 2 ** level
            block = (2 * k + 1 - bit) * 2 ** level + low
            go(rcopy(pb.at[block, :, at], landing[level].at[k, :, at], z_s.at[i, bases[level] + k],
                     z_r.at[i, bases[level] + k], peer))

    def z_add(i, level):
        bit, peer = z_peer(level)
        at = cols_of(i)
        start, size = sz.chunks[i]
        for k in range(sz.nz // 2 ** (level + 1)):
            low = z % 2 ** level
            block = (2 * k + bit) * 2 ** level + low
            sem = bases[level] + k
            rcopy(landing[level].at[k, :, at], landing[level].at[k, :, at], z_s.at[i, sem], z_r.at[i, sem], peer).wait_recv()
            for n in range(0, size, 128):
                cut = slice(start + n, start + n + 128)
                value = pb[pl.ds(block, 1), :, cut].astype(F32)[0] + landing[level][k, :, cut].astype(F32)
                if level + 1 < sz.levels:
                    pb[pl.ds(block, 1), :, cut] = value.astype(BF)[None]
                elif start + n < C:
                    proj_out[:, cut] = value
                elif start + n < 3 * C:
                    inner_out[:, start + n - C:start + n - C + 128] = value
                else:
                    extra_out[:, start + n - 3 * C:start + n - 3 * C + 128] = value

    def partial_sum(i, turned):
        at = cols_of(i)
        start, size = sz.chunks[i]
        rcopy(yb.at[1, :, at], yb.at[1, :, at], quad_s.at[i, 0], quad_r.at[i, 0], sib).wait_recv()
        rcopy(yb.at[3, :, at], yb.at[3, :, at], quad_s.at[i, 2], quad_r.at[i, 2], sib).wait_recv()
        n = 384 if size % 256 else 256

        def body(k, carry):
            at = pl.ds(pl.multiple_of(start + k * n, 128), n)
            part = dot_nn(turned[...], yb[:, :, at].reshape(4 * R, n))
            pb[:, :, at] = part.astype(BF).reshape(sz.nz, sz.share, n)
            return carry
        lax.fori_loop(0, size // n, body, 0)
        z_send(i, 0)

    for i in range(4):
        quad_send(i)
    turn_quarter(0, xA, tA)

    def out_half(side, dst, cast):
        def body(n, carry):
            at = pl.ds(pl.multiple_of(side * H + n * 256, 256), 256)
            dst[:, pl.ds(pl.multiple_of(n * 256, 256), 256)] = dot_nn(yb[0, :, :C], wout[:, at]).astype(cast)
            return carry
        lax.fori_loop(0, H // 256, body, 0)
    out_half(o, half_s.at[0], BF)
    go(rcopy(half_s.at[0], half_r.at[0], y_s.at[1], y_r.at[1], g, o))
    out_half(t, gr, F32)
    turn_quarter(1, xE, tE)

    igrad[...] = jnp.zeros_like(igrad)
    sgr[...] = jnp.zeros_like(sgr)
    rgr[...] = jnp.zeros_like(rgr)
    ptile[...] = jnp.zeros_like(ptile)

    def scan_back(p, carry):
        at = lanes(p)
        lane = iota((R, 128), 1)
        grad = ng[:, at]
        act = xa[:, at]
        stepw = step_columns(p, lane)
        driven = (act * stepw).astype(BF)
        parts = [jnp.where(lane < 64, grad, 0.0).astype(BF), jnp.where(lane >= 64, grad, 0.0).astype(BF)]
        cols = [pick(lac[...], lane, 2 * p + k) for k in range(2)]
        pieces = []
        for b in range(R // B):
            skip = 128 * ((b * B) // 128)
            cut = slice(b * B, (b + 1) * B)
            causal = iota((B, R - skip), 1) + skip >= iota((B, R - skip), 0) + b * B
            turned = interT[cut, skip:]
            piece = jnp.zeros((B, 128), F32)
            total = igrad[cut, skip:]
            for k in range(2):
                spread = lar[pl.ds(2 * p + k, 1), :][:, skip:] - cols[k][cut]
                fading = jnp.exp(jnp.where(causal, spread, NEG))
                faded = dot_nt(driven[cut], parts[k][skip:]) * fading
                total = total + faded
                piece = piece + dot_nn((turned * fading).astype(BF), parts[k][skip:])
                ptile[k, cut, skip:] = (faded * turned).astype(BF)
            igrad[cut, skip:] = total
            pieces.append(piece)
        strict = one_hot(iota((R, R), 0) > iota((R, R), 1))
        for k in range(2):
            found = []
            for b in range(R // B):
                skip = 128 * ((b * B) // 128)
                cut = slice(b * B, (b + 1) * B)
                causal = iota((B, R - skip), 1) + skip >= iota((B, R - skip), 0) + b * B
                sums = dot_nn(strict[cut], ptile[k, :, skip:])
                found.append(jnp.sum(jnp.where(causal, sums, 0.0), axis=1, keepdims=True))
            rgr[...] = jnp.where(lane == 2 * p + k, jnp.concatenate(found, axis=0), rgr[...])
        driven_grad = jnp.concatenate(pieces, axis=0)
        pulled = driven_grad * act
        low = jnp.sum(jnp.where(lane < 64, pulled, 0.0), axis=1, keepdims=True)
        high = jnp.sum(jnp.where(lane >= 64, pulled, 0.0), axis=1, keepdims=True)
        sgr[...] = jnp.where(lane == 2 * p, low, jnp.where(lane == 2 * p + 1, high, sgr[...]))
        conv_grad = (par[7:8, at] * grad + stepw * driven_grad) * xs[:, at].astype(F32)
        raw = xr[:, at]
        raw_grad = par[0:1, at] * conv_grad
        sms[0, 0:1, at] = jnp.sum(conv_grad * raw, axis=0, keepdims=True)
        sms[0, 4:5, at] = jnp.sum(conv_grad, axis=0, keepdims=True)
        for tap in range(1, 4):
            up = rows_up(conv_grad, tap)
            raw_grad = raw_grad + par[tap:tap + 1, at] * up
            sms[0, tap:tap + 1, at] = jnp.sum(up * raw, axis=0, keepdims=True)
        yb[0, :, pl.ds(pl.multiple_of(2 * C + p * 128, 128), 128)] = raw_grad.astype(BF)
        return carry

    lax.fori_loop(0, NT_ // 2, scan_back, 0)
    quad_send(4)

    rcopy(half_r.at[0], half_r.at[0], y_s.at[1], y_r.at[1], g, o).wait_recv()

    def answer(table, value, dst):
        for k in range(2):
            n = sz.slots // 2
            part = dot_tn(table[:, k * n:(k + 1) * n], value).astype(BF)
            dst[k * (dp // 2):(k + 1) * (dp // 2)] = part.reshape(dp // 2, sz.cap, H)

    pieces = []
    mine = hid[pl.ds(t, 1)][0]
    for k in range(H // 128):
        cut = slice(k * 128, (k + 1) * 128)
        branch = gr[:, cut] + half_r[0, :, cut].astype(F32)
        pieces.append((mine[:, cut].astype(F32) + live * branch).astype(BF))
    settle(rows_away)
    answer(q_bk, jnp.concatenate(pieces, axis=1), pk_in)
    sent.extend(exchange(2, pk_in, gn_o))
    quad_pass(0)
    quad_pass(1)

    lax.fori_loop(NT_ // 2, NT_, scan_back, 0)
    quad_send(5)
    quad_pass(2)

    ig = igrad[...].astype(BF)
    st_s[:, :S] = dot_nn(ig, wr[:, S:]).astype(BF)
    st_s[:, S:] = dot_tn(ig, wr[:, :S]).astype(BF)
    go(rcopy(st_s, st_r, y_s.at[2], y_r.at[2], g, o))
    step_grad = (sgr[...] + rgr[...] * rate) * stepsig[...]
    yb[0, :, 3 * C + 2 * S:] = step_grad.astype(BF)
    sms[0, 7:8, 10 * S:10 * S + 128] = jnp.sum(step_grad, axis=0, keepdims=True)
    sms[0, 7:8, 10 * S + 128:10 * S + 256] = jnp.sum(rgr[...] * dtv[...], axis=0, keepdims=True) * rate
    partial_sum(0, tE)
    rcopy(st_r, st_r, y_s.at[2], y_r.at[2], g, o).wait_recv()
    for k in range(2):
        cut = slice(k * S, (k + 1) * S)
        conv_grad = (st_s[:, cut].astype(F32) + st_r[:, cut].astype(F32)) * sslope[:, cut]
        raw = sraw[:, cut]
        raw_grad = par[8:9, cut] * conv_grad
        sms[0, 7:8, cut] = jnp.sum(conv_grad * raw, axis=0, keepdims=True)
        sms[0, 7:8, 8 * S + k * S:8 * S + (k + 1) * S] = jnp.sum(conv_grad, axis=0, keepdims=True)
        for tap in range(1, 4):
            up = rows_up(conv_grad, tap)
            taps = slice(tap * 2 * S + k * S, tap * 2 * S + (k + 1) * S)
            raw_grad = raw_grad + par[8:9, taps] * up
            sms[0, 7:8, taps] = jnp.sum(up * raw, axis=0, keepdims=True)
        yb[0, :, 3 * C + k * S:3 * C + (k + 1) * S] = raw_grad.astype(BF)
    quad_send(6)

    acc1[...] = jnp.zeros_like(acc1)

    def normed_grad(side, dst, cast):
        def body(n, carry):
            at = pl.ds(pl.multiple_of(side * H + n * 256, 256), 256)
            value = dot_nt(yb[0, :, C:3 * C], win[at, :])
            mine_state = pl.ds(pl.multiple_of(t * S, 128), S)
            value = value + dot_nt(yb[0, :, pl.ds(pl.multiple_of(3 * C + t * S, 128), S)], wst[at, mine_state])
            value = value + dot_nt(yb[0, :, 3 * C + 2 * S:], wstep[at, :])
            for k in range(2):
                cut = slice(k * 128, (k + 1) * 128)
                here = pl.ds(pl.multiple_of(n * 256 + k * 128, 128), 128)
                there = pl.ds(pl.multiple_of(side * H + n * 256 + k * 128, 128), 128)
                acc1[...] += hid[pl.ds(side, 1), :, here][0].astype(F32) * (par[6:7, there] * value[:, cut])
            dst[:, pl.ds(pl.multiple_of(n * 256, 256), 256)] = value.astype(cast)
            return carry
        lax.fori_loop(0, H // 256, body, 0)
    normed_grad(o, half_s.at[1], BF)
    go(rcopy(half_s.at[1], half_r.at[1], y_s.at[3], y_r.at[3], g, o))
    normed_grad(t, gr, F32)
    inner_sum = jnp.where(lane == 0, jnp.sum(acc1[...], axis=1, keepdims=True), 0.0)
    stat_s[1] = jnp.transpose(inner_sum)[:8]
    go(rcopy(stat_s.at[1], stat_r.at[1], y_s.at[4], y_r.at[4], g, o))
    quad_pass(3)
    partial_sum(1, tE)

    rcopy(half_r.at[1], half_r.at[1], y_s.at[3], y_r.at[3], g, o).wait_recv()
    rcopy(stat_r.at[1], stat_r.at[1], y_s.at[4], y_r.at[4], g, o).wait_recv()
    both = jnp.transpose(jnp.concatenate([stat_s[1] + stat_r[1], jnp.zeros((120, R), F32)], axis=0))
    pull = pick(both, lane, 0) / W * (scale[...] * scale[...] * scale[...])
    pieces = []
    mine = hid[pl.ds(t, 1)][0]
    mine_ct = cts[pl.ds(t, 1)][0]
    gall[pl.ds(g, 1)] = jnp.zeros((1, 8, 128), F32)
    for k in range(H // 128):
        cut = slice(k * 128, (k + 1) * 128)
        there = pl.ds(pl.multiple_of(t * H + k * 128, 128), 128)
        value = gr[:, cut] + half_r[1, :, cut].astype(F32)
        rows_here = mine[:, cut].astype(F32)
        gall[pl.ds(g, 1), k:k + 1, :] = jnp.sum(value * rows_here * scale[...], axis=0, keepdims=True)[None]
        pieces.append((scale[...] * (par[6:7, there] * value) - rows_here * pull
                       + mine_ct[:, cut].astype(F32)).astype(BF))
    settle(grads_away)
    answer(q_in, jnp.concatenate(pieces, axis=1), pk_ct)
    for off in far:
        peer = (g + off) % dp
        go(rcopy(gall.at[g], gall.at[g], gg_s.at[peer], gg_r.at[g], peer))
    sent.extend(exchange(3, pk_ct, gn_g))

    quad_pass(4)
    quad_pass(5)
    quad_pass(6)
    z_add(0, 0)
    z_send(0, 1)
    partial_sum(2, tA)
    z_add(1, 0)
    z_send(1, 1)
    partial_sum(3, tA)
    z_add(2, 0)
    z_send(2, 1)
    partial_sum(4, tA)
    z_add(3, 0)
    z_send(3, 1)
    partial_sum(5, tA)
    partial_sum(6, tA)

    for level in range(dp.bit_length() - 1):
        bit = (g // 2 ** level) % 2
        peer = g + (1 - 2 * bit) * 2 ** level
        go(rcopy(sms.at[level], smr.at[level], sm_s.at[level], sm_r.at[level], peer)).wait_recv()
        if level + 1 < dp.bit_length() - 1:
            sms[level + 1] = sms[level] + smr[level]
        else:
            small_out[...] = sms[level] + smr[level]
    for off in far:
        src = (g + off) % dp
        rcopy(gall.at[src], gall.at[src], gg_s.at[src], gg_r.at[src], src).wait_recv()
    summed = gall[0]
    for d in range(1, dp):
        summed = summed + gall[d]
    gsum[pl.ds(t, 1)] = summed[None]
    go(rcopy(gsum.at[t], gsum.at[t], y_s.at[5], y_r.at[5], g, o))

    def give(i, value, stage, dst):
        n = R // sz.cap
        stage[:n] = value.astype(BF).reshape(n, sz.cap, H)
        copies = [pltpu.make_async_copy(stage.at[k], dst.at[pl.ds(k * sz.cap, sz.cap)], o_s.at[i, k]) for k in range(n)]
        for copy in copies:
            copy.start()
        return copies

    for i in range(4, 7):
        z_add(i, 0)
        z_send(i, 1)

    for off in far:
        arrived(2, gn_o, (g + off) % dp)
    stores = give(0, dot_tn(p_bk[...], gn_o[...].reshape(sz.slots, H)), ry_in, out_rows)
    for i in range(7):
        z_add(i, 1)
    for off in far:
        arrived(3, gn_g, (g + off) % dp)
    stores += give(1, dot_tn(p_in[...], gn_g[...].reshape(sz.slots, H)), ry_ct, out_grads)
    rcopy(gsum.at[o], gsum.at[o], y_s.at[5], y_r.at[5], g, o).wait_recv()
    gain_out[...] = gsum[...]
    for copy in sent:
        copy.wait_send()
    for store in stores:
        store.wait()


def fused(sz, block_in, cotangent, lengths, dest_slot, return_slot, norm_gain, inner_weight, state_weight,
          step_weight, conv_inner, conv_inner_bias, conv_state, conv_state_bias, step_bias, log_rate,
          skip_gain, gate_gain, out_weight):
    dp, R, H, C, S = sz.dp, sz.rows, sz.half, sz.inner, sz.state
    W = sz.width

    def line(v):
        return jnp.pad(v.reshape(1, -1), ((0, 0), (0, C - v.size)))
    params = jnp.concatenate([
        conv_inner, line(conv_inner_bias), line(gate_gain), line(norm_gain),
        line(jnp.repeat(skip_gain, C // sz.heads)),
        line(jnp.concatenate([conv_state.reshape(-1), conv_state_bias])),
        line(step_bias), line(log_rate), jnp.zeros((5, C), F32)], axis=0)
    win = inner_weight.reshape(W, 2 * C)
    wstep = jnp.pad(step_weight, ((0, 0), (0, 128 - sz.heads)))
    vm = pl.BlockSpec(memory_space=pltpu.VMEM)
    hb = pl.BlockSpec(memory_space=pl.ANY)
    sm = pl.BlockSpec(memory_space=pltpu.SMEM)
    V = pltpu.VMEM
    packed = V((dp, sz.cap, H), BF)
    D = pltpu.SemaphoreType.DMA
    nch = len(sz.chunks)
    scratch = [
        V((W, 2 * C), BF), V((C, W), BF), V((W, 2 * S), BF), V((W, 128), BF),
        *[packed] * 8,
        V((sz.slots, R), BF), V((sz.slots, R), BF), V((R, sz.slots), BF), V((R, sz.slots), BF),
        V((2, R, H), BF), V((2, R, H), BF), V((R, W), BF), V((R, W), BF),
        V((4, R, sz.quarter), BF), V((4, R, sz.quarter), BF), V((4, R, sz.quarter), BF),
        V((sz.quarter, 4 * R), BF), V((sz.quarter, 4 * R), BF),
        V((R, C), F32), V((R, C), F32), V((R, C), F32), V((R, C), BF), V((R, C), F32), V((R, C), F32),
        V((4, R, sz.cols), BF), V((sz.nz, sz.share, sz.cols), BF), V((2, sz.share, sz.cols), BF), V((1, sz.share, sz.cols), BF),
        V((R, R), F32), V((R, R), F32), V((R, R), F32), V((2, R, R), BF),
        V((R, 2 * S), F32), V((R, 2 * S), F32), V((R, 2 * S), BF), V((R, 128), F32), V((R, 128), F32), V((128, R), F32),
        V((R, 128), F32), V((R, 128), F32), V((R, 128), F32), V((R, 128), F32), V((R, 128), F32), V((R, 128), F32),
        V((2, 8, R), F32), V((2, 8, R), F32), V((2, R, H), BF), V((2, R, H), BF),
        V((R, 2 * S), BF), V((R, 2 * S), BF),
        V((4, 8, C), F32), V((4, 8, C), F32), V((dp, 8, 128), F32), V((2, 8, 128), F32),
        D((4, dp)), D((4, dp)), D((2, dp)), D((2, dp)), D((nch, 3)), D((nch, 3)), D((2, 3)), D((2, 3)),
        D((nch, sz.nz - 1)), D((nch, sz.nz - 1)), D((6,)), D((6,)), D((dp,)), D((dp,)), D((4,)), D((4,)), D((6,)), D((2, dp)),
    ]
    out = jax.ShapeDtypeStruct
    rows_out, grads_out, inner_g, proj_g, extra_g, small, gain = pl.pallas_call(
        functools.partial(block_kernel, sz),
        out_shape=(out((R, H), BF), out((R, H), BF), out((sz.share, 2 * C), F32), out((sz.share, C), F32),
                   out((sz.share, sz.extra), F32), out((8, C), F32), out((2, 8, 128), F32)),
        in_specs=[vm, vm, sm, hb, hb, hb, hb, hb, hb, vm],
        out_specs=(hb, hb) + (vm,) * 5,
        scratch_shapes=scratch,
        compiler_params=pltpu.CompilerParams(collective_id=0, has_side_effects=True, vmem_limit_bytes=66000000),
        name="block",
    )(dest_slot.reshape(dp, R), return_slot.reshape(dp, R), lengths, block_in, cotangent, win, out_weight,
      state_weight, wstep, params)
    own = lax.axis_index("dp")
    gain_sum = gain[:, :H // 128].reshape(W)
    heads = sz.heads
    return (
        rows_out, grads_out,
        lax.dynamic_slice_in_dim(gain_sum, own * sz.share, sz.share),
        inner_g.reshape(sz.share, 2, C),
        extra_g[:, :2 * S], extra_g[:, 2 * S:2 * S + heads],
        small[:4], small[4], small[7, :8 * S].reshape(4, 2 * S), small[7, 8 * S:10 * S],
        small[7, 10 * S:10 * S + heads], small[7, 10 * S + 128:10 * S + 128 + heads],
        jnp.sum(small[6].reshape(heads, -1), axis=1), small[5], proj_g.T,
    )


def with_collectives(
    block_in,
    cotangent,
    lengths,
    dest_slot,
    return_slot,
    norm_gain,
    inner_weight,
    state_weight,
    step_weight,
    conv_inner,
    conv_inner_bias,
    conv_state,
    conv_state_bias,
    step_bias,
    log_rate,
    skip_gain,
    gate_gain,
    out_weight,
):
    groups = lax.axis_size("dp")
    group_rows = block_in.shape[0]
    half_width = block_in.shape[1]
    capacity = 2 * group_rows // groups
    own_group = lax.axis_index("dp")
    own_dest = lax.dynamic_slice_in_dim(dest_slot, own_group * group_rows, group_rows)
    own_return = lax.dynamic_slice_in_dim(return_slot, own_group * group_rows, group_rows)
    send_spot = send_layout(own_dest, group_rows, capacity, groups)
    back_spot = send_layout(own_return, group_rows, capacity, groups)
    slots_in = arrivals(dest_slot, group_rows, capacity, groups, own_group)
    slots_back = arrivals(return_slot, group_rows, capacity, groups, own_group)
    blank_rows = jnp.zeros((groups * capacity, half_width), jnp.bfloat16)
    packed_rows = blank_rows.at[send_spot].set(block_in).reshape(groups, capacity, half_width)
    packed_grads = blank_rows.at[back_spot].set(cotangent).reshape(groups, capacity, half_width)
    came_rows, came_grads = (
        lax.all_to_all(packed_rows, "dp", split_axis=0, concat_axis=0, tiled=True),
        lax.all_to_all(packed_grads, "dp", split_axis=0, concat_axis=0, tiled=True),
    )
    empty_rows = jnp.zeros((group_rows, half_width), jnp.bfloat16)
    own_rows = empty_rows.at[slots_in].set(came_rows.reshape(-1, half_width), mode="drop")
    own_grads = empty_rows.at[slots_back].set(came_grads.reshape(-1, half_width), mode="drop")
    full_rows, full_grads = (
        lax.all_gather(own_rows, "tensor", axis=1, tiled=True),
        lax.all_gather(own_grads, "tensor", axis=1, tiled=True),
    )
    seq_pos, live_mask, keep_state = stretch_layout(lengths[0], STRETCH)
    live_col = live_mask[:, None]
    hidden = full_rows.astype(jnp.float32)
    norm_scale = lax.rsqrt(jnp.mean(hidden * hidden, axis=1, keepdims=True) + EPSILON)
    normed = (hidden * norm_scale * norm_gain).astype(jnp.bfloat16)
    inner_local = inner_weight.shape[2]
    zx_weight = inner_weight.reshape(inner_weight.shape[0], 2 * inner_local)
    projected = jnp.dot(normed, zx_weight, preferred_element_type=jnp.float32)
    gate_raw = projected[:, :inner_local]
    conv_in_x = projected[:, inner_local:]
    conv_in_state = jnp.dot(normed, state_weight, preferred_element_type=jnp.float32)
    step_raw = jnp.dot(normed, step_weight, preferred_element_type=jnp.float32)
    x_conv = conv_forward(conv_in_x, conv_inner, conv_inner_bias, seq_pos)
    state_conv = conv_forward(conv_in_state, conv_state, conv_state_bias, seq_pos)
    x_act = jax.nn.silu(x_conv)
    state_act = jax.nn.silu(state_conv)
    state_width = state_act.shape[1] // 2
    heads_local = step_weight.shape[1]
    head_dim = inner_local // heads_local
    stretches = group_rows // STRETCH
    step_input = step_raw + step_bias[None, :]
    step_size = jax.nn.softplus(step_input) * live_col
    decay_rate = -jnp.exp(log_rate)
    skip_wide = jnp.repeat(skip_gain, head_dim)[None, :]
    scanned, saved = state_forward(
        x_act.reshape(group_rows, heads_local, head_dim),
        state_act[:, :state_width],
        state_act[:, state_width:],
        step_size,
        decay_rate,
        STRETCH,
    )
    mixed = scanned + skip_wide * x_act
    gate_act = jax.nn.silu(gate_raw)
    gated = mixed * gate_act
    inner_total = inner_local * lax.axis_size("tensor")
    square_sum = lax.psum(jnp.sum(gated * gated, axis=1), "tensor")
    gate_scale = lax.rsqrt(square_sum / inner_total + EPSILON)[:, None]
    gate_normed = (gated * gate_scale * gate_gain).astype(jnp.bfloat16)
    partial_out = jnp.dot(gate_normed, out_weight, preferred_element_type=jnp.float32)
    branch_half = lax.psum_scatter(partial_out, "tensor", scatter_dimension=1, tiled=True)
    half_index = lax.axis_index("tensor")
    out_half = (own_rows.astype(jnp.float32) + live_col * branch_half).astype(jnp.bfloat16)
    zero_row = jnp.zeros((1, half_width), jnp.bfloat16)
    reply_rows = jnp.concatenate([out_half, zero_row], axis=0)[slots_back]
    returned = lax.all_to_all(
        reply_rows.reshape(groups, capacity, half_width),
        "dp",
        split_axis=0,
        concat_axis=0,
        tiled=True,
    )
    block_out = returned.reshape(-1, half_width)[back_spot]
    owner_ct = full_grads.astype(jnp.float32)
    out_grad = (owner_ct * live_col).astype(jnp.bfloat16)
    out_weight_grad = jnp.einsum(
        "ti,td->id", gate_normed, out_grad, preferred_element_type=jnp.float32
    )
    normed_out_grad = jnp.einsum(
        "td,id->ti", out_grad, out_weight, preferred_element_type=jnp.float32
    )
    gate_gain_grad = jnp.sum(normed_out_grad * gated * gate_scale, axis=0)
    scaled_grad = gate_gain * normed_out_grad
    cross = lax.psum(jnp.sum(gated * scaled_grad, axis=1), "tensor")[:, None]
    gated_grad = gate_scale * scaled_grad - gated * gate_scale**3 * cross / inner_total
    mixed_grad = gated_grad * gate_act
    gate_raw_grad = gated_grad * mixed * silu_slope(gate_raw)
    skip_gain_grad = jnp.sum(
        (mixed_grad * x_act).reshape(group_rows, heads_local, head_dim), axis=(0, 2)
    )
    x_state_grad, written_grad, readout_grad, step_grad, rate_total = state_backward(
        saved, mixed_grad.reshape(stretches, STRETCH, heads_local, head_dim), decay_rate
    )
    x_act_grad = x_state_grad.reshape(group_rows, inner_local) + skip_wide * mixed_grad
    state_grad = lax.psum(
        jnp.concatenate(
            [written_grad.reshape(group_rows, -1), readout_grad.reshape(group_rows, -1)], axis=1
        ),
        "tensor",
    )
    state_conv_grad = state_grad * silu_slope(state_conv)
    x_conv_grad = x_act_grad * silu_slope(x_conv)
    state_raw_grad, conv_state_grad, conv_state_bias_grad = conv_backward(
        conv_in_state, conv_state, seq_pos, state_conv_grad
    )
    x_raw_grad, conv_inner_grad, conv_inner_bias_grad = conv_backward(
        conv_in_x, conv_inner, seq_pos, x_conv_grad
    )
    step_raw_grad = (
        step_grad.reshape(group_rows, heads_local) * live_col * jax.nn.sigmoid(step_input)
    )
    step_bias_grad = jnp.sum(step_raw_grad, axis=0)
    log_rate_grad = rate_total * decay_rate
    zx_low = jnp.concatenate([gate_raw_grad, x_raw_grad], axis=1).astype(jnp.bfloat16)
    state_low = state_raw_grad.astype(jnp.bfloat16)
    step_low = step_raw_grad.astype(jnp.bfloat16)
    inner_weight_grad = jnp.einsum(
        "td,tk->dk", normed, zx_low, preferred_element_type=jnp.float32
    )
    state_weight_grad = jnp.einsum(
        "td,tk->dk", normed, state_low, preferred_element_type=jnp.float32
    )
    step_weight_grad = jnp.einsum("td,tk->dk", normed, step_low, preferred_element_type=jnp.float32)
    lead_share = (half_index == 0).astype(jnp.float32)
    normed_grad = jnp.einsum("tk,dk->td", zx_low, zx_weight, preferred_element_type=jnp.float32)
    normed_grad = normed_grad + jnp.einsum(
        "tk,dk->td", step_low, step_weight, preferred_element_type=jnp.float32
    )
    normed_grad = normed_grad + lead_share * jnp.einsum(
        "tk,dk->td", state_low, state_weight, preferred_element_type=jnp.float32
    )
    normed_grad = lax.psum(normed_grad, "tensor")
    norm_gain_grad = jnp.sum(normed_grad * hidden * norm_scale, axis=0)
    input_scaled = norm_gain * normed_grad
    hidden_grad = (
        norm_scale * input_scaled
        - hidden * norm_scale**3 * jnp.mean(hidden * input_scaled, axis=1, keepdims=True)
        + owner_ct
    )
    own_grad = lax.dynamic_slice_in_dim(hidden_grad, half_index * half_width, half_width, 1).astype(
        jnp.bfloat16
    )
    answer_rows = jnp.concatenate([own_grad, zero_row], axis=0)[slots_in]
    gone = lax.all_to_all(
        answer_rows.reshape(groups, capacity, half_width),
        "dp",
        split_axis=0,
        concat_axis=0,
        tiled=True,
    )
    input_grad = gone.reshape(-1, half_width)[send_spot]
    (
        conv_inner_grad,
        conv_inner_bias_grad,
        conv_state_grad,
        conv_state_bias_grad,
        step_bias_grad,
        log_rate_grad,
        skip_gain_grad,
        gate_gain_grad,
    ) = lax.psum(
        (
            conv_inner_grad,
            conv_inner_bias_grad,
            conv_state_grad,
            conv_state_bias_grad,
            step_bias_grad,
            log_rate_grad,
            skip_gain_grad,
            gate_gain_grad,
        ),
        "dp",
    )
    zx_share, state_share, step_share, gain_share, out_share = (
        lax.psum_scatter(inner_weight_grad.astype(jnp.bfloat16), "dp", scatter_dimension=0, tiled=True),
        lax.psum_scatter(state_weight_grad, "dp", scatter_dimension=0, tiled=True),
        lax.psum_scatter(step_weight_grad, "dp", scatter_dimension=0, tiled=True),
        lax.psum_scatter(norm_gain_grad, "dp", scatter_dimension=0, tiled=True),
        lax.psum_scatter(out_weight_grad.astype(jnp.bfloat16), "dp", scatter_dimension=1, tiled=True),
    )
    zx_share = zx_share.astype(jnp.float32).reshape((-1,) + inner_weight.shape[1:])
    out_share = out_share.astype(jnp.float32)
    return (
        block_out,
        input_grad,
        gain_share,
        zx_share,
        state_share,
        step_share,
        conv_inner_grad,
        conv_inner_bias_grad,
        conv_state_grad,
        conv_state_bias_grad,
        step_bias_grad,
        log_rate_grad,
        skip_gain_grad,
        gate_gain_grad,
        out_share,
    )


def on_device(*args):
    groups = lax.axis_size("dp")
    rows, half = args[0].shape
    inner, heads, state = args[6].shape[2], args[8].shape[1], args[7].shape[1] // 2
    capacity = 2 * rows // groups
    fits = (
        groups % 4 == 0 and 16 <= 4 * groups <= 64 and capacity % 16 == 0 and (2 * half // groups) % 16 == 0
        and rows == STRETCH and args[2].shape[1] == 1 and inner == 64 * heads and inner == 2 * half
    )
    if fits:
        return fused(Sizes(groups, rows, half, inner, heads, state, capacity), *args)
    return with_collectives(*args)


def solution(mesh):
    placed = (
        P("dp", "tensor"),
        P("dp", "tensor"),
        P("dp", None),
        P(),
        P(),
        P(),
        P(None, None, "tensor"),
        P(),
        P(None, "tensor"),
        P(None, "tensor"),
        P("tensor"),
        P(),
        P(),
        P("tensor"),
        P("tensor"),
        P("tensor"),
        P("tensor"),
        P("tensor", None),
    )
    return jax.shard_map(
        on_device,
        mesh=mesh,
        in_specs=placed,
        out_specs=(
            P("dp", "tensor"),
            P("dp", "tensor"),
            P("dp"),
            P("dp", None, "tensor"),
            P("dp", None),
            P("dp", "tensor"),
            P(None, "tensor"),
            P("tensor"),
            P(),
            P(),
            P("tensor"),
            P("tensor"),
            P("tensor"),
            P("tensor"),
            P("tensor", "dp"),
        ),
        check_vma=False,
    )
```

```python
import functools

import jax
import jax.numpy as jnp
from jax import lax
from jax.experimental import pallas as pl
from jax.experimental.pallas import tpu as pltpu
from jax.sharding import PartitionSpec as P

STRETCH = 256


PRECISE = lax.Precision.HIGHEST
EPSILON = 1e-05


def silu_slope(values):
    logistic = jax.nn.sigmoid(values)
    return logistic * (1.0 + values * (1.0 - logistic))


def stretch_layout(seq_lengths, stretch_rows):
    total_stretches = seq_lengths.shape[0]
    numbers = jnp.arange(total_stretches, dtype=jnp.int32)
    begins = seq_lengths > 0
    first_stretch = jnp.max(
        jnp.where(begins[None, :] & (numbers[None, :] <= numbers[:, None]), numbers[None, :], 0),
        axis=1,
    )
    seq_length = jnp.sum(
        jnp.where(numbers[None, :] == first_stretch[:, None], seq_lengths[None, :], 0), axis=1
    )
    within = (
        jnp.arange(stretch_rows, dtype=jnp.int32)[None, :]
        + ((numbers - first_stretch) * stretch_rows)[:, None]
    )
    live_mask = (within < seq_length[:, None]).astype(jnp.float32).reshape(-1)
    keep_state = 1.0 - begins.astype(jnp.float32)
    return (within.reshape(-1), live_mask, keep_state)


def shift_down(values, steps):
    return jnp.concatenate(
        [jnp.zeros((steps,) + values.shape[1:], values.dtype), values[:-steps]], axis=0
    )


def shift_up(values, steps):
    return jnp.concatenate(
        [values[steps:], jnp.zeros((steps,) + values.shape[1:], values.dtype)], axis=0
    )


def conv_forward(raw_in, tap_weights, tap_bias, seq_pos):
    total = tap_bias[None, :] + tap_weights[0][None, :] * raw_in
    for tap_index in range(1, tap_weights.shape[0]):
        valid = (seq_pos >= tap_index).astype(jnp.float32)[:, None]
        total = total + tap_weights[tap_index][None, :] * shift_down(raw_in, tap_index) * valid
    return total


def conv_backward(raw_in, tap_weights, seq_pos, conv_grad):
    tap_grads = [jnp.sum(conv_grad * raw_in, axis=0)]
    raw_grad = tap_weights[0][None, :] * conv_grad
    for tap_index in range(1, tap_weights.shape[0]):
        masked = conv_grad * (seq_pos >= tap_index).astype(jnp.float32)[:, None]
        tap_grads.append(jnp.sum(masked * shift_down(raw_in, tap_index), axis=0))
        raw_grad = raw_grad + tap_weights[tap_index][None, :] * shift_up(masked, tap_index)
    return (raw_grad, jnp.stack(tap_grads, axis=0), jnp.sum(conv_grad, axis=0))


def send_layout(targets, group_rows, capacity, groups):
    owner_group = targets // group_rows
    onehot = (owner_group[:, None] == jnp.arange(groups, dtype=jnp.int32)[None, :]).astype(
        jnp.int32
    )
    arrival = jnp.sum(jnp.cumsum(onehot, axis=0) * onehot, axis=1) - 1
    return owner_group * capacity + arrival


def arrivals(targets, group_rows, capacity, groups, own_group):
    by_source = targets.reshape(groups, group_rows)
    owner_group = by_source // group_rows
    is_mine = (owner_group == own_group).astype(jnp.int32)
    arrival = jnp.cumsum(is_mine, axis=1) - 1
    position = jnp.arange(groups, dtype=jnp.int32)[:, None] * capacity + arrival
    position = jnp.where(is_mine > 0, position, groups * capacity)
    filler = jnp.full((groups * capacity,), group_rows, jnp.int32)
    return filler.at[position.reshape(-1)].set(
        (by_source - owner_group * group_rows).reshape(-1), mode="drop"
    )


def state_forward(x_heads, written, readout, step_size, decay_rate, stretch_rows):
    rows_all, heads, head_dim = x_heads.shape
    stretches = rows_all // stretch_rows
    x_blocks = x_heads.reshape(stretches, stretch_rows, heads, head_dim)
    w_blocks = written.reshape(stretches, stretch_rows, -1)
    r_blocks = readout.reshape(stretches, stretch_rows, -1)
    step_blocks = step_size.reshape(stretches, stretch_rows, heads)
    log_decay = jnp.cumsum(step_blocks * decay_rate[None, None, :], axis=1)
    by_head = jnp.transpose(log_decay, (0, 2, 1))
    causal = jnp.arange(stretch_rows)[:, None] >= jnp.arange(stretch_rows)[None, :]
    spread = by_head[:, :, :, None] - by_head[:, :, None, :]
    fading = jnp.where(causal, jnp.exp(jnp.where(causal, spread, 0.0)), 0.0)
    intersection = jnp.einsum("cin,cjn->cij", r_blocks, w_blocks, precision=PRECISE)
    mixing = intersection[:, None, :, :] * fading
    driven = step_blocks[..., None] * x_blocks
    to_end = jnp.exp(log_decay[:, -1:, :] - log_decay)
    stretch_state = jnp.einsum(
        "cjhp,cjn->chpn", to_end[..., None] * driven, w_blocks, precision=PRECISE
    )
    end_fade = jnp.exp(log_decay[:, -1, :])
    running = jnp.zeros(stretch_state.shape[1:], jnp.float32)
    entering = []
    entering.append(running)
    entering = jnp.stack(entering)
    from_start = jnp.exp(log_decay)
    carried_out = from_start[..., None] * jnp.einsum(
        "chpn,cin->cihp", entering, r_blocks, precision=PRECISE
    )
    inner_out = jnp.einsum("chij,cjhp->cihp", mixing, driven, precision=PRECISE)
    saved = (
        x_blocks,
        w_blocks,
        r_blocks,
        step_blocks,
        causal,
        fading,
        mixing,
        driven,
        to_end,
        entering,
        end_fade,
        from_start,
        carried_out,
    )
    return ((inner_out + carried_out).reshape(rows_all, heads * head_dim), saved)


def state_backward(saved, mixed_grad, decay_rate):
    (
        x_blocks,
        w_blocks,
        r_blocks,
        step_blocks,
        causal,
        fading,
        mixing,
        driven,
        to_end,
        entering,
        end_fade,
        from_start,
        carried_out,
    ) = saved
    stretches = x_blocks.shape[0]
    scaled = from_start[..., None] * mixed_grad
    readout_grad = jnp.einsum("cihp,chpn->cin", scaled, entering, precision=PRECISE)
    from_out = jnp.einsum("cihp,cin->chpn", scaled, r_blocks, precision=PRECISE)
    decay_grad = jnp.sum(carried_out * mixed_grad, axis=3)
    downstream = jnp.zeros(from_out.shape[1:], jnp.float32)
    passed = []
    end_grads = []
    for number in reversed(range(stretches)):
        handed = jnp.zeros_like(downstream)
        passed.append(handed)
        end_grads.append(jnp.sum(handed * entering[number], axis=(1, 2)))
        downstream = from_out[number] + end_fade[number][:, None, None] * handed
    passed = jnp.stack(passed[::-1])
    end_grads = jnp.stack(end_grads[::-1])
    pulled = jnp.einsum("chpn,cjn->cjhp", passed, w_blocks, precision=PRECISE)
    driven_grad = to_end[..., None] * pulled
    written_grad = jnp.einsum(
        "cjhp,chpn->cjn", to_end[..., None] * driven, passed, precision=PRECISE
    )
    tail_grad = jnp.sum(pulled * driven, axis=3) * to_end
    decay_grad = decay_grad - tail_grad
    last_extra = jnp.sum(tail_grad, axis=1) + end_grads * end_fade
    mixing_grad = jnp.where(
        causal, jnp.einsum("cihp,cjhp->chij", mixed_grad, driven, precision=PRECISE), 0.0
    )
    driven_grad = driven_grad + jnp.einsum("chij,cihp->cjhp", mixing, mixed_grad, precision=PRECISE)
    intersection_grad = jnp.sum(mixing_grad * fading, axis=1)
    readout_grad = readout_grad + jnp.einsum(
        "cij,cjn->cin", intersection_grad, w_blocks, precision=PRECISE
    )
    written_grad = written_grad + jnp.einsum(
        "cij,cin->cjn", intersection_grad, r_blocks, precision=PRECISE
    )
    product = mixing_grad * mixing
    decay_grad = decay_grad + jnp.transpose(
        jnp.sum(product, axis=3) - jnp.sum(product, axis=2), (0, 2, 1)
    )
    decay_grad = decay_grad.at[:, -1, :].add(last_extra)
    step_grad = jnp.sum(driven_grad * x_blocks, axis=3)
    x_state_grad = step_blocks[..., None] * driven_grad
    rate_grad = jnp.flip(jnp.cumsum(jnp.flip(decay_grad, axis=1), axis=1), axis=1)
    step_grad = step_grad + rate_grad * decay_rate[None, None, :]
    rate_total = jnp.sum(rate_grad * step_blocks, axis=(0, 1))
    return (x_state_grad, written_grad, readout_grad, step_grad, rate_total)


MESH = pl.DeviceIdType.MESH
BF = jnp.bfloat16
F32 = jnp.float32
NEG = -1e30


def dot_nn(a, b):
    return lax.dot_general(a, b, (((1,), (0,)), ((), ())), preferred_element_type=F32)


def dot_nt(a, b):
    return lax.dot_general(a, b, (((1,), (1,)), ((), ())), preferred_element_type=F32)


def dot_tn(a, b):
    return lax.dot_general(a, b, (((0,), (0,)), ((), ())), preferred_element_type=F32)


def iota(shape, axis):
    return lax.broadcasted_iota(jnp.int32, shape, axis)


def one_hot(cond):
    return jnp.where(cond, 1.0, 0.0).astype(BF)


def split3(v):
    high = v.astype(BF)
    rest = v - high.astype(F32)
    mid = rest.astype(BF)
    return high, mid, (rest - mid.astype(F32)).astype(BF)


def sigmoid(v):
    return 1.0 / (1.0 + jnp.exp(-v))


def rows_down(v, k):
    return jnp.where(iota(v.shape, 0) >= k, pltpu.roll(v, k, 0), 0.0)


def rows_up(v, k):
    n = v.shape[0]
    return jnp.where(iota(v.shape, 0) < n - k, pltpu.roll(v, n - k, 0), 0.0)


def pick(v, lane, index):
    return jnp.sum(jnp.where(lane == index, v, 0.0), axis=1, keepdims=True)


class Sizes:
    def __init__(self, dp, rows, half, inner, heads, state, capacity):
        self.dp, self.rows, self.half, self.inner = dp, rows, half, inner
        self.heads, self.state, self.cap = heads, state, capacity
        self.width = 2 * half
        self.nz = dp // 4
        self.share = self.width // dp
        self.quarter = self.nz * self.share
        self.slots = dp * capacity
        self.tiles = inner // 128
        self.extra = 2 * state + 128
        self.cols = 3 * inner + self.extra
        n = inner // 2
        self.chunks = [(i * n, n) for i in range(6)] + [(6 * n, self.extra)]
        self.levels = self.nz.bit_length() - 1


def targets_of(lines, sz):
    n = sz.rows // 128
    return jnp.concatenate([lines[pl.ds(k, sz.dp, stride=n), :] for k in range(n)], axis=1)


def send_table(targets, g, sz):
    strict = one_hot(iota((sz.rows, sz.rows), 0) < iota((sz.rows, sz.rows), 1))
    every = targets_of(targets, sz)
    own = jnp.sum(jnp.where(iota(every.shape, 0) == g, every, 0), axis=0, keepdims=True)
    group = lax.shift_right_logical(own, 8)
    hot = jnp.where(iota((sz.dp, sz.rows), 0) == group, 1.0, 0.0)
    before = dot_nn(hot.astype(BF), strict)
    rank = jnp.sum(hot * before, axis=0, keepdims=True)
    spot = group.astype(F32) * sz.cap + rank
    return one_hot(iota((sz.slots, sz.rows), 0).astype(F32) == spot)


def owner_table(targets, g, sz):
    strict = one_hot(iota((sz.rows, sz.rows), 0) < iota((sz.rows, sz.rows), 1))
    every = targets_of(targets, sz)
    mine = jnp.where(lax.shift_right_logical(every, 8) == g, 1.0, 0.0)
    rank = dot_nn(mine.astype(BF), strict)
    slot = mine * ((every & 255) + 1).astype(F32)
    lane = iota((sz.dp, 128), 1)
    found = jnp.zeros((sz.dp, 128), F32)
    for a in range(sz.cap):
        one = jnp.sum(jnp.where(rank == float(a), slot, 0.0), axis=1, keepdims=True)
        found = jnp.where(lane == a, one, found)
    place = iota((128, sz.slots), 1)
    spread = one_hot((place % sz.cap) == iota((128, sz.slots), 0))
    wide = dot_nn(found.astype(BF), spread)
    keep = (iota((sz.dp, sz.slots), 1) // sz.cap) == iota((sz.dp, sz.slots), 0)
    row = jnp.sum(jnp.where(keep, wide, 0.0), axis=0, keepdims=True) - 1.0
    return one_hot(iota((sz.rows, sz.slots), 0).astype(F32) == row)


def block_kernel(sz, *refs):
    (dest, back, length, rows_hbm, ct_hbm, win_hbm, wout_hbm, wst_hbm, wstep_in,
     tap_x, bias_x, gain_g, gain_n, skip_in, tap_s, bias_s, bias_step, log_rate,
     out_rows, out_grads, inner_out, proj_out, extra_out, small_out, gain_out,
     win, wout, wst, wstep, lines,
     pk_in, pk_ct, rc_in, rc_ct, ry_in, ry_ct, gn_o, gn_g,
     p_in, p_bk, q_in, q_bk,
     hid, cts, normed, lowct, perm, xA, xE, tA, tE,
     yb, pb, r0, rl,
     inter, interT, igrad, ptile,
     sraw, sslope, wr, dtv, lac, lar, sgr, rgr, stepsig, acc1, acc2, scale,
     stat_s, stat_r, half_s, half_r, st_s, st_r,
     sms, smr, gall, gsum,
     a2a_s, a2a_r, fw_s, fw_r, quad_s, quad_r, xq_s, xq_r, z_s, z_r, y_s, y_r, gg_s, gg_r, sm_s, sm_r, w_s, o_s) = refs
    dp, R, H, C = sz.dp, sz.rows, sz.half, sz.inner
    W, NT_ = sz.width, sz.tiles
    g = lax.axis_index("dp")
    t = lax.axis_index("tensor")
    o = 1 - t
    c, x, z = g % 2, (g // 2) % 2, g // 4
    q = g % 4
    sib, xp = g + 1 - 2 * c, g + 2 - 4 * x
    diag = sib + 2 - 4 * x

    def rcopy(src, dst, ss, rs, peer, side=None):
        return pltpu.make_async_remote_copy(
            src_ref=src, dst_ref=dst, send_sem=ss, recv_sem=rs,
            device_id=(peer, t if side is None else side), device_id_type=MESH)

    sent = []

    def go(copy):
        copy.start()
        sent.append(copy)
        return copy

    loads = [pltpu.make_async_copy(a, b, w_s.at[i]) for i, (a, b) in enumerate(
        [(rows_hbm, cts.at[0]), (ct_hbm, cts.at[1]), (wst_hbm, wst), (wout_hbm, wout)])]
    for load in loads[:2]:
        load.start()

    barrier = pltpu.get_barrier_semaphore()
    for off in range(1, dp):
        pl.semaphore_signal(barrier, inc=1, device_id=((g + off) % dp, t), device_id_type=MESH)
    pl.semaphore_signal(barrier, inc=1, device_id=(g, o), device_id_type=MESH)

    far = [(g + k) % dp for k in sorted(range(1, dp), key=lambda k: (abs(k - dp // 2), k))]

    def exchange(i, source, target):
        copies = []
        for peer in far:
            copies.append(rcopy(source.at[peer], target.at[g], a2a_s.at[i, peer], a2a_r.at[i, g], peer))
            copies[-1].start()
        target[pl.ds(g, 1)] = source[pl.ds(g, 1)]
        return copies

    def settle(copies):
        for copy in copies:
            copy.wait_send()

    def arrived(i, target, src):
        rcopy(target.at[src], target.at[src], a2a_s.at[i, src], a2a_r.at[i, src], src).wait_recv()

    def pack(table, source, target):
        for k in range(2):
            n = sz.slots // 2
            part = dot_nn(table[k * n:(k + 1) * n, :], source[...]).astype(BF)
            target[k * (dp // 2):(k + 1) * (dp // 2)] = part.reshape(dp // 2, sz.cap, H)

    p_in[...] = send_table(dest, g, sz)
    loads[0].wait()
    pack(p_in, cts.at[0], pk_in)
    pl.semaphore_wait(barrier, dp)
    rows_away = exchange(0, pk_in, rc_in)
    for load in loads[2:]:
        load.start()
    p_bk[...] = send_table(back, g, sz)
    loads[1].wait()
    pack(p_bk, cts.at[1], pk_ct)
    grads_away = exchange(1, pk_ct, rc_ct)
    q_in[...] = owner_table(dest, g, sz)
    q_bk[...] = owner_table(back, g, sz)

    def forward(i, arr, dst, src):
        arrived(i, arr, src)
        return rcopy(arr.at[src], dst.at[src], fw_s.at[i, src], fw_r.at[i, src], g, o)

    def own_forward(i, arr, dst):
        go(rcopy(arr.at[g], dst.at[g], fw_s.at[i, g], fw_r.at[i, g], g, o))

    own_forward(0, rc_in, ry_in)
    row_forwards = [rcopy(rc_in.at[src], ry_in.at[src], fw_s.at[0, src], fw_r.at[0, src], g, o) for src in far]
    sent.extend(row_forwards)

    def forward_rows(k):
        arrived(0, rc_in, far[k])
        row_forwards[k].start()

    def take_apart(stage, sems):
        n = W // 128
        fetch = [pltpu.make_async_copy(win_hbm.at[pl.ds(k * 128, 128)], stage.at[k % 4], sems.at[k % 4]) for k in range(n)]
        for copy in fetch[:4]:
            copy.start()
        place = iota((256, 256), 0)
        order = one_hot(iota((256, 256), 1) == jnp.where(place < 128, 2 * place, 2 * place - 255))
        for k in range(n):
            fetch[k].wait()
            for m in range(0, C, 256):
                pair = jnp.concatenate(
                    [stage[k % 4, :, :, m + e:m + e + 128].reshape(256, 128) for e in (0, 128)], axis=1)
                both = dot_nn(order, pair).astype(BF)
                win[k * 128:(k + 1) * 128, m:m + 256] = both[:128]
                win[k * 128:(k + 1) * 128, C + m:C + m + 256] = both[128:]
            if k + 4 < n:
                fetch[k + 4].start()
            if k < dp - 1:
                forward_rows(k)

    pl.run_scoped(take_apart, pltpu.VMEM((4, 128, 2, C), BF), pltpu.SemaphoreType.DMA((4,)))
    for k in range(W // 128, dp - 1):
        forward_rows(k)
    own_forward(1, rc_ct, ry_ct)
    hid[pl.ds(t, 1)] = dot_nn(q_in[...], rc_in[...].reshape(sz.slots, H)).astype(BF)[None]
    for d in range(dp):
        rcopy(ry_in.at[d], ry_in.at[d], fw_s.at[0, d], fw_r.at[0, d], g, o).wait_recv()
    hid[pl.ds(o, 1)] = dot_nn(q_in[...], ry_in[...].reshape(sz.slots, H)).astype(BF)[None]

    total = jnp.zeros((R, 128), F32)
    for k in range(W // 128):
        v = hid[k // (H // 128), :, (k % (H // 128)) * 128:(k % (H // 128)) * 128 + 128].astype(F32)
        total = total + v * v
    norm_scale = lax.rsqrt(jnp.sum(total, axis=1, keepdims=True) / W + EPSILON)
    scale[...] = jnp.broadcast_to(norm_scale, (R, 128))
    for k in range(W // 128):
        v = hid[k // (H // 128), :, (k % (H // 128)) * 128:(k % (H // 128)) * 128 + 128].astype(F32)
        normed[:, k * 128:(k + 1) * 128] = (v * scale[...] * gain_n[:, k * 128:(k + 1) * 128]).astype(BF)

    def quarters(source):
        for qq in range(4):
            perm[qq] = jnp.concatenate(
                [source[:, sz.share * (4 * zz + qq):sz.share * (4 * zz + qq + 1)] for zz in range(sz.nz)], axis=1)

    def send_quarter(i, dst):
        copies = [
            rcopy(perm.at[peer % 4], dst.at[rel], xq_s.at[i, rel - 1], xq_r.at[i, rel - 1], peer)
            for rel, peer in ((2, xp), (3, diag), (1, sib))]
        for copy in copies:
            copy.start()
        dst[0:1] = perm[pl.ds(q, 1)]
        return copies

    def turn_quarter(i, dst, turned):
        for rel, peer in ((1, sib), (2, xp), (3, diag)):
            rcopy(dst.at[rel], dst.at[rel], xq_s.at[i, rel - 1], xq_r.at[i, rel - 1], peer).wait_recv()
        for rel in range(4):
            turned[:, rel * R:(rel + 1) * R] = jnp.transpose(dst[rel].astype(F32)).astype(BF)

    quarters(normed)
    quarter_away = send_quarter(0, xA)

    loads[2].wait()
    wstep[...] = jnp.zeros_like(wstep)
    wstep[:sz.heads] = wstep_in[...]
    lines[...] = jnp.zeros_like(lines)
    lines[0:1, :sz.heads] = bias_step[...]
    lines[1:2, :sz.heads] = log_rate[...]
    row = iota((R, 128), 0)
    lane = iota((R, 128), 1)
    live = jnp.where(row < length[0, 0], 1.0, 0.0)
    sraw[...] = dot_nn(normed[...], wst[...])
    step_in = dot_nt(normed[...], wstep[...]) + lines[0:1, :]
    S = sz.state
    for k in range(2):
        cut = slice(k * S, (k + 1) * S)
        raw = sraw[:, cut]
        conv = bias_s[:, cut] + tap_s[0:1, cut] * raw
        for tap in range(1, 4):
            conv = conv + tap_s[tap:tap + 1, cut] * rows_down(raw, tap)
        sg = sigmoid(conv)
        sslope[:, cut] = sg * (1.0 + conv * (1.0 - sg))
        wr[:, cut] = (conv * sg).astype(BF)
    written, readout = wr[:, :S], wr[:, S:]
    inter[...] = dot_nt(readout, written)
    interT[...] = dot_nt(written, readout)
    stepsig[...] = sigmoid(step_in) * live
    heads_live = jnp.where(lane < sz.heads, live, 0.0)
    step = (jnp.maximum(step_in, 0.0) + jnp.log1p(jnp.exp(-jnp.abs(step_in)))) * heads_live
    rate = -jnp.exp(lines[1:2, :])
    dtv[...] = step
    lower = one_hot(iota((R, R), 0) >= iota((R, R), 1))
    log_decay = sum(dot_nn(lower, part) for part in split3(step * rate))
    lac[...] = log_decay
    lar[...] = jnp.transpose(log_decay)

    def cols_of(i):
        return pl.ds(sz.chunks[i][0], sz.chunks[i][1])

    def quad_send(i):
        at = cols_of(i)
        go(rcopy(yb.at[0, :, at], yb.at[2, :, at], quad_s.at[i, 1], quad_r.at[i, 1], xp))
        go(rcopy(yb.at[0, :, at], yb.at[1, :, at], quad_s.at[i, 0], quad_r.at[i, 0], sib))

    def quad_pass(i):
        at = cols_of(i)
        rcopy(yb.at[2, :, at], yb.at[2, :, at], quad_s.at[i, 1], quad_r.at[i, 1], xp).wait_recv()
        go(rcopy(yb.at[2, :, at], yb.at[3, :, at], quad_s.at[i, 2], quad_r.at[i, 2], sib))

    def z_peer(level):
        bit = (z // 2 ** level) % 2
        return bit, g + (1 - 2 * bit) * 4 * 2 ** level

    bases = []
    at0 = 0
    for level in range(sz.levels):
        bases.append(at0)
        at0 += sz.nz // 2 ** (level + 1)
    landing = [r0, rl]

    def z_send(i, level):
        bit, peer = z_peer(level)
        at = cols_of(i)
        for k in range(sz.nz // 2 ** (level + 1)):
            low = z % 2 ** level
            block = (2 * k + 1 - bit) * 2 ** level + low
            go(rcopy(pb.at[block, :, at], landing[level].at[k, :, at], z_s.at[i, bases[level] + k],
                     z_r.at[i, bases[level] + k], peer))

    def z_add(i, level):
        bit, peer = z_peer(level)
        at = cols_of(i)
        start, size = sz.chunks[i]
        for k in range(sz.nz // 2 ** (level + 1)):
            low = z % 2 ** level
            block = (2 * k + bit) * 2 ** level + low
            sem = bases[level] + k
            rcopy(landing[level].at[k, :, at], landing[level].at[k, :, at], z_s.at[i, sem], z_r.at[i, sem], peer).wait_recv()
            for n in range(0, size, 128):
                cut = slice(start + n, start + n + 128)
                value = pb[pl.ds(block, 1), :, cut].astype(F32)[0] + landing[level][k, :, cut].astype(F32)
                if level + 1 < sz.levels:
                    pb[pl.ds(block, 1), :, cut] = value.astype(BF)[None]
                elif start + n < C:
                    proj_out[:, cut] = value
                elif start + n < 3 * C:
                    inner_out[:, start + n - C:start + n - C + 128] = value
                else:
                    extra_out[:, start + n - 3 * C:start + n - 3 * C + 128] = value

    def partial_sum(i, turned):
        at = cols_of(i)
        start, size = sz.chunks[i]
        rcopy(yb.at[1, :, at], yb.at[1, :, at], quad_s.at[i, 0], quad_r.at[i, 0], sib).wait_recv()
        rcopy(yb.at[3, :, at], yb.at[3, :, at], quad_s.at[i, 2], quad_r.at[i, 2], sib).wait_recv()
        n = 384 if size % 256 else 256

        def body(k, carry):
            at = pl.ds(pl.multiple_of(start + k * n, 128), n)
            part = dot_nn(turned[...], yb[:, :, at].reshape(4 * R, n))
            pb[:, :, at] = part.astype(BF).reshape(sz.nz, sz.share, n)
            return carry
        lax.fori_loop(0, size // n, body, 0)
        z_send(i, 0)

    def remainder(gr, xr, xa, xs, mx, ng):
        def project(dst, base):
            def body(n, carry):
                at = pl.multiple_of(n * 256, 256)
                dst[:, pl.ds(at, 256)] = dot_nn(normed[...], win[:, pl.ds(pl.multiple_of(base + n * 256, 256), 256)])
                return carry
            lax.fori_loop(0, C // 256, body, 0)

        project(xr, C)
        project(gr, 0)

        def send_ct(first, last):
            for src in far[first:last]:
                go(forward(1, rc_ct, ry_ct, src))

        send_ct(0, 7)

        def lanes(p):
            return pl.ds(pl.multiple_of(p * 128, 128), 128)

        B = 64

        def head_line(v, p):
            first = iota((1, 128), 1) < 64
            spot = iota(v.shape, 1)
            return jnp.where(first, pick(v, spot, 2 * p), pick(v, spot, 2 * p + 1))

        def step_columns(p, lane):
            first = lane < 64
            return jnp.where(first, pick(dtv[...], lane, 2 * p), pick(dtv[...], lane, 2 * p + 1))

        acc1[...] = jnp.zeros_like(acc1)
        acc2[...] = jnp.zeros_like(acc2)

        def scan(p, carry):
            at = lanes(p)
            lane = iota((R, 128), 1)
            raw = xr[:, at]
            conv = bias_x[:, at] + tap_x[0:1, at] * raw
            for tap in range(1, 4):
                conv = conv + tap_x[tap:tap + 1, at] * rows_down(raw, tap)
            sg = sigmoid(conv)
            act = conv * sg
            xa[:, at] = act
            xs[:, at] = (sg * (1.0 + conv * (1.0 - sg))).astype(BF)
            driven = act * step_columns(p, lane)
            parts = [jnp.where(lane < 64, driven, 0.0).astype(BF), jnp.where(lane >= 64, driven, 0.0).astype(BF)]
            cols = [pick(lac[...], lane, 2 * p + k) for k in range(2)]
            skip = head_line(skip_in[...], p)
            for b in range(R // B):
                reach = 128 * ((b * B) // 128 + 1)
                cut = slice(b * B, (b + 1) * B)
                causal = iota((B, reach), 0) + b * B >= iota((B, reach), 1)
                mixed = skip * act[cut]
                for k in range(2):
                    spread = cols[k][cut] - lar[pl.ds(2 * p + k, 1), :][:, :reach]
                    fading = jnp.exp(jnp.where(causal, spread, NEG))
                    mixing = (inter[cut, :reach] * fading).astype(BF)
                    mixed = mixed + dot_nn(mixing, parts[k][:reach])
                mx[cut, at] = mixed
                gate = gr[cut, at]
                gated = mixed * gate * sigmoid(gate)
                acc1[cut] += gated * gated
            return carry

        step4 = NT_ // 4
        for k in range(4):
            lax.fori_loop(k * step4, (k + 1) * step4, scan, 0)
            send_ct(7 + k, 8 + k)

        whole = float(2 * C)

        def total_over_sides(i, value):
            stat_s[i] = jnp.transpose(jnp.where(lane == 0, jnp.sum(value, axis=1, keepdims=True), 0.0))[:8]
            return go(rcopy(stat_s.at[i], stat_r.at[i], y_s.at[i], y_r.at[i], g, o))

        def total_here(i):
            both = jnp.concatenate([stat_s[i] + stat_r[i], jnp.zeros((120, R), F32)], axis=0)
            return pick(jnp.transpose(both), lane, 0)

        total_over_sides(0, acc1[...]).wait_recv()
        gate_scale = lax.rsqrt(total_here(0) / whole + EPSILON)
        acc1[...] = jnp.broadcast_to(gate_scale, (R, 128))

        def gate_forward(p, carry):
            at = lanes(p)
            gate = gr[:, at]
            yb[0, :, at] = (mx[:, at] * (gate * sigmoid(gate)) * acc1[...] * gain_g[:, at]).astype(BF)
            return carry
        lax.fori_loop(0, NT_, gate_forward, 0)
        turn_quarter(0, xA, tA)
        quad_send(0)
        quad_send(1)

        send_ct(11, dp - 1)
        loads[3].wait()

        def out_half(side, dst, cast):
            def body(n, carry):
                at = pl.ds(pl.multiple_of(side * H + n * 256, 256), 256)
                dst[:, pl.ds(pl.multiple_of(n * 256, 256), 256)] = dot_nn(yb[0, :, :C], wout[:, at]).astype(cast)
                return carry
            lax.fori_loop(0, H // 256, body, 0)
        out_half(o, half_s.at[0], BF)
        cts[pl.ds(t, 1)] = dot_nn(q_bk[...], rc_ct[...].reshape(sz.slots, H)).astype(BF)[None]
        for d in range(dp):
            rcopy(ry_ct.at[d], ry_ct.at[d], fw_s.at[1, d], fw_r.at[1, d], g, o).wait_recv()
        cts[pl.ds(o, 1)] = dot_nn(q_bk[...], ry_ct[...].reshape(sz.slots, H)).astype(BF)[None]
        for k in range(W // 128):
            v = cts[k // (H // 128), :, (k % (H // 128)) * 128:(k % (H // 128)) * 128 + 128].astype(F32)
            lowct[:, k * 128:(k + 1) * 128] = (v * live).astype(BF)

        def back_project(n, carry):
            at = pl.ds(pl.multiple_of(n * 256, 256), 256)
            ng[:, at] = dot_nt(lowct[...], wout[at, :])
            for k in range(2):
                here = pl.ds(pl.multiple_of(n * 256 + k * 128, 128), 128)
                gate = gr[:, here]
                acc2[...] += mx[:, here] * (gate * sigmoid(gate)) * (gain_g[:, here] * ng[:, here])
            return carry
        lax.fori_loop(0, C // 256, back_project, 0)
        crossed = total_over_sides(1, acc2[...])
        settle(quarter_away)
        quarters(lowct)
        sent.extend(send_quarter(1, xE))
        crossed.wait_recv()
        go(rcopy(half_s.at[0], half_r.at[0], y_s.at[2], y_r.at[2], g, o))
        acc2[...] = acc1[...] * acc1[...] * acc1[...] * (total_here(1) / whole)

        def gate_back(p, carry):
            at = lanes(p)
            gate, mixed, grad = gr[:, at], mx[:, at], ng[:, at]
            sg = sigmoid(gate)
            act = gate * sg
            gated = mixed * act
            gated_grad = acc1[...] * (gain_g[:, at] * grad) - gated * acc2[...]
            sms[0, 5:6, at] = jnp.sum(grad * gated * acc1[...], axis=0, keepdims=True)
            mixed_grad = gated_grad * act
            ng[:, at] = mixed_grad
            sms[0, 6:7, at] = jnp.sum(mixed_grad * xa[:, at], axis=0, keepdims=True)
            yb[0, :, pl.ds(pl.multiple_of(C + p * 128, 128), 128)] = (
                gated_grad * mixed * (sg * (1.0 + gate * (1.0 - sg)))).astype(BF)
            return carry
        lax.fori_loop(0, NT_, gate_back, 0)
        quad_send(2)
        quad_send(3)
        out_half(t, gr, F32)

        igrad[...] = jnp.zeros_like(igrad)
        sgr[...] = jnp.zeros_like(sgr)
        rgr[...] = jnp.zeros_like(rgr)
        ptile[...] = jnp.zeros_like(ptile)

        def scan_back(p, carry):
            at = lanes(p)
            lane = iota((R, 128), 1)
            grad = ng[:, at]
            act = xa[:, at]
            stepw = step_columns(p, lane)
            driven = (act * stepw).astype(BF)
            parts = [jnp.where(lane < 64, grad, 0.0).astype(BF), jnp.where(lane >= 64, grad, 0.0).astype(BF)]
            cols = [pick(lac[...], lane, 2 * p + k) for k in range(2)]
            pieces = []
            for b in range(R // B):
                skip = 128 * ((b * B) // 128)
                cut = slice(b * B, (b + 1) * B)
                causal = iota((B, R - skip), 1) + skip >= iota((B, R - skip), 0) + b * B
                turned = interT[cut, skip:]
                piece = jnp.zeros((B, 128), F32)
                total = igrad[cut, skip:]
                for k in range(2):
                    spread = lar[pl.ds(2 * p + k, 1), :][:, skip:] - cols[k][cut]
                    fading = jnp.exp(jnp.where(causal, spread, NEG))
                    faded = dot_nt(driven[cut], parts[k][skip:]) * fading
                    total = total + faded
                    piece = piece + dot_nn((turned * fading).astype(BF), parts[k][skip:])
                    ptile[k, cut, skip:] = (faded * turned).astype(BF)
                igrad[cut, skip:] = total
                pieces.append(piece)
            strict = one_hot(iota((R, R), 0) > iota((R, R), 1))
            for k in range(2):
                found = []
                for b in range(R // B):
                    skip = 128 * ((b * B) // 128)
                    cut = slice(b * B, (b + 1) * B)
                    causal = iota((B, R - skip), 1) + skip >= iota((B, R - skip), 0) + b * B
                    sums = dot_nn(strict[cut], ptile[k, :, skip:])
                    found.append(jnp.sum(jnp.where(causal, sums, 0.0), axis=1, keepdims=True))
                rgr[...] = jnp.where(lane == 2 * p + k, jnp.concatenate(found, axis=0), rgr[...])
            driven_grad = jnp.concatenate(pieces, axis=0)
            pulled = driven_grad * act
            low = jnp.sum(jnp.where(lane < 64, pulled, 0.0), axis=1, keepdims=True)
            high = jnp.sum(jnp.where(lane >= 64, pulled, 0.0), axis=1, keepdims=True)
            sgr[...] = jnp.where(lane == 2 * p, low, jnp.where(lane == 2 * p + 1, high, sgr[...]))
            conv_grad = (head_line(skip_in[...], p) * grad + stepw * driven_grad) * xs[:, at].astype(F32)
            raw = xr[:, at]
            raw_grad = tap_x[0:1, at] * conv_grad
            sms[0, 0:1, at] = jnp.sum(conv_grad * raw, axis=0, keepdims=True)
            sms[0, 4:5, at] = jnp.sum(conv_grad, axis=0, keepdims=True)
            for tap in range(1, 4):
                up = rows_up(conv_grad, tap)
                raw_grad = raw_grad + tap_x[tap:tap + 1, at] * up
                sms[0, tap:tap + 1, at] = jnp.sum(up * raw, axis=0, keepdims=True)
            yb[0, :, pl.ds(pl.multiple_of(2 * C + p * 128, 128), 128)] = raw_grad.astype(BF)
            return carry

        lax.fori_loop(0, NT_ // 2, scan_back, 0)
        quad_send(4)
        turn_quarter(1, xE, tE)
        quad_pass(0)
        quad_pass(1)
        partial_sum(0, tE)

        rcopy(half_r.at[0], half_r.at[0], y_s.at[2], y_r.at[2], g, o).wait_recv()

        def answer(table, value, dst):
            for k in range(2):
                n = sz.slots // 2
                part = dot_tn(table[:, k * n:(k + 1) * n], value).astype(BF)
                dst[k * (dp // 2):(k + 1) * (dp // 2)] = part.reshape(dp // 2, sz.cap, H)

        pieces = []
        mine = hid[pl.ds(t, 1)][0]
        for k in range(H // 128):
            cut = slice(k * 128, (k + 1) * 128)
            branch = gr[:, cut] + half_r[0, :, cut].astype(F32)
            pieces.append((mine[:, cut].astype(F32) + live * branch).astype(BF))
        settle(rows_away)
        answer(q_bk, jnp.concatenate(pieces, axis=1), pk_in)
        sent.extend(exchange(2, pk_in, gn_o))

        lax.fori_loop(NT_ // 2, NT_, scan_back, 0)
        quad_send(5)

        ig = igrad[...].astype(BF)
        st_s[:, :S] = dot_nn(ig, wr[:, S:]).astype(BF)
        st_s[:, S:] = dot_tn(ig, wr[:, :S]).astype(BF)
        go(rcopy(st_s, st_r, y_s.at[3], y_r.at[3], g, o))
        step_grad = (sgr[...] + rgr[...] * rate) * stepsig[...]
        yb[0, :, 3 * C + 2 * S:] = step_grad.astype(BF)
        sms[0, 7:8, 10 * S:10 * S + 128] = jnp.sum(step_grad, axis=0, keepdims=True)
        sms[0, 7:8, 10 * S + 128:10 * S + 256] = jnp.sum(rgr[...] * dtv[...], axis=0, keepdims=True) * rate
        partial_sum(1, tE)
        rcopy(st_r, st_r, y_s.at[3], y_r.at[3], g, o).wait_recv()
        for k in range(2):
            cut = slice(k * S, (k + 1) * S)
            conv_grad = (st_s[:, cut].astype(F32) + st_r[:, cut].astype(F32)) * sslope[:, cut]
            raw = sraw[:, cut]
            raw_grad = tap_s[0:1, cut] * conv_grad
            sms[0, 7:8, cut] = jnp.sum(conv_grad * raw, axis=0, keepdims=True)
            sms[0, 7:8, 8 * S + k * S:8 * S + (k + 1) * S] = jnp.sum(conv_grad, axis=0, keepdims=True)
            for tap in range(1, 4):
                up = rows_up(conv_grad, tap)
                raw_grad = raw_grad + tap_s[tap:tap + 1, cut] * up
                sms[0, 7:8, tap * 2 * S + k * S:tap * 2 * S + (k + 1) * S] = jnp.sum(up * raw, axis=0, keepdims=True)
            yb[0, :, 3 * C + k * S:3 * C + (k + 1) * S] = raw_grad.astype(BF)
        quad_send(6)

        hops = [2 ** k for k in range(2, dp.bit_length() - 1)] + [1, 2]

        def small_start(i):
            bit = (g // hops[i]) % 2
            go(rcopy(sms.at[i], smr.at[i], sm_s.at[i], sm_r.at[i], g + (1 - 2 * bit) * hops[i]))

        def small_end(i):
            bit = (g // hops[i]) % 2
            rcopy(sms.at[i], smr.at[i], sm_s.at[i], sm_r.at[i], g + (1 - 2 * bit) * hops[i]).wait_recv()
            if i + 1 < len(hops):
                sms[i + 1] = sms[i] + smr[i]
                small_start(i + 1)
            else:
                small_out[...] = sms[i] + smr[i]
        small_start(0)

        acc1[...] = jnp.zeros_like(acc1)

        def normed_grad(side, dst, cast):
            def body(n, carry):
                at = pl.ds(pl.multiple_of(side * H + n * 256, 256), 256)
                value = dot_nt(yb[0, :, C:3 * C], win[at, :])
                mine_state = pl.ds(pl.multiple_of(t * S, 128), S)
                value = value + dot_nt(yb[0, :, pl.ds(pl.multiple_of(3 * C + t * S, 128), S)], wst[at, mine_state])
                value = value + dot_nn(yb[0, :, 3 * C + 2 * S:], wstep[:, at])
                for k in range(2):
                    cut = slice(k * 128, (k + 1) * 128)
                    here = pl.ds(pl.multiple_of(n * 256 + k * 128, 128), 128)
                    there = pl.ds(pl.multiple_of(side * H + n * 256 + k * 128, 128), 128)
                    acc1[...] += hid[pl.ds(side, 1), :, here][0].astype(F32) * (gain_n[:, there] * value[:, cut])
                dst[:, pl.ds(pl.multiple_of(n * 256, 256), 256)] = value.astype(cast)
                return carry
            lax.fori_loop(0, H // 256, body, 0)
        normed_grad(o, half_s.at[1], BF)
        go(rcopy(half_s.at[1], half_r.at[1], y_s.at[4], y_r.at[4], g, o))
        normed_grad(t, gr, F32)
        summed_rows = total_over_sides(2, acc1[...])
        z_add(0, 0)
        z_send(0, 1)
        quad_pass(2)
        partial_sum(2, tA)
        small_end(0)

        rcopy(half_r.at[1], half_r.at[1], y_s.at[4], y_r.at[4], g, o).wait_recv()
        summed_rows.wait_recv()
        pull = total_here(2) / W * (scale[...] * scale[...] * scale[...])
        pieces = []
        mine = hid[pl.ds(t, 1)][0]
        mine_ct = cts[pl.ds(t, 1)][0]
        gall[pl.ds(g, 1)] = jnp.zeros((1, 8, 128), F32)
        for k in range(H // 128):
            cut = slice(k * 128, (k + 1) * 128)
            there = pl.ds(pl.multiple_of(t * H + k * 128, 128), 128)
            value = gr[:, cut] + half_r[1, :, cut].astype(F32)
            rows_here = mine[:, cut].astype(F32)
            gall[pl.ds(g, 1), k:k + 1, :] = jnp.sum(value * rows_here * scale[...], axis=0, keepdims=True)[None]
            pieces.append((scale[...] * (gain_n[:, there] * value) - rows_here * pull
                           + mine_ct[:, cut].astype(F32)).astype(BF))
        settle(grads_away)
        answer(q_in, jnp.concatenate(pieces, axis=1), pk_ct)
        for peer in far:
            go(rcopy(gall.at[g], gall.at[g], gg_s.at[peer], gg_r.at[g], peer))
        sent.extend(exchange(3, pk_ct, gn_g))

        def reduce_further(i):
            z_add(i, 0)
            z_send(i, 1)

        reduce_further(1)
        quad_pass(3)
        partial_sum(3, tA)
        reduce_further(2)
        small_end(1)
        quad_pass(4)
        partial_sum(4, tA)
        reduce_further(3)
        small_end(2)
        z_add(0, 1)
        z_add(1, 1)
        quad_pass(5)
        partial_sum(5, tA)
        reduce_further(4)
        quad_pass(6)
        partial_sum(6, tA)
        z_add(2, 1)
        z_add(3, 1)

        def give(i, value, stage, dst):
            n = R // sz.cap
            stage[:n] = value.astype(BF).reshape(n, sz.cap, H)
            copies = [pltpu.make_async_copy(stage.at[k], dst.at[pl.ds(k * sz.cap, sz.cap)], o_s.at[i, k]) for k in range(n)]
            for copy in copies:
                copy.start()
            return copies

        for src in far:
            arrived(2, gn_o, src)
        stores = give(0, dot_tn(p_bk[...], gn_o[...].reshape(sz.slots, H)), ry_in, out_rows)
        reduce_further(5)
        reduce_further(6)
        small_end(3)
        for src in far:
            rcopy(gall.at[src], gall.at[src], gg_s.at[src], gg_r.at[src], src).wait_recv()
        summed = gall[0]
        for d in range(1, dp):
            summed = summed + gall[d]
        gsum[pl.ds(t, 1)] = summed[None]
        go(rcopy(gsum.at[t], gsum.at[t], y_s.at[5], y_r.at[5], g, o))
        for src in far:
            arrived(3, gn_g, src)
        stores += give(1, dot_tn(p_in[...], gn_g[...].reshape(sz.slots, H)), ry_ct, out_grads)
        z_add(4, 1)
        z_add(5, 1)
        z_add(6, 1)
        rcopy(gsum.at[o], gsum.at[o], y_s.at[5], y_r.at[5], g, o).wait_recv()
        gain_out[...] = gsum[...]
        for copy in sent:
            copy.wait_send()
        for store in stores:
            store.wait()

    big = pltpu.VMEM((R, C), F32)
    pl.run_scoped(remainder, big, big, big, pltpu.VMEM((R, C), BF), big, big)


def finish_kernel(sz, rows, grads, inner, proj, extra, small, gain, o_rows, o_grads, o_gain, o_inner, o_state, o_step,
                  o_tap_x, o_bias_x, o_tap_s, o_bias_s, o_bias_step, o_rate, o_skip, o_gate, o_proj):
    C, S = sz.inner, sz.state
    o_rows[...] = rows[...]
    o_grads[...] = grads[...]
    o_inner[:, 0, :] = inner[:, :C]
    o_inner[:, 1, :] = inner[:, C:]
    o_proj[...] = jnp.transpose(proj[...])
    o_state[...] = extra[:, :2 * S]
    o_step[...] = extra[:, 2 * S:2 * S + sz.heads]
    o_tap_x[...] = small[0:4, :]
    o_bias_x[...] = small[4, :]
    o_gate[...] = small[5, :]
    for k in range(4):
        o_tap_s[k:k + 1, :] = small[7:8, k * 2 * S:(k + 1) * 2 * S]
    o_bias_s[...] = small[7, 8 * S:10 * S]
    o_bias_step[...] = small[7, 10 * S:10 * S + sz.heads]
    o_rate[...] = small[7, 10 * S + 128:10 * S + 128 + sz.heads]
    shape = (C, sz.heads)
    member = one_hot(iota(shape, 0) // (C // sz.heads) == iota(shape, 1))
    skip = jnp.broadcast_to(small[6:7, :], (8, C))
    o_skip[...] = sum(dot_nn(part, member) for part in split3(skip))[0]
    flat = jnp.concatenate([gain[h, k:k + 1, :] for h in range(2) for k in range(sz.half // 128)], axis=1)
    start = lax.axis_index("dp") * sz.share
    moved = pltpu.roll(jnp.broadcast_to(flat, (8, sz.width)), lax.rem(sz.width - start, sz.width), 1)
    o_gain[...] = moved[0, :sz.share]


def fused(sz, block_in, cotangent, lengths, dest_slot, return_slot, norm_gain, inner_weight, state_weight,
          step_weight, conv_inner, conv_inner_bias, conv_state, conv_state_bias, step_bias, log_rate,
          skip_gain, gate_gain, out_weight):
    dp, R, H, C, S = sz.dp, sz.rows, sz.half, sz.inner, sz.state
    W = sz.width

    vm = pl.BlockSpec(memory_space=pltpu.VMEM)
    hb = pl.BlockSpec(memory_space=pl.ANY)
    sm = pl.BlockSpec(memory_space=pltpu.SMEM)
    V = pltpu.VMEM
    packed = V((dp, sz.cap, H), BF)
    D = pltpu.SemaphoreType.DMA
    nch = len(sz.chunks)
    scratch = [
        V((W, 2 * C), BF), V((C, W), BF), V((W, 2 * S), BF), V((128, W), BF), V((8, 128), F32),
        *[packed] * 8,
        V((sz.slots, R), BF), V((sz.slots, R), BF), V((R, sz.slots), BF), V((R, sz.slots), BF),
        V((2, R, H), BF), V((2, R, H), BF), V((R, W), BF), V((R, W), BF),
        V((4, R, sz.quarter), BF), V((4, R, sz.quarter), BF), V((4, R, sz.quarter), BF),
        V((sz.quarter, 4 * R), BF), V((sz.quarter, 4 * R), BF),
        V((4, R, sz.cols), BF), V((sz.nz, sz.share, sz.cols), BF), V((2, sz.share, sz.cols), BF), V((1, sz.share, sz.cols), BF),
        V((R, R), F32), V((R, R), F32), V((R, R), F32), V((2, R, R), BF),
        V((R, 2 * S), F32), V((R, 2 * S), F32), V((R, 2 * S), BF), V((R, 128), F32), V((R, 128), F32), V((128, R), F32),
        V((R, 128), F32), V((R, 128), F32), V((R, 128), F32), V((R, 128), F32), V((R, 128), F32), V((R, 128), F32),
        V((3, 8, R), F32), V((3, 8, R), F32), V((2, R, H), BF), V((2, R, H), BF),
        V((R, 2 * S), BF), V((R, 2 * S), BF),
        V((4, 8, C), F32), V((4, 8, C), F32), V((dp, 8, 128), F32), V((2, 8, 128), F32),
        D((4, dp)), D((4, dp)), D((2, dp)), D((2, dp)), D((nch, 3)), D((nch, 3)), D((2, 3)), D((2, 3)),
        D((nch, sz.nz - 1)), D((nch, sz.nz - 1)), D((6,)), D((6,)), D((dp,)), D((dp,)), D((4,)), D((4,)), D((4,)), D((2, dp)),
    ]
    out = jax.ShapeDtypeStruct
    rows_out, grads_out, inner_g, proj_g, extra_g, small, gain = pl.pallas_call(
        functools.partial(block_kernel, sz),
        out_shape=(out((R, H), BF), out((R, H), BF), out((sz.share, 2 * C), F32), out((sz.share, C), F32),
                   out((sz.share, sz.extra), F32), out((8, C), F32), out((2, 8, 128), F32)),
        in_specs=[vm, vm, sm, hb, hb, hb, hb, hb] + [vm] * 10,
        out_specs=(hb, hb) + (vm,) * 5,
        scratch_shapes=scratch,
        compiler_params=pltpu.CompilerParams(collective_id=0, has_side_effects=True, vmem_limit_bytes=66000000),
        name="block",
    )(dest_slot.reshape(-1, 128), return_slot.reshape(-1, 128), lengths, block_in, cotangent, inner_weight, out_weight,
      state_weight, step_weight.T, conv_inner, conv_inner_bias[None], gate_gain[None], norm_gain[None], skip_gain[None],
      conv_state, conv_state_bias[None], step_bias[None], log_rate[None])
    return pl.pallas_call(
        functools.partial(finish_kernel, sz),
        out_shape=(out((R, H), BF), out((R, H), BF), out((sz.share,), F32), out((sz.share, 2, C), F32),
                   out((sz.share, 2 * S), F32), out((sz.share, sz.heads), F32), out((4, C), F32), out((C,), F32),
                   out((4, 2 * S), F32), out((2 * S,), F32), out((sz.heads,), F32), out((sz.heads,), F32),
                   out((sz.heads,), F32), out((C,), F32), out((C, sz.share), F32)),
        in_specs=[vm] * 7,
        out_specs=(vm,) * 15,
        name="finish",
    )(rows_out, grads_out, inner_g, proj_g, extra_g, small, gain)


def with_collectives(
    block_in,
    cotangent,
    lengths,
    dest_slot,
    return_slot,
    norm_gain,
    inner_weight,
    state_weight,
    step_weight,
    conv_inner,
    conv_inner_bias,
    conv_state,
    conv_state_bias,
    step_bias,
    log_rate,
    skip_gain,
    gate_gain,
    out_weight,
):
    groups = lax.axis_size("dp")
    group_rows = block_in.shape[0]
    half_width = block_in.shape[1]
    capacity = 2 * group_rows // groups
    own_group = lax.axis_index("dp")
    own_dest = lax.dynamic_slice_in_dim(dest_slot, own_group * group_rows, group_rows)
    own_return = lax.dynamic_slice_in_dim(return_slot, own_group * group_rows, group_rows)
    send_spot = send_layout(own_dest, group_rows, capacity, groups)
    back_spot = send_layout(own_return, group_rows, capacity, groups)
    slots_in = arrivals(dest_slot, group_rows, capacity, groups, own_group)
    slots_back = arrivals(return_slot, group_rows, capacity, groups, own_group)
    blank_rows = jnp.zeros((groups * capacity, half_width), jnp.bfloat16)
    packed_rows = blank_rows.at[send_spot].set(block_in).reshape(groups, capacity, half_width)
    packed_grads = blank_rows.at[back_spot].set(cotangent).reshape(groups, capacity, half_width)
    came_rows, came_grads = (
        lax.all_to_all(packed_rows, "dp", split_axis=0, concat_axis=0, tiled=True),
        lax.all_to_all(packed_grads, "dp", split_axis=0, concat_axis=0, tiled=True),
    )
    empty_rows = jnp.zeros((group_rows, half_width), jnp.bfloat16)
    own_rows = empty_rows.at[slots_in].set(came_rows.reshape(-1, half_width), mode="drop")
    own_grads = empty_rows.at[slots_back].set(came_grads.reshape(-1, half_width), mode="drop")
    full_rows, full_grads = (
        lax.all_gather(own_rows, "tensor", axis=1, tiled=True),
        lax.all_gather(own_grads, "tensor", axis=1, tiled=True),
    )
    seq_pos, live_mask, keep_state = stretch_layout(lengths[0], STRETCH)
    live_col = live_mask[:, None]
    hidden = full_rows.astype(jnp.float32)
    norm_scale = lax.rsqrt(jnp.mean(hidden * hidden, axis=1, keepdims=True) + EPSILON)
    normed = (hidden * norm_scale * norm_gain).astype(jnp.bfloat16)
    inner_local = inner_weight.shape[2]
    zx_weight = inner_weight.reshape(inner_weight.shape[0], 2 * inner_local)
    projected = jnp.dot(normed, zx_weight, preferred_element_type=jnp.float32)
    gate_raw = projected[:, :inner_local]
    conv_in_x = projected[:, inner_local:]
    conv_in_state = jnp.dot(normed, state_weight, preferred_element_type=jnp.float32)
    step_raw = jnp.dot(normed, step_weight, preferred_element_type=jnp.float32)
    x_conv = conv_forward(conv_in_x, conv_inner, conv_inner_bias, seq_pos)
    state_conv = conv_forward(conv_in_state, conv_state, conv_state_bias, seq_pos)
    x_act = jax.nn.silu(x_conv)
    state_act = jax.nn.silu(state_conv)
    state_width = state_act.shape[1] // 2
    heads_local = step_weight.shape[1]
    head_dim = inner_local // heads_local
    stretches = group_rows // STRETCH
    step_input = step_raw + step_bias[None, :]
    step_size = jax.nn.softplus(step_input) * live_col
    decay_rate = -jnp.exp(log_rate)
    skip_wide = jnp.repeat(skip_gain, head_dim)[None, :]
    scanned, saved = state_forward(
        x_act.reshape(group_rows, heads_local, head_dim),
        state_act[:, :state_width],
        state_act[:, state_width:],
        step_size,
        decay_rate,
        STRETCH,
    )
    mixed = scanned + skip_wide * x_act
    gate_act = jax.nn.silu(gate_raw)
    gated = mixed * gate_act
    inner_total = inner_local * lax.axis_size("tensor")
    square_sum = lax.psum(jnp.sum(gated * gated, axis=1), "tensor")
    gate_scale = lax.rsqrt(square_sum / inner_total + EPSILON)[:, None]
    gate_normed = (gated * gate_scale * gate_gain).astype(jnp.bfloat16)
    partial_out = jnp.dot(gate_normed, out_weight, preferred_element_type=jnp.float32)
    branch_half = lax.psum_scatter(partial_out, "tensor", scatter_dimension=1, tiled=True)
    half_index = lax.axis_index("tensor")
    out_half = (own_rows.astype(jnp.float32) + live_col * branch_half).astype(jnp.bfloat16)
    zero_row = jnp.zeros((1, half_width), jnp.bfloat16)
    reply_rows = jnp.concatenate([out_half, zero_row], axis=0)[slots_back]
    returned = lax.all_to_all(
        reply_rows.reshape(groups, capacity, half_width),
        "dp",
        split_axis=0,
        concat_axis=0,
        tiled=True,
    )
    block_out = returned.reshape(-1, half_width)[back_spot]
    owner_ct = full_grads.astype(jnp.float32)
    out_grad = (owner_ct * live_col).astype(jnp.bfloat16)
    out_weight_grad = jnp.einsum(
        "ti,td->id", gate_normed, out_grad, preferred_element_type=jnp.float32
    )
    normed_out_grad = jnp.einsum(
        "td,id->ti", out_grad, out_weight, preferred_element_type=jnp.float32
    )
    gate_gain_grad = jnp.sum(normed_out_grad * gated * gate_scale, axis=0)
    scaled_grad = gate_gain * normed_out_grad
    cross = lax.psum(jnp.sum(gated * scaled_grad, axis=1), "tensor")[:, None]
    gated_grad = gate_scale * scaled_grad - gated * gate_scale**3 * cross / inner_total
    mixed_grad = gated_grad * gate_act
    gate_raw_grad = gated_grad * mixed * silu_slope(gate_raw)
    skip_gain_grad = jnp.sum(
        (mixed_grad * x_act).reshape(group_rows, heads_local, head_dim), axis=(0, 2)
    )
    x_state_grad, written_grad, readout_grad, step_grad, rate_total = state_backward(
        saved, mixed_grad.reshape(stretches, STRETCH, heads_local, head_dim), decay_rate
    )
    x_act_grad = x_state_grad.reshape(group_rows, inner_local) + skip_wide * mixed_grad
    state_grad = lax.psum(
        jnp.concatenate(
            [written_grad.reshape(group_rows, -1), readout_grad.reshape(group_rows, -1)], axis=1
        ),
        "tensor",
    )
    state_conv_grad = state_grad * silu_slope(state_conv)
    x_conv_grad = x_act_grad * silu_slope(x_conv)
    state_raw_grad, conv_state_grad, conv_state_bias_grad = conv_backward(
        conv_in_state, conv_state, seq_pos, state_conv_grad
    )
    x_raw_grad, conv_inner_grad, conv_inner_bias_grad = conv_backward(
        conv_in_x, conv_inner, seq_pos, x_conv_grad
    )
    step_raw_grad = (
        step_grad.reshape(group_rows, heads_local) * live_col * jax.nn.sigmoid(step_input)
    )
    step_bias_grad = jnp.sum(step_raw_grad, axis=0)
    log_rate_grad = rate_total * decay_rate
    zx_low = jnp.concatenate([gate_raw_grad, x_raw_grad], axis=1).astype(jnp.bfloat16)
    state_low = state_raw_grad.astype(jnp.bfloat16)
    step_low = step_raw_grad.astype(jnp.bfloat16)
    inner_weight_grad = jnp.einsum(
        "td,tk->dk", normed, zx_low, preferred_element_type=jnp.float32
    )
    state_weight_grad = jnp.einsum(
        "td,tk->dk", normed, state_low, preferred_element_type=jnp.float32
    )
    step_weight_grad = jnp.einsum("td,tk->dk", normed, step_low, preferred_element_type=jnp.float32)
    lead_share = (half_index == 0).astype(jnp.float32)
    normed_grad = jnp.einsum("tk,dk->td", zx_low, zx_weight, preferred_element_type=jnp.float32)
    normed_grad = normed_grad + jnp.einsum(
        "tk,dk->td", step_low, step_weight, preferred_element_type=jnp.float32
    )
    normed_grad = normed_grad + lead_share * jnp.einsum(
        "tk,dk->td", state_low, state_weight, preferred_element_type=jnp.float32
    )
    normed_grad = lax.psum(normed_grad, "tensor")
    norm_gain_grad = jnp.sum(normed_grad * hidden * norm_scale, axis=0)
    input_scaled = norm_gain * normed_grad
    hidden_grad = (
        norm_scale * input_scaled
        - hidden * norm_scale**3 * jnp.mean(hidden * input_scaled, axis=1, keepdims=True)
        + owner_ct
    )
    own_grad = lax.dynamic_slice_in_dim(hidden_grad, half_index * half_width, half_width, 1).astype(
        jnp.bfloat16
    )
    answer_rows = jnp.concatenate([own_grad, zero_row], axis=0)[slots_in]
    gone = lax.all_to_all(
        answer_rows.reshape(groups, capacity, half_width),
        "dp",
        split_axis=0,
        concat_axis=0,
        tiled=True,
    )
    input_grad = gone.reshape(-1, half_width)[send_spot]
    (
        conv_inner_grad,
        conv_inner_bias_grad,
        conv_state_grad,
        conv_state_bias_grad,
        step_bias_grad,
        log_rate_grad,
        skip_gain_grad,
        gate_gain_grad,
    ) = lax.psum(
        (
            conv_inner_grad,
            conv_inner_bias_grad,
            conv_state_grad,
            conv_state_bias_grad,
            step_bias_grad,
            log_rate_grad,
            skip_gain_grad,
            gate_gain_grad,
        ),
        "dp",
    )
    zx_share, state_share, step_share, gain_share, out_share = (
        lax.psum_scatter(inner_weight_grad.astype(jnp.bfloat16), "dp", scatter_dimension=0, tiled=True),
        lax.psum_scatter(state_weight_grad, "dp", scatter_dimension=0, tiled=True),
        lax.psum_scatter(step_weight_grad, "dp", scatter_dimension=0, tiled=True),
        lax.psum_scatter(norm_gain_grad, "dp", scatter_dimension=0, tiled=True),
        lax.psum_scatter(out_weight_grad.astype(jnp.bfloat16), "dp", scatter_dimension=1, tiled=True),
    )
    zx_share = zx_share.astype(jnp.float32).reshape((-1,) + inner_weight.shape[1:])
    out_share = out_share.astype(jnp.float32)
    return (
        block_out,
        input_grad,
        gain_share,
        zx_share,
        state_share,
        step_share,
        conv_inner_grad,
        conv_inner_bias_grad,
        conv_state_grad,
        conv_state_bias_grad,
        step_bias_grad,
        log_rate_grad,
        skip_gain_grad,
        gate_gain_grad,
        out_share,
    )


def on_device(*args):
    groups = lax.axis_size("dp")
    rows, half = args[0].shape
    inner, heads, state = args[6].shape[2], args[8].shape[1], args[7].shape[1] // 2
    capacity = 2 * rows // groups
    fits = (
        groups % 4 == 0 and 16 <= 4 * groups <= 64 and capacity % 16 == 0 and (2 * half // groups) % 16 == 0
        and rows == STRETCH and args[2].shape[1] == 1 and inner == 64 * heads and inner == 2 * half
    )
    if fits:
        return fused(Sizes(groups, rows, half, inner, heads, state, capacity), *args)
    return with_collectives(*args)


def solution(mesh):
    placed = (
        P("dp", "tensor"),
        P("dp", "tensor"),
        P("dp", None),
        P(),
        P(),
        P(),
        P(None, None, "tensor"),
        P(),
        P(None, "tensor"),
        P(None, "tensor"),
        P("tensor"),
        P(),
        P(),
        P("tensor"),
        P("tensor"),
        P("tensor"),
        P("tensor"),
        P("tensor", None),
    )
    return jax.shard_map(
        on_device,
        mesh=mesh,
        in_specs=placed,
        out_specs=(
            P("dp", "tensor"),
            P("dp", "tensor"),
            P("dp"),
            P("dp", None, "tensor"),
            P("dp", None),
            P("dp", "tensor"),
            P(None, "tensor"),
            P("tensor"),
            P(),
            P(),
            P("tensor"),
            P("tensor"),
            P("tensor"),
            P("tensor"),
            P("tensor", "dp"),
        ),
        check_vma=False,
    )
```

```python
import functools

import jax
import jax.numpy as jnp
from jax import lax
from jax.experimental import pallas as pl
from jax.experimental.pallas import tpu as pltpu
from jax.sharding import PartitionSpec as P

STRETCH = 256


PRECISE = lax.Precision.HIGHEST
EPSILON = 1e-05


def silu_slope(values):
    logistic = jax.nn.sigmoid(values)
    return logistic * (1.0 + values * (1.0 - logistic))


def stretch_layout(seq_lengths, stretch_rows):
    total_stretches = seq_lengths.shape[0]
    numbers = jnp.arange(total_stretches, dtype=jnp.int32)
    begins = seq_lengths > 0
    first_stretch = jnp.max(
        jnp.where(begins[None, :] & (numbers[None, :] <= numbers[:, None]), numbers[None, :], 0),
        axis=1,
    )
    seq_length = jnp.sum(
        jnp.where(numbers[None, :] == first_stretch[:, None], seq_lengths[None, :], 0), axis=1
    )
    within = (
        jnp.arange(stretch_rows, dtype=jnp.int32)[None, :]
        + ((numbers - first_stretch) * stretch_rows)[:, None]
    )
    live_mask = (within < seq_length[:, None]).astype(jnp.float32).reshape(-1)
    keep_state = 1.0 - begins.astype(jnp.float32)
    return (within.reshape(-1), live_mask, keep_state)


def shift_down(values, steps):
    return jnp.concatenate(
        [jnp.zeros((steps,) + values.shape[1:], values.dtype), values[:-steps]], axis=0
    )


def shift_up(values, steps):
    return jnp.concatenate(
        [values[steps:], jnp.zeros((steps,) + values.shape[1:], values.dtype)], axis=0
    )


def conv_forward(raw_in, tap_weights, tap_bias, seq_pos):
    total = tap_bias[None, :] + tap_weights[0][None, :] * raw_in
    for tap_index in range(1, tap_weights.shape[0]):
        valid = (seq_pos >= tap_index).astype(jnp.float32)[:, None]
        total = total + tap_weights[tap_index][None, :] * shift_down(raw_in, tap_index) * valid
    return total


def conv_backward(raw_in, tap_weights, seq_pos, conv_grad):
    tap_grads = [jnp.sum(conv_grad * raw_in, axis=0)]
    raw_grad = tap_weights[0][None, :] * conv_grad
    for tap_index in range(1, tap_weights.shape[0]):
        masked = conv_grad * (seq_pos >= tap_index).astype(jnp.float32)[:, None]
        tap_grads.append(jnp.sum(masked * shift_down(raw_in, tap_index), axis=0))
        raw_grad = raw_grad + tap_weights[tap_index][None, :] * shift_up(masked, tap_index)
    return (raw_grad, jnp.stack(tap_grads, axis=0), jnp.sum(conv_grad, axis=0))


def send_layout(targets, group_rows, capacity, groups):
    owner_group = targets // group_rows
    onehot = (owner_group[:, None] == jnp.arange(groups, dtype=jnp.int32)[None, :]).astype(
        jnp.int32
    )
    arrival = jnp.sum(jnp.cumsum(onehot, axis=0) * onehot, axis=1) - 1
    return owner_group * capacity + arrival


def arrivals(targets, group_rows, capacity, groups, own_group):
    by_source = targets.reshape(groups, group_rows)
    owner_group = by_source // group_rows
    is_mine = (owner_group == own_group).astype(jnp.int32)
    arrival = jnp.cumsum(is_mine, axis=1) - 1
    position = jnp.arange(groups, dtype=jnp.int32)[:, None] * capacity + arrival
    position = jnp.where(is_mine > 0, position, groups * capacity)
    filler = jnp.full((groups * capacity,), group_rows, jnp.int32)
    return filler.at[position.reshape(-1)].set(
        (by_source - owner_group * group_rows).reshape(-1), mode="drop"
    )


def state_forward(x_heads, written, readout, step_size, decay_rate, stretch_rows):
    rows_all, heads, head_dim = x_heads.shape
    stretches = rows_all // stretch_rows
    x_blocks = x_heads.reshape(stretches, stretch_rows, heads, head_dim)
    w_blocks = written.reshape(stretches, stretch_rows, -1)
    r_blocks = readout.reshape(stretches, stretch_rows, -1)
    step_blocks = step_size.reshape(stretches, stretch_rows, heads)
    log_decay = jnp.cumsum(step_blocks * decay_rate[None, None, :], axis=1)
    by_head = jnp.transpose(log_decay, (0, 2, 1))
    causal = jnp.arange(stretch_rows)[:, None] >= jnp.arange(stretch_rows)[None, :]
    spread = by_head[:, :, :, None] - by_head[:, :, None, :]
    fading = jnp.where(causal, jnp.exp(jnp.where(causal, spread, 0.0)), 0.0)
    intersection = jnp.einsum("cin,cjn->cij", r_blocks, w_blocks, precision=PRECISE)
    mixing = intersection[:, None, :, :] * fading
    driven = step_blocks[..., None] * x_blocks
    to_end = jnp.exp(log_decay[:, -1:, :] - log_decay)
    stretch_state = jnp.einsum(
        "cjhp,cjn->chpn", to_end[..., None] * driven, w_blocks, precision=PRECISE
    )
    end_fade = jnp.exp(log_decay[:, -1, :])
    running = jnp.zeros(stretch_state.shape[1:], jnp.float32)
    entering = []
    entering.append(running)
    entering = jnp.stack(entering)
    from_start = jnp.exp(log_decay)
    carried_out = from_start[..., None] * jnp.einsum(
        "chpn,cin->cihp", entering, r_blocks, precision=PRECISE
    )
    inner_out = jnp.einsum("chij,cjhp->cihp", mixing, driven, precision=PRECISE)
    saved = (
        x_blocks,
        w_blocks,
        r_blocks,
        step_blocks,
        causal,
        fading,
        mixing,
        driven,
        to_end,
        entering,
        end_fade,
        from_start,
        carried_out,
    )
    return ((inner_out + carried_out).reshape(rows_all, heads * head_dim), saved)


def state_backward(saved, mixed_grad, decay_rate):
    (
        x_blocks,
        w_blocks,
        r_blocks,
        step_blocks,
        causal,
        fading,
        mixing,
        driven,
        to_end,
        entering,
        end_fade,
        from_start,
        carried_out,
    ) = saved
    stretches = x_blocks.shape[0]
    scaled = from_start[..., None] * mixed_grad
    readout_grad = jnp.einsum("cihp,chpn->cin", scaled, entering, precision=PRECISE)
    from_out = jnp.einsum("cihp,cin->chpn", scaled, r_blocks, precision=PRECISE)
    decay_grad = jnp.sum(carried_out * mixed_grad, axis=3)
    downstream = jnp.zeros(from_out.shape[1:], jnp.float32)
    passed = []
    end_grads = []
    for number in reversed(range(stretches)):
        handed = jnp.zeros_like(downstream)
        passed.append(handed)
        end_grads.append(jnp.sum(handed * entering[number], axis=(1, 2)))
        downstream = from_out[number] + end_fade[number][:, None, None] * handed
    passed = jnp.stack(passed[::-1])
    end_grads = jnp.stack(end_grads[::-1])
    pulled = jnp.einsum("chpn,cjn->cjhp", passed, w_blocks, precision=PRECISE)
    driven_grad = to_end[..., None] * pulled
    written_grad = jnp.einsum(
        "cjhp,chpn->cjn", to_end[..., None] * driven, passed, precision=PRECISE
    )
    tail_grad = jnp.sum(pulled * driven, axis=3) * to_end
    decay_grad = decay_grad - tail_grad
    last_extra = jnp.sum(tail_grad, axis=1) + end_grads * end_fade
    mixing_grad = jnp.where(
        causal, jnp.einsum("cihp,cjhp->chij", mixed_grad, driven, precision=PRECISE), 0.0
    )
    driven_grad = driven_grad + jnp.einsum("chij,cihp->cjhp", mixing, mixed_grad, precision=PRECISE)
    intersection_grad = jnp.sum(mixing_grad * fading, axis=1)
    readout_grad = readout_grad + jnp.einsum(
        "cij,cjn->cin", intersection_grad, w_blocks, precision=PRECISE
    )
    written_grad = written_grad + jnp.einsum(
        "cij,cin->cjn", intersection_grad, r_blocks, precision=PRECISE
    )
    product = mixing_grad * mixing
    decay_grad = decay_grad + jnp.transpose(
        jnp.sum(product, axis=3) - jnp.sum(product, axis=2), (0, 2, 1)
    )
    decay_grad = decay_grad.at[:, -1, :].add(last_extra)
    step_grad = jnp.sum(driven_grad * x_blocks, axis=3)
    x_state_grad = step_blocks[..., None] * driven_grad
    rate_grad = jnp.flip(jnp.cumsum(jnp.flip(decay_grad, axis=1), axis=1), axis=1)
    step_grad = step_grad + rate_grad * decay_rate[None, None, :]
    rate_total = jnp.sum(rate_grad * step_blocks, axis=(0, 1))
    return (x_state_grad, written_grad, readout_grad, step_grad, rate_total)


MESH = pl.DeviceIdType.MESH
BF = jnp.bfloat16
F32 = jnp.float32
NEG = -1e30


def dot_nn(a, b):
    return lax.dot_general(a, b, (((1,), (0,)), ((), ())), preferred_element_type=F32)


def dot_nt(a, b):
    return lax.dot_general(a, b, (((1,), (1,)), ((), ())), preferred_element_type=F32)


def dot_tn(a, b):
    return lax.dot_general(a, b, (((0,), (0,)), ((), ())), preferred_element_type=F32)


def iota(shape, axis):
    return lax.broadcasted_iota(jnp.int32, shape, axis)


def one_hot(cond):
    return jnp.where(cond, 1.0, 0.0).astype(BF)


def split3(v):
    high = v.astype(BF)
    rest = v - high.astype(F32)
    mid = rest.astype(BF)
    return high, mid, (rest - mid.astype(F32)).astype(BF)


def sigmoid(v):
    return 1.0 / (1.0 + jnp.exp(-v))


def rows_down(v, k):
    return jnp.where(iota(v.shape, 0) >= k, pltpu.roll(v, k, 0), 0.0)


def rows_up(v, k):
    n = v.shape[0]
    return jnp.where(iota(v.shape, 0) < n - k, pltpu.roll(v, n - k, 0), 0.0)


def pick(v, lane, index):
    return jnp.sum(jnp.where(lane == index, v, 0.0), axis=1, keepdims=True)


class Sizes:
    def __init__(self, dp, rows, half, inner, heads, state, capacity):
        self.dp, self.rows, self.half, self.inner = dp, rows, half, inner
        self.heads, self.state, self.cap = heads, state, capacity
        self.width = 2 * half
        self.nz = dp // 4
        self.share = self.width // dp
        self.quarter = self.nz * self.share
        self.slots = dp * capacity
        self.tiles = inner // 128
        self.extra = 2 * state + 128
        self.cols = 3 * inner + self.extra
        n = inner // 2
        self.chunks = [(i * n, n) for i in range(6)] + [(6 * n, self.extra)]
        self.levels = self.nz.bit_length() - 1


def targets_of(lines, sz):
    n = sz.rows // 128
    return jnp.concatenate([lines[pl.ds(k, sz.dp, stride=n), :] for k in range(n)], axis=1)


def send_table(targets, g, sz):
    strict = one_hot(iota((sz.rows, sz.rows), 0) < iota((sz.rows, sz.rows), 1))
    every = targets_of(targets, sz)
    own = jnp.sum(jnp.where(iota(every.shape, 0) == g, every, 0), axis=0, keepdims=True)
    group = lax.shift_right_logical(own, 8)
    hot = jnp.where(iota((sz.dp, sz.rows), 0) == group, 1.0, 0.0)
    before = dot_nn(hot.astype(BF), strict)
    rank = jnp.sum(hot * before, axis=0, keepdims=True)
    spot = group.astype(F32) * sz.cap + rank
    return one_hot(iota((sz.slots, sz.rows), 0).astype(F32) == spot)


def owner_table(targets, g, sz):
    strict = one_hot(iota((sz.rows, sz.rows), 0) < iota((sz.rows, sz.rows), 1))
    every = targets_of(targets, sz)
    mine = jnp.where(lax.shift_right_logical(every, 8) == g, 1.0, 0.0)
    rank = dot_nn(mine.astype(BF), strict)
    slot = mine * ((every & 255) + 1).astype(F32)
    lane = iota((sz.dp, 128), 1)
    found = jnp.zeros((sz.dp, 128), F32)
    for a in range(sz.cap):
        one = jnp.sum(jnp.where(rank == float(a), slot, 0.0), axis=1, keepdims=True)
        found = jnp.where(lane == a, one, found)
    place = iota((128, sz.slots), 1)
    spread = one_hot((place % sz.cap) == iota((128, sz.slots), 0))
    wide = dot_nn(found.astype(BF), spread)
    keep = (iota((sz.dp, sz.slots), 1) // sz.cap) == iota((sz.dp, sz.slots), 0)
    row = jnp.sum(jnp.where(keep, wide, 0.0), axis=0, keepdims=True) - 1.0
    return one_hot(iota((sz.rows, sz.slots), 0).astype(F32) == row)


def block_kernel(sz, *refs):
    (dest, back, length, rows_hbm, ct_hbm, win_hbm, wout_hbm, wst_hbm, wstep_in,
     tap_x, bias_x, gain_g, gain_n, skip_in, tap_s, bias_s, bias_step, log_rate,
     out_rows, out_grads, inner_out, proj_out, extra_out, small_out, gain_out,
     win, wout, wst, wstep, lines,
     pk_in, pk_ct, rc_in, rc_ct, gn_o, gn_g,
     p_own, q_in, q_bk,
     hid, cts, normed, lowct, perm, xA, xE, tA, tE,
     yb, pb, r0, r1,
     inter, igrad, ptile,
     sraw, sslope, wr, dtv, lac, lar, sgr, rgr, stepsig, acc1, acc2, scale,
     stat_s, stat_r, half_s, half_r, raw_r, st_s, st_r,
     sms, smr, gall, gsum,
     a2a_s, a2a_r, fw_s, fw_r, quad_s, quad_r, xq_s, xq_r, z_s, z_r, y_s, y_r, gg_s, gg_r, sm_s, sm_r, w_s, own_s, relay_s, raw_sem, taken) = refs
    dp, R, H, C = sz.dp, sz.rows, sz.half, sz.inner
    W, NT_ = sz.width, sz.tiles
    g = lax.axis_index("dp")
    t = lax.axis_index("tensor")
    o = 1 - t
    c, x, z = g % 2, (g // 2) % 2, g // 4
    q = g % 4
    sib, xp = g + 1 - 2 * c, g + 2 - 4 * x
    diag = sib + 2 - 4 * x

    def rcopy(src, dst, ss, rs, peer, side=None):
        return pltpu.make_async_remote_copy(
            src_ref=src, dst_ref=dst, send_sem=ss, recv_sem=rs,
            device_id=(peer, t if side is None else side), device_id_type=MESH)

    sent = []

    def go(copy):
        copy.start()
        sent.append(copy)
        return copy

    loads = [pltpu.make_async_copy(a, b, w_s.at[i]) for i, (a, b) in enumerate(
        [(rows_hbm, lowct.at[:, pl.ds(0, H)]), (ct_hbm, lowct.at[:, pl.ds(H, H)]), (wst_hbm, wst), (wout_hbm, wout)])]
    for load in loads[:2]:
        load.start()

    barrier = pltpu.get_barrier_semaphore()
    for off in range(1, dp):
        pl.semaphore_signal(barrier, inc=1, device_id=((g + off) % dp, t), device_id_type=MESH)
    pl.semaphore_signal(barrier, inc=1, device_id=(g, o), device_id_type=MESH)

    side = z // 2
    zo, zi, fi, fo = 3 * side, 1 + side, 2 - side, 3 - 3 * side
    is_outer = (z + side + 1) % 2
    is_inner = 1 - is_outer
    far = [
        ((z + dz) % sz.nz) * 4 + ((x + dx) % 2) * 2 + (c + dc) % 2
        for dz in (2, 1, 3, 0) for dx in (1, 0) for dc in (1, 0) if dz + dx + dc]
    level = [z * 4 + ((x + dx) % 2) * 2 + (c + dc) % 2 for dx, dc in ((1, 1), (1, 0), (0, 1))]
    across = [zz * 4 + ((x + dx) % 2) * 2 + (c + dc) % 2 for zz in (fo, fi) for dx in (1, 0) for dc in (1, 0)]
    beside_z = is_outer * zi + (1 - is_outer) * zo
    beside = [beside_z * 4 + ((x + dx) % 2) * 2 + (c + dc) % 2 for dx, dc in ((1, 1), (1, 0), (0, 1))]
    partner = beside_z * 4 + q
    parts = [pl.ds(0, H // 3 * 2), pl.ds(H // 3 * 2, H // 3)]

    def exchange(i, source, target, at=slice(None)):
        copies = [
            rcopy(source.at[peer, :, at], target.at[g, :, at], a2a_s.at[i, peer], a2a_r.at[i, g], peer) for peer in far]
        for copy in copies:
            copy.start()
        return copies

    def settle(copies):
        for copy in copies:
            copy.wait_send()

    def arrived(i, target, at=slice(None)):
        for src in far:
            rcopy(target.at[src, :, at], target.at[src, :, at], a2a_s.at[i, src], a2a_r.at[i, src], src).wait_recv()

    def answer(table, value, dst):
        for k in range(2):
            n = sz.slots // 2
            part = dot_tn(table[:, k * n:(k + 1) * n], value).astype(BF)
            dst[k * (dp // 2):(k + 1) * (dp // 2)] = part.reshape(dp // 2, sz.cap, H)

    def block_to(i, source, target, peer, owner, sems):
        return rcopy(source.at[peer], target.at[owner], sems.at[i - 4, peer], a2a_r.at[i, owner], peer)

    def raw_copy(i):
        return rcopy(lowct.at[:, pl.ds((i - 4) * H, H)], raw_r, raw_sem.at[0, i - 4], raw_sem.at[1, i - 4], partner)

    def near_x(peers, same):
        if len(peers) == 3:
            return peers[2:] if same else peers[:2]
        return [peer for k, peer in enumerate(peers) if (k % 4 >= 2) == same]

    def reply_send(i, packed, target, same):
        @pl.when(is_outer == 0)
        def _():
            for peer in near_x(across, same) + near_x(beside, same) + ([partner] if same else []):
                block_to(i, packed, target, peer, g, own_s).start()
        for peer in near_x(level, same):
            block_to(i, packed, target, peer, g, own_s).start()

    def reply(i, table, value, packed, target):
        answer(table, value, packed)
        target[pl.ds(g, 1)] = packed[pl.ds(g, 1)]

        @pl.when(is_outer == 1)
        def _():
            if i == 5:
                pl.semaphore_wait(taken, 1)
            lowct[:, (i - 4) * H:(i - 3) * H] = value
            raw_copy(i).start()

    def relay_send(i, packed, target, same):
        @pl.when(is_outer == 0)
        def _():
            for peer in near_x(across, same) + near_x(level, same):
                block_to(i, packed, target, peer, partner, relay_s).start()

    def relay(i, targets, packed, target):
        @pl.when(is_outer == 0)
        def _():
            raw_copy(i).wait_recv()
            answer(owner_table(targets, partner, sz), raw_r[...], packed)
            if i == 4:
                pl.semaphore_signal(taken, inc=1, device_id=(partner, t), device_id_type=MESH)
            target[pl.ds(partner, 1)] = packed[pl.ds(g, 1)]

    def replied(i, target):
        def wait(src):
            rcopy(target.at[src], target.at[src], own_s.at[i - 4, src], a2a_r.at[i, src], src).wait_recv()
        for src in level + across + beside:
            wait(src)

        @pl.when(is_outer == 1)
        def _():
            wait(partner)

    def reply_settle(i, packed, passed, target):
        for peer in level:
            block_to(i, packed, target, peer, g, own_s).wait_send()

        @pl.when(is_outer == 0)
        def _():
            for peer in across + beside + [partner]:
                block_to(i, packed, target, peer, g, own_s).wait_send()
            for peer in across + level:
                block_to(i, passed, target, peer, partner, relay_s).wait_send()

    def pack(table, source, target):
        for k in range(2):
            n = sz.slots // 2
            part = dot_nn(table[k * n:(k + 1) * n, :], source[...]).astype(BF)
            target[k * (dp // 2):(k + 1) * (dp // 2)] = part.reshape(dp // 2, sz.cap, H)

    p_own[...] = send_table(dest, g, sz)
    loads[0].wait()
    pack(p_own, lowct.at[:, pl.ds(0, H)], pk_in)
    pl.semaphore_wait(barrier, dp)
    rows_away = exchange(0, pk_in, rc_in, parts[0]) + exchange(1, pk_in, rc_in, parts[1])
    rc_in[pl.ds(g, 1)] = pk_in[pl.ds(g, 1)]
    for load in loads[2:]:
        load.start()
    p_own[...] = send_table(back, g, sz)
    loads[1].wait()
    pack(p_own, lowct.at[:, pl.ds(H, H)], pk_ct)
    rc_ct[pl.ds(g, 1)] = pk_ct[pl.ds(g, 1)]
    q_in[...] = owner_table(dest, g, sz)
    q_bk[...] = owner_table(back, g, sz)

    def unpack(i, table, source, full, part):
        at = parts[part]
        arrived(2 * i + part, source, at)
        n = at.size
        full[pl.ds(t, 1), :, at] = dot_nn(table[...], source[:, :, at].reshape(sz.slots, n)).astype(BF)[None]
        go(rcopy(full.at[t, :, at], full.at[t, :, at], fw_s.at[i, part], fw_r.at[i, part], g, o))

    def other_half(i, full):
        for part in range(2):
            at = parts[part]
            rcopy(full.at[o, :, at], full.at[o, :, at], fw_s.at[i, part], fw_r.at[i, part], g, o).wait_recv()

    def take_apart(stage, sems):
        n = W // 128
        fetch = [pltpu.make_async_copy(win_hbm.at[pl.ds(k * 128, 128)], stage.at[k % 4], sems.at[k % 4]) for k in range(n)]
        for copy in fetch[:4]:
            copy.start()
        place = iota((256, 256), 0)
        order = one_hot(iota((256, 256), 1) == jnp.where(place < 128, 2 * place, 2 * place - 255))
        for k in range(n):
            fetch[k].wait()
            for m in range(0, C, 256):
                pair = jnp.concatenate(
                    [stage[k % 4, :, :, m + e:m + e + 128].reshape(256, 128) for e in (0, 128)], axis=1)
                both = dot_nn(order, pair).astype(BF)
                win[k * 128:(k + 1) * 128, m:m + 256] = both[:128]
                win[k * 128:(k + 1) * 128, C + m:C + m + 256] = both[128:]
            if k + 4 < n:
                fetch[k + 4].start()

    pl.run_scoped(take_apart, pltpu.VMEM((4, 128, 2, C), BF), pltpu.SemaphoreType.DMA((4,)))
    grads_away = exchange(2, pk_ct, rc_ct, parts[0])
    unpack(0, q_in, rc_in, hid, 0)
    grads_away += exchange(3, pk_ct, rc_ct, parts[1])
    unpack(0, q_in, rc_in, hid, 1)
    other_half(0, hid)

    total = jnp.zeros((R, 128), F32)
    for k in range(W // 128):
        v = hid[k // (H // 128), :, (k % (H // 128)) * 128:(k % (H // 128)) * 128 + 128].astype(F32)
        total = total + v * v
    norm_scale = lax.rsqrt(jnp.sum(total, axis=1, keepdims=True) / W + EPSILON)
    scale[...] = jnp.broadcast_to(norm_scale, (R, 128))
    for k in range(W // 128):
        v = hid[k // (H // 128), :, (k % (H // 128)) * 128:(k % (H // 128)) * 128 + 128].astype(F32)
        normed[:, k * 128:(k + 1) * 128] = (v * scale[...] * gain_n[k:k + 1, :]).astype(BF)

    def quarters(source):
        for qq in range(4):
            perm[qq] = jnp.concatenate(
                [source[:, sz.share * (4 * zz + qq):sz.share * (4 * zz + qq + 1)] for zz in range(sz.nz)], axis=1)

    def send_quarter(i, dst):
        copies = [
            rcopy(perm.at[peer % 4], dst.at[rel], xq_s.at[i, rel - 1], xq_r.at[i, rel - 1], peer)
            for rel, peer in ((2, xp), (3, diag), (1, sib))]
        for copy in copies:
            copy.start()
        dst[0:1] = perm[pl.ds(q, 1)]
        return copies

    def turn_quarter(dst, turned):
        for rel, peer in ((1, sib), (2, xp), (3, diag)):
            rcopy(dst.at[rel], dst.at[rel], xq_s.at[0, rel - 1], xq_r.at[0, rel - 1], peer).wait_recv()
        for rel in range(4):
            turned[:, rel * R:(rel + 1) * R] = jnp.transpose(dst[rel].astype(F32)).astype(BF)

    def fold_half(which, place):
        value = cts[pl.ds(which, 1)][0]
        for qq in range(4):
            cut = jnp.concatenate(
                [value[:, sz.share * (4 * zz + qq):sz.share * (4 * zz + qq + 1)] for zz in range(sz.nz // 2)], axis=1)
            cut = jnp.where(iota(cut.shape, 0) < length[0, 0], cut.astype(F32), 0.0).astype(BF)
            perm[qq, place * (R // 2):(place + 1) * (R // 2)] = jnp.concatenate([cut[:R // 2], cut[R // 2:]], axis=1)

    def fold_copy(sem, quarter, place, half, rel, peer, to):
        return rcopy(perm.at[quarter, pl.ds(place * (R // 2), R // 2)], xE.at[half, rel], xq_s.at[1, sem], xq_r.at[1, sem], peer, to)

    def fold_pass(rel, half):
        return rcopy(xE.at[half, rel], xE.at[half, rel], xq_s.at[1, 2 + rel], xq_r.at[1, 2 + rel], g, o)

    def turn_folds():
        fold_copy(0, 0, 0, t, 1, sib, t).wait_recv()
        fold_copy(3, 0, 0, o, 1, sib, t).wait_recv()
        for rel in (2, 3):
            fold_pass(rel, o).wait_recv()
        n = sz.quarter // 2
        for half in range(2):
            for rel in range(4):
                flat = jnp.transpose(xE[half, rel].astype(F32)).astype(BF)
                tE[half * n:(half + 1) * n, rel * R:rel * R + R // 2] = flat[:n]
                tE[half * n:(half + 1) * n, rel * R + R // 2:(rel + 1) * R] = flat[n:]

    quarters(normed)
    quarter_away = send_quarter(0, xA)

    loads[2].wait()
    wstep[...] = jnp.zeros_like(wstep)
    wstep[:sz.heads] = wstep_in[...]
    lines[...] = jnp.zeros_like(lines)
    lines[0:1, :sz.heads] = bias_step[...]
    lines[1:2, :sz.heads] = log_rate[...]
    row = iota((R, 128), 0)
    lane = iota((R, 128), 1)
    live = jnp.where(row < length[0, 0], 1.0, 0.0)
    sraw[...] = dot_nn(normed[...], wst[...])
    step_in = dot_nt(normed[...], wstep[...]) + lines[0:1, :]
    S = sz.state
    for k in range(2):
        cut = slice(k * S, (k + 1) * S)
        raw = sraw[:, cut]
        conv = bias_s[:, cut] + tap_s[0:1, cut] * raw
        for tap in range(1, 4):
            conv = conv + tap_s[tap:tap + 1, cut] * rows_down(raw, tap)
        sg = sigmoid(conv)
        sslope[:, cut] = sg * (1.0 + conv * (1.0 - sg))
        wr[:, cut] = (conv * sg).astype(BF)
    written, readout = wr[:, :S], wr[:, S:]
    inter[...] = dot_nt(readout, written)
    stepsig[...] = sigmoid(step_in) * live
    heads_live = jnp.where(lane < sz.heads, live, 0.0)
    step = (jnp.maximum(step_in, 0.0) + jnp.log1p(jnp.exp(-jnp.abs(step_in)))) * heads_live
    rate = -jnp.exp(lines[1:2, :])
    dtv[...] = step
    lower = one_hot(iota((R, R), 0) >= iota((R, R), 1))
    log_decay = sum(dot_nn(lower, part) for part in split3(step * rate))
    lac[...] = log_decay
    lar[...] = jnp.transpose(log_decay)

    def cols_of(i):
        return pl.ds(sz.chunks[i][0], sz.chunks[i][1])

    def quad_send(i):
        at = cols_of(i)
        go(rcopy(yb.at[0, :, at], yb.at[2, :, at], quad_s.at[i, 1], quad_r.at[i, 1], xp))
        go(rcopy(yb.at[0, :, at], yb.at[1, :, at], quad_s.at[i, 0], quad_r.at[i, 0], sib))

    def quad_pass(i):
        at = cols_of(i)
        rcopy(yb.at[2, :, at], yb.at[2, :, at], quad_s.at[i, 1], quad_r.at[i, 1], xp).wait_recv()
        go(rcopy(yb.at[2, :, at], yb.at[3, :, at], quad_s.at[i, 2], quad_r.at[i, 2], sib))

    def z_copy(i, k):
        at = cols_of(i)
        column = g % 4
        if k < 3:
            block, slot, peer = (zi, fi, fo)[k], r0.at[k], zi
        elif k < 5:
            block, slot, peer = (fi, fo)[k - 3], r1.at[k - 3], fi
        else:
            block, slot, peer = zo, r0.at[0], zo
        return rcopy(pb.at[block, :, at], slot.at[:, at], z_s.at[i, k], z_r.at[i, k], peer * 4 + column)

    def z_wait(i, k):
        at = cols_of(i)
        slot = r0.at[k] if k < 3 else r1.at[k - 3] if k < 5 else r0.at[0]
        rcopy(slot.at[:, at], slot.at[:, at], z_s.at[i, k], z_r.at[i, k], g + 4 - 8 * (z // 3)).wait_recv()

    def each_tile(i, block, landed, keep):
        start, size = sz.chunks[i]
        for n in range(0, size, 128):
            cut = slice(start + n, start + n + 128)
            value = pb[pl.ds(block, 1), :, cut].astype(F32)[0] + landed[:, cut].astype(F32)
            if keep:
                pb[pl.ds(block, 1), :, cut] = value.astype(BF)[None]
            elif start + n < C:
                proj_out[:, cut] = value
            elif start + n < 3 * C:
                inner_out[:, start + n - C:start + n - C + 128] = value
            else:
                extra_out[:, start + n - 3 * C:start + n - 3 * C + 128] = value

    def z_first(i):
        @pl.when(is_outer == 1)
        def _():
            for k in range(3):
                z_copy(i, 2 - k).start()

    def z_second(i):
        @pl.when(is_outer == 0)
        def _():
            for k in (2, 1):
                z_wait(i, k)
                each_tile(i, (zi, fi, fo)[k], r0.at[k], True)
                z_copy(i, 2 + k).start()
            z_wait(i, 0)
            each_tile(i, zi, r0.at[0], True)

    def z_third(i):
        @pl.when(is_outer == 0)
        def _():
            z_wait(i, 4)
            each_tile(i, zo, r1.at[1], True)
            z_copy(i, 5).start()
            z_wait(i, 3)
            each_tile(i, zi, r1.at[0], False)

    def z_fourth(i):
        @pl.when(is_outer == 1)
        def _():
            z_wait(i, 5)
            each_tile(i, zo, r0.at[0], False)

    def z_settle():
        @pl.when(is_outer == 1)
        def _():
            for i in range(len(sz.chunks)):
                for k in range(3):
                    z_copy(i, k).wait_send()

        @pl.when(is_outer == 0)
        def _():
            for i in range(len(sz.chunks)):
                for k in range(3, 6):
                    z_copy(i, k).wait_send()

    def partial_sum(i, turned):
        at = cols_of(i)
        start, size = sz.chunks[i]
        rcopy(yb.at[1, :, at], yb.at[1, :, at], quad_s.at[i, 0], quad_r.at[i, 0], sib).wait_recv()
        rcopy(yb.at[3, :, at], yb.at[3, :, at], quad_s.at[i, 2], quad_r.at[i, 2], sib).wait_recv()
        n = 384 if size % 256 else 256

        def body(k, carry):
            at = pl.ds(pl.multiple_of(start + k * n, 128), n)
            part = dot_nn(turned[...], yb[:, :, at].reshape(4 * R, n))
            pb[:, :, at] = part.astype(BF).reshape(sz.nz, sz.share, n)
            return carry
        lax.fori_loop(0, size // n, body, 0)
        z_first(i)

    def remainder(gr, xr, xa, xs, mx, ng):
        def project(dst, base):
            def body(n, carry):
                at = pl.multiple_of(n * 256, 256)
                dst[:, pl.ds(at, 256)] = dot_nn(normed[...], win[:, pl.ds(pl.multiple_of(base + n * 256, 256), 256)])
                return carry
            lax.fori_loop(0, C // 256, body, 0)

        project(xr, C)
        project(gr, 0)

        unpack(1, q_bk, rc_ct, cts, 0)

        def lanes(p):
            return pl.ds(pl.multiple_of(p * 128, 128), 128)

        B = 64

        def head_line(v, p):
            first = iota((1, 128), 1) < 64
            spot = iota(v.shape, 1)
            return jnp.where(first, pick(v, spot, 2 * p), pick(v, spot, 2 * p + 1))

        def step_columns(p, lane):
            first = lane < 64
            return jnp.where(first, pick(dtv[...], lane, 2 * p), pick(dtv[...], lane, 2 * p + 1))

        acc1[...] = jnp.zeros_like(acc1)
        acc2[...] = jnp.zeros_like(acc2)

        def scan(p, carry):
            at = lanes(p)
            lane = iota((R, 128), 1)
            raw = xr[:, at]
            conv = bias_x[pl.ds(p, 1), :] + tap_x[0:1, at] * raw
            for tap in range(1, 4):
                conv = conv + tap_x[tap:tap + 1, at] * rows_down(raw, tap)
            sg = sigmoid(conv)
            act = conv * sg
            xa[:, at] = act
            xs[:, at] = (sg * (1.0 + conv * (1.0 - sg))).astype(BF)
            driven = act * step_columns(p, lane)
            parts = [jnp.where(lane < 64, driven, 0.0).astype(BF), jnp.where(lane >= 64, driven, 0.0).astype(BF)]
            cols = [pick(lac[...], lane, 2 * p + k) for k in range(2)]
            skip = head_line(skip_in[...], p)
            for b in range(R // B):
                reach = 128 * ((b * B) // 128 + 1)
                cut = slice(b * B, (b + 1) * B)
                causal = iota((B, reach), 0) + b * B >= iota((B, reach), 1)
                mixed = skip * act[cut]
                for k in range(2):
                    spread = cols[k][cut] - lar[pl.ds(2 * p + k, 1), :][:, :reach]
                    fading = jnp.exp(jnp.where(causal, spread, NEG))
                    mixing = (inter[cut, :reach] * fading).astype(BF)
                    mixed = mixed + dot_nn(mixing, parts[k][:reach])
                mx[cut, at] = mixed
                gate = gr[cut, at]
                gated = mixed * gate * sigmoid(gate)
                acc1[cut] += gated * gated
            return carry

        lax.fori_loop(0, NT_, scan, 0)

        whole = float(2 * C)

        def total_over_sides(i, value):
            stat_s[i] = jnp.transpose(jnp.where(lane == 0, jnp.sum(value, axis=1, keepdims=True), 0.0))[:8]
            return go(rcopy(stat_s.at[i], stat_r.at[i], y_s.at[i], y_r.at[i], g, o))

        def total_here(i):
            both = jnp.concatenate([stat_s[i] + stat_r[i], jnp.zeros((120, R), F32)], axis=0)
            return pick(jnp.transpose(both), lane, 0)

        squares = total_over_sides(0, acc1[...])
        unpack(1, q_bk, rc_ct, cts, 1)
        turn_quarter(xA, tA)
        settle(quarter_away)
        fold_half(t, 0)
        for rel, peer in ((2, xp), (3, diag)):
            go(fold_copy(rel - 1, peer % 4, 0, t, rel, peer, t))
        squares.wait_recv()
        gate_scale = lax.rsqrt(total_here(0) / whole + EPSILON)
        acc1[...] = jnp.broadcast_to(gate_scale, (R, 128))

        def gate_forward(p, carry):
            at = lanes(p)
            gate = gr[:, at]
            yb[0, :, at] = (mx[:, at] * (gate * sigmoid(gate)) * acc1[...] * gain_g[pl.ds(p, 1), :]).astype(BF)
            return carry
        lax.fori_loop(0, NT_, gate_forward, 0)
        quad_send(0)

        other_half(1, cts)
        for k in range(W // 128):
            v = cts[k // (H // 128), :, (k % (H // 128)) * 128:(k % (H // 128)) * 128 + 128].astype(F32)
            lowct[:, k * 128:(k + 1) * 128] = (v * live).astype(BF)
        fold_half(o, 1)
        xE[t, 0] = perm[q, :R // 2]
        xE[o, 0] = perm[q, R // 2:]
        go(fold_copy(0, sib % 4, 0, t, 1, sib, t))
        go(fold_copy(3, sib % 4, 1, o, 1, sib, t))
        quad_send(1)
        loads[3].wait()

        def out_half(side, dst, cast):
            def body(n, carry):
                at = pl.ds(pl.multiple_of(side * H + n * 256, 256), 256)
                dst[:, pl.ds(pl.multiple_of(n * 256, 256), 256)] = dot_nn(yb[0, :, :C], wout[:, at]).astype(cast)
                return carry
            lax.fori_loop(0, H // 256, body, 0)

        def back_project(n, carry):
            at = pl.ds(pl.multiple_of(n * 256, 256), 256)
            ng[:, at] = dot_nt(lowct[...], wout[at, :])
            for k in range(2):
                here = pl.ds(pl.multiple_of(n * 256 + k * 128, 128), 128)
                gate = gr[:, here]
                acc2[...] += mx[:, here] * (gate * sigmoid(gate)) * (gain_g[pl.ds(2 * n + k, 1), :] * ng[:, here])
            return carry
        lax.fori_loop(0, C // 256, back_project, 0)
        crossed = total_over_sides(1, acc2[...])
        for rel in (2, 3):
            fold_copy(rel - 1, 0, 0, t, rel, xp, t).wait_recv()
            go(fold_pass(rel, t))
        out_half(o, half_s, BF)
        branch_away = rcopy(half_s, half_r, y_s.at[2], y_r.at[2], g, o)
        branch_away.start()
        crossed.wait_recv()
        acc2[...] = acc1[...] * acc1[...] * acc1[...] * (total_here(1) / whole)

        def gate_back(p, carry):
            at = lanes(p)
            gate, mixed, grad = gr[:, at], mx[:, at], ng[:, at]
            sg = sigmoid(gate)
            act = gate * sg
            gated = mixed * act
            gated_grad = acc1[...] * (gain_g[pl.ds(p, 1), :] * grad) - gated * acc2[...]
            sms[0, 5:6, at] = jnp.sum(grad * gated * acc1[...], axis=0, keepdims=True)
            mixed_grad = gated_grad * act
            ng[:, at] = mixed_grad
            sms[0, 6:7, at] = jnp.sum(mixed_grad * xa[:, at], axis=0, keepdims=True)
            yb[0, :, pl.ds(pl.multiple_of(C + p * 128, 128), 128)] = (
                gated_grad * mixed * (sg * (1.0 + gate * (1.0 - sg)))).astype(BF)
            return carry
        lax.fori_loop(0, NT_, gate_back, 0)
        quad_send(2)
        quad_send(3)
        out_half(t, gr, F32)

        inter[...] = dot_nt(written, readout)
        igrad[...] = jnp.zeros_like(igrad)
        sgr[...] = jnp.zeros_like(sgr)
        rgr[...] = jnp.zeros_like(rgr)
        ptile[...] = jnp.zeros_like(ptile)

        def scan_back(p, carry):
            at = lanes(p)
            lane = iota((R, 128), 1)
            grad = ng[:, at]
            act = xa[:, at]
            stepw = step_columns(p, lane)
            driven = (act * stepw).astype(BF)
            parts = [jnp.where(lane < 64, grad, 0.0).astype(BF), jnp.where(lane >= 64, grad, 0.0).astype(BF)]
            cols = [pick(lac[...], lane, 2 * p + k) for k in range(2)]
            pieces = []
            for b in range(R // B):
                skip = 128 * ((b * B) // 128)
                cut = slice(b * B, (b + 1) * B)
                causal = iota((B, R - skip), 1) + skip >= iota((B, R - skip), 0) + b * B
                turned = inter[cut, skip:]
                piece = jnp.zeros((B, 128), F32)
                total = igrad[cut, skip:]
                for k in range(2):
                    spread = lar[pl.ds(2 * p + k, 1), :][:, skip:] - cols[k][cut]
                    fading = jnp.exp(jnp.where(causal, spread, NEG))
                    faded = dot_nt(driven[cut], parts[k][skip:]) * fading
                    total = total + faded
                    piece = piece + dot_nn((turned * fading).astype(BF), parts[k][skip:])
                    ptile[k, cut, skip:] = (faded * turned).astype(BF)
                igrad[cut, skip:] = total
                pieces.append(piece)
            strict = one_hot(iota((R, R), 0) > iota((R, R), 1))
            for k in range(2):
                found = []
                for b in range(R // B):
                    skip = 128 * ((b * B) // 128)
                    cut = slice(b * B, (b + 1) * B)
                    causal = iota((B, R - skip), 1) + skip >= iota((B, R - skip), 0) + b * B
                    sums = dot_nn(strict[cut], ptile[k, :, skip:])
                    found.append(jnp.sum(jnp.where(causal, sums, 0.0), axis=1, keepdims=True))
                rgr[...] = jnp.where(lane == 2 * p + k, jnp.concatenate(found, axis=0), rgr[...])
            driven_grad = jnp.concatenate(pieces, axis=0)
            pulled = driven_grad * act
            low = jnp.sum(jnp.where(lane < 64, pulled, 0.0), axis=1, keepdims=True)
            high = jnp.sum(jnp.where(lane >= 64, pulled, 0.0), axis=1, keepdims=True)
            sgr[...] = jnp.where(lane == 2 * p, low, jnp.where(lane == 2 * p + 1, high, sgr[...]))
            conv_grad = (head_line(skip_in[...], p) * grad + stepw * driven_grad) * xs[:, at].astype(F32)
            raw = xr[:, at]
            raw_grad = tap_x[0:1, at] * conv_grad
            sms[0, 0:1, at] = jnp.sum(conv_grad * raw, axis=0, keepdims=True)
            sms[0, 4:5, at] = jnp.sum(conv_grad, axis=0, keepdims=True)
            for tap in range(1, 4):
                up = rows_up(conv_grad, tap)
                raw_grad = raw_grad + tap_x[tap:tap + 1, at] * up
                sms[0, tap:tap + 1, at] = jnp.sum(up * raw, axis=0, keepdims=True)
            yb[0, :, pl.ds(pl.multiple_of(2 * C + p * 128, 128), 128)] = raw_grad.astype(BF)
            return carry

        quad_pass(0)
        lax.fori_loop(0, NT_ // 4, scan_back, 0)
        turn_folds()
        partial_sum(0, tE)
        lax.fori_loop(NT_ // 4, NT_ // 2, scan_back, 0)
        quad_send(4)

        rcopy(half_r, half_r, y_s.at[2], y_r.at[2], g, o).wait_recv()

        pieces = []
        mine = hid[pl.ds(t, 1)][0]
        for k in range(H // 128):
            cut = slice(k * 128, (k + 1) * 128)
            branch = gr[:, cut] + half_r[:, cut].astype(F32)
            pieces.append((mine[:, cut].astype(F32) + live * branch).astype(BF))
        settle(rows_away)
        reply(4, q_bk, jnp.concatenate(pieces, axis=1), pk_in, gn_o)
        reply_send(4, pk_in, gn_o, True)

        lax.fori_loop(NT_ // 2, NT_, scan_back, 0)
        quad_send(5)

        ig = igrad[...].astype(BF)
        st_s[:, :S] = dot_nn(ig, wr[:, S:]).astype(BF)
        st_s[:, S:] = dot_tn(ig, wr[:, :S]).astype(BF)
        go(rcopy(st_s, st_r, y_s.at[3], y_r.at[3], g, o))
        step_grad = (sgr[...] + rgr[...] * rate) * stepsig[...]
        yb[0, :, 3 * C + 2 * S:] = step_grad.astype(BF)
        sms[0, 7:8, 10 * S:10 * S + 128] = jnp.sum(step_grad, axis=0, keepdims=True)
        sms[0, 7:8, 10 * S + 128:10 * S + 256] = jnp.sum(rgr[...] * dtv[...], axis=0, keepdims=True) * rate
        quad_pass(1)
        z_second(0)
        rcopy(st_r, st_r, y_s.at[3], y_r.at[3], g, o).wait_recv()
        for k in range(2):
            cut = slice(k * S, (k + 1) * S)
            conv_grad = (st_s[:, cut].astype(F32) + st_r[:, cut].astype(F32)) * sslope[:, cut]
            raw = sraw[:, cut]
            raw_grad = tap_s[0:1, cut] * conv_grad
            sms[0, 7:8, cut] = jnp.sum(conv_grad * raw, axis=0, keepdims=True)
            sms[0, 7:8, 8 * S + k * S:8 * S + (k + 1) * S] = jnp.sum(conv_grad, axis=0, keepdims=True)
            for tap in range(1, 4):
                up = rows_up(conv_grad, tap)
                raw_grad = raw_grad + tap_s[tap:tap + 1, cut] * up
                sms[0, 7:8, tap * 2 * S + k * S:tap * 2 * S + (k + 1) * S] = jnp.sum(up * raw, axis=0, keepdims=True)
            yb[0, :, 3 * C + k * S:3 * C + (k + 1) * S] = raw_grad.astype(BF)
        quad_send(6)
        reply_send(4, pk_in, gn_o, False)

        hops = [2 ** k for k in range(2, dp.bit_length() - 1)] + [1, 2]

        def small_start(i):
            bit = (g // hops[i]) % 2
            go(rcopy(sms.at[i], smr.at[i], sm_s.at[i], sm_r.at[i], g + (1 - 2 * bit) * hops[i]))

        def small_end(i):
            bit = (g // hops[i]) % 2
            rcopy(sms.at[i], smr.at[i], sm_s.at[i], sm_r.at[i], g + (1 - 2 * bit) * hops[i]).wait_recv()
            if i + 1 < len(hops):
                sms[i + 1] = sms[i] + smr[i]
                small_start(i + 1)
            else:
                small_out[...] = sms[i] + smr[i]
        small_start(0)

        acc1[...] = jnp.zeros_like(acc1)

        def normed_grad(side, dst, cast):
            def body(n, carry):
                at = pl.ds(pl.multiple_of(side * H + n * 256, 256), 256)
                value = dot_nt(yb[0, :, C:3 * C], win[at, :])
                mine_state = pl.ds(pl.multiple_of(t * S, 128), S)
                value = value + dot_nt(yb[0, :, pl.ds(pl.multiple_of(3 * C + t * S, 128), S)], wst[at, mine_state])
                value = value + dot_nn(yb[0, :, 3 * C + 2 * S:], wstep[:, at])
                for k in range(2):
                    cut = slice(k * 128, (k + 1) * 128)
                    here = pl.ds(pl.multiple_of(n * 256 + k * 128, 128), 128)
                    there = pl.ds(pl.multiple_of(side * H + n * 256 + k * 128, 128), 128)
                    acc1[...] += hid[pl.ds(side, 1), :, here][0].astype(F32) * (gain_n[pl.ds(side * (H // 128) + 2 * n + k, 1), :] * value[:, cut])
                dst[:, pl.ds(pl.multiple_of(n * 256, 256), 256)] = value.astype(cast)
                return carry
            lax.fori_loop(0, H // 256, body, 0)
        branch_away.wait_send()
        normed_grad(o, half_s, BF)
        go(rcopy(half_s, half_r, y_s.at[4], y_r.at[4], g, o))
        normed_grad(t, gr, F32)
        summed_rows = total_over_sides(2, acc1[...])
        partial_sum(1, tE)
        relay(4, back, rc_ct, gn_o)
        relay_send(4, rc_ct, gn_o, True)
        relay_send(4, rc_ct, gn_o, False)
        quad_pass(2)
        partial_sum(2, tA)

        rcopy(half_r, half_r, y_s.at[4], y_r.at[4], g, o).wait_recv()
        summed_rows.wait_recv()
        pull = total_here(2) / W * (scale[...] * scale[...] * scale[...])
        pieces = []
        mine = hid[pl.ds(t, 1)][0]
        mine_ct = cts[pl.ds(t, 1)][0]
        gall[pl.ds(g, 1)] = jnp.zeros((1, 8, 128), F32)
        for k in range(H // 128):
            cut = slice(k * 128, (k + 1) * 128)
            there = pl.ds(pl.multiple_of(t * H + k * 128, 128), 128)
            value = gr[:, cut] + half_r[:, cut].astype(F32)
            rows_here = mine[:, cut].astype(F32)
            gall[pl.ds(g, 1), k:k + 1, :] = jnp.sum(value * rows_here * scale[...], axis=0, keepdims=True)[None]
            pieces.append((scale[...] * (gain_n[pl.ds(t * (H // 128) + k, 1), :] * value) - rows_here * pull
                           + mine_ct[:, cut].astype(F32)).astype(BF))
        settle(grads_away)
        reply(5, q_in, jnp.concatenate(pieces, axis=1), pk_ct, gn_g)
        reply_send(5, pk_ct, gn_g, True)
        reply_send(5, pk_ct, gn_g, False)
        for peer in far:
            go(rcopy(gall.at[g], gall.at[g], gg_s.at[peer], gg_r.at[g], peer))

        small_end(0)
        z_second(1)
        quad_pass(3)
        partial_sum(3, tA)
        z_second(2)
        z_third(0)
        relay(5, dest, rc_in, gn_g)
        relay_send(5, rc_in, gn_g, True)
        relay_send(5, rc_in, gn_g, False)
        z_third(1)
        quad_pass(4)
        partial_sum(4, tA)
        small_end(1)
        z_third(2)
        z_second(3)
        quad_pass(5)
        partial_sum(5, tA)
        z_second(4)
        quad_pass(6)
        small_end(2)
        z_third(3)
        partial_sum(6, tA)
        z_third(4)
        z_second(5)
        z_second(6)

        def give(i, value, dst):
            lowct[:, i * H:(i + 1) * H] = value.astype(BF)
            store = pltpu.make_async_copy(lowct.at[:, pl.ds(i * H, H)], dst, w_s.at[i])
            store.start()
            return store

        replied(4, gn_o)

        @pl.when(is_outer == 1)
        def _():
            raw_copy(4).wait_send()
            raw_copy(5).wait_send()
        stores = [give(0, dot_tn(p_own[...], gn_o[...].reshape(sz.slots, H)), out_rows)]
        p_own[...] = send_table(dest, g, sz)
        for i in range(4):
            z_fourth(i)
        small_end(3)
        for src in far:
            rcopy(gall.at[src], gall.at[src], gg_s.at[src], gg_r.at[src], src).wait_recv()
        summed = gall[0]
        for d in range(1, dp):
            summed = summed + gall[d]
        gsum[pl.ds(t, 1)] = summed[None]
        go(rcopy(gsum.at[t], gsum.at[t], y_s.at[5], y_r.at[5], g, o))
        replied(5, gn_g)
        stores.append(give(1, dot_tn(p_own[...], gn_g[...].reshape(sz.slots, H)), out_grads))
        z_third(5)
        z_third(6)
        for i in range(4, 7):
            z_fourth(i)
        rcopy(gsum.at[o], gsum.at[o], y_s.at[5], y_r.at[5], g, o).wait_recv()
        gain_out[...] = gsum[...]
        for copy in sent:
            copy.wait_send()
        z_settle()
        reply_settle(4, pk_in, rc_ct, gn_o)
        reply_settle(5, pk_ct, rc_in, gn_g)
        for store in stores:
            store.wait()

    big = pltpu.VMEM((R, C), F32)
    pl.run_scoped(remainder, big, big, big, pltpu.VMEM((R, C), BF), big, big)


def finish_kernel(sz, rows, grads, inner, proj, extra, small, gain, o_rows, o_grads, o_gain, o_inner, o_state, o_step,
                  o_tap_x, o_bias_x, o_tap_s, o_bias_s, o_bias_step, o_rate, o_skip, o_gate, o_proj):
    C, S = sz.inner, sz.state
    o_rows[...] = rows[...]
    o_grads[...] = grads[...]
    o_inner[:, 0, :] = inner[:, :C]
    o_inner[:, 1, :] = inner[:, C:]
    o_proj[...] = proj[...]
    o_state[...] = extra[:, :2 * S]
    o_step[...] = jnp.transpose(extra[:, 2 * S:])[:sz.heads]
    o_tap_x[...] = small[0:4, :]
    o_bias_x[...] = small[4, :]
    o_gate[...] = small[5, :]
    for k in range(4):
        o_tap_s[k:k + 1, :] = small[7:8, k * 2 * S:(k + 1) * 2 * S]
    o_bias_s[...] = small[7, 8 * S:10 * S]
    o_bias_step[...] = small[7, 10 * S:10 * S + sz.heads]
    o_rate[...] = small[7, 10 * S + 128:10 * S + 128 + sz.heads]
    shape = (C, sz.heads)
    member = one_hot(iota(shape, 0) // (C // sz.heads) == iota(shape, 1))
    skip = jnp.broadcast_to(small[6:7, :], (8, C))
    o_skip[...] = sum(dot_nn(part, member) for part in split3(skip))[0]
    flat = jnp.concatenate([gain[h, k:k + 1, :] for h in range(2) for k in range(sz.half // 128)], axis=1)
    start = lax.axis_index("dp") * sz.share
    moved = pltpu.roll(jnp.broadcast_to(flat, (8, sz.width)), lax.rem(sz.width - start, sz.width), 1)
    o_gain[...] = moved[0, :sz.share]


def fused(sz, block_in, cotangent, lengths, dest_slot, return_slot, norm_gain, inner_weight, state_weight,
          step_weight, conv_inner, conv_inner_bias, conv_state, conv_state_bias, step_bias, log_rate,
          skip_gain, gate_gain, out_weight):
    dp, R, H, C, S = sz.dp, sz.rows, sz.half, sz.inner, sz.state
    W = sz.width

    vm = pl.BlockSpec(memory_space=pltpu.VMEM)
    hb = pl.BlockSpec(memory_space=pl.ANY)
    sm = pl.BlockSpec(memory_space=pltpu.SMEM)
    V = pltpu.VMEM
    packed = V((dp, sz.cap, H), BF)
    D = pltpu.SemaphoreType.DMA
    nch = len(sz.chunks)
    scratch = [
        V((W, 2 * C), BF), V((C, W), BF), V((W, 2 * S), BF), V((128, W), BF), V((8, 128), F32),
        *[packed] * 6,
        V((sz.slots, R), BF), V((R, sz.slots), BF), V((R, sz.slots), BF),
        V((2, R, H), BF), V((2, R, H), BF), V((R, W), BF), V((R, W), BF),
        V((4, R, sz.quarter), BF), V((4, R, sz.quarter), BF), V((2, 4, R // 2, sz.quarter), BF),
        V((sz.quarter, 4 * R), BF), V((sz.quarter, 4 * R), BF),
        V((4, R, sz.cols), BF), V((sz.nz, sz.share, sz.cols), BF), V((3, sz.share, sz.cols), BF), V((2, sz.share, sz.cols), BF),
        V((R, R), F32), V((R, R), F32), V((2, R, R), BF),
        V((R, 2 * S), F32), V((R, 2 * S), F32), V((R, 2 * S), BF), V((R, 128), F32), V((R, 128), F32), V((128, R), F32),
        V((R, 128), F32), V((R, 128), F32), V((R, 128), F32), V((R, 128), F32), V((R, 128), F32), V((R, 128), F32),
        V((3, 8, R), F32), V((3, 8, R), F32), V((R, H), BF), V((R, H), BF), V((R, H), BF),
        V((R, 2 * S), BF), V((R, 2 * S), BF),
        V((4, 8, C), F32), V((4, 8, C), F32), V((dp, 8, 128), F32), V((2, 8, 128), F32),
        D((6, dp)), D((6, dp)), D((2, 2)), D((2, 2)), D((nch, 3)), D((nch, 3)), D((2, 6)), D((2, 6)),
        D((nch, 6)), D((nch, 6)), D((6,)), D((6,)), D((dp,)), D((dp,)), D((4,)), D((4,)), D((4,)), D((2, dp)), D((2, dp)), D((2, 2)),
        pltpu.SemaphoreType.REGULAR,
    ]
    out = jax.ShapeDtypeStruct
    rows_out, grads_out, inner_g, proj_g, extra_g, small, gain = pl.pallas_call(
        functools.partial(block_kernel, sz),
        out_shape=(out((R, H), BF), out((R, H), BF), out((sz.share, 2 * C), F32), out((sz.share, C), F32),
                   out((sz.share, sz.extra), F32), out((8, C), F32), out((2, 8, 128), F32)),
        in_specs=[vm, vm, sm, hb, hb, hb, hb, hb] + [vm] * 10,
        out_specs=(hb, hb) + (vm,) * 5,
        scratch_shapes=scratch,
        compiler_params=pltpu.CompilerParams(collective_id=0, has_side_effects=True, vmem_limit_bytes=66000000),
        name="block",
    )(dest_slot.reshape(-1, 128), return_slot.reshape(-1, 128), lengths, block_in, cotangent, inner_weight, out_weight,
      state_weight, step_weight.T, conv_inner, conv_inner_bias.reshape(-1, 128), gate_gain.reshape(-1, 128), norm_gain.reshape(-1, 128), skip_gain[None],
      conv_state, conv_state_bias[None], step_bias[None], log_rate[None])
    results = pl.pallas_call(
        functools.partial(finish_kernel, sz),
        out_shape=(out((R, H), BF), out((R, H), BF), out((sz.share,), F32), out((sz.share, 2, C), F32),
                   out((sz.share, 2 * S), F32), out((sz.heads, sz.share), F32), out((4, C), F32), out((C,), F32),
                   out((4, 2 * S), F32), out((2 * S,), F32), out((sz.heads,), F32), out((sz.heads,), F32),
                   out((sz.heads,), F32), out((C,), F32), out((sz.share, C), F32)),
        in_specs=[vm] * 7,
        out_specs=(vm,) * 15,
        name="finish",
    )(rows_out, grads_out, inner_g, proj_g, extra_g, small, gain)
    return results[:5] + (results[5].T,) + results[6:14] + (results[14].T,)


def with_collectives(
    block_in,
    cotangent,
    lengths,
    dest_slot,
    return_slot,
    norm_gain,
    inner_weight,
    state_weight,
    step_weight,
    conv_inner,
    conv_inner_bias,
    conv_state,
    conv_state_bias,
    step_bias,
    log_rate,
    skip_gain,
    gate_gain,
    out_weight,
):
    groups = lax.axis_size("dp")
    group_rows = block_in.shape[0]
    half_width = block_in.shape[1]
    capacity = 2 * group_rows // groups
    own_group = lax.axis_index("dp")
    own_dest = lax.dynamic_slice_in_dim(dest_slot, own_group * group_rows, group_rows)
    own_return = lax.dynamic_slice_in_dim(return_slot, own_group * group_rows, group_rows)
    send_spot = send_layout(own_dest, group_rows, capacity, groups)
    back_spot = send_layout(own_return, group_rows, capacity, groups)
    slots_in = arrivals(dest_slot, group_rows, capacity, groups, own_group)
    slots_back = arrivals(return_slot, group_rows, capacity, groups, own_group)
    blank_rows = jnp.zeros((groups * capacity, half_width), jnp.bfloat16)
    packed_rows = blank_rows.at[send_spot].set(block_in).reshape(groups, capacity, half_width)
    packed_grads = blank_rows.at[back_spot].set(cotangent).reshape(groups, capacity, half_width)
    came_rows, came_grads = (
        lax.all_to_all(packed_rows, "dp", split_axis=0, concat_axis=0, tiled=True),
        lax.all_to_all(packed_grads, "dp", split_axis=0, concat_axis=0, tiled=True),
    )
    empty_rows = jnp.zeros((group_rows, half_width), jnp.bfloat16)
    own_rows = empty_rows.at[slots_in].set(came_rows.reshape(-1, half_width), mode="drop")
    own_grads = empty_rows.at[slots_back].set(came_grads.reshape(-1, half_width), mode="drop")
    full_rows, full_grads = (
        lax.all_gather(own_rows, "tensor", axis=1, tiled=True),
        lax.all_gather(own_grads, "tensor", axis=1, tiled=True),
    )
    seq_pos, live_mask, keep_state = stretch_layout(lengths[0], STRETCH)
    live_col = live_mask[:, None]
    hidden = full_rows.astype(jnp.float32)
    norm_scale = lax.rsqrt(jnp.mean(hidden * hidden, axis=1, keepdims=True) + EPSILON)
    normed = (hidden * norm_scale * norm_gain).astype(jnp.bfloat16)
    inner_local = inner_weight.shape[2]
    zx_weight = inner_weight.reshape(inner_weight.shape[0], 2 * inner_local)
    projected = jnp.dot(normed, zx_weight, preferred_element_type=jnp.float32)
    gate_raw = projected[:, :inner_local]
    conv_in_x = projected[:, inner_local:]
    conv_in_state = jnp.dot(normed, state_weight, preferred_element_type=jnp.float32)
    step_raw = jnp.dot(normed, step_weight, preferred_element_type=jnp.float32)
    x_conv = conv_forward(conv_in_x, conv_inner, conv_inner_bias, seq_pos)
    state_conv = conv_forward(conv_in_state, conv_state, conv_state_bias, seq_pos)
    x_act = jax.nn.silu(x_conv)
    state_act = jax.nn.silu(state_conv)
    state_width = state_act.shape[1] // 2
    heads_local = step_weight.shape[1]
    head_dim = inner_local // heads_local
    stretches = group_rows // STRETCH
    step_input = step_raw + step_bias[None, :]
    step_size = jax.nn.softplus(step_input) * live_col
    decay_rate = -jnp.exp(log_rate)
    skip_wide = jnp.repeat(skip_gain, head_dim)[None, :]
    scanned, saved = state_forward(
        x_act.reshape(group_rows, heads_local, head_dim),
        state_act[:, :state_width],
        state_act[:, state_width:],
        step_size,
        decay_rate,
        STRETCH,
    )
    mixed = scanned + skip_wide * x_act
    gate_act = jax.nn.silu(gate_raw)
    gated = mixed * gate_act
    inner_total = inner_local * lax.axis_size("tensor")
    square_sum = lax.psum(jnp.sum(gated * gated, axis=1), "tensor")
    gate_scale = lax.rsqrt(square_sum / inner_total + EPSILON)[:, None]
    gate_normed = (gated * gate_scale * gate_gain).astype(jnp.bfloat16)
    partial_out = jnp.dot(gate_normed, out_weight, preferred_element_type=jnp.float32)
    branch_half = lax.psum_scatter(partial_out, "tensor", scatter_dimension=1, tiled=True)
    half_index = lax.axis_index("tensor")
    out_half = (own_rows.astype(jnp.float32) + live_col * branch_half).astype(jnp.bfloat16)
    zero_row = jnp.zeros((1, half_width), jnp.bfloat16)
    reply_rows = jnp.concatenate([out_half, zero_row], axis=0)[slots_back]
    returned = lax.all_to_all(
        reply_rows.reshape(groups, capacity, half_width),
        "dp",
        split_axis=0,
        concat_axis=0,
        tiled=True,
    )
    block_out = returned.reshape(-1, half_width)[back_spot]
    owner_ct = full_grads.astype(jnp.float32)
    out_grad = (owner_ct * live_col).astype(jnp.bfloat16)
    out_weight_grad = jnp.einsum(
        "ti,td->id", gate_normed, out_grad, preferred_element_type=jnp.float32
    )
    normed_out_grad = jnp.einsum(
        "td,id->ti", out_grad, out_weight, preferred_element_type=jnp.float32
    )
    gate_gain_grad = jnp.sum(normed_out_grad * gated * gate_scale, axis=0)
    scaled_grad = gate_gain * normed_out_grad
    cross = lax.psum(jnp.sum(gated * scaled_grad, axis=1), "tensor")[:, None]
    gated_grad = gate_scale * scaled_grad - gated * gate_scale**3 * cross / inner_total
    mixed_grad = gated_grad * gate_act
    gate_raw_grad = gated_grad * mixed * silu_slope(gate_raw)
    skip_gain_grad = jnp.sum(
        (mixed_grad * x_act).reshape(group_rows, heads_local, head_dim), axis=(0, 2)
    )
    x_state_grad, written_grad, readout_grad, step_grad, rate_total = state_backward(
        saved, mixed_grad.reshape(stretches, STRETCH, heads_local, head_dim), decay_rate
    )
    x_act_grad = x_state_grad.reshape(group_rows, inner_local) + skip_wide * mixed_grad
    state_grad = lax.psum(
        jnp.concatenate(
            [written_grad.reshape(group_rows, -1), readout_grad.reshape(group_rows, -1)], axis=1
        ),
        "tensor",
    )
    state_conv_grad = state_grad * silu_slope(state_conv)
    x_conv_grad = x_act_grad * silu_slope(x_conv)
    state_raw_grad, conv_state_grad, conv_state_bias_grad = conv_backward(
        conv_in_state, conv_state, seq_pos, state_conv_grad
    )
    x_raw_grad, conv_inner_grad, conv_inner_bias_grad = conv_backward(
        conv_in_x, conv_inner, seq_pos, x_conv_grad
    )
    step_raw_grad = (
        step_grad.reshape(group_rows, heads_local) * live_col * jax.nn.sigmoid(step_input)
    )
    step_bias_grad = jnp.sum(step_raw_grad, axis=0)
    log_rate_grad = rate_total * decay_rate
    zx_low = jnp.concatenate([gate_raw_grad, x_raw_grad], axis=1).astype(jnp.bfloat16)
    state_low = state_raw_grad.astype(jnp.bfloat16)
    step_low = step_raw_grad.astype(jnp.bfloat16)
    inner_weight_grad = jnp.einsum(
        "td,tk->dk", normed, zx_low, preferred_element_type=jnp.float32
    )
    state_weight_grad = jnp.einsum(
        "td,tk->dk", normed, state_low, preferred_element_type=jnp.float32
    )
    step_weight_grad = jnp.einsum("td,tk->dk", normed, step_low, preferred_element_type=jnp.float32)
    lead_share = (half_index == 0).astype(jnp.float32)
    normed_grad = jnp.einsum("tk,dk->td", zx_low, zx_weight, preferred_element_type=jnp.float32)
    normed_grad = normed_grad + jnp.einsum(
        "tk,dk->td", step_low, step_weight, preferred_element_type=jnp.float32
    )
    normed_grad = normed_grad + lead_share * jnp.einsum(
        "tk,dk->td", state_low, state_weight, preferred_element_type=jnp.float32
    )
    normed_grad = lax.psum(normed_grad, "tensor")
    norm_gain_grad = jnp.sum(normed_grad * hidden * norm_scale, axis=0)
    input_scaled = norm_gain * normed_grad
    hidden_grad = (
        norm_scale * input_scaled
        - hidden * norm_scale**3 * jnp.mean(hidden * input_scaled, axis=1, keepdims=True)
        + owner_ct
    )
    own_grad = lax.dynamic_slice_in_dim(hidden_grad, half_index * half_width, half_width, 1).astype(
        jnp.bfloat16
    )
    answer_rows = jnp.concatenate([own_grad, zero_row], axis=0)[slots_in]
    gone = lax.all_to_all(
        answer_rows.reshape(groups, capacity, half_width),
        "dp",
        split_axis=0,
        concat_axis=0,
        tiled=True,
    )
    input_grad = gone.reshape(-1, half_width)[send_spot]
    (
        conv_inner_grad,
        conv_inner_bias_grad,
        conv_state_grad,
        conv_state_bias_grad,
        step_bias_grad,
        log_rate_grad,
        skip_gain_grad,
        gate_gain_grad,
    ) = lax.psum(
        (
            conv_inner_grad,
            conv_inner_bias_grad,
            conv_state_grad,
            conv_state_bias_grad,
            step_bias_grad,
            log_rate_grad,
            skip_gain_grad,
            gate_gain_grad,
        ),
        "dp",
    )
    zx_share, state_share, step_share, gain_share, out_share = (
        lax.psum_scatter(inner_weight_grad.astype(jnp.bfloat16), "dp", scatter_dimension=0, tiled=True),
        lax.psum_scatter(state_weight_grad, "dp", scatter_dimension=0, tiled=True),
        lax.psum_scatter(step_weight_grad, "dp", scatter_dimension=0, tiled=True),
        lax.psum_scatter(norm_gain_grad, "dp", scatter_dimension=0, tiled=True),
        lax.psum_scatter(out_weight_grad.astype(jnp.bfloat16), "dp", scatter_dimension=1, tiled=True),
    )
    zx_share = zx_share.astype(jnp.float32).reshape((-1,) + inner_weight.shape[1:])
    out_share = out_share.astype(jnp.float32)
    return (
        block_out,
        input_grad,
        gain_share,
        zx_share,
        state_share,
        step_share,
        conv_inner_grad,
        conv_inner_bias_grad,
        conv_state_grad,
        conv_state_bias_grad,
        step_bias_grad,
        log_rate_grad,
        skip_gain_grad,
        gate_gain_grad,
        out_share,
    )


def on_device(*args):
    groups = lax.axis_size("dp")
    rows, half = args[0].shape
    inner, heads, state = args[6].shape[2], args[8].shape[1], args[7].shape[1] // 2
    capacity = 2 * rows // groups
    fits = (
        groups == 16 and capacity % 16 == 0 and (2 * half // groups) % 16 == 0
        and rows == STRETCH and args[2].shape[1] == 1 and inner == 64 * heads and inner == 2 * half
    )
    if fits:
        return fused(Sizes(groups, rows, half, inner, heads, state, capacity), *args)
    return with_collectives(*args)


def solution(mesh):
    placed = (
        P("dp", "tensor"),
        P("dp", "tensor"),
        P("dp", None),
        P(),
        P(),
        P(),
        P(None, None, "tensor"),
        P(),
        P(None, "tensor"),
        P(None, "tensor"),
        P("tensor"),
        P(),
        P(),
        P("tensor"),
        P("tensor"),
        P("tensor"),
        P("tensor"),
        P("tensor", None),
    )
    return jax.shard_map(
        on_device,
        mesh=mesh,
        in_specs=placed,
        out_specs=(
            P("dp", "tensor"),
            P("dp", "tensor"),
            P("dp"),
            P("dp", None, "tensor"),
            P("dp", None),
            P("dp", "tensor"),
            P(None, "tensor"),
            P("tensor"),
            P(),
            P(),
            P("tensor"),
            P("tensor"),
            P("tensor"),
            P("tensor"),
            P("tensor", "dp"),
        ),
        check_vma=False,
    )
```

```python
import functools

import jax
import jax.numpy as jnp
from jax import lax
from jax.experimental import pallas as pl
from jax.experimental.pallas import tpu as pltpu
from jax.sharding import PartitionSpec as P

STRETCH = 256


PRECISE = lax.Precision.HIGHEST
EPSILON = 1e-05


def silu_slope(values):
    logistic = jax.nn.sigmoid(values)
    return logistic * (1.0 + values * (1.0 - logistic))


def stretch_layout(seq_lengths, stretch_rows):
    total_stretches = seq_lengths.shape[0]
    numbers = jnp.arange(total_stretches, dtype=jnp.int32)
    begins = seq_lengths > 0
    first_stretch = jnp.max(
        jnp.where(begins[None, :] & (numbers[None, :] <= numbers[:, None]), numbers[None, :], 0),
        axis=1,
    )
    seq_length = jnp.sum(
        jnp.where(numbers[None, :] == first_stretch[:, None], seq_lengths[None, :], 0), axis=1
    )
    within = (
        jnp.arange(stretch_rows, dtype=jnp.int32)[None, :]
        + ((numbers - first_stretch) * stretch_rows)[:, None]
    )
    live_mask = (within < seq_length[:, None]).astype(jnp.float32).reshape(-1)
    keep_state = 1.0 - begins.astype(jnp.float32)
    return (within.reshape(-1), live_mask, keep_state)


def shift_down(values, steps):
    return jnp.concatenate(
        [jnp.zeros((steps,) + values.shape[1:], values.dtype), values[:-steps]], axis=0
    )


def shift_up(values, steps):
    return jnp.concatenate(
        [values[steps:], jnp.zeros((steps,) + values.shape[1:], values.dtype)], axis=0
    )


def conv_forward(raw_in, tap_weights, tap_bias, seq_pos):
    total = tap_bias[None, :] + tap_weights[0][None, :] * raw_in
    for tap_index in range(1, tap_weights.shape[0]):
        valid = (seq_pos >= tap_index).astype(jnp.float32)[:, None]
        total = total + tap_weights[tap_index][None, :] * shift_down(raw_in, tap_index) * valid
    return total


def conv_backward(raw_in, tap_weights, seq_pos, conv_grad):
    tap_grads = [jnp.sum(conv_grad * raw_in, axis=0)]
    raw_grad = tap_weights[0][None, :] * conv_grad
    for tap_index in range(1, tap_weights.shape[0]):
        masked = conv_grad * (seq_pos >= tap_index).astype(jnp.float32)[:, None]
        tap_grads.append(jnp.sum(masked * shift_down(raw_in, tap_index), axis=0))
        raw_grad = raw_grad + tap_weights[tap_index][None, :] * shift_up(masked, tap_index)
    return (raw_grad, jnp.stack(tap_grads, axis=0), jnp.sum(conv_grad, axis=0))


def send_layout(targets, group_rows, capacity, groups):
    owner_group = targets // group_rows
    onehot = (owner_group[:, None] == jnp.arange(groups, dtype=jnp.int32)[None, :]).astype(
        jnp.int32
    )
    arrival = jnp.sum(jnp.cumsum(onehot, axis=0) * onehot, axis=1) - 1
    return owner_group * capacity + arrival


def arrivals(targets, group_rows, capacity, groups, own_group):
    by_source = targets.reshape(groups, group_rows)
    owner_group = by_source // group_rows
    is_mine = (owner_group == own_group).astype(jnp.int32)
    arrival = jnp.cumsum(is_mine, axis=1) - 1
    position = jnp.arange(groups, dtype=jnp.int32)[:, None] * capacity + arrival
    position = jnp.where(is_mine > 0, position, groups * capacity)
    filler = jnp.full((groups * capacity,), group_rows, jnp.int32)
    return filler.at[position.reshape(-1)].set(
        (by_source - owner_group * group_rows).reshape(-1), mode="drop"
    )


def state_forward(x_heads, written, readout, step_size, decay_rate, stretch_rows):
    rows_all, heads, head_dim = x_heads.shape
    stretches = rows_all // stretch_rows
    x_blocks = x_heads.reshape(stretches, stretch_rows, heads, head_dim)
    w_blocks = written.reshape(stretches, stretch_rows, -1)
    r_blocks = readout.reshape(stretches, stretch_rows, -1)
    step_blocks = step_size.reshape(stretches, stretch_rows, heads)
    log_decay = jnp.cumsum(step_blocks * decay_rate[None, None, :], axis=1)
    by_head = jnp.transpose(log_decay, (0, 2, 1))
    causal = jnp.arange(stretch_rows)[:, None] >= jnp.arange(stretch_rows)[None, :]
    spread = by_head[:, :, :, None] - by_head[:, :, None, :]
    fading = jnp.where(causal, jnp.exp(jnp.where(causal, spread, 0.0)), 0.0)
    intersection = jnp.einsum("cin,cjn->cij", r_blocks, w_blocks, precision=PRECISE)
    mixing = intersection[:, None, :, :] * fading
    driven = step_blocks[..., None] * x_blocks
    to_end = jnp.exp(log_decay[:, -1:, :] - log_decay)
    stretch_state = jnp.einsum(
        "cjhp,cjn->chpn", to_end[..., None] * driven, w_blocks, precision=PRECISE
    )
    end_fade = jnp.exp(log_decay[:, -1, :])
    running = jnp.zeros(stretch_state.shape[1:], jnp.float32)
    entering = []
    entering.append(running)
    entering = jnp.stack(entering)
    from_start = jnp.exp(log_decay)
    carried_out = from_start[..., None] * jnp.einsum(
        "chpn,cin->cihp", entering, r_blocks, precision=PRECISE
    )
    inner_out = jnp.einsum("chij,cjhp->cihp", mixing, driven, precision=PRECISE)
    saved = (
        x_blocks,
        w_blocks,
        r_blocks,
        step_blocks,
        causal,
        fading,
        mixing,
        driven,
        to_end,
        entering,
        end_fade,
        from_start,
        carried_out,
    )
    return ((inner_out + carried_out).reshape(rows_all, heads * head_dim), saved)


def state_backward(saved, mixed_grad, decay_rate):
    (
        x_blocks,
        w_blocks,
        r_blocks,
        step_blocks,
        causal,
        fading,
        mixing,
        driven,
        to_end,
        entering,
        end_fade,
        from_start,
        carried_out,
    ) = saved
    stretches = x_blocks.shape[0]
    scaled = from_start[..., None] * mixed_grad
    readout_grad = jnp.einsum("cihp,chpn->cin", scaled, entering, precision=PRECISE)
    from_out = jnp.einsum("cihp,cin->chpn", scaled, r_blocks, precision=PRECISE)
    decay_grad = jnp.sum(carried_out * mixed_grad, axis=3)
    downstream = jnp.zeros(from_out.shape[1:], jnp.float32)
    passed = []
    end_grads = []
    for number in reversed(range(stretches)):
        handed = jnp.zeros_like(downstream)
        passed.append(handed)
        end_grads.append(jnp.sum(handed * entering[number], axis=(1, 2)))
        downstream = from_out[number] + end_fade[number][:, None, None] * handed
    passed = jnp.stack(passed[::-1])
    end_grads = jnp.stack(end_grads[::-1])
    pulled = jnp.einsum("chpn,cjn->cjhp", passed, w_blocks, precision=PRECISE)
    driven_grad = to_end[..., None] * pulled
    written_grad = jnp.einsum(
        "cjhp,chpn->cjn", to_end[..., None] * driven, passed, precision=PRECISE
    )
    tail_grad = jnp.sum(pulled * driven, axis=3) * to_end
    decay_grad = decay_grad - tail_grad
    last_extra = jnp.sum(tail_grad, axis=1) + end_grads * end_fade
    mixing_grad = jnp.where(
        causal, jnp.einsum("cihp,cjhp->chij", mixed_grad, driven, precision=PRECISE), 0.0
    )
    driven_grad = driven_grad + jnp.einsum("chij,cihp->cjhp", mixing, mixed_grad, precision=PRECISE)
    intersection_grad = jnp.sum(mixing_grad * fading, axis=1)
    readout_grad = readout_grad + jnp.einsum(
        "cij,cjn->cin", intersection_grad, w_blocks, precision=PRECISE
    )
    written_grad = written_grad + jnp.einsum(
        "cij,cin->cjn", intersection_grad, r_blocks, precision=PRECISE
    )
    product = mixing_grad * mixing
    decay_grad = decay_grad + jnp.transpose(
        jnp.sum(product, axis=3) - jnp.sum(product, axis=2), (0, 2, 1)
    )
    decay_grad = decay_grad.at[:, -1, :].add(last_extra)
    step_grad = jnp.sum(driven_grad * x_blocks, axis=3)
    x_state_grad = step_blocks[..., None] * driven_grad
    rate_grad = jnp.flip(jnp.cumsum(jnp.flip(decay_grad, axis=1), axis=1), axis=1)
    step_grad = step_grad + rate_grad * decay_rate[None, None, :]
    rate_total = jnp.sum(rate_grad * step_blocks, axis=(0, 1))
    return (x_state_grad, written_grad, readout_grad, step_grad, rate_total)


MESH = pl.DeviceIdType.MESH
BF = jnp.bfloat16
F32 = jnp.float32
NEG = -1e30


def dot_nn(a, b):
    return lax.dot_general(a, b, (((1,), (0,)), ((), ())), preferred_element_type=F32)


def dot_nt(a, b):
    return lax.dot_general(a, b, (((1,), (1,)), ((), ())), preferred_element_type=F32)


def dot_tn(a, b):
    return lax.dot_general(a, b, (((0,), (0,)), ((), ())), preferred_element_type=F32)


def iota(shape, axis):
    return lax.broadcasted_iota(jnp.int32, shape, axis)


def one_hot(cond):
    return jnp.where(cond, 1.0, 0.0).astype(BF)


def split3(v):
    high = v.astype(BF)
    rest = v - high.astype(F32)
    mid = rest.astype(BF)
    return high, mid, (rest - mid.astype(F32)).astype(BF)


def sigmoid(v):
    return 1.0 / (1.0 + jnp.exp(-v))


def rows_down(v, k):
    return jnp.where(iota(v.shape, 0) >= k, pltpu.roll(v, k, 0), 0.0)


def rows_up(v, k):
    n = v.shape[0]
    return jnp.where(iota(v.shape, 0) < n - k, pltpu.roll(v, n - k, 0), 0.0)


def pick(v, lane, index):
    return jnp.sum(jnp.where(lane == index, v, 0.0), axis=1, keepdims=True)


class Sizes:
    def __init__(self, dp, rows, half, inner, heads, state, capacity):
        self.dp, self.rows, self.half, self.inner = dp, rows, half, inner
        self.heads, self.state, self.cap = heads, state, capacity
        self.width = 2 * half
        self.nz = dp // 4
        self.share = self.width // dp
        self.quarter = self.nz * self.share
        self.slots = dp * capacity
        self.tiles = inner // 128
        self.extra = 2 * state + 128
        self.cols = 3 * inner + self.extra
        n = inner // 2
        sizes = [n // 3 * 2, n // 3 * 4, n, n, n, n, self.extra]
        self.chunks = [(sum(sizes[:k]), size) for k, size in enumerate(sizes)]
        self.levels = self.nz.bit_length() - 1


def targets_of(lines, sz):
    n = sz.rows // 128
    return jnp.concatenate([lines[pl.ds(k, sz.dp, stride=n), :] for k in range(n)], axis=1)


def send_table(targets, g, sz):
    strict = one_hot(iota((sz.rows, sz.rows), 0) < iota((sz.rows, sz.rows), 1))
    every = targets_of(targets, sz)
    own = jnp.sum(jnp.where(iota(every.shape, 0) == g, every, 0), axis=0, keepdims=True)
    group = lax.shift_right_logical(own, 8)
    hot = jnp.where(iota((sz.dp, sz.rows), 0) == group, 1.0, 0.0)
    before = dot_nn(hot.astype(BF), strict)
    rank = jnp.sum(hot * before, axis=0, keepdims=True)
    spot = group.astype(F32) * sz.cap + rank
    return one_hot(iota((sz.slots, sz.rows), 0).astype(F32) == spot)


def owner_table(targets, g, sz):
    strict = one_hot(iota((sz.rows, sz.rows), 0) < iota((sz.rows, sz.rows), 1))
    every = targets_of(targets, sz)
    mine = jnp.where(lax.shift_right_logical(every, 8) == g, 1.0, 0.0)
    rank = dot_nn(mine.astype(BF), strict)
    slot = mine * ((every & 255) + 1).astype(F32)
    lane = iota((sz.dp, 128), 1)
    found = jnp.zeros((sz.dp, 128), F32)
    for a in range(sz.cap):
        one = jnp.sum(jnp.where(rank == float(a), slot, 0.0), axis=1, keepdims=True)
        found = jnp.where(lane == a, one, found)
    place = iota((128, sz.slots), 1)
    spread = one_hot((place % sz.cap) == iota((128, sz.slots), 0))
    wide = dot_nn(found.astype(BF), spread)
    keep = (iota((sz.dp, sz.slots), 1) // sz.cap) == iota((sz.dp, sz.slots), 0)
    row = jnp.sum(jnp.where(keep, wide, 0.0), axis=0, keepdims=True) - 1.0
    return one_hot(iota((sz.rows, sz.slots), 0).astype(F32) == row)


def block_kernel(sz, *refs):
    (dest, back, length, rows_hbm, ct_hbm, win_hbm, wout_hbm, wst_hbm, wstep_in,
     tap_x, bias_x, gain_g, gain_n, skip_in, tap_s, bias_s, bias_step, log_rate,
     out_rows, out_grads, inner_out, proj_out, extra_out, small_out, gain_out,
     win, wout, wst, wstep, lines,
     pk_in, pk_ct, rc_in, rc_ct, gn_o, gn_g,
     p_own, q_in, q_bk,
     hid, cts, normed, lowct, perm, xA, xE, tA, tE,
     yb, pb, r0, r1, f_inner, f_proj, f_extra,
     inter, igrad, ptile,
     sraw, sslope, wr, dtv, lac, lar, sgr, rgr, stepsig, acc1, acc2, scale,
     stat_s, stat_r, half_s, half_r, raw_r, st_s, st_r,
     sms, smr, gall, gsum,
     a2a_s, a2a_r, fw_s, fw_r, quad_s, quad_r, xq_s, xq_r, z_s, z_r, y_s, y_r, gg_s, gg_r, sm_s, sm_r, w_s, own_s, relay_s, raw_sem, o_s, taken) = refs
    dp, R, H, C = sz.dp, sz.rows, sz.half, sz.inner
    W, NT_ = sz.width, sz.tiles
    g = lax.axis_index("dp")
    t = lax.axis_index("tensor")
    o = 1 - t
    c, x, z = g % 2, (g // 2) % 2, g // 4
    q = g % 4
    sib, xp = g + 1 - 2 * c, g + 2 - 4 * x
    diag = sib + 2 - 4 * x

    def rcopy(src, dst, ss, rs, peer, side=None):
        return pltpu.make_async_remote_copy(
            src_ref=src, dst_ref=dst, send_sem=ss, recv_sem=rs,
            device_id=(peer, t if side is None else side), device_id_type=MESH)

    sent = []

    def go(copy):
        copy.start()
        sent.append(copy)
        return copy

    loads = [pltpu.make_async_copy(a, b, w_s.at[i]) for i, (a, b) in enumerate(
        [(rows_hbm, lowct.at[:, pl.ds(0, H)]), (ct_hbm, lowct.at[:, pl.ds(H, H)]), (wst_hbm, wst), (wout_hbm, wout)])]
    for load in loads[:2]:
        load.start()

    barrier = pltpu.get_barrier_semaphore()
    for off in range(1, dp):
        pl.semaphore_signal(barrier, inc=1, device_id=((g + off) % dp, t), device_id_type=MESH)
    pl.semaphore_signal(barrier, inc=1, device_id=(g, o), device_id_type=MESH)

    side = z // 2
    zo, zi, fi, fo = 3 * side, 1 + side, 2 - side, 3 - 3 * side
    is_outer = (z + side + 1) % 2
    is_inner = 1 - is_outer
    far = [
        ((z + dz) % sz.nz) * 4 + ((x + dx) % 2) * 2 + (c + dc) % 2
        for dz in (2, 1, 3, 0) for dx in (1, 0) for dc in (1, 0) if dz + dx + dc]
    level = [z * 4 + ((x + dx) % 2) * 2 + (c + dc) % 2 for dx, dc in ((1, 1), (1, 0), (0, 1))]
    across = [zz * 4 + ((x + dx) % 2) * 2 + (c + dc) % 2 for zz in (fo, fi) for dx in (1, 0) for dc in (1, 0)]
    beside_z = is_outer * zi + (1 - is_outer) * zo
    beside = [beside_z * 4 + ((x + dx) % 2) * 2 + (c + dc) % 2 for dx, dc in ((1, 1), (1, 0), (0, 1))]
    partner = beside_z * 4 + q
    parts = [pl.ds(0, H // 3 * 2), pl.ds(H // 3 * 2, H // 3)]

    def span(ref, n, ss, rs, at=slice(None)):
        return rcopy(ref.at[pl.ds(0, n), :, at], ref.at[pl.ds(0, n), :, at], ss, rs, partner)

    def exchange(i, source, target, at=slice(None)):
        for peer in far:
            rcopy(source.at[peer, :, at], target.at[g, :, at], a2a_s.at[i], a2a_r.at[i], peer).start()
        return [span(source, dp - 1, a2a_s.at[i], a2a_r.at[i], at)]

    def settle(copies):
        for copy in copies:
            copy.wait_send()

    def arrived(i, target, at=slice(None)):
        span(target, dp - 1, a2a_s.at[i], a2a_r.at[i], at).wait_recv()

    def answer(table, value, dst):
        for k in range(2):
            n = sz.slots // 2
            part = dot_tn(table[:, k * n:(k + 1) * n], value).astype(BF)
            dst[k * (dp // 2):(k + 1) * (dp // 2)] = part.reshape(dp // 2, sz.cap, H)

    def block_to(i, source, target, peer, owner, sems):
        return rcopy(source.at[peer], target.at[owner], sems.at[i - 4], a2a_r.at[i], peer)

    def raw_copy(i):
        return rcopy(lowct.at[:, pl.ds((i - 4) * H, H)], raw_r, raw_sem.at[0, i - 4], raw_sem.at[1, i - 4], partner)

    def near_x(peers, same):
        if len(peers) == 3:
            return peers[2:] if same else peers[:2]
        return [peer for k, peer in enumerate(peers) if (k % 4 >= 2) == same]

    def reply_send(i, packed, target, same):
        @pl.when(is_outer == 0)
        def _():
            for peer in near_x(across, same) + near_x(beside, same) + ([partner] if same else []):
                block_to(i, packed, target, peer, g, own_s).start()
        for peer in near_x(level, same):
            block_to(i, packed, target, peer, g, own_s).start()

    def reply(i, table, value, packed, target):
        answer(table, value, packed)
        target[pl.ds(g, 1)] = packed[pl.ds(g, 1)]

        @pl.when(is_outer == 1)
        def _():
            if i == 5:
                pl.semaphore_wait(taken, 1)
            lowct[:, (i - 4) * H:(i - 3) * H] = value
            raw_copy(i).start()

    def relay_send(i, packed, target, same):
        @pl.when(is_outer == 0)
        def _():
            for peer in near_x(across, same) + near_x(level, same):
                block_to(i, packed, target, peer, partner, relay_s).start()

    def relay(i, targets, packed, target):
        @pl.when(is_outer == 0)
        def _():
            raw_copy(i).wait_recv()
            answer(owner_table(targets, partner, sz), raw_r[...], packed)
            if i == 4:
                pl.semaphore_signal(taken, inc=1, device_id=(partner, t), device_id_type=MESH)
            target[pl.ds(partner, 1)] = packed[pl.ds(g, 1)]

    def replied(i, target):
        @pl.when(is_outer == 1)
        def _():
            span(target, dp - 1, own_s.at[i - 4], a2a_r.at[i]).wait_recv()

        @pl.when(is_outer == 0)
        def _():
            span(target, dp - 2, own_s.at[i - 4], a2a_r.at[i]).wait_recv()

    def reply_settle(i, packed):
        @pl.when(is_outer == 1)
        def _():
            span(packed, len(level), own_s.at[i - 4], a2a_r.at[i]).wait_send()

        @pl.when(is_outer == 0)
        def _():
            span(packed, dp - 1, own_s.at[i - 4], a2a_r.at[i]).wait_send()
            span(packed, len(across + level), relay_s.at[i - 4], a2a_r.at[i]).wait_send()

    def pack(table, source, target):
        for k in range(2):
            n = sz.slots // 2
            part = dot_nn(table[k * n:(k + 1) * n, :], source[...]).astype(BF)
            target[k * (dp // 2):(k + 1) * (dp // 2)] = part.reshape(dp // 2, sz.cap, H)

    p_own[...] = send_table(dest, g, sz)
    loads[0].wait()
    pack(p_own, lowct.at[:, pl.ds(0, H)], pk_in)
    pl.semaphore_wait(barrier, dp)
    rows_away = exchange(0, pk_in, rc_in, parts[0]) + exchange(1, pk_in, rc_in, parts[1])
    rc_in[pl.ds(g, 1)] = pk_in[pl.ds(g, 1)]
    for load in loads[2:]:
        load.start()
    p_own[...] = send_table(back, g, sz)
    loads[1].wait()
    pack(p_own, lowct.at[:, pl.ds(H, H)], pk_ct)
    rc_ct[pl.ds(g, 1)] = pk_ct[pl.ds(g, 1)]
    q_in[...] = owner_table(dest, g, sz)
    q_bk[...] = owner_table(back, g, sz)

    def unpack(i, table, source, full, part):
        at = parts[part]
        arrived(2 * i + part, source, at)
        n = at.size
        full[pl.ds(t, 1), :, at] = dot_nn(table[...], source[:, :, at].reshape(sz.slots, n)).astype(BF)[None]
        go(rcopy(full.at[t, :, at], full.at[t, :, at], fw_s.at[i, part], fw_r.at[i, part], g, o))

    def other_half(i, full):
        for part in range(2):
            at = parts[part]
            rcopy(full.at[o, :, at], full.at[o, :, at], fw_s.at[i, part], fw_r.at[i, part], g, o).wait_recv()

    def take_apart(stage, sems):
        n = W // 128
        fetch = [pltpu.make_async_copy(win_hbm.at[pl.ds(k * 128, 128)], stage.at[k % 4], sems.at[k % 4]) for k in range(n)]
        for copy in fetch[:4]:
            copy.start()
        place = iota((256, 256), 0)
        order = one_hot(iota((256, 256), 1) == jnp.where(place < 128, 2 * place, 2 * place - 255))
        for k in range(n):
            fetch[k].wait()
            for m in range(0, C, 256):
                pair = jnp.concatenate(
                    [stage[k % 4, :, :, m + e:m + e + 128].reshape(256, 128) for e in (0, 128)], axis=1)
                both = dot_nn(order, pair).astype(BF)
                win[k * 128:(k + 1) * 128, m:m + 256] = both[:128]
                win[k * 128:(k + 1) * 128, C + m:C + m + 256] = both[128:]
            if k + 4 < n:
                fetch[k + 4].start()

    pl.run_scoped(take_apart, pltpu.VMEM((4, 128, 2, C), BF), pltpu.SemaphoreType.DMA((4,)))
    grads_away = exchange(2, pk_ct, rc_ct, parts[0])
    unpack(0, q_in, rc_in, hid, 0)
    grads_away += exchange(3, pk_ct, rc_ct, parts[1])
    unpack(0, q_in, rc_in, hid, 1)
    other_half(0, hid)

    total = jnp.zeros((R, 128), F32)
    for k in range(W // 128):
        v = hid[k // (H // 128), :, (k % (H // 128)) * 128:(k % (H // 128)) * 128 + 128].astype(F32)
        total = total + v * v
    norm_scale = lax.rsqrt(jnp.sum(total, axis=1, keepdims=True) / W + EPSILON)
    scale[...] = jnp.broadcast_to(norm_scale, (R, 128))
    for k in range(W // 128):
        v = hid[k // (H // 128), :, (k % (H // 128)) * 128:(k % (H // 128)) * 128 + 128].astype(F32)
        normed[:, k * 128:(k + 1) * 128] = (v * scale[...] * gain_n[k:k + 1, :]).astype(BF)

    def quarters(source):
        for qq in range(4):
            perm[qq] = jnp.concatenate(
                [source[:, sz.share * (4 * zz + qq):sz.share * (4 * zz + qq + 1)] for zz in range(sz.nz)], axis=1)

    def send_quarter(i, dst):
        copies = [
            rcopy(perm.at[peer % 4], dst.at[rel], xq_s.at[i, rel - 1], xq_r.at[i, rel - 1], peer)
            for rel, peer in ((2, xp), (3, diag), (1, sib))]
        for copy in copies:
            copy.start()
        dst[0:1] = perm[pl.ds(q, 1)]
        return copies

    def turn_quarter(dst, turned):
        for rel, peer in ((1, sib), (2, xp), (3, diag)):
            rcopy(dst.at[rel], dst.at[rel], xq_s.at[0, rel - 1], xq_r.at[0, rel - 1], peer).wait_recv()
        for rel in range(4):
            turned[:, rel * R:(rel + 1) * R] = jnp.transpose(dst[rel].astype(F32)).astype(BF)

    def fold_half(which, place):
        value = cts[pl.ds(which, 1)][0]
        for qq in range(4):
            cut = jnp.concatenate(
                [value[:, sz.share * (4 * zz + qq):sz.share * (4 * zz + qq + 1)] for zz in range(sz.nz // 2)], axis=1)
            cut = jnp.where(iota(cut.shape, 0) < length[0, 0], cut.astype(F32), 0.0).astype(BF)
            perm[qq, place * (R // 2):(place + 1) * (R // 2)] = jnp.concatenate([cut[:R // 2], cut[R // 2:]], axis=1)

    def fold_copy(sem, quarter, place, half, rel, peer, to):
        return rcopy(perm.at[quarter, pl.ds(place * (R // 2), R // 2)], xE.at[half, rel], xq_s.at[1, sem], xq_r.at[1, sem], peer, to)

    def fold_pass(rel, half):
        return rcopy(xE.at[half, rel], xE.at[half, rel], xq_s.at[1, 2 + rel], xq_r.at[1, 2 + rel], g, o)

    def turn_folds():
        fold_copy(0, 0, 0, t, 1, sib, t).wait_recv()
        fold_copy(3, 0, 0, o, 1, sib, t).wait_recv()
        for rel in (2, 3):
            fold_pass(rel, o).wait_recv()
        n = sz.quarter // 2
        for half in range(2):
            for rel in range(4):
                flat = jnp.transpose(xE[half, rel].astype(F32)).astype(BF)
                tE[half * n:(half + 1) * n, rel * R:rel * R + R // 2] = flat[:n]
                tE[half * n:(half + 1) * n, rel * R + R // 2:(rel + 1) * R] = flat[n:]

    quarters(normed)
    quarter_away = send_quarter(0, xA)

    loads[2].wait()
    wstep[...] = jnp.zeros_like(wstep)
    wstep[:sz.heads] = wstep_in[...]
    lines[...] = jnp.zeros_like(lines)
    lines[0:1, :sz.heads] = bias_step[...]
    lines[1:2, :sz.heads] = log_rate[...]
    row = iota((R, 128), 0)
    lane = iota((R, 128), 1)
    live = jnp.where(row < length[0, 0], 1.0, 0.0)
    sraw[...] = dot_nn(normed[...], wst[...])
    step_in = dot_nt(normed[...], wstep[...]) + lines[0:1, :]
    S = sz.state
    for k in range(2):
        cut = slice(k * S, (k + 1) * S)
        raw = sraw[:, cut]
        conv = bias_s[:, cut] + tap_s[0:1, cut] * raw
        for tap in range(1, 4):
            conv = conv + tap_s[tap:tap + 1, cut] * rows_down(raw, tap)
        sg = sigmoid(conv)
        sslope[:, cut] = sg * (1.0 + conv * (1.0 - sg))
        wr[:, cut] = (conv * sg).astype(BF)
    written, readout = wr[:, :S], wr[:, S:]
    inter[...] = dot_nt(readout, written)
    stepsig[...] = sigmoid(step_in) * live
    heads_live = jnp.where(lane < sz.heads, live, 0.0)
    step = (jnp.maximum(step_in, 0.0) + jnp.log1p(jnp.exp(-jnp.abs(step_in)))) * heads_live
    rate = -jnp.exp(lines[1:2, :])
    dtv[...] = step
    lower = one_hot(iota((R, R), 0) >= iota((R, R), 1))
    log_decay = sum(dot_nn(lower, part) for part in split3(step * rate))
    lac[...] = log_decay
    lar[...] = jnp.transpose(log_decay)

    def cols_of(i):
        return pl.ds(sz.chunks[i][0], sz.chunks[i][1])

    def quad_send(i):
        at = cols_of(i)
        rcopy(yb.at[0, :, at], yb.at[2, :, at], quad_s.at[1], quad_r.at[i, 1], xp).start()
        rcopy(yb.at[0, :, at], yb.at[1, :, at], quad_s.at[0], quad_r.at[i, 0], sib).start()

    def quad_pass(i):
        at = cols_of(i)
        rcopy(yb.at[2, :, at], yb.at[2, :, at], quad_s.at[1], quad_r.at[i, 1], xp).wait_recv()
        rcopy(yb.at[2, :, at], yb.at[3, :, at], quad_s.at[2], quad_r.at[i, 2], sib).start()

    def z_copy(i, k):
        at = cols_of(i)
        column = g % 4
        if k < 3:
            block, slot, peer = (zi, fi, fo)[k], r0.at[k], zi
        elif k < 5:
            block, slot, peer = (fi, fo)[k - 3], r1.at[k - 3], fi
        else:
            block, slot, peer = zo, r0.at[0], zo
        return rcopy(pb.at[block, :, at], slot.at[:, at], z_s, z_r.at[i, k], peer * 4 + column)

    def z_wait(i, k):
        at = cols_of(i)
        slot = r0.at[k] if k < 3 else r1.at[k - 3] if k < 5 else r0.at[0]
        rcopy(slot.at[:, at], slot.at[:, at], z_s, z_r.at[i, k], g + 4 - 8 * (z // 3)).wait_recv()

    def each_tile(i, block, landed, keep):
        start, size = sz.chunks[i]
        for n in range(0, size, 128):
            cut = slice(start + n, start + n + 128)
            value = pb[pl.ds(block, 1), :, cut].astype(F32)[0] + landed[:, cut].astype(F32)
            if keep:
                pb[pl.ds(block, 1), :, cut] = value.astype(BF)[None]
            elif start + n < C:
                f_proj[:, cut] = value
            elif start + n < 3 * C:
                f_inner[:, start + n - C:start + n - C + 128] = value
            else:
                f_extra[:, start + n - 3 * C:start + n - 3 * C + 128] = value

    def z_first(i):
        @pl.when(is_outer == 1)
        def _():
            for k in range(3):
                z_copy(i, 2 - k).start()

    def z_second(i):
        @pl.when(is_outer == 0)
        def _():
            for k in (2, 1):
                z_wait(i, k)
                each_tile(i, (zi, fi, fo)[k], r0.at[k], True)
                z_copy(i, 2 + k).start()
            z_wait(i, 0)
            each_tile(i, zi, r0.at[0], True)

    def z_third(i):
        @pl.when(is_outer == 0)
        def _():
            z_wait(i, 4)
            each_tile(i, zo, r1.at[1], True)
            z_copy(i, 5).start()
            z_wait(i, 3)
            each_tile(i, zi, r1.at[0], False)

    def z_fourth(i):
        @pl.when(is_outer == 1)
        def _():
            z_wait(i, 5)
            each_tile(i, zo, r0.at[0], False)

    def write_out(i):
        start, size = sz.chunks[i]
        if i < 2:
            pairs = [(f_proj.at[:, pl.ds(start, size)], proj_out.at[:, pl.ds(start, size)])]
        elif i < 6:
            cut = pl.ds(start - C, size)
            pairs = [(f_inner.at[:, cut], inner_out.at[:, cut])]
        else:
            pairs = [(f_extra, extra_out)]
        copies = [pltpu.make_async_copy(a, b, o_s.at[i]) for a, b in pairs]
        for copy in copies:
            copy.start()
        return copies

    def settle_sums():
        for k in range(3):
            rcopy(yb.at[0], yb.at[0], quad_s.at[k], quad_r.at[0, k], sib).wait_send()
        rcopy(r0, r0, z_s, z_r.at[0, 0], partner).wait_send()

    def partial_sum(i, turned):
        at = cols_of(i)
        start, size = sz.chunks[i]
        rcopy(yb.at[1, :, at], yb.at[1, :, at], quad_s.at[0], quad_r.at[i, 0], sib).wait_recv()
        rcopy(yb.at[3, :, at], yb.at[3, :, at], quad_s.at[2], quad_r.at[i, 2], sib).wait_recv()
        n = 384 if size % 256 else 256

        def body(k, carry):
            at = pl.ds(pl.multiple_of(start + k * n, 128), n)
            part = dot_nn(turned[...], yb[:, :, at].reshape(4 * R, n))
            pb[:, :, at] = part.astype(BF).reshape(sz.nz, sz.share, n)
            return carry
        lax.fori_loop(0, size // n, body, 0)
        z_first(i)

    def remainder(gr, xr, xa, xs, mx, ng):
        def project(dst, base):
            def body(n, carry):
                at = pl.multiple_of(n * 256, 256)
                dst[:, pl.ds(at, 256)] = dot_nn(normed[...], win[:, pl.ds(pl.multiple_of(base + n * 256, 256), 256)])
                return carry
            lax.fori_loop(0, C // 256, body, 0)

        project(xr, C)
        project(gr, 0)

        unpack(1, q_bk, rc_ct, cts, 0)

        def lanes(p):
            return pl.ds(pl.multiple_of(p * 128, 128), 128)

        B = 64

        def head_line(v, p):
            first = iota((1, 128), 1) < 64
            spot = iota(v.shape, 1)
            return jnp.where(first, pick(v, spot, 2 * p), pick(v, spot, 2 * p + 1))

        def step_columns(p, lane):
            first = lane < 64
            return jnp.where(first, pick(dtv[...], lane, 2 * p), pick(dtv[...], lane, 2 * p + 1))

        acc1[...] = jnp.zeros_like(acc1)
        acc2[...] = jnp.zeros_like(acc2)

        def scan(p, carry):
            at = lanes(p)
            lane = iota((R, 128), 1)
            raw = xr[:, at]
            conv = bias_x[pl.ds(p, 1), :] + tap_x[0:1, at] * raw
            for tap in range(1, 4):
                conv = conv + tap_x[tap:tap + 1, at] * rows_down(raw, tap)
            sg = sigmoid(conv)
            act = conv * sg
            xa[:, at] = act
            xs[:, at] = (sg * (1.0 + conv * (1.0 - sg))).astype(BF)
            driven = act * step_columns(p, lane)
            parts = [jnp.where(lane < 64, driven, 0.0).astype(BF), jnp.where(lane >= 64, driven, 0.0).astype(BF)]
            cols = [pick(lac[...], lane, 2 * p + k) for k in range(2)]
            skip = head_line(skip_in[...], p)
            for b in range(R // B):
                reach = 128 * ((b * B) // 128 + 1)
                cut = slice(b * B, (b + 1) * B)
                causal = iota((B, reach), 0) + b * B >= iota((B, reach), 1)
                mixed = skip * act[cut]
                for k in range(2):
                    spread = cols[k][cut] - lar[pl.ds(2 * p + k, 1), :][:, :reach]
                    fading = jnp.exp(jnp.where(causal, spread, NEG))
                    mixing = (inter[cut, :reach] * fading).astype(BF)
                    mixed = mixed + dot_nn(mixing, parts[k][:reach])
                mx[cut, at] = mixed
                gate = gr[cut, at]
                gated = mixed * gate * sigmoid(gate)
                acc1[cut] += gated * gated
            return carry

        lax.fori_loop(0, NT_, scan, 0)

        whole = float(2 * C)

        def total_over_sides(i, value):
            stat_s[i] = jnp.transpose(jnp.where(lane == 0, jnp.sum(value, axis=1, keepdims=True), 0.0))[:8]
            return go(rcopy(stat_s.at[i], stat_r.at[i], y_s.at[i], y_r.at[i], g, o))

        def total_here(i):
            both = jnp.concatenate([stat_s[i] + stat_r[i], jnp.zeros((120, R), F32)], axis=0)
            return pick(jnp.transpose(both), lane, 0)

        squares = total_over_sides(0, acc1[...])
        unpack(1, q_bk, rc_ct, cts, 1)
        turn_quarter(xA, tA)
        settle(quarter_away)
        fold_half(t, 0)
        for rel, peer in ((2, xp), (3, diag)):
            go(fold_copy(rel - 1, peer % 4, 0, t, rel, peer, t))
        squares.wait_recv()
        gate_scale = lax.rsqrt(total_here(0) / whole + EPSILON)
        acc1[...] = jnp.broadcast_to(gate_scale, (R, 128))

        def gate_forward(p, carry):
            at = lanes(p)
            gate = gr[:, at]
            yb[0, :, at] = (mx[:, at] * (gate * sigmoid(gate)) * acc1[...] * gain_g[pl.ds(p, 1), :]).astype(BF)
            return carry
        lax.fori_loop(0, NT_, gate_forward, 0)
        quad_send(0)

        other_half(1, cts)
        for k in range(W // 128):
            v = cts[k // (H // 128), :, (k % (H // 128)) * 128:(k % (H // 128)) * 128 + 128].astype(F32)
            lowct[:, k * 128:(k + 1) * 128] = (v * live).astype(BF)
        fold_half(o, 1)
        xE[t, 0] = perm[q, :R // 2]
        xE[o, 0] = perm[q, R // 2:]
        go(fold_copy(0, sib % 4, 0, t, 1, sib, t))
        go(fold_copy(3, sib % 4, 1, o, 1, sib, t))
        quad_send(1)
        loads[3].wait()

        def out_half(side, dst, cast):
            def body(n, carry):
                at = pl.ds(pl.multiple_of(side * H + n * 256, 256), 256)
                dst[:, pl.ds(pl.multiple_of(n * 256, 256), 256)] = dot_nn(yb[0, :, :C], wout[:, at]).astype(cast)
                return carry
            lax.fori_loop(0, H // 256, body, 0)

        def back_project(n, carry):
            at = pl.ds(pl.multiple_of(n * 256, 256), 256)
            ng[:, at] = dot_nt(lowct[...], wout[at, :])
            for k in range(2):
                here = pl.ds(pl.multiple_of(n * 256 + k * 128, 128), 128)
                gate = gr[:, here]
                acc2[...] += mx[:, here] * (gate * sigmoid(gate)) * (gain_g[pl.ds(2 * n + k, 1), :] * ng[:, here])
            return carry
        lax.fori_loop(0, C // 256, back_project, 0)
        crossed = total_over_sides(1, acc2[...])
        for rel in (2, 3):
            fold_copy(rel - 1, 0, 0, t, rel, xp, t).wait_recv()
            go(fold_pass(rel, t))
        out_half(o, half_s, BF)
        branch_away = rcopy(half_s, half_r, y_s.at[2], y_r.at[2], g, o)
        branch_away.start()
        crossed.wait_recv()
        acc2[...] = acc1[...] * acc1[...] * acc1[...] * (total_here(1) / whole)

        def gate_back(p, carry):
            at = lanes(p)
            gate, mixed, grad = gr[:, at], mx[:, at], ng[:, at]
            sg = sigmoid(gate)
            act = gate * sg
            gated = mixed * act
            gated_grad = acc1[...] * (gain_g[pl.ds(p, 1), :] * grad) - gated * acc2[...]
            sms[0, 5:6, at] = jnp.sum(grad * gated * acc1[...], axis=0, keepdims=True)
            mixed_grad = gated_grad * act
            ng[:, at] = mixed_grad
            sms[0, 6:7, at] = jnp.sum(mixed_grad * xa[:, at], axis=0, keepdims=True)
            yb[0, :, pl.ds(pl.multiple_of(C + p * 128, 128), 128)] = (
                gated_grad * mixed * (sg * (1.0 + gate * (1.0 - sg)))).astype(BF)
            return carry
        lax.fori_loop(0, NT_, gate_back, 0)
        quad_send(2)
        quad_send(3)
        out_half(t, gr, F32)
        quad_pass(0)
        turn_folds()
        partial_sum(0, tE)

        inter[...] = dot_nt(written, readout)
        igrad[...] = jnp.zeros_like(igrad)
        sgr[...] = jnp.zeros_like(sgr)
        rgr[...] = jnp.zeros_like(rgr)
        ptile[...] = jnp.zeros_like(ptile)

        def scan_back(p, carry):
            at = lanes(p)
            lane = iota((R, 128), 1)
            grad = ng[:, at]
            act = xa[:, at]
            stepw = step_columns(p, lane)
            driven = (act * stepw).astype(BF)
            parts = [jnp.where(lane < 64, grad, 0.0).astype(BF), jnp.where(lane >= 64, grad, 0.0).astype(BF)]
            cols = [pick(lac[...], lane, 2 * p + k) for k in range(2)]
            pieces = []
            for b in range(R // B):
                skip = 128 * ((b * B) // 128)
                cut = slice(b * B, (b + 1) * B)
                causal = iota((B, R - skip), 1) + skip >= iota((B, R - skip), 0) + b * B
                turned = inter[cut, skip:]
                piece = jnp.zeros((B, 128), F32)
                total = igrad[cut, skip:]
                for k in range(2):
                    spread = lar[pl.ds(2 * p + k, 1), :][:, skip:] - cols[k][cut]
                    fading = jnp.exp(jnp.where(causal, spread, NEG))
                    faded = dot_nt(driven[cut], parts[k][skip:]) * fading
                    total = total + faded
                    piece = piece + dot_nn((turned * fading).astype(BF), parts[k][skip:])
                    ptile[k, cut, skip:] = (faded * turned).astype(BF)
                igrad[cut, skip:] = total
                pieces.append(piece)
            strict = one_hot(iota((R, R), 0) > iota((R, R), 1))
            for k in range(2):
                found = []
                for b in range(R // B):
                    skip = 128 * ((b * B) // 128)
                    cut = slice(b * B, (b + 1) * B)
                    causal = iota((B, R - skip), 1) + skip >= iota((B, R - skip), 0) + b * B
                    sums = dot_nn(strict[cut], ptile[k, :, skip:])
                    found.append(jnp.sum(jnp.where(causal, sums, 0.0), axis=1, keepdims=True))
                rgr[...] = jnp.where(lane == 2 * p + k, jnp.concatenate(found, axis=0), rgr[...])
            driven_grad = jnp.concatenate(pieces, axis=0)
            pulled = driven_grad * act
            low = jnp.sum(jnp.where(lane < 64, pulled, 0.0), axis=1, keepdims=True)
            high = jnp.sum(jnp.where(lane >= 64, pulled, 0.0), axis=1, keepdims=True)
            sgr[...] = jnp.where(lane == 2 * p, low, jnp.where(lane == 2 * p + 1, high, sgr[...]))
            conv_grad = (head_line(skip_in[...], p) * grad + stepw * driven_grad) * xs[:, at].astype(F32)
            raw = xr[:, at]
            raw_grad = tap_x[0:1, at] * conv_grad
            sms[0, 0:1, at] = jnp.sum(conv_grad * raw, axis=0, keepdims=True)
            sms[0, 4:5, at] = jnp.sum(conv_grad, axis=0, keepdims=True)
            for tap in range(1, 4):
                up = rows_up(conv_grad, tap)
                raw_grad = raw_grad + tap_x[tap:tap + 1, at] * up
                sms[0, tap:tap + 1, at] = jnp.sum(up * raw, axis=0, keepdims=True)
            yb[0, :, pl.ds(pl.multiple_of(2 * C + p * 128, 128), 128)] = raw_grad.astype(BF)
            return carry

        lax.fori_loop(0, NT_ // 2, scan_back, 0)
        quad_send(4)

        rcopy(half_r, half_r, y_s.at[2], y_r.at[2], g, o).wait_recv()

        pieces = []
        mine = hid[pl.ds(t, 1)][0]
        for k in range(H // 128):
            cut = slice(k * 128, (k + 1) * 128)
            branch = gr[:, cut] + half_r[:, cut].astype(F32)
            pieces.append((mine[:, cut].astype(F32) + live * branch).astype(BF))
        settle(rows_away)
        reply(4, q_bk, jnp.concatenate(pieces, axis=1), pk_in, gn_o)
        reply_send(4, pk_in, gn_o, True)

        quad_pass(1)
        lax.fori_loop(NT_ // 2, NT_, scan_back, 0)
        quad_send(5)

        ig = igrad[...].astype(BF)
        st_s[:, :S] = dot_nn(ig, wr[:, S:]).astype(BF)
        st_s[:, S:] = dot_tn(ig, wr[:, :S]).astype(BF)
        go(rcopy(st_s, st_r, y_s.at[3], y_r.at[3], g, o))
        step_grad = (sgr[...] + rgr[...] * rate) * stepsig[...]
        yb[0, :, 3 * C + 2 * S:] = step_grad.astype(BF)
        sms[0, 7:8, 10 * S:10 * S + 128] = jnp.sum(step_grad, axis=0, keepdims=True)
        sms[0, 7:8, 10 * S + 128:10 * S + 256] = jnp.sum(rgr[...] * dtv[...], axis=0, keepdims=True) * rate
        partial_sum(1, tE)
        z_second(0)
        rcopy(st_r, st_r, y_s.at[3], y_r.at[3], g, o).wait_recv()
        for k in range(2):
            cut = slice(k * S, (k + 1) * S)
            conv_grad = (st_s[:, cut].astype(F32) + st_r[:, cut].astype(F32)) * sslope[:, cut]
            raw = sraw[:, cut]
            raw_grad = tap_s[0:1, cut] * conv_grad
            sms[0, 7:8, cut] = jnp.sum(conv_grad * raw, axis=0, keepdims=True)
            sms[0, 7:8, 8 * S + k * S:8 * S + (k + 1) * S] = jnp.sum(conv_grad, axis=0, keepdims=True)
            for tap in range(1, 4):
                up = rows_up(conv_grad, tap)
                raw_grad = raw_grad + tap_s[tap:tap + 1, cut] * up
                sms[0, 7:8, tap * 2 * S + k * S:tap * 2 * S + (k + 1) * S] = jnp.sum(up * raw, axis=0, keepdims=True)
            yb[0, :, 3 * C + k * S:3 * C + (k + 1) * S] = raw_grad.astype(BF)
        quad_send(6)
        reply_send(4, pk_in, gn_o, False)

        hops = [2 ** k for k in range(2, dp.bit_length() - 1)] + [1, 2]

        def small_start(i):
            bit = (g // hops[i]) % 2
            go(rcopy(sms.at[i], smr.at[i], sm_s.at[i], sm_r.at[i], g + (1 - 2 * bit) * hops[i]))

        def small_end(i):
            bit = (g // hops[i]) % 2
            rcopy(sms.at[i], smr.at[i], sm_s.at[i], sm_r.at[i], g + (1 - 2 * bit) * hops[i]).wait_recv()
            if i + 1 < len(hops):
                sms[i + 1] = sms[i] + smr[i]
                small_start(i + 1)
            else:
                smr[0] = sms[i] + smr[i]
        small_start(0)

        acc1[...] = jnp.zeros_like(acc1)

        def normed_grad(side, dst, cast):
            def body(n, carry):
                at = pl.ds(pl.multiple_of(side * H + n * 256, 256), 256)
                value = dot_nt(yb[0, :, C:3 * C], win[at, :])
                mine_state = pl.ds(pl.multiple_of(t * S, 128), S)
                value = value + dot_nt(yb[0, :, pl.ds(pl.multiple_of(3 * C + t * S, 128), S)], wst[at, mine_state])
                value = value + dot_nn(yb[0, :, 3 * C + 2 * S:], wstep[:, at])
                for k in range(2):
                    cut = slice(k * 128, (k + 1) * 128)
                    here = pl.ds(pl.multiple_of(n * 256 + k * 128, 128), 128)
                    there = pl.ds(pl.multiple_of(side * H + n * 256 + k * 128, 128), 128)
                    acc1[...] += hid[pl.ds(side, 1), :, here][0].astype(F32) * (gain_n[pl.ds(side * (H // 128) + 2 * n + k, 1), :] * value[:, cut])
                dst[:, pl.ds(pl.multiple_of(n * 256, 256), 256)] = value.astype(cast)
                return carry
            lax.fori_loop(0, H // 256, body, 0)
        branch_away.wait_send()
        normed_grad(o, half_s, BF)
        go(rcopy(half_s, half_r, y_s.at[4], y_r.at[4], g, o))
        normed_grad(t, gr, F32)
        summed_rows = total_over_sides(2, acc1[...])
        relay(4, back, rc_ct, gn_o)
        relay_send(4, rc_ct, gn_o, True)
        relay_send(4, rc_ct, gn_o, False)
        quad_pass(2)
        partial_sum(2, tA)

        rcopy(half_r, half_r, y_s.at[4], y_r.at[4], g, o).wait_recv()
        summed_rows.wait_recv()
        pull = total_here(2) / W * (scale[...] * scale[...] * scale[...])
        pieces = []
        mine = hid[pl.ds(t, 1)][0]
        mine_ct = cts[pl.ds(t, 1)][0]
        gall[pl.ds(g, 1)] = jnp.zeros((1, 8, 128), F32)
        for k in range(H // 128):
            cut = slice(k * 128, (k + 1) * 128)
            there = pl.ds(pl.multiple_of(t * H + k * 128, 128), 128)
            value = gr[:, cut] + half_r[:, cut].astype(F32)
            rows_here = mine[:, cut].astype(F32)
            gall[pl.ds(g, 1), k:k + 1, :] = jnp.sum(value * rows_here * scale[...], axis=0, keepdims=True)[None]
            pieces.append((scale[...] * (gain_n[pl.ds(t * (H // 128) + k, 1), :] * value) - rows_here * pull
                           + mine_ct[:, cut].astype(F32)).astype(BF))
        settle(grads_away)
        reply(5, q_in, jnp.concatenate(pieces, axis=1), pk_ct, gn_g)
        reply_send(5, pk_ct, gn_g, True)
        reply_send(5, pk_ct, gn_g, False)
        for peer in far:
            rcopy(gall.at[g], gall.at[g], gg_s, gg_r, peer).start()

        small_end(0)
        z_second(1)
        quad_pass(3)
        partial_sum(3, tA)
        z_second(2)
        z_third(0)
        relay(5, dest, rc_in, gn_g)
        relay_send(5, rc_in, gn_g, True)
        relay_send(5, rc_in, gn_g, False)
        quad_pass(4)
        partial_sum(4, tA)
        z_third(1)
        quad_pass(5)
        partial_sum(5, tA)
        z_third(2)
        z_second(3)
        quad_pass(6)
        partial_sum(6, tA)
        small_end(1)
        z_second(4)
        small_end(2)
        z_third(3)
        z_second(5)

        def give(i, value, dst):
            lowct[:, i * H:(i + 1) * H] = value.astype(BF)
            store = pltpu.make_async_copy(lowct.at[:, pl.ds(i * H, H)], dst, w_s.at[i])
            store.start()
            return store

        replied(4, gn_o)

        @pl.when(is_outer == 1)
        def _():
            raw_copy(4).wait_send()
            raw_copy(5).wait_send()
        stores = [give(0, dot_tn(p_own[...], gn_o[...].reshape(sz.slots, H)), out_rows)]
        p_own[...] = send_table(dest, g, sz)
        for i in range(4):
            z_fourth(i)
            stores += write_out(i)
        small_end(3)
        stores.append(pltpu.make_async_copy(smr.at[0], small_out, o_s.at[7]))
        stores[-1].start()
        span(gall, dp - 1, gg_s, gg_r).wait_recv()
        sent.append(span(gall, dp - 1, gg_s, gg_r))
        summed = gall[0]
        for d in range(1, dp):
            summed = summed + gall[d]
        gsum[pl.ds(t, 1)] = summed[None]
        go(rcopy(gsum.at[t], gsum.at[t], y_s.at[5], y_r.at[5], g, o))
        replied(5, gn_g)
        stores.append(give(1, dot_tn(p_own[...], gn_g[...].reshape(sz.slots, H)), out_grads))
        z_second(6)
        z_third(4)
        z_fourth(4)
        stores += write_out(4)
        z_third(5)
        z_fourth(5)
        stores += write_out(5)
        z_third(6)
        z_fourth(6)
        stores += write_out(6)
        rcopy(gsum.at[o], gsum.at[o], y_s.at[5], y_r.at[5], g, o).wait_recv()
        stores.append(pltpu.make_async_copy(gsum, gain_out, o_s.at[8]))
        stores[-1].start()
        for copy in sent:
            copy.wait_send()
        settle_sums()
        reply_settle(4, pk_in)
        reply_settle(5, pk_ct)
        for store in stores:
            store.wait()

    big = pltpu.VMEM((R, C), F32)
    pl.run_scoped(remainder, big, big, big, pltpu.VMEM((R, C), BF), big, big)


def finish_kernel(sz, rows, grads, inner, proj, extra, small, gain, o_rows, o_grads, o_gain, o_inner, o_state, o_step,
                  o_tap_x, o_bias_x, o_tap_s, o_bias_s, o_bias_step, o_rate, o_skip, o_gate, o_proj):
    C, S = sz.inner, sz.state
    o_rows[...] = rows[...]
    o_grads[...] = grads[...]
    o_inner[:, 0, :] = inner[:, :C]
    o_inner[:, 1, :] = inner[:, C:]
    o_proj[...] = proj[...]
    o_state[...] = extra[:, :2 * S]
    o_step[...] = jnp.transpose(extra[:, 2 * S:])[:sz.heads]
    o_tap_x[...] = small[0:4, :]
    o_bias_x[...] = small[4, :]
    o_gate[...] = small[5, :]
    for k in range(4):
        o_tap_s[k:k + 1, :] = small[7:8, k * 2 * S:(k + 1) * 2 * S]
    o_bias_s[...] = small[7, 8 * S:10 * S]
    o_bias_step[...] = small[7, 10 * S:10 * S + sz.heads]
    o_rate[...] = small[7, 10 * S + 128:10 * S + 128 + sz.heads]
    shape = (C, sz.heads)
    member = one_hot(iota(shape, 0) // (C // sz.heads) == iota(shape, 1))
    skip = jnp.broadcast_to(small[6:7, :], (8, C))
    o_skip[...] = sum(dot_nn(part, member) for part in split3(skip))[0]
    flat = jnp.concatenate([gain[h, k:k + 1, :] for h in range(2) for k in range(sz.half // 128)], axis=1)
    start = lax.axis_index("dp") * sz.share
    moved = pltpu.roll(jnp.broadcast_to(flat, (8, sz.width)), lax.rem(sz.width - start, sz.width), 1)
    o_gain[...] = moved[0, :sz.share]


def fused(sz, block_in, cotangent, lengths, dest_slot, return_slot, norm_gain, inner_weight, state_weight,
          step_weight, conv_inner, conv_inner_bias, conv_state, conv_state_bias, step_bias, log_rate,
          skip_gain, gate_gain, out_weight):
    dp, R, H, C, S = sz.dp, sz.rows, sz.half, sz.inner, sz.state
    W = sz.width

    vm = pl.BlockSpec(memory_space=pltpu.VMEM)
    hb = pl.BlockSpec(memory_space=pl.ANY)
    sm = pl.BlockSpec(memory_space=pltpu.SMEM)
    V = pltpu.VMEM
    packed = V((dp, sz.cap, H), BF)
    D = pltpu.SemaphoreType.DMA
    nch = len(sz.chunks)
    scratch = [
        V((W, 2 * C), BF), V((C, W), BF), V((W, 2 * S), BF), V((128, W), BF), V((8, 128), F32),
        *[packed] * 6,
        V((sz.slots, R), BF), V((R, sz.slots), BF), V((R, sz.slots), BF),
        V((2, R, H), BF), V((2, R, H), BF), V((R, W), BF), V((R, W), BF),
        V((4, R, sz.quarter), BF), V((4, R, sz.quarter), BF), V((2, 4, R // 2, sz.quarter), BF),
        V((sz.quarter, 4 * R), BF), V((sz.quarter, 4 * R), BF),
        V((4, R, sz.cols), BF), V((sz.nz, sz.share, sz.cols), BF), V((3, sz.share, sz.cols), BF), V((2, sz.share, sz.cols), BF),
        V((sz.share, 2 * C), F32), V((sz.share, C), F32), V((sz.share, sz.extra), F32),
        V((R, R), F32), V((R, R), F32), V((2, R, R), BF),
        V((R, 2 * S), F32), V((R, 2 * S), F32), V((R, 2 * S), BF), V((R, 128), F32), V((R, 128), F32), V((128, R), F32),
        V((R, 128), F32), V((R, 128), F32), V((R, 128), F32), V((R, 128), F32), V((R, 128), F32), V((R, 128), F32),
        V((3, 8, R), F32), V((3, 8, R), F32), V((R, H), BF), V((R, H), BF), V((R, H), BF),
        V((R, 2 * S), BF), V((R, 2 * S), BF),
        V((4, 8, C), F32), V((4, 8, C), F32), V((dp, 8, 128), F32), V((2, 8, 128), F32),
        D((6,)), D((6,)), D((2, 2)), D((2, 2)), D((3,)), D((nch, 3)), D((2, 6)), D((2, 6)),
        D, D((nch, 6)), D((6,)), D((6,)), D, D, D((4,)), D((4,)), D((4,)), D((2,)), D((2,)), D((2, 2)), D((9,)),
        pltpu.SemaphoreType.REGULAR,
    ]
    out = jax.ShapeDtypeStruct
    rows_out, grads_out, inner_g, proj_g, extra_g, small, gain = pl.pallas_call(
        functools.partial(block_kernel, sz),
        out_shape=(out((R, H), BF), out((R, H), BF), out((sz.share, 2 * C), F32), out((sz.share, C), F32),
                   out((sz.share, sz.extra), F32), out((8, C), F32), out((2, 8, 128), F32)),
        in_specs=[vm, vm, sm, hb, hb, hb, hb, hb] + [vm] * 10,
        out_specs=(hb,) * 7,
        scratch_shapes=scratch,
        compiler_params=pltpu.CompilerParams(collective_id=0, has_side_effects=True, vmem_limit_bytes=66000000),
        name="block",
    )(dest_slot.reshape(-1, 128), return_slot.reshape(-1, 128), lengths, block_in, cotangent, inner_weight, out_weight,
      state_weight, step_weight.T, conv_inner, conv_inner_bias.reshape(-1, 128), gate_gain.reshape(-1, 128), norm_gain.reshape(-1, 128), skip_gain[None],
      conv_state, conv_state_bias[None], step_bias[None], log_rate[None])
    results = pl.pallas_call(
        functools.partial(finish_kernel, sz),
        out_shape=(out((R, H), BF), out((R, H), BF), out((sz.share,), F32), out((sz.share, 2, C), F32),
                   out((sz.share, 2 * S), F32), out((sz.heads, sz.share), F32), out((4, C), F32), out((C,), F32),
                   out((4, 2 * S), F32), out((2 * S,), F32), out((sz.heads,), F32), out((sz.heads,), F32),
                   out((sz.heads,), F32), out((C,), F32), out((sz.share, C), F32)),
        in_specs=[vm] * 7,
        out_specs=(vm,) * 15,
        name="finish",
    )(rows_out, grads_out, inner_g, proj_g, extra_g, small, gain)
    return results[:5] + (results[5].T,) + results[6:14] + (results[14].T,)


def with_collectives(
    block_in,
    cotangent,
    lengths,
    dest_slot,
    return_slot,
    norm_gain,
    inner_weight,
    state_weight,
    step_weight,
    conv_inner,
    conv_inner_bias,
    conv_state,
    conv_state_bias,
    step_bias,
    log_rate,
    skip_gain,
    gate_gain,
    out_weight,
):
    groups = lax.axis_size("dp")
    group_rows = block_in.shape[0]
    half_width = block_in.shape[1]
    capacity = 2 * group_rows // groups
    own_group = lax.axis_index("dp")
    own_dest = lax.dynamic_slice_in_dim(dest_slot, own_group * group_rows, group_rows)
    own_return = lax.dynamic_slice_in_dim(return_slot, own_group * group_rows, group_rows)
    send_spot = send_layout(own_dest, group_rows, capacity, groups)
    back_spot = send_layout(own_return, group_rows, capacity, groups)
    slots_in = arrivals(dest_slot, group_rows, capacity, groups, own_group)
    slots_back = arrivals(return_slot, group_rows, capacity, groups, own_group)
    blank_rows = jnp.zeros((groups * capacity, half_width), jnp.bfloat16)
    packed_rows = blank_rows.at[send_spot].set(block_in).reshape(groups, capacity, half_width)
    packed_grads = blank_rows.at[back_spot].set(cotangent).reshape(groups, capacity, half_width)
    came_rows, came_grads = (
        lax.all_to_all(packed_rows, "dp", split_axis=0, concat_axis=0, tiled=True),
        lax.all_to_all(packed_grads, "dp", split_axis=0, concat_axis=0, tiled=True),
    )
    empty_rows = jnp.zeros((group_rows, half_width), jnp.bfloat16)
    own_rows = empty_rows.at[slots_in].set(came_rows.reshape(-1, half_width), mode="drop")
    own_grads = empty_rows.at[slots_back].set(came_grads.reshape(-1, half_width), mode="drop")
    full_rows, full_grads = (
        lax.all_gather(own_rows, "tensor", axis=1, tiled=True),
        lax.all_gather(own_grads, "tensor", axis=1, tiled=True),
    )
    seq_pos, live_mask, keep_state = stretch_layout(lengths[0], STRETCH)
    live_col = live_mask[:, None]
    hidden = full_rows.astype(jnp.float32)
    norm_scale = lax.rsqrt(jnp.mean(hidden * hidden, axis=1, keepdims=True) + EPSILON)
    normed = (hidden * norm_scale * norm_gain).astype(jnp.bfloat16)
    inner_local = inner_weight.shape[2]
    zx_weight = inner_weight.reshape(inner_weight.shape[0], 2 * inner_local)
    projected = jnp.dot(normed, zx_weight, preferred_element_type=jnp.float32)
    gate_raw = projected[:, :inner_local]
    conv_in_x = projected[:, inner_local:]
    conv_in_state = jnp.dot(normed, state_weight, preferred_element_type=jnp.float32)
    step_raw = jnp.dot(normed, step_weight, preferred_element_type=jnp.float32)
    x_conv = conv_forward(conv_in_x, conv_inner, conv_inner_bias, seq_pos)
    state_conv = conv_forward(conv_in_state, conv_state, conv_state_bias, seq_pos)
    x_act = jax.nn.silu(x_conv)
    state_act = jax.nn.silu(state_conv)
    state_width = state_act.shape[1] // 2
    heads_local = step_weight.shape[1]
    head_dim = inner_local // heads_local
    stretches = group_rows // STRETCH
    step_input = step_raw + step_bias[None, :]
    step_size = jax.nn.softplus(step_input) * live_col
    decay_rate = -jnp.exp(log_rate)
    skip_wide = jnp.repeat(skip_gain, head_dim)[None, :]
    scanned, saved = state_forward(
        x_act.reshape(group_rows, heads_local, head_dim),
        state_act[:, :state_width],
        state_act[:, state_width:],
        step_size,
        decay_rate,
        STRETCH,
    )
    mixed = scanned + skip_wide * x_act
    gate_act = jax.nn.silu(gate_raw)
    gated = mixed * gate_act
    inner_total = inner_local * lax.axis_size("tensor")
    square_sum = lax.psum(jnp.sum(gated * gated, axis=1), "tensor")
    gate_scale = lax.rsqrt(square_sum / inner_total + EPSILON)[:, None]
    gate_normed = (gated * gate_scale * gate_gain).astype(jnp.bfloat16)
    partial_out = jnp.dot(gate_normed, out_weight, preferred_element_type=jnp.float32)
    branch_half = lax.psum_scatter(partial_out, "tensor", scatter_dimension=1, tiled=True)
    half_index = lax.axis_index("tensor")
    out_half = (own_rows.astype(jnp.float32) + live_col * branch_half).astype(jnp.bfloat16)
    zero_row = jnp.zeros((1, half_width), jnp.bfloat16)
    reply_rows = jnp.concatenate([out_half, zero_row], axis=0)[slots_back]
    returned = lax.all_to_all(
        reply_rows.reshape(groups, capacity, half_width),
        "dp",
        split_axis=0,
        concat_axis=0,
        tiled=True,
    )
    block_out = returned.reshape(-1, half_width)[back_spot]
    owner_ct = full_grads.astype(jnp.float32)
    out_grad = (owner_ct * live_col).astype(jnp.bfloat16)
    out_weight_grad = jnp.einsum(
        "ti,td->id", gate_normed, out_grad, preferred_element_type=jnp.float32
    )
    normed_out_grad = jnp.einsum(
        "td,id->ti", out_grad, out_weight, preferred_element_type=jnp.float32
    )
    gate_gain_grad = jnp.sum(normed_out_grad * gated * gate_scale, axis=0)
    scaled_grad = gate_gain * normed_out_grad
    cross = lax.psum(jnp.sum(gated * scaled_grad, axis=1), "tensor")[:, None]
    gated_grad = gate_scale * scaled_grad - gated * gate_scale**3 * cross / inner_total
    mixed_grad = gated_grad * gate_act
    gate_raw_grad = gated_grad * mixed * silu_slope(gate_raw)
    skip_gain_grad = jnp.sum(
        (mixed_grad * x_act).reshape(group_rows, heads_local, head_dim), axis=(0, 2)
    )
    x_state_grad, written_grad, readout_grad, step_grad, rate_total = state_backward(
        saved, mixed_grad.reshape(stretches, STRETCH, heads_local, head_dim), decay_rate
    )
    x_act_grad = x_state_grad.reshape(group_rows, inner_local) + skip_wide * mixed_grad
    state_grad = lax.psum(
        jnp.concatenate(
            [written_grad.reshape(group_rows, -1), readout_grad.reshape(group_rows, -1)], axis=1
        ),
        "tensor",
    )
    state_conv_grad = state_grad * silu_slope(state_conv)
    x_conv_grad = x_act_grad * silu_slope(x_conv)
    state_raw_grad, conv_state_grad, conv_state_bias_grad = conv_backward(
        conv_in_state, conv_state, seq_pos, state_conv_grad
    )
    x_raw_grad, conv_inner_grad, conv_inner_bias_grad = conv_backward(
        conv_in_x, conv_inner, seq_pos, x_conv_grad
    )
    step_raw_grad = (
        step_grad.reshape(group_rows, heads_local) * live_col * jax.nn.sigmoid(step_input)
    )
    step_bias_grad = jnp.sum(step_raw_grad, axis=0)
    log_rate_grad = rate_total * decay_rate
    zx_low = jnp.concatenate([gate_raw_grad, x_raw_grad], axis=1).astype(jnp.bfloat16)
    state_low = state_raw_grad.astype(jnp.bfloat16)
    step_low = step_raw_grad.astype(jnp.bfloat16)
    inner_weight_grad = jnp.einsum(
        "td,tk->dk", normed, zx_low, preferred_element_type=jnp.float32
    )
    state_weight_grad = jnp.einsum(
        "td,tk->dk", normed, state_low, preferred_element_type=jnp.float32
    )
    step_weight_grad = jnp.einsum("td,tk->dk", normed, step_low, preferred_element_type=jnp.float32)
    lead_share = (half_index == 0).astype(jnp.float32)
    normed_grad = jnp.einsum("tk,dk->td", zx_low, zx_weight, preferred_element_type=jnp.float32)
    normed_grad = normed_grad + jnp.einsum(
        "tk,dk->td", step_low, step_weight, preferred_element_type=jnp.float32
    )
    normed_grad = normed_grad + lead_share * jnp.einsum(
        "tk,dk->td", state_low, state_weight, preferred_element_type=jnp.float32
    )
    normed_grad = lax.psum(normed_grad, "tensor")
    norm_gain_grad = jnp.sum(normed_grad * hidden * norm_scale, axis=0)
    input_scaled = norm_gain * normed_grad
    hidden_grad = (
        norm_scale * input_scaled
        - hidden * norm_scale**3 * jnp.mean(hidden * input_scaled, axis=1, keepdims=True)
        + owner_ct
    )
    own_grad = lax.dynamic_slice_in_dim(hidden_grad, half_index * half_width, half_width, 1).astype(
        jnp.bfloat16
    )
    answer_rows = jnp.concatenate([own_grad, zero_row], axis=0)[slots_in]
    gone = lax.all_to_all(
        answer_rows.reshape(groups, capacity, half_width),
        "dp",
        split_axis=0,
        concat_axis=0,
        tiled=True,
    )
    input_grad = gone.reshape(-1, half_width)[send_spot]
    (
        conv_inner_grad,
        conv_inner_bias_grad,
        conv_state_grad,
        conv_state_bias_grad,
        step_bias_grad,
        log_rate_grad,
        skip_gain_grad,
        gate_gain_grad,
    ) = lax.psum(
        (
            conv_inner_grad,
            conv_inner_bias_grad,
            conv_state_grad,
            conv_state_bias_grad,
            step_bias_grad,
            log_rate_grad,
            skip_gain_grad,
            gate_gain_grad,
        ),
        "dp",
    )
    zx_share, state_share, step_share, gain_share, out_share = (
        lax.psum_scatter(inner_weight_grad.astype(jnp.bfloat16), "dp", scatter_dimension=0, tiled=True),
        lax.psum_scatter(state_weight_grad, "dp", scatter_dimension=0, tiled=True),
        lax.psum_scatter(step_weight_grad, "dp", scatter_dimension=0, tiled=True),
        lax.psum_scatter(norm_gain_grad, "dp", scatter_dimension=0, tiled=True),
        lax.psum_scatter(out_weight_grad.astype(jnp.bfloat16), "dp", scatter_dimension=1, tiled=True),
    )
    zx_share = zx_share.astype(jnp.float32).reshape((-1,) + inner_weight.shape[1:])
    out_share = out_share.astype(jnp.float32)
    return (
        block_out,
        input_grad,
        gain_share,
        zx_share,
        state_share,
        step_share,
        conv_inner_grad,
        conv_inner_bias_grad,
        conv_state_grad,
        conv_state_bias_grad,
        step_bias_grad,
        log_rate_grad,
        skip_gain_grad,
        gate_gain_grad,
        out_share,
    )


def on_device(*args):
    groups = lax.axis_size("dp")
    rows, half = args[0].shape
    inner, heads, state = args[6].shape[2], args[8].shape[1], args[7].shape[1] // 2
    capacity = 2 * rows // groups
    fits = (
        groups == 16 and capacity % 16 == 0 and (2 * half // groups) % 16 == 0
        and rows == STRETCH and args[2].shape[1] == 1 and inner == 64 * heads and inner == 2 * half
    )
    if fits:
        return fused(Sizes(groups, rows, half, inner, heads, state, capacity), *args)
    return with_collectives(*args)


def solution(mesh):
    placed = (
        P("dp", "tensor"),
        P("dp", "tensor"),
        P("dp", None),
        P(),
        P(),
        P(),
        P(None, None, "tensor"),
        P(),
        P(None, "tensor"),
        P(None, "tensor"),
        P("tensor"),
        P(),
        P(),
        P("tensor"),
        P("tensor"),
        P("tensor"),
        P("tensor"),
        P("tensor", None),
    )
    return jax.shard_map(
        on_device,
        mesh=mesh,
        in_specs=placed,
        out_specs=(
            P("dp", "tensor"),
            P("dp", "tensor"),
            P("dp"),
            P("dp", None, "tensor"),
            P("dp", None),
            P("dp", "tensor"),
            P(None, "tensor"),
            P("tensor"),
            P(),
            P(),
            P("tensor"),
            P("tensor"),
            P("tensor"),
            P("tensor"),
            P("tensor", "dp"),
        ),
        check_vma=False,
    )
```

```python
import functools

import jax
import jax.numpy as jnp
from jax import lax
from jax.experimental import pallas as pl
from jax.experimental.pallas import tpu as pltpu
from jax.sharding import PartitionSpec as P

STRETCH = 256


PRECISE = lax.Precision.HIGHEST
EPSILON = 1e-05


def silu_slope(values):
    logistic = jax.nn.sigmoid(values)
    return logistic * (1.0 + values * (1.0 - logistic))


def stretch_layout(seq_lengths, stretch_rows):
    total_stretches = seq_lengths.shape[0]
    numbers = jnp.arange(total_stretches, dtype=jnp.int32)
    begins = seq_lengths > 0
    first_stretch = jnp.max(
        jnp.where(begins[None, :] & (numbers[None, :] <= numbers[:, None]), numbers[None, :], 0),
        axis=1,
    )
    seq_length = jnp.sum(
        jnp.where(numbers[None, :] == first_stretch[:, None], seq_lengths[None, :], 0), axis=1
    )
    within = (
        jnp.arange(stretch_rows, dtype=jnp.int32)[None, :]
        + ((numbers - first_stretch) * stretch_rows)[:, None]
    )
    live_mask = (within < seq_length[:, None]).astype(jnp.float32).reshape(-1)
    keep_state = 1.0 - begins.astype(jnp.float32)
    return (within.reshape(-1), live_mask, keep_state)


def shift_down(values, steps):
    return jnp.concatenate(
        [jnp.zeros((steps,) + values.shape[1:], values.dtype), values[:-steps]], axis=0
    )


def shift_up(values, steps):
    return jnp.concatenate(
        [values[steps:], jnp.zeros((steps,) + values.shape[1:], values.dtype)], axis=0
    )


def conv_forward(raw_in, tap_weights, tap_bias, seq_pos):
    total = tap_bias[None, :] + tap_weights[0][None, :] * raw_in
    for tap_index in range(1, tap_weights.shape[0]):
        valid = (seq_pos >= tap_index).astype(jnp.float32)[:, None]
        total = total + tap_weights[tap_index][None, :] * shift_down(raw_in, tap_index) * valid
    return total


def conv_backward(raw_in, tap_weights, seq_pos, conv_grad):
    tap_grads = [jnp.sum(conv_grad * raw_in, axis=0)]
    raw_grad = tap_weights[0][None, :] * conv_grad
    for tap_index in range(1, tap_weights.shape[0]):
        masked = conv_grad * (seq_pos >= tap_index).astype(jnp.float32)[:, None]
        tap_grads.append(jnp.sum(masked * shift_down(raw_in, tap_index), axis=0))
        raw_grad = raw_grad + tap_weights[tap_index][None, :] * shift_up(masked, tap_index)
    return (raw_grad, jnp.stack(tap_grads, axis=0), jnp.sum(conv_grad, axis=0))


def send_layout(targets, group_rows, capacity, groups):
    owner_group = targets // group_rows
    onehot = (owner_group[:, None] == jnp.arange(groups, dtype=jnp.int32)[None, :]).astype(
        jnp.int32
    )
    arrival = jnp.sum(jnp.cumsum(onehot, axis=0) * onehot, axis=1) - 1
    return owner_group * capacity + arrival


def arrivals(targets, group_rows, capacity, groups, own_group):
    by_source = targets.reshape(groups, group_rows)
    owner_group = by_source // group_rows
    is_mine = (owner_group == own_group).astype(jnp.int32)
    arrival = jnp.cumsum(is_mine, axis=1) - 1
    position = jnp.arange(groups, dtype=jnp.int32)[:, None] * capacity + arrival
    position = jnp.where(is_mine > 0, position, groups * capacity)
    filler = jnp.full((groups * capacity,), group_rows, jnp.int32)
    return filler.at[position.reshape(-1)].set(
        (by_source - owner_group * group_rows).reshape(-1), mode="drop"
    )


def state_forward(x_heads, written, readout, step_size, decay_rate, stretch_rows):
    rows_all, heads, head_dim = x_heads.shape
    stretches = rows_all // stretch_rows
    x_blocks = x_heads.reshape(stretches, stretch_rows, heads, head_dim)
    w_blocks = written.reshape(stretches, stretch_rows, -1)
    r_blocks = readout.reshape(stretches, stretch_rows, -1)
    step_blocks = step_size.reshape(stretches, stretch_rows, heads)
    log_decay = jnp.cumsum(step_blocks * decay_rate[None, None, :], axis=1)
    by_head = jnp.transpose(log_decay, (0, 2, 1))
    causal = jnp.arange(stretch_rows)[:, None] >= jnp.arange(stretch_rows)[None, :]
    spread = by_head[:, :, :, None] - by_head[:, :, None, :]
    fading = jnp.where(causal, jnp.exp(jnp.where(causal, spread, 0.0)), 0.0)
    intersection = jnp.einsum("cin,cjn->cij", r_blocks, w_blocks, precision=PRECISE)
    mixing = intersection[:, None, :, :] * fading
    driven = step_blocks[..., None] * x_blocks
    to_end = jnp.exp(log_decay[:, -1:, :] - log_decay)
    stretch_state = jnp.einsum(
        "cjhp,cjn->chpn", to_end[..., None] * driven, w_blocks, precision=PRECISE
    )
    end_fade = jnp.exp(log_decay[:, -1, :])
    running = jnp.zeros(stretch_state.shape[1:], jnp.float32)
    entering = []
    entering.append(running)
    entering = jnp.stack(entering)
    from_start = jnp.exp(log_decay)
    carried_out = from_start[..., None] * jnp.einsum(
        "chpn,cin->cihp", entering, r_blocks, precision=PRECISE
    )
    inner_out = jnp.einsum("chij,cjhp->cihp", mixing, driven, precision=PRECISE)
    saved = (
        x_blocks,
        w_blocks,
        r_blocks,
        step_blocks,
        causal,
        fading,
        mixing,
        driven,
        to_end,
        entering,
        end_fade,
        from_start,
        carried_out,
    )
    return ((inner_out + carried_out).reshape(rows_all, heads * head_dim), saved)


def state_backward(saved, mixed_grad, decay_rate):
    (
        x_blocks,
        w_blocks,
        r_blocks,
        step_blocks,
        causal,
        fading,
        mixing,
        driven,
        to_end,
        entering,
        end_fade,
        from_start,
        carried_out,
    ) = saved
    stretches = x_blocks.shape[0]
    scaled = from_start[..., None] * mixed_grad
    readout_grad = jnp.einsum("cihp,chpn->cin", scaled, entering, precision=PRECISE)
    from_out = jnp.einsum("cihp,cin->chpn", scaled, r_blocks, precision=PRECISE)
    decay_grad = jnp.sum(carried_out * mixed_grad, axis=3)
    downstream = jnp.zeros(from_out.shape[1:], jnp.float32)
    passed = []
    end_grads = []
    for number in reversed(range(stretches)):
        handed = jnp.zeros_like(downstream)
        passed.append(handed)
        end_grads.append(jnp.sum(handed * entering[number], axis=(1, 2)))
        downstream = from_out[number] + end_fade[number][:, None, None] * handed
    passed = jnp.stack(passed[::-1])
    end_grads = jnp.stack(end_grads[::-1])
    pulled = jnp.einsum("chpn,cjn->cjhp", passed, w_blocks, precision=PRECISE)
    driven_grad = to_end[..., None] * pulled
    written_grad = jnp.einsum(
        "cjhp,chpn->cjn", to_end[..., None] * driven, passed, precision=PRECISE
    )
    tail_grad = jnp.sum(pulled * driven, axis=3) * to_end
    decay_grad = decay_grad - tail_grad
    last_extra = jnp.sum(tail_grad, axis=1) + end_grads * end_fade
    mixing_grad = jnp.where(
        causal, jnp.einsum("cihp,cjhp->chij", mixed_grad, driven, precision=PRECISE), 0.0
    )
    driven_grad = driven_grad + jnp.einsum("chij,cihp->cjhp", mixing, mixed_grad, precision=PRECISE)
    intersection_grad = jnp.sum(mixing_grad * fading, axis=1)
    readout_grad = readout_grad + jnp.einsum(
        "cij,cjn->cin", intersection_grad, w_blocks, precision=PRECISE
    )
    written_grad = written_grad + jnp.einsum(
        "cij,cin->cjn", intersection_grad, r_blocks, precision=PRECISE
    )
    product = mixing_grad * mixing
    decay_grad = decay_grad + jnp.transpose(
        jnp.sum(product, axis=3) - jnp.sum(product, axis=2), (0, 2, 1)
    )
    decay_grad = decay_grad.at[:, -1, :].add(last_extra)
    step_grad = jnp.sum(driven_grad * x_blocks, axis=3)
    x_state_grad = step_blocks[..., None] * driven_grad
    rate_grad = jnp.flip(jnp.cumsum(jnp.flip(decay_grad, axis=1), axis=1), axis=1)
    step_grad = step_grad + rate_grad * decay_rate[None, None, :]
    rate_total = jnp.sum(rate_grad * step_blocks, axis=(0, 1))
    return (x_state_grad, written_grad, readout_grad, step_grad, rate_total)


MESH = pl.DeviceIdType.MESH
BF = jnp.bfloat16
F32 = jnp.float32
NEG = -1e30


def dot_nn(a, b):
    return lax.dot_general(a, b, (((1,), (0,)), ((), ())), preferred_element_type=F32)


def dot_nt(a, b):
    return lax.dot_general(a, b, (((1,), (1,)), ((), ())), preferred_element_type=F32)


def dot_tn(a, b):
    return lax.dot_general(a, b, (((0,), (0,)), ((), ())), preferred_element_type=F32)


def iota(shape, axis):
    return lax.broadcasted_iota(jnp.int32, shape, axis)


def one_hot(cond):
    return jnp.where(cond, 1.0, 0.0).astype(BF)


def split3(v):
    high = v.astype(BF)
    rest = v - high.astype(F32)
    mid = rest.astype(BF)
    return high, mid, (rest - mid.astype(F32)).astype(BF)


def sigmoid(v):
    return 1.0 / (1.0 + jnp.exp(-v))


def rows_down(v, k):
    return jnp.where(iota(v.shape, 0) >= k, pltpu.roll(v, k, 0), 0.0)


def rows_up(v, k):
    n = v.shape[0]
    return jnp.where(iota(v.shape, 0) < n - k, pltpu.roll(v, n - k, 0), 0.0)


def pick(v, lane, index):
    return jnp.sum(jnp.where(lane == index, v, 0.0), axis=1, keepdims=True)


class Sizes:
    def __init__(self, dp, rows, half, inner, heads, state, capacity):
        self.dp, self.rows, self.half, self.inner = dp, rows, half, inner
        self.heads, self.state, self.cap = heads, state, capacity
        self.width = 2 * half
        self.nz = dp // 4
        self.share = self.width // dp
        self.quarter = self.nz * self.share
        self.slots = dp * capacity
        self.tiles = inner // 128
        self.extra = 2 * state + 128
        self.cols = 3 * inner + self.extra
        n = inner // 2
        sizes = [n // 3 * 2, n // 3 * 4, n, n, n, n, self.extra]
        self.chunks = [(sum(sizes[:k]), size) for k, size in enumerate(sizes)]
        self.levels = self.nz.bit_length() - 1


def targets_of(lines, sz):
    n = sz.rows // 128
    return jnp.concatenate([lines[pl.ds(k, sz.dp, stride=n), :] for k in range(n)], axis=1)


def send_table(targets, g, sz):
    strict = one_hot(iota((sz.rows, sz.rows), 0) < iota((sz.rows, sz.rows), 1))
    every = targets_of(targets, sz)
    own = jnp.sum(jnp.where(iota(every.shape, 0) == g, every, 0), axis=0, keepdims=True)
    group = lax.shift_right_logical(own, 8)
    hot = jnp.where(iota((sz.dp, sz.rows), 0) == group, 1.0, 0.0)
    before = dot_nn(hot.astype(BF), strict)
    rank = jnp.sum(hot * before, axis=0, keepdims=True)
    spot = group.astype(F32) * sz.cap + rank
    return one_hot(iota((sz.slots, sz.rows), 0).astype(F32) == spot)


def owner_table(targets, g, sz):
    strict = one_hot(iota((sz.rows, sz.rows), 0) < iota((sz.rows, sz.rows), 1))
    every = targets_of(targets, sz)
    mine = jnp.where(lax.shift_right_logical(every, 8) == g, 1.0, 0.0)
    rank = dot_nn(mine.astype(BF), strict)
    slot = mine * ((every & 255) + 1).astype(F32)
    lane = iota((sz.dp, 128), 1)
    found = jnp.zeros((sz.dp, 128), F32)
    for a in range(sz.cap):
        one = jnp.sum(jnp.where(rank == float(a), slot, 0.0), axis=1, keepdims=True)
        found = jnp.where(lane == a, one, found)
    place = iota((128, sz.slots), 1)
    spread = one_hot((place % sz.cap) == iota((128, sz.slots), 0))
    wide = dot_nn(found.astype(BF), spread)
    keep = (iota((sz.dp, sz.slots), 1) // sz.cap) == iota((sz.dp, sz.slots), 0)
    row = jnp.sum(jnp.where(keep, wide, 0.0), axis=0, keepdims=True) - 1.0
    return one_hot(iota((sz.rows, sz.slots), 0).astype(F32) == row)


def block_kernel(sz, *refs):
    (dest, back, length, rows_hbm, ct_hbm, win_hbm, wout_hbm, wst_hbm, wstep_in,
     tap_x, bias_x, gain_g, gain_n, skip_in, tap_s, bias_s, bias_step, log_rate,
     out_rows, out_grads, inner_out, proj_out, extra_out, small_out, gain_out,
     win, wout, wst, wstep, lines,
     pk_in, pk_ct, rc_in, rc_ct, gn_o, gn_g,
     p_own, q_in, q_bk,
     hid, cts, normed, lowct, perm, xA, xE, tA, tE,
     yb, pb, r0, r1, f_inner, f_proj, f_extra,
     inter, igrad, ptile,
     sraw, sslope, wr, dtv, lac, lar, sgr, rgr, stepsig, acc1, acc2, scale,
     stat_s, stat_r, half_s, half_r, raw_r, st_s, st_r,
     sms, smr, gall, gsum,
     a2a_s, a2a_r, fw_s, fw_r, quad_s, quad_r, xq_s, xq_r, z_s, z_r, y_s, y_r, gg_s, gg_r, sm_s, sm_r, w_s, own_s, relay_s, raw_sem, o_s, taken) = refs
    dp, R, H, C = sz.dp, sz.rows, sz.half, sz.inner
    W, NT_ = sz.width, sz.tiles
    g = lax.axis_index("dp")
    t = lax.axis_index("tensor")
    o = 1 - t
    c, x, z = g % 2, (g // 2) % 2, g // 4
    q = g % 4
    sib, xp = g + 1 - 2 * c, g + 2 - 4 * x
    diag = sib + 2 - 4 * x

    def rcopy(src, dst, ss, rs, peer, side=None):
        return pltpu.make_async_remote_copy(
            src_ref=src, dst_ref=dst, send_sem=ss, recv_sem=rs,
            device_id=(peer, t if side is None else side), device_id_type=MESH)

    sent = []

    def go(copy):
        copy.start()
        sent.append(copy)
        return copy

    loads = [pltpu.make_async_copy(a, b, w_s.at[i]) for i, (a, b) in enumerate(
        [(rows_hbm, lowct.at[:, pl.ds(0, H)]), (ct_hbm, lowct.at[:, pl.ds(H, H)]), (wst_hbm, wst), (wout_hbm, wout)])]
    for load in loads[:2]:
        load.start()

    barrier = pltpu.get_barrier_semaphore()
    for off in range(1, dp):
        pl.semaphore_signal(barrier, inc=1, device_id=((g + off) % dp, t), device_id_type=MESH)
    pl.semaphore_signal(barrier, inc=1, device_id=(g, o), device_id_type=MESH)

    side = z // 2
    zo, zi, fi, fo = 3 * side, 1 + side, 2 - side, 3 - 3 * side
    is_outer = (z + side + 1) % 2
    is_inner = 1 - is_outer
    far = [
        ((z + dz) % sz.nz) * 4 + ((x + dx) % 2) * 2 + (c + dc) % 2
        for dz in (2, 1, 3, 0) for dx in (1, 0) for dc in (1, 0) if dz + dx + dc]
    level = [z * 4 + ((x + dx) % 2) * 2 + (c + dc) % 2 for dx, dc in ((1, 1), (1, 0), (0, 1))]
    across = [zz * 4 + ((x + dx) % 2) * 2 + (c + dc) % 2 for zz in (fo, fi) for dx in (1, 0) for dc in (1, 0)]
    beside_z = is_outer * zi + (1 - is_outer) * zo
    beside = [beside_z * 4 + ((x + dx) % 2) * 2 + (c + dc) % 2 for dx, dc in ((1, 1), (1, 0), (0, 1))]
    partner = beside_z * 4 + q
    parts = [pl.ds(k * (H // 3), H // 3) for k in range(3)]

    def span(ref, n, ss, rs, at=slice(None)):
        return rcopy(ref.at[pl.ds(0, n), :, at], ref.at[pl.ds(0, n), :, at], ss, rs, partner)

    def exchange(i, source, target, at=slice(None)):
        for peer in far:
            rcopy(source.at[peer, :, at], target.at[g, :, at], a2a_s.at[i], a2a_r.at[i], peer).start()

    def settle(copies):
        for copy in copies:
            copy.wait_send()

    def arrived(i, target, at=slice(None)):
        span(target, dp - 1, a2a_s.at[i], a2a_r.at[i], at).wait_recv()

    def answer(table, value, dst):
        for k in range(2):
            n = sz.slots // 2
            part = dot_tn(table[:, k * n:(k + 1) * n], value).astype(BF)
            dst[k * (dp // 2):(k + 1) * (dp // 2)] = part.reshape(dp // 2, sz.cap, H)

    def block_to(i, source, target, peer, owner, sems):
        return rcopy(source.at[peer], target.at[owner], sems.at[i - 4], a2a_r.at[i + 2], peer)

    def raw_copy(i):
        return rcopy(lowct.at[:, pl.ds((i - 4) * H, H)], raw_r, raw_sem.at[0, i - 4], raw_sem.at[1, i - 4], partner)

    def near_x(peers, same):
        if len(peers) == 3:
            return peers[2:] if same else peers[:2]
        return [peer for k, peer in enumerate(peers) if (k % 4 >= 2) == same]

    def reply_send(i, packed, target, same):
        @pl.when(is_outer == 0)
        def _():
            for peer in near_x(across, same) + near_x(beside, same) + ([partner] if same else []):
                block_to(i, packed, target, peer, g, own_s).start()
        for peer in near_x(level, same):
            block_to(i, packed, target, peer, g, own_s).start()

    def reply(i, table, value, packed, target):
        answer(table, value, packed)
        target[pl.ds(g, 1)] = packed[pl.ds(g, 1)]

        @pl.when(is_outer == 1)
        def _():
            if i == 5:
                pl.semaphore_wait(taken, 1)
            lowct[:, (i - 4) * H:(i - 3) * H] = value
            raw_copy(i).start()

    def relay_send(i, packed, target, same):
        @pl.when(is_outer == 0)
        def _():
            for peer in near_x(across, same) + near_x(level, same):
                block_to(i, packed, target, peer, partner, relay_s).start()

    def relay(i, targets, packed, target):
        @pl.when(is_outer == 0)
        def _():
            raw_copy(i).wait_recv()
            answer(owner_table(targets, partner, sz), raw_r[...], packed)
            if i == 4:
                pl.semaphore_signal(taken, inc=1, device_id=(partner, t), device_id_type=MESH)
            target[pl.ds(partner, 1)] = packed[pl.ds(g, 1)]

    def replied(i, target):
        @pl.when(is_outer == 1)
        def _():
            span(target, dp - 1, own_s.at[i - 4], a2a_r.at[i + 2]).wait_recv()

        @pl.when(is_outer == 0)
        def _():
            span(target, dp - 2, own_s.at[i - 4], a2a_r.at[i + 2]).wait_recv()

    def reply_settle(i, packed):
        @pl.when(is_outer == 1)
        def _():
            span(packed, len(level), own_s.at[i - 4], a2a_r.at[i + 2]).wait_send()

        @pl.when(is_outer == 0)
        def _():
            span(packed, dp - 1, own_s.at[i - 4], a2a_r.at[i + 2]).wait_send()
            span(packed, len(across + level), relay_s.at[i - 4], a2a_r.at[i + 2]).wait_send()

    def pack(table, source, target):
        for k in range(2):
            n = sz.slots // 2
            part = dot_nn(table[k * n:(k + 1) * n, :], source[...]).astype(BF)
            target[k * (dp // 2):(k + 1) * (dp // 2)] = part.reshape(dp // 2, sz.cap, H)

    def unpack(i, table, source, full, part):
        at = parts[part]
        arrived(3 * i + part, source, at)
        n = at.size
        full[pl.ds(t, 1), :, at] = dot_nn(table[...], source[:, :, at].reshape(sz.slots, n)).astype(BF)[None]
        go(rcopy(full.at[t, :, at], full.at[t, :, at], fw_s.at[i, part], fw_r.at[i, part], g, o))

    def other_half(i, full):
        for part in range(3):
            at = parts[part]
            rcopy(full.at[o, :, at], full.at[o, :, at], fw_s.at[i, part], fw_r.at[i, part], g, o).wait_recv()

    def take_apart(stage, sems):
        n, held = W // 128, stage.shape[0]
        fetch = [
            pltpu.make_async_copy(win_hbm.at[pl.ds(k * 128, 128)], stage.at[k % held], sems.at[k % held]) for k in range(n)]
        for copy in fetch[:held] + loads[2:]:
            copy.start()
        p_own[...] = send_table(dest, g, sz)
        loads[0].wait()
        pack(p_own, lowct.at[:, pl.ds(0, H)], pk_in)
        pl.semaphore_wait(barrier, dp)
        for k in range(3):
            exchange(k, pk_in, rc_in, parts[k])
        rc_in[pl.ds(g, 1)] = pk_in[pl.ds(g, 1)]
        p_own[...] = send_table(back, g, sz)
        loads[1].wait()
        pack(p_own, lowct.at[:, pl.ds(H, H)], pk_ct)
        rc_ct[pl.ds(g, 1)] = pk_ct[pl.ds(g, 1)]
        q_in[...] = owner_table(dest, g, sz)
        q_bk[...] = owner_table(back, g, sz)
        place = iota((256, 256), 0)
        order = one_hot(iota((256, 256), 1) == jnp.where(place < 128, 2 * place, 2 * place - 255))
        for k in range(n):
            fetch[k].wait()
            for m in range(0, C, 256):
                pair = jnp.concatenate(
                    [stage[k % held, :, :, m + e:m + e + 128].reshape(256, 128) for e in (0, 128)], axis=1)
                both = dot_nn(order, pair).astype(BF)
                win[k * 128:(k + 1) * 128, m:m + 256] = both[:128]
                win[k * 128:(k + 1) * 128, C + m:C + m + 256] = both[128:]
            if k + held < n:
                fetch[k + held].start()

    pl.run_scoped(take_apart, pltpu.VMEM((10, 128, 2, C), BF), pltpu.SemaphoreType.DMA((10,)))
    for k in range(3):
        unpack(0, q_in, rc_in, hid, k)
    for k in range(3):
        exchange(3 + k, pk_ct, rc_ct, parts[k])
    other_half(0, hid)

    total = jnp.zeros((R, 128), F32)
    for k in range(W // 128):
        v = hid[k // (H // 128), :, (k % (H // 128)) * 128:(k % (H // 128)) * 128 + 128].astype(F32)
        total = total + v * v
    norm_scale = lax.rsqrt(jnp.sum(total, axis=1, keepdims=True) / W + EPSILON)
    scale[...] = jnp.broadcast_to(norm_scale, (R, 128))
    for k in range(W // 128):
        v = hid[k // (H // 128), :, (k % (H // 128)) * 128:(k % (H // 128)) * 128 + 128].astype(F32)
        normed[:, k * 128:(k + 1) * 128] = (v * scale[...] * gain_n[k:k + 1, :]).astype(BF)

    def quarters(source):
        for qq in range(4):
            perm[qq] = jnp.concatenate(
                [source[:, sz.share * (4 * zz + qq):sz.share * (4 * zz + qq + 1)] for zz in range(sz.nz)], axis=1)

    def send_quarter(i, dst):
        copies = [
            rcopy(perm.at[peer % 4], dst.at[rel], xq_s.at[i, rel - 1], xq_r.at[i, rel - 1], peer)
            for rel, peer in ((2, xp), (3, diag), (1, sib))]
        for copy in copies:
            copy.start()
        dst[0:1] = perm[pl.ds(q, 1)]
        return copies

    def turn_quarter(dst, turned):
        for rel, peer in ((1, sib), (2, xp), (3, diag)):
            rcopy(dst.at[rel], dst.at[rel], xq_s.at[0, rel - 1], xq_r.at[0, rel - 1], peer).wait_recv()
        for rel in range(4):
            turned[:, rel * R:(rel + 1) * R] = jnp.transpose(dst[rel].astype(F32)).astype(BF)

    def fold_half(which, place):
        value = cts[pl.ds(which, 1)][0]
        for qq in range(4):
            cut = jnp.concatenate(
                [value[:, sz.share * (4 * zz + qq):sz.share * (4 * zz + qq + 1)] for zz in range(sz.nz // 2)], axis=1)
            cut = jnp.where(iota(cut.shape, 0) < length[0, 0], cut.astype(F32), 0.0).astype(BF)
            perm[qq, place * (R // 2):(place + 1) * (R // 2)] = jnp.concatenate([cut[:R // 2], cut[R // 2:]], axis=1)

    def fold_copy(sem, quarter, place, half, rel, peer, to):
        return rcopy(perm.at[quarter, pl.ds(place * (R // 2), R // 2)], xE.at[half, rel], xq_s.at[1, sem], xq_r.at[1, sem], peer, to)

    def fold_pass(rel, half):
        return rcopy(xE.at[half, rel], xE.at[half, rel], xq_s.at[1, 2 + rel], xq_r.at[1, 2 + rel], g, o)

    def turn_folds():
        fold_copy(0, 0, 0, t, 1, sib, t).wait_recv()
        fold_copy(3, 0, 0, o, 1, sib, t).wait_recv()
        for rel in (2, 3):
            fold_pass(rel, o).wait_recv()
        n = sz.quarter // 2
        for half in range(2):
            for rel in range(4):
                flat = jnp.transpose(xE[half, rel].astype(F32)).astype(BF)
                tE[half * n:(half + 1) * n, rel * R:rel * R + R // 2] = flat[:n]
                tE[half * n:(half + 1) * n, rel * R + R // 2:(rel + 1) * R] = flat[n:]

    quarters(normed)
    quarter_away = send_quarter(0, xA)

    loads[2].wait()
    wstep[...] = jnp.zeros_like(wstep)
    wstep[:sz.heads] = wstep_in[...]
    lines[...] = jnp.zeros_like(lines)
    lines[0:1, :sz.heads] = bias_step[...]
    lines[1:2, :sz.heads] = log_rate[...]
    row = iota((R, 128), 0)
    lane = iota((R, 128), 1)
    live = jnp.where(row < length[0, 0], 1.0, 0.0)
    sraw[...] = dot_nn(normed[...], wst[...])
    step_in = dot_nt(normed[...], wstep[...]) + lines[0:1, :]
    S = sz.state
    for k in range(2):
        cut = slice(k * S, (k + 1) * S)
        raw = sraw[:, cut]
        conv = bias_s[:, cut] + tap_s[0:1, cut] * raw
        for tap in range(1, 4):
            conv = conv + tap_s[tap:tap + 1, cut] * rows_down(raw, tap)
        sg = sigmoid(conv)
        sslope[:, cut] = sg * (1.0 + conv * (1.0 - sg))
        wr[:, cut] = (conv * sg).astype(BF)
    written, readout = wr[:, :S], wr[:, S:]
    inter[...] = dot_nt(readout, written)
    stepsig[...] = sigmoid(step_in) * live
    heads_live = jnp.where(lane < sz.heads, live, 0.0)
    step = (jnp.maximum(step_in, 0.0) + jnp.log1p(jnp.exp(-jnp.abs(step_in)))) * heads_live
    rate = -jnp.exp(lines[1:2, :])
    dtv[...] = step
    lower = one_hot(iota((R, R), 0) >= iota((R, R), 1))
    log_decay = sum(dot_nn(lower, part) for part in split3(step * rate))
    lac[...] = log_decay
    lar[...] = jnp.transpose(log_decay)

    def cols_of(i):
        return pl.ds(sz.chunks[i][0], sz.chunks[i][1])

    def quad_send(i):
        at = cols_of(i)
        rcopy(yb.at[0, :, at], yb.at[2, :, at], quad_s.at[1], quad_r.at[i, 1], xp).start()
        rcopy(yb.at[0, :, at], yb.at[1, :, at], quad_s.at[0], quad_r.at[i, 0], sib).start()

    def quad_pass(i):
        at = cols_of(i)
        rcopy(yb.at[2, :, at], yb.at[2, :, at], quad_s.at[1], quad_r.at[i, 1], xp).wait_recv()
        rcopy(yb.at[2, :, at], yb.at[3, :, at], quad_s.at[2], quad_r.at[i, 2], sib).start()

    def z_copy(i, k):
        at = cols_of(i)
        column = g % 4
        if k < 3:
            block, slot, peer = (zi, fi, fo)[k], r0.at[k], zi
        elif k < 5:
            block, slot, peer = (fi, fo)[k - 3], r1.at[k - 3], fi
        else:
            block, slot, peer = zo, r0.at[0], zo
        return rcopy(pb.at[block, :, at], slot.at[:, at], z_s, z_r.at[i, k], peer * 4 + column)

    def z_wait(i, k):
        at = cols_of(i)
        slot = r0.at[k] if k < 3 else r1.at[k - 3] if k < 5 else r0.at[0]
        rcopy(slot.at[:, at], slot.at[:, at], z_s, z_r.at[i, k], g + 4 - 8 * (z // 3)).wait_recv()

    def each_tile(i, block, landed, keep):
        start, size = sz.chunks[i]
        for n in range(0, size, 128):
            cut = slice(start + n, start + n + 128)
            value = pb[pl.ds(block, 1), :, cut].astype(F32)[0] + landed[:, cut].astype(F32)
            if keep:
                pb[pl.ds(block, 1), :, cut] = value.astype(BF)[None]
            elif start + n < C:
                f_proj[:, cut] = value
            elif start + n < 3 * C:
                f_inner[:, start + n - C:start + n - C + 128] = value
            else:
                f_extra[:, start + n - 3 * C:start + n - 3 * C + 128] = value

    def z_first(i):
        @pl.when(is_outer == 1)
        def _():
            for k in range(3):
                z_copy(i, 2 - k).start()

    def z_second(i):
        @pl.when(is_outer == 0)
        def _():
            for k in (2, 1):
                z_wait(i, k)
                each_tile(i, (zi, fi, fo)[k], r0.at[k], True)
                z_copy(i, 2 + k).start()
            z_wait(i, 0)
            each_tile(i, zi, r0.at[0], True)

    def z_third(i):
        @pl.when(is_outer == 0)
        def _():
            z_wait(i, 4)
            each_tile(i, zo, r1.at[1], True)
            z_copy(i, 5).start()
            z_wait(i, 3)
            each_tile(i, zi, r1.at[0], False)

    def z_fourth(i):
        @pl.when(is_outer == 1)
        def _():
            z_wait(i, 5)
            each_tile(i, zo, r0.at[0], False)

    def write_out(i):
        start, size = sz.chunks[i]
        if i < 2:
            pairs = [(f_proj.at[:, pl.ds(start, size)], proj_out.at[:, pl.ds(start, size)])]
        elif i < 6:
            cut = pl.ds(start - C, size)
            pairs = [(f_inner.at[:, cut], inner_out.at[:, cut])]
        else:
            pairs = [(f_extra, extra_out)]
        copies = [pltpu.make_async_copy(a, b, o_s.at[i]) for a, b in pairs]
        for copy in copies:
            copy.start()
        return copies

    def settle_sums():
        for k in range(3):
            rcopy(yb.at[0], yb.at[0], quad_s.at[k], quad_r.at[0, k], sib).wait_send()
        rcopy(r0, r0, z_s, z_r.at[0, 0], partner).wait_send()

    def partial_sum(i, turned):
        at = cols_of(i)
        start, size = sz.chunks[i]
        rcopy(yb.at[1, :, at], yb.at[1, :, at], quad_s.at[0], quad_r.at[i, 0], sib).wait_recv()
        rcopy(yb.at[3, :, at], yb.at[3, :, at], quad_s.at[2], quad_r.at[i, 2], sib).wait_recv()
        n = 384 if size % 256 else 256

        def body(k, carry):
            at = pl.ds(pl.multiple_of(start + k * n, 128), n)
            part = dot_nn(turned[...], yb[:, :, at].reshape(4 * R, n))
            pb[:, :, at] = part.astype(BF).reshape(sz.nz, sz.share, n)
            return carry
        lax.fori_loop(0, size // n, body, 0)
        z_first(i)

    def remainder(gr, xr, xa, xs, mx, ng):
        def project(dst, base):
            def body(n, carry):
                at = pl.multiple_of(n * 256, 256)
                dst[:, pl.ds(at, 256)] = dot_nn(normed[...], win[:, pl.ds(pl.multiple_of(base + n * 256, 256), 256)])
                return carry
            lax.fori_loop(0, C // 256, body, 0)

        project(xr, C)
        project(gr, 0)

        unpack(1, q_bk, rc_ct, cts, 0)

        def lanes(p):
            return pl.ds(pl.multiple_of(p * 128, 128), 128)

        B = 64

        def head_line(v, p):
            first = iota((1, 128), 1) < 64
            spot = iota(v.shape, 1)
            return jnp.where(first, pick(v, spot, 2 * p), pick(v, spot, 2 * p + 1))

        def step_columns(p, lane):
            first = lane < 64
            return jnp.where(first, pick(dtv[...], lane, 2 * p), pick(dtv[...], lane, 2 * p + 1))

        acc1[...] = jnp.zeros_like(acc1)
        acc2[...] = jnp.zeros_like(acc2)

        def scan(p, carry):
            at = lanes(p)
            lane = iota((R, 128), 1)
            raw = xr[:, at]
            conv = bias_x[pl.ds(p, 1), :] + tap_x[0:1, at] * raw
            for tap in range(1, 4):
                conv = conv + tap_x[tap:tap + 1, at] * rows_down(raw, tap)
            sg = sigmoid(conv)
            act = conv * sg
            xa[:, at] = act
            xs[:, at] = (sg * (1.0 + conv * (1.0 - sg))).astype(BF)
            driven = act * step_columns(p, lane)
            parts = [jnp.where(lane < 64, driven, 0.0).astype(BF), jnp.where(lane >= 64, driven, 0.0).astype(BF)]
            cols = [pick(lac[...], lane, 2 * p + k) for k in range(2)]
            skip = head_line(skip_in[...], p)
            for b in range(R // B):
                reach = 128 * ((b * B) // 128 + 1)
                cut = slice(b * B, (b + 1) * B)
                causal = iota((B, reach), 0) + b * B >= iota((B, reach), 1)
                mixed = skip * act[cut]
                for k in range(2):
                    spread = cols[k][cut] - lar[pl.ds(2 * p + k, 1), :][:, :reach]
                    fading = jnp.exp(jnp.where(causal, spread, NEG))
                    mixing = (inter[cut, :reach] * fading).astype(BF)
                    mixed = mixed + dot_nn(mixing, parts[k][:reach])
                mx[cut, at] = mixed
                gate = gr[cut, at]
                gated = mixed * gate * sigmoid(gate)
                acc1[cut] += gated * gated
            return carry

        lax.fori_loop(0, NT_, scan, 0)

        whole = float(2 * C)

        def total_over_sides(i, value):
            stat_s[i] = jnp.transpose(jnp.where(lane == 0, jnp.sum(value, axis=1, keepdims=True), 0.0))[:8]
            return go(rcopy(stat_s.at[i], stat_r.at[i], y_s.at[i], y_r.at[i], g, o))

        def total_here(i):
            both = jnp.concatenate([stat_s[i] + stat_r[i], jnp.zeros((120, R), F32)], axis=0)
            return pick(jnp.transpose(both), lane, 0)

        squares = total_over_sides(0, acc1[...])
        unpack(1, q_bk, rc_ct, cts, 1)
        unpack(1, q_bk, rc_ct, cts, 2)
        turn_quarter(xA, tA)
        settle(quarter_away)
        fold_half(t, 0)
        for rel, peer in ((2, xp), (3, diag)):
            go(fold_copy(rel - 1, peer % 4, 0, t, rel, peer, t))
        squares.wait_recv()
        gate_scale = lax.rsqrt(total_here(0) / whole + EPSILON)
        acc1[...] = jnp.broadcast_to(gate_scale, (R, 128))

        def gate_forward(p, carry):
            at = lanes(p)
            gate = gr[:, at]
            yb[0, :, at] = (mx[:, at] * (gate * sigmoid(gate)) * acc1[...] * gain_g[pl.ds(p, 1), :]).astype(BF)
            return carry
        lax.fori_loop(0, NT_, gate_forward, 0)
        quad_send(0)

        other_half(1, cts)
        for k in range(W // 128):
            v = cts[k // (H // 128), :, (k % (H // 128)) * 128:(k % (H // 128)) * 128 + 128].astype(F32)
            lowct[:, k * 128:(k + 1) * 128] = (v * live).astype(BF)
        fold_half(o, 1)
        xE[t, 0] = perm[q, :R // 2]
        xE[o, 0] = perm[q, R // 2:]
        go(fold_copy(0, sib % 4, 0, t, 1, sib, t))
        go(fold_copy(3, sib % 4, 1, o, 1, sib, t))
        quad_send(1)
        loads[3].wait()

        def out_half(side, dst, cast):
            def body(n, carry):
                at = pl.ds(pl.multiple_of(side * H + n * 256, 256), 256)
                dst[:, pl.ds(pl.multiple_of(n * 256, 256), 256)] = dot_nn(yb[0, :, :C], wout[:, at]).astype(cast)
                return carry
            lax.fori_loop(0, H // 256, body, 0)

        def back_project(n, carry):
            at = pl.ds(pl.multiple_of(n * 256, 256), 256)
            ng[:, at] = dot_nt(lowct[...], wout[at, :])
            for k in range(2):
                here = pl.ds(pl.multiple_of(n * 256 + k * 128, 128), 128)
                gate = gr[:, here]
                acc2[...] += mx[:, here] * (gate * sigmoid(gate)) * (gain_g[pl.ds(2 * n + k, 1), :] * ng[:, here])
            return carry
        lax.fori_loop(0, C // 256, back_project, 0)
        crossed = total_over_sides(1, acc2[...])
        for rel in (2, 3):
            fold_copy(rel - 1, 0, 0, t, rel, xp, t).wait_recv()
            go(fold_pass(rel, t))
        out_half(o, half_s, BF)
        branch_away = rcopy(half_s, half_r, y_s.at[2], y_r.at[2], g, o)
        branch_away.start()
        crossed.wait_recv()
        acc2[...] = acc1[...] * acc1[...] * acc1[...] * (total_here(1) / whole)

        def gate_back(p, carry):
            at = lanes(p)
            gate, mixed, grad = gr[:, at], mx[:, at], ng[:, at]
            sg = sigmoid(gate)
            act = gate * sg
            gated = mixed * act
            gated_grad = acc1[...] * (gain_g[pl.ds(p, 1), :] * grad) - gated * acc2[...]
            sms[0, 5:6, at] = jnp.sum(grad * gated * acc1[...], axis=0, keepdims=True)
            mixed_grad = gated_grad * act
            ng[:, at] = mixed_grad
            sms[0, 6:7, at] = jnp.sum(mixed_grad * xa[:, at], axis=0, keepdims=True)
            yb[0, :, pl.ds(pl.multiple_of(C + p * 128, 128), 128)] = (
                gated_grad * mixed * (sg * (1.0 + gate * (1.0 - sg)))).astype(BF)
            return carry
        lax.fori_loop(0, NT_, gate_back, 0)
        quad_send(2)
        quad_send(3)
        out_half(t, gr, F32)
        quad_pass(0)
        turn_folds()
        partial_sum(0, tE)

        inter[...] = dot_nt(written, readout)
        igrad[...] = jnp.zeros_like(igrad)
        sgr[...] = jnp.zeros_like(sgr)
        rgr[...] = jnp.zeros_like(rgr)
        ptile[...] = jnp.zeros_like(ptile)

        def scan_back(p, carry):
            at = lanes(p)
            lane = iota((R, 128), 1)
            grad = ng[:, at]
            act = xa[:, at]
            stepw = step_columns(p, lane)
            driven = (act * stepw).astype(BF)
            parts = [jnp.where(lane < 64, grad, 0.0).astype(BF), jnp.where(lane >= 64, grad, 0.0).astype(BF)]
            cols = [pick(lac[...], lane, 2 * p + k) for k in range(2)]
            pieces = []
            for b in range(R // B):
                skip = 128 * ((b * B) // 128)
                cut = slice(b * B, (b + 1) * B)
                causal = iota((B, R - skip), 1) + skip >= iota((B, R - skip), 0) + b * B
                turned = inter[cut, skip:]
                piece = jnp.zeros((B, 128), F32)
                total = igrad[cut, skip:]
                for k in range(2):
                    spread = lar[pl.ds(2 * p + k, 1), :][:, skip:] - cols[k][cut]
                    fading = jnp.exp(jnp.where(causal, spread, NEG))
                    faded = dot_nt(driven[cut], parts[k][skip:]) * fading
                    total = total + faded
                    piece = piece + dot_nn((turned * fading).astype(BF), parts[k][skip:])
                    ptile[k, cut, skip:] = (faded * turned).astype(BF)
                igrad[cut, skip:] = total
                pieces.append(piece)
            strict = one_hot(iota((R, R), 0) > iota((R, R), 1))
            for k in range(2):
                found = []
                for b in range(R // B):
                    skip = 128 * ((b * B) // 128)
                    cut = slice(b * B, (b + 1) * B)
                    causal = iota((B, R - skip), 1) + skip >= iota((B, R - skip), 0) + b * B
                    sums = dot_nn(strict[cut], ptile[k, :, skip:])
                    found.append(jnp.sum(jnp.where(causal, sums, 0.0), axis=1, keepdims=True))
                rgr[...] = jnp.where(lane == 2 * p + k, jnp.concatenate(found, axis=0), rgr[...])
            driven_grad = jnp.concatenate(pieces, axis=0)
            pulled = driven_grad * act
            low = jnp.sum(jnp.where(lane < 64, pulled, 0.0), axis=1, keepdims=True)
            high = jnp.sum(jnp.where(lane >= 64, pulled, 0.0), axis=1, keepdims=True)
            sgr[...] = jnp.where(lane == 2 * p, low, jnp.where(lane == 2 * p + 1, high, sgr[...]))
            conv_grad = (head_line(skip_in[...], p) * grad + stepw * driven_grad) * xs[:, at].astype(F32)
            raw = xr[:, at]
            raw_grad = tap_x[0:1, at] * conv_grad
            sms[0, 0:1, at] = jnp.sum(conv_grad * raw, axis=0, keepdims=True)
            sms[0, 4:5, at] = jnp.sum(conv_grad, axis=0, keepdims=True)
            for tap in range(1, 4):
                up = rows_up(conv_grad, tap)
                raw_grad = raw_grad + tap_x[tap:tap + 1, at] * up
                sms[0, tap:tap + 1, at] = jnp.sum(up * raw, axis=0, keepdims=True)
            yb[0, :, pl.ds(pl.multiple_of(2 * C + p * 128, 128), 128)] = raw_grad.astype(BF)
            return carry

        lax.fori_loop(0, NT_ // 2, scan_back, 0)
        quad_send(4)

        rcopy(half_r, half_r, y_s.at[2], y_r.at[2], g, o).wait_recv()

        pieces = []
        mine = hid[pl.ds(t, 1)][0]
        for k in range(H // 128):
            cut = slice(k * 128, (k + 1) * 128)
            branch = gr[:, cut] + half_r[:, cut].astype(F32)
            pieces.append((mine[:, cut].astype(F32) + live * branch).astype(BF))
        for k in range(3):
            span(pk_in, dp - 1, a2a_s.at[k], a2a_r.at[k], parts[k]).wait_send()
        reply(4, q_bk, jnp.concatenate(pieces, axis=1), pk_in, gn_o)
        reply_send(4, pk_in, gn_o, True)

        quad_pass(1)
        lax.fori_loop(NT_ // 2, NT_, scan_back, 0)
        quad_send(5)

        ig = igrad[...].astype(BF)
        st_s[:, :S] = dot_nn(ig, wr[:, S:]).astype(BF)
        st_s[:, S:] = dot_tn(ig, wr[:, :S]).astype(BF)
        go(rcopy(st_s, st_r, y_s.at[3], y_r.at[3], g, o))
        step_grad = (sgr[...] + rgr[...] * rate) * stepsig[...]
        yb[0, :, 3 * C + 2 * S:] = step_grad.astype(BF)
        sms[0, 7:8, 10 * S:10 * S + 128] = jnp.sum(step_grad, axis=0, keepdims=True)
        sms[0, 7:8, 10 * S + 128:10 * S + 256] = jnp.sum(rgr[...] * dtv[...], axis=0, keepdims=True) * rate
        partial_sum(1, tE)
        z_second(0)
        rcopy(st_r, st_r, y_s.at[3], y_r.at[3], g, o).wait_recv()
        for k in range(2):
            cut = slice(k * S, (k + 1) * S)
            conv_grad = (st_s[:, cut].astype(F32) + st_r[:, cut].astype(F32)) * sslope[:, cut]
            raw = sraw[:, cut]
            raw_grad = tap_s[0:1, cut] * conv_grad
            sms[0, 7:8, cut] = jnp.sum(conv_grad * raw, axis=0, keepdims=True)
            sms[0, 7:8, 8 * S + k * S:8 * S + (k + 1) * S] = jnp.sum(conv_grad, axis=0, keepdims=True)
            for tap in range(1, 4):
                up = rows_up(conv_grad, tap)
                raw_grad = raw_grad + tap_s[tap:tap + 1, cut] * up
                sms[0, 7:8, tap * 2 * S + k * S:tap * 2 * S + (k + 1) * S] = jnp.sum(up * raw, axis=0, keepdims=True)
            yb[0, :, 3 * C + k * S:3 * C + (k + 1) * S] = raw_grad.astype(BF)
        quad_send(6)
        reply_send(4, pk_in, gn_o, False)

        hops = [2 ** k for k in range(2, dp.bit_length() - 1)] + [1, 2]

        def small_start(i):
            bit = (g // hops[i]) % 2
            go(rcopy(sms.at[i], smr.at[i], sm_s.at[i], sm_r.at[i], g + (1 - 2 * bit) * hops[i]))

        def small_end(i):
            bit = (g // hops[i]) % 2
            rcopy(sms.at[i], smr.at[i], sm_s.at[i], sm_r.at[i], g + (1 - 2 * bit) * hops[i]).wait_recv()
            if i + 1 < len(hops):
                sms[i + 1] = sms[i] + smr[i]
                small_start(i + 1)
            else:
                smr[0] = sms[i] + smr[i]
        small_start(0)

        acc1[...] = jnp.zeros_like(acc1)

        def normed_grad(side, dst, cast):
            def body(n, carry):
                at = pl.ds(pl.multiple_of(side * H + n * 256, 256), 256)
                value = dot_nt(yb[0, :, C:3 * C], win[at, :])
                mine_state = pl.ds(pl.multiple_of(t * S, 128), S)
                value = value + dot_nt(yb[0, :, pl.ds(pl.multiple_of(3 * C + t * S, 128), S)], wst[at, mine_state])
                value = value + dot_nn(yb[0, :, 3 * C + 2 * S:], wstep[:, at])
                for k in range(2):
                    cut = slice(k * 128, (k + 1) * 128)
                    here = pl.ds(pl.multiple_of(n * 256 + k * 128, 128), 128)
                    there = pl.ds(pl.multiple_of(side * H + n * 256 + k * 128, 128), 128)
                    acc1[...] += hid[pl.ds(side, 1), :, here][0].astype(F32) * (gain_n[pl.ds(side * (H // 128) + 2 * n + k, 1), :] * value[:, cut])
                dst[:, pl.ds(pl.multiple_of(n * 256, 256), 256)] = value.astype(cast)
                return carry
            lax.fori_loop(0, H // 256, body, 0)
        branch_away.wait_send()
        normed_grad(o, half_s, BF)
        go(rcopy(half_s, half_r, y_s.at[4], y_r.at[4], g, o))
        normed_grad(t, gr, F32)
        summed_rows = total_over_sides(2, acc1[...])
        relay(4, back, rc_ct, gn_o)
        relay_send(4, rc_ct, gn_o, True)
        relay_send(4, rc_ct, gn_o, False)
        quad_pass(2)
        partial_sum(2, tA)

        rcopy(half_r, half_r, y_s.at[4], y_r.at[4], g, o).wait_recv()
        summed_rows.wait_recv()
        pull = total_here(2) / W * (scale[...] * scale[...] * scale[...])
        pieces = []
        mine = hid[pl.ds(t, 1)][0]
        mine_ct = cts[pl.ds(t, 1)][0]
        gall[pl.ds(g, 1)] = jnp.zeros((1, 8, 128), F32)
        for k in range(H // 128):
            cut = slice(k * 128, (k + 1) * 128)
            there = pl.ds(pl.multiple_of(t * H + k * 128, 128), 128)
            value = gr[:, cut] + half_r[:, cut].astype(F32)
            rows_here = mine[:, cut].astype(F32)
            gall[pl.ds(g, 1), k:k + 1, :] = jnp.sum(value * rows_here * scale[...], axis=0, keepdims=True)[None]
            pieces.append((scale[...] * (gain_n[pl.ds(t * (H // 128) + k, 1), :] * value) - rows_here * pull
                           + mine_ct[:, cut].astype(F32)).astype(BF))
        for k in range(3):
            span(pk_ct, dp - 1, a2a_s.at[3 + k], a2a_r.at[3 + k], parts[k]).wait_send()
        reply(5, q_in, jnp.concatenate(pieces, axis=1), pk_ct, gn_g)
        reply_send(5, pk_ct, gn_g, True)
        reply_send(5, pk_ct, gn_g, False)
        for peer in far:
            rcopy(gall.at[g], gall.at[g], gg_s, gg_r, peer).start()

        small_end(0)
        z_second(1)
        quad_pass(3)
        partial_sum(3, tA)
        z_second(2)
        z_third(0)
        relay(5, dest, rc_in, gn_g)
        relay_send(5, rc_in, gn_g, True)
        relay_send(5, rc_in, gn_g, False)
        quad_pass(4)
        partial_sum(4, tA)
        z_third(1)
        quad_pass(5)
        partial_sum(5, tA)
        z_third(2)
        z_second(3)
        quad_pass(6)
        partial_sum(6, tA)
        small_end(1)
        z_second(4)
        small_end(2)
        z_third(3)
        z_second(5)

        def give(i, value, dst):
            lowct[:, i * H:(i + 1) * H] = value.astype(BF)
            store = pltpu.make_async_copy(lowct.at[:, pl.ds(i * H, H)], dst, w_s.at[i])
            store.start()
            return store

        replied(4, gn_o)

        @pl.when(is_outer == 1)
        def _():
            raw_copy(4).wait_send()
            raw_copy(5).wait_send()
        stores = [give(0, dot_tn(p_own[...], gn_o[...].reshape(sz.slots, H)), out_rows)]
        p_own[...] = send_table(dest, g, sz)
        for i in range(4):
            z_fourth(i)
            stores += write_out(i)
        small_end(3)
        stores.append(pltpu.make_async_copy(smr.at[0], small_out, o_s.at[7]))
        stores[-1].start()
        span(gall, dp - 1, gg_s, gg_r).wait_recv()
        sent.append(span(gall, dp - 1, gg_s, gg_r))
        summed = gall[0]
        for d in range(1, dp):
            summed = summed + gall[d]
        gsum[pl.ds(t, 1)] = summed[None]
        go(rcopy(gsum.at[t], gsum.at[t], y_s.at[5], y_r.at[5], g, o))
        replied(5, gn_g)
        stores.append(give(1, dot_tn(p_own[...], gn_g[...].reshape(sz.slots, H)), out_grads))
        z_second(6)
        z_third(4)
        z_fourth(4)
        stores += write_out(4)
        z_third(5)
        z_fourth(5)
        stores += write_out(5)
        z_third(6)
        z_fourth(6)
        stores += write_out(6)
        rcopy(gsum.at[o], gsum.at[o], y_s.at[5], y_r.at[5], g, o).wait_recv()
        stores.append(pltpu.make_async_copy(gsum, gain_out, o_s.at[8]))
        stores[-1].start()
        for copy in sent:
            copy.wait_send()
        settle_sums()
        reply_settle(4, pk_in)
        reply_settle(5, pk_ct)
        for store in stores:
            store.wait()

    big = pltpu.VMEM((R, C), F32)
    pl.run_scoped(remainder, big, big, big, pltpu.VMEM((R, C), BF), big, big)


def finish_kernel(sz, rows, grads, inner, proj, extra, small, gain, o_rows, o_grads, o_gain, o_inner, o_state, o_step,
                  o_tap_x, o_bias_x, o_tap_s, o_bias_s, o_bias_step, o_rate, o_skip, o_gate, o_proj):
    C, S = sz.inner, sz.state
    o_rows[...] = rows[...]
    o_grads[...] = grads[...]
    o_inner[:, 0, :] = inner[:, :C]
    o_inner[:, 1, :] = inner[:, C:]
    o_proj[...] = proj[...]
    o_state[...] = extra[:, :2 * S]
    o_step[...] = jnp.transpose(extra[:, 2 * S:])[:sz.heads]
    o_tap_x[...] = small[0:4, :]
    o_bias_x[...] = small[4, :]
    o_gate[...] = small[5, :]
    for k in range(4):
        o_tap_s[k:k + 1, :] = small[7:8, k * 2 * S:(k + 1) * 2 * S]
    o_bias_s[...] = small[7, 8 * S:10 * S]
    o_bias_step[...] = small[7, 10 * S:10 * S + sz.heads]
    o_rate[...] = small[7, 10 * S + 128:10 * S + 128 + sz.heads]
    shape = (C, sz.heads)
    member = one_hot(iota(shape, 0) // (C // sz.heads) == iota(shape, 1))
    skip = jnp.broadcast_to(small[6:7, :], (8, C))
    o_skip[...] = sum(dot_nn(part, member) for part in split3(skip))[0]
    flat = jnp.concatenate([gain[h, k:k + 1, :] for h in range(2) for k in range(sz.half // 128)], axis=1)
    start = lax.axis_index("dp") * sz.share
    moved = pltpu.roll(jnp.broadcast_to(flat, (8, sz.width)), lax.rem(sz.width - start, sz.width), 1)
    o_gain[...] = moved[0, :sz.share]


def fused(sz, block_in, cotangent, lengths, dest_slot, return_slot, norm_gain, inner_weight, state_weight,
          step_weight, conv_inner, conv_inner_bias, conv_state, conv_state_bias, step_bias, log_rate,
          skip_gain, gate_gain, out_weight):
    dp, R, H, C, S = sz.dp, sz.rows, sz.half, sz.inner, sz.state
    W = sz.width

    vm = pl.BlockSpec(memory_space=pltpu.VMEM)
    hb = pl.BlockSpec(memory_space=pl.ANY)
    sm = pl.BlockSpec(memory_space=pltpu.SMEM)
    V = pltpu.VMEM
    packed = V((dp, sz.cap, H), BF)
    D = pltpu.SemaphoreType.DMA
    nch = len(sz.chunks)
    scratch = [
        V((W, 2 * C), BF), V((C, W), BF), V((W, 2 * S), BF), V((128, W), BF), V((8, 128), F32),
        *[packed] * 6,
        V((sz.slots, R), BF), V((R, sz.slots), BF), V((R, sz.slots), BF),
        V((2, R, H), BF), V((2, R, H), BF), V((R, W), BF), V((R, W), BF),
        V((4, R, sz.quarter), BF), V((4, R, sz.quarter), BF), V((2, 4, R // 2, sz.quarter), BF),
        V((sz.quarter, 4 * R), BF), V((sz.quarter, 4 * R), BF),
        V((4, R, sz.cols), BF), V((sz.nz, sz.share, sz.cols), BF), V((3, sz.share, sz.cols), BF), V((2, sz.share, sz.cols), BF),
        V((sz.share, 2 * C), F32), V((sz.share, C), F32), V((sz.share, sz.extra), F32),
        V((R, R), F32), V((R, R), F32), V((2, R, R), BF),
        V((R, 2 * S), F32), V((R, 2 * S), F32), V((R, 2 * S), BF), V((R, 128), F32), V((R, 128), F32), V((128, R), F32),
        V((R, 128), F32), V((R, 128), F32), V((R, 128), F32), V((R, 128), F32), V((R, 128), F32), V((R, 128), F32),
        V((3, 8, R), F32), V((3, 8, R), F32), V((R, H), BF), V((R, H), BF), V((R, H), BF),
        V((R, 2 * S), BF), V((R, 2 * S), BF),
        V((4, 8, C), F32), V((4, 8, C), F32), V((dp, 8, 128), F32), V((2, 8, 128), F32),
        D((6,)), D((8,)), D((2, 3)), D((2, 3)), D((3,)), D((nch, 3)), D((2, 6)), D((2, 6)),
        D, D((nch, 6)), D((6,)), D((6,)), D, D, D((4,)), D((4,)), D((4,)), D((2,)), D((2,)), D((2, 2)), D((9,)),
        pltpu.SemaphoreType.REGULAR,
    ]
    out = jax.ShapeDtypeStruct
    rows_out, grads_out, inner_g, proj_g, extra_g, small, gain = pl.pallas_call(
        functools.partial(block_kernel, sz),
        out_shape=(out((R, H), BF), out((R, H), BF), out((sz.share, 2 * C), F32), out((sz.share, C), F32),
                   out((sz.share, sz.extra), F32), out((8, C), F32), out((2, 8, 128), F32)),
        in_specs=[vm, vm, sm, hb, hb, hb, hb, hb] + [vm] * 10,
        out_specs=(hb,) * 7,
        scratch_shapes=scratch,
        compiler_params=pltpu.CompilerParams(collective_id=0, has_side_effects=True, vmem_limit_bytes=66000000),
        name="block",
    )(dest_slot.reshape(-1, 128), return_slot.reshape(-1, 128), lengths, block_in, cotangent, inner_weight, out_weight,
      state_weight, step_weight.T, conv_inner, conv_inner_bias.reshape(-1, 128), gate_gain.reshape(-1, 128), norm_gain.reshape(-1, 128), skip_gain[None],
      conv_state, conv_state_bias[None], step_bias[None], log_rate[None])
    results = pl.pallas_call(
        functools.partial(finish_kernel, sz),
        out_shape=(out((R, H), BF), out((R, H), BF), out((sz.share,), F32), out((sz.share, 2, C), F32),
                   out((sz.share, 2 * S), F32), out((sz.heads, sz.share), F32), out((4, C), F32), out((C,), F32),
                   out((4, 2 * S), F32), out((2 * S,), F32), out((sz.heads,), F32), out((sz.heads,), F32),
                   out((sz.heads,), F32), out((C,), F32), out((sz.share, C), F32)),
        in_specs=[vm] * 7,
        out_specs=(vm,) * 15,
        name="finish",
    )(rows_out, grads_out, inner_g, proj_g, extra_g, small, gain)
    return results[:5] + (results[5].T,) + results[6:14] + (results[14].T,)


def with_collectives(
    block_in,
    cotangent,
    lengths,
    dest_slot,
    return_slot,
    norm_gain,
    inner_weight,
    state_weight,
    step_weight,
    conv_inner,
    conv_inner_bias,
    conv_state,
    conv_state_bias,
    step_bias,
    log_rate,
    skip_gain,
    gate_gain,
    out_weight,
):
    groups = lax.axis_size("dp")
    group_rows = block_in.shape[0]
    half_width = block_in.shape[1]
    capacity = 2 * group_rows // groups
    own_group = lax.axis_index("dp")
    own_dest = lax.dynamic_slice_in_dim(dest_slot, own_group * group_rows, group_rows)
    own_return = lax.dynamic_slice_in_dim(return_slot, own_group * group_rows, group_rows)
    send_spot = send_layout(own_dest, group_rows, capacity, groups)
    back_spot = send_layout(own_return, group_rows, capacity, groups)
    slots_in = arrivals(dest_slot, group_rows, capacity, groups, own_group)
    slots_back = arrivals(return_slot, group_rows, capacity, groups, own_group)
    blank_rows = jnp.zeros((groups * capacity, half_width), jnp.bfloat16)
    packed_rows = blank_rows.at[send_spot].set(block_in).reshape(groups, capacity, half_width)
    packed_grads = blank_rows.at[back_spot].set(cotangent).reshape(groups, capacity, half_width)
    came_rows, came_grads = (
        lax.all_to_all(packed_rows, "dp", split_axis=0, concat_axis=0, tiled=True),
        lax.all_to_all(packed_grads, "dp", split_axis=0, concat_axis=0, tiled=True),
    )
    empty_rows = jnp.zeros((group_rows, half_width), jnp.bfloat16)
    own_rows = empty_rows.at[slots_in].set(came_rows.reshape(-1, half_width), mode="drop")
    own_grads = empty_rows.at[slots_back].set(came_grads.reshape(-1, half_width), mode="drop")
    full_rows, full_grads = (
        lax.all_gather(own_rows, "tensor", axis=1, tiled=True),
        lax.all_gather(own_grads, "tensor", axis=1, tiled=True),
    )
    seq_pos, live_mask, keep_state = stretch_layout(lengths[0], STRETCH)
    live_col = live_mask[:, None]
    hidden = full_rows.astype(jnp.float32)
    norm_scale = lax.rsqrt(jnp.mean(hidden * hidden, axis=1, keepdims=True) + EPSILON)
    normed = (hidden * norm_scale * norm_gain).astype(jnp.bfloat16)
    inner_local = inner_weight.shape[2]
    zx_weight = inner_weight.reshape(inner_weight.shape[0], 2 * inner_local)
    projected = jnp.dot(normed, zx_weight, preferred_element_type=jnp.float32)
    gate_raw = projected[:, :inner_local]
    conv_in_x = projected[:, inner_local:]
    conv_in_state = jnp.dot(normed, state_weight, preferred_element_type=jnp.float32)
    step_raw = jnp.dot(normed, step_weight, preferred_element_type=jnp.float32)
    x_conv = conv_forward(conv_in_x, conv_inner, conv_inner_bias, seq_pos)
    state_conv = conv_forward(conv_in_state, conv_state, conv_state_bias, seq_pos)
    x_act = jax.nn.silu(x_conv)
    state_act = jax.nn.silu(state_conv)
    state_width = state_act.shape[1] // 2
    heads_local = step_weight.shape[1]
    head_dim = inner_local // heads_local
    stretches = group_rows // STRETCH
    step_input = step_raw + step_bias[None, :]
    step_size = jax.nn.softplus(step_input) * live_col
    decay_rate = -jnp.exp(log_rate)
    skip_wide = jnp.repeat(skip_gain, head_dim)[None, :]
    scanned, saved = state_forward(
        x_act.reshape(group_rows, heads_local, head_dim),
        state_act[:, :state_width],
        state_act[:, state_width:],
        step_size,
        decay_rate,
        STRETCH,
    )
    mixed = scanned + skip_wide * x_act
    gate_act = jax.nn.silu(gate_raw)
    gated = mixed * gate_act
    inner_total = inner_local * lax.axis_size("tensor")
    square_sum = lax.psum(jnp.sum(gated * gated, axis=1), "tensor")
    gate_scale = lax.rsqrt(square_sum / inner_total + EPSILON)[:, None]
    gate_normed = (gated * gate_scale * gate_gain).astype(jnp.bfloat16)
    partial_out = jnp.dot(gate_normed, out_weight, preferred_element_type=jnp.float32)
    branch_half = lax.psum_scatter(partial_out, "tensor", scatter_dimension=1, tiled=True)
    half_index = lax.axis_index("tensor")
    out_half = (own_rows.astype(jnp.float32) + live_col * branch_half).astype(jnp.bfloat16)
    zero_row = jnp.zeros((1, half_width), jnp.bfloat16)
    reply_rows = jnp.concatenate([out_half, zero_row], axis=0)[slots_back]
    returned = lax.all_to_all(
        reply_rows.reshape(groups, capacity, half_width),
        "dp",
        split_axis=0,
        concat_axis=0,
        tiled=True,
    )
    block_out = returned.reshape(-1, half_width)[back_spot]
    owner_ct = full_grads.astype(jnp.float32)
    out_grad = (owner_ct * live_col).astype(jnp.bfloat16)
    out_weight_grad = jnp.einsum(
        "ti,td->id", gate_normed, out_grad, preferred_element_type=jnp.float32
    )
    normed_out_grad = jnp.einsum(
        "td,id->ti", out_grad, out_weight, preferred_element_type=jnp.float32
    )
    gate_gain_grad = jnp.sum(normed_out_grad * gated * gate_scale, axis=0)
    scaled_grad = gate_gain * normed_out_grad
    cross = lax.psum(jnp.sum(gated * scaled_grad, axis=1), "tensor")[:, None]
    gated_grad = gate_scale * scaled_grad - gated * gate_scale**3 * cross / inner_total
    mixed_grad = gated_grad * gate_act
    gate_raw_grad = gated_grad * mixed * silu_slope(gate_raw)
    skip_gain_grad = jnp.sum(
        (mixed_grad * x_act).reshape(group_rows, heads_local, head_dim), axis=(0, 2)
    )
    x_state_grad, written_grad, readout_grad, step_grad, rate_total = state_backward(
        saved, mixed_grad.reshape(stretches, STRETCH, heads_local, head_dim), decay_rate
    )
    x_act_grad = x_state_grad.reshape(group_rows, inner_local) + skip_wide * mixed_grad
    state_grad = lax.psum(
        jnp.concatenate(
            [written_grad.reshape(group_rows, -1), readout_grad.reshape(group_rows, -1)], axis=1
        ),
        "tensor",
    )
    state_conv_grad = state_grad * silu_slope(state_conv)
    x_conv_grad = x_act_grad * silu_slope(x_conv)
    state_raw_grad, conv_state_grad, conv_state_bias_grad = conv_backward(
        conv_in_state, conv_state, seq_pos, state_conv_grad
    )
    x_raw_grad, conv_inner_grad, conv_inner_bias_grad = conv_backward(
        conv_in_x, conv_inner, seq_pos, x_conv_grad
    )
    step_raw_grad = (
        step_grad.reshape(group_rows, heads_local) * live_col * jax.nn.sigmoid(step_input)
    )
    step_bias_grad = jnp.sum(step_raw_grad, axis=0)
    log_rate_grad = rate_total * decay_rate
    zx_low = jnp.concatenate([gate_raw_grad, x_raw_grad], axis=1).astype(jnp.bfloat16)
    state_low = state_raw_grad.astype(jnp.bfloat16)
    step_low = step_raw_grad.astype(jnp.bfloat16)
    inner_weight_grad = jnp.einsum(
        "td,tk->dk", normed, zx_low, preferred_element_type=jnp.float32
    )
    state_weight_grad = jnp.einsum(
        "td,tk->dk", normed, state_low, preferred_element_type=jnp.float32
    )
    step_weight_grad = jnp.einsum("td,tk->dk", normed, step_low, preferred_element_type=jnp.float32)
    lead_share = (half_index == 0).astype(jnp.float32)
    normed_grad = jnp.einsum("tk,dk->td", zx_low, zx_weight, preferred_element_type=jnp.float32)
    normed_grad = normed_grad + jnp.einsum(
        "tk,dk->td", step_low, step_weight, preferred_element_type=jnp.float32
    )
    normed_grad = normed_grad + lead_share * jnp.einsum(
        "tk,dk->td", state_low, state_weight, preferred_element_type=jnp.float32
    )
    normed_grad = lax.psum(normed_grad, "tensor")
    norm_gain_grad = jnp.sum(normed_grad * hidden * norm_scale, axis=0)
    input_scaled = norm_gain * normed_grad
    hidden_grad = (
        norm_scale * input_scaled
        - hidden * norm_scale**3 * jnp.mean(hidden * input_scaled, axis=1, keepdims=True)
        + owner_ct
    )
    own_grad = lax.dynamic_slice_in_dim(hidden_grad, half_index * half_width, half_width, 1).astype(
        jnp.bfloat16
    )
    answer_rows = jnp.concatenate([own_grad, zero_row], axis=0)[slots_in]
    gone = lax.all_to_all(
        answer_rows.reshape(groups, capacity, half_width),
        "dp",
        split_axis=0,
        concat_axis=0,
        tiled=True,
    )
    input_grad = gone.reshape(-1, half_width)[send_spot]
    (
        conv_inner_grad,
        conv_inner_bias_grad,
        conv_state_grad,
        conv_state_bias_grad,
        step_bias_grad,
        log_rate_grad,
        skip_gain_grad,
        gate_gain_grad,
    ) = lax.psum(
        (
            conv_inner_grad,
            conv_inner_bias_grad,
            conv_state_grad,
            conv_state_bias_grad,
            step_bias_grad,
            log_rate_grad,
            skip_gain_grad,
            gate_gain_grad,
        ),
        "dp",
    )
    zx_share, state_share, step_share, gain_share, out_share = (
        lax.psum_scatter(inner_weight_grad.astype(jnp.bfloat16), "dp", scatter_dimension=0, tiled=True),
        lax.psum_scatter(state_weight_grad, "dp", scatter_dimension=0, tiled=True),
        lax.psum_scatter(step_weight_grad, "dp", scatter_dimension=0, tiled=True),
        lax.psum_scatter(norm_gain_grad, "dp", scatter_dimension=0, tiled=True),
        lax.psum_scatter(out_weight_grad.astype(jnp.bfloat16), "dp", scatter_dimension=1, tiled=True),
    )
    zx_share = zx_share.astype(jnp.float32).reshape((-1,) + inner_weight.shape[1:])
    out_share = out_share.astype(jnp.float32)
    return (
        block_out,
        input_grad,
        gain_share,
        zx_share,
        state_share,
        step_share,
        conv_inner_grad,
        conv_inner_bias_grad,
        conv_state_grad,
        conv_state_bias_grad,
        step_bias_grad,
        log_rate_grad,
        skip_gain_grad,
        gate_gain_grad,
        out_share,
    )


def on_device(*args):
    groups = lax.axis_size("dp")
    rows, half = args[0].shape
    inner, heads, state = args[6].shape[2], args[8].shape[1], args[7].shape[1] // 2
    capacity = 2 * rows // groups
    fits = (
        groups == 16 and capacity % 16 == 0 and (2 * half // groups) % 16 == 0
        and rows == STRETCH and args[2].shape[1] == 1 and inner == 64 * heads and inner == 2 * half
    )
    if fits:
        return fused(Sizes(groups, rows, half, inner, heads, state, capacity), *args)
    return with_collectives(*args)


def solution(mesh):
    placed = (
        P("dp", "tensor"),
        P("dp", "tensor"),
        P("dp", None),
        P(),
        P(),
        P(),
        P(None, None, "tensor"),
        P(),
        P(None, "tensor"),
        P(None, "tensor"),
        P("tensor"),
        P(),
        P(),
        P("tensor"),
        P("tensor"),
        P("tensor"),
        P("tensor"),
        P("tensor", None),
    )
    return jax.shard_map(
        on_device,
        mesh=mesh,
        in_specs=placed,
        out_specs=(
            P("dp", "tensor"),
            P("dp", "tensor"),
            P("dp"),
            P("dp", None, "tensor"),
            P("dp", None),
            P("dp", "tensor"),
            P(None, "tensor"),
            P("tensor"),
            P(),
            P(),
            P("tensor"),
            P("tensor"),
            P("tensor"),
            P("tensor"),
            P("tensor", "dp"),
        ),
        check_vma=False,
    )
```

```python
import functools

import jax
import jax.numpy as jnp
from jax import lax
from jax.experimental import pallas as pl
from jax.experimental.pallas import tpu as pltpu
from jax.sharding import PartitionSpec as P

STRETCH = 256


PRECISE = lax.Precision.HIGHEST
EPSILON = 1e-05


def silu_slope(values):
    logistic = jax.nn.sigmoid(values)
    return logistic * (1.0 + values * (1.0 - logistic))


def stretch_layout(seq_lengths, stretch_rows):
    total_stretches = seq_lengths.shape[0]
    numbers = jnp.arange(total_stretches, dtype=jnp.int32)
    begins = seq_lengths > 0
    first_stretch = jnp.max(
        jnp.where(begins[None, :] & (numbers[None, :] <= numbers[:, None]), numbers[None, :], 0),
        axis=1,
    )
    seq_length = jnp.sum(
        jnp.where(numbers[None, :] == first_stretch[:, None], seq_lengths[None, :], 0), axis=1
    )
    within = (
        jnp.arange(stretch_rows, dtype=jnp.int32)[None, :]
        + ((numbers - first_stretch) * stretch_rows)[:, None]
    )
    live_mask = (within < seq_length[:, None]).astype(jnp.float32).reshape(-1)
    keep_state = 1.0 - begins.astype(jnp.float32)
    return (within.reshape(-1), live_mask, keep_state)


def shift_down(values, steps):
    return jnp.concatenate(
        [jnp.zeros((steps,) + values.shape[1:], values.dtype), values[:-steps]], axis=0
    )


def shift_up(values, steps):
    return jnp.concatenate(
        [values[steps:], jnp.zeros((steps,) + values.shape[1:], values.dtype)], axis=0
    )


def conv_forward(raw_in, tap_weights, tap_bias, seq_pos):
    total = tap_bias[None, :] + tap_weights[0][None, :] * raw_in
    for tap_index in range(1, tap_weights.shape[0]):
        valid = (seq_pos >= tap_index).astype(jnp.float32)[:, None]
        total = total + tap_weights[tap_index][None, :] * shift_down(raw_in, tap_index) * valid
    return total


def conv_backward(raw_in, tap_weights, seq_pos, conv_grad):
    tap_grads = [jnp.sum(conv_grad * raw_in, axis=0)]
    raw_grad = tap_weights[0][None, :] * conv_grad
    for tap_index in range(1, tap_weights.shape[0]):
        masked = conv_grad * (seq_pos >= tap_index).astype(jnp.float32)[:, None]
        tap_grads.append(jnp.sum(masked * shift_down(raw_in, tap_index), axis=0))
        raw_grad = raw_grad + tap_weights[tap_index][None, :] * shift_up(masked, tap_index)
    return (raw_grad, jnp.stack(tap_grads, axis=0), jnp.sum(conv_grad, axis=0))


def send_layout(targets, group_rows, capacity, groups):
    owner_group = targets // group_rows
    onehot = (owner_group[:, None] == jnp.arange(groups, dtype=jnp.int32)[None, :]).astype(
        jnp.int32
    )
    arrival = jnp.sum(jnp.cumsum(onehot, axis=0) * onehot, axis=1) - 1
    return owner_group * capacity + arrival


def arrivals(targets, group_rows, capacity, groups, own_group):
    by_source = targets.reshape(groups, group_rows)
    owner_group = by_source // group_rows
    is_mine = (owner_group == own_group).astype(jnp.int32)
    arrival = jnp.cumsum(is_mine, axis=1) - 1
    position = jnp.arange(groups, dtype=jnp.int32)[:, None] * capacity + arrival
    position = jnp.where(is_mine > 0, position, groups * capacity)
    filler = jnp.full((groups * capacity,), group_rows, jnp.int32)
    return filler.at[position.reshape(-1)].set(
        (by_source - owner_group * group_rows).reshape(-1), mode="drop"
    )


def state_forward(x_heads, written, readout, step_size, decay_rate, stretch_rows):
    rows_all, heads, head_dim = x_heads.shape
    stretches = rows_all // stretch_rows
    x_blocks = x_heads.reshape(stretches, stretch_rows, heads, head_dim)
    w_blocks = written.reshape(stretches, stretch_rows, -1)
    r_blocks = readout.reshape(stretches, stretch_rows, -1)
    step_blocks = step_size.reshape(stretches, stretch_rows, heads)
    log_decay = jnp.cumsum(step_blocks * decay_rate[None, None, :], axis=1)
    by_head = jnp.transpose(log_decay, (0, 2, 1))
    causal = jnp.arange(stretch_rows)[:, None] >= jnp.arange(stretch_rows)[None, :]
    spread = by_head[:, :, :, None] - by_head[:, :, None, :]
    fading = jnp.where(causal, jnp.exp(jnp.where(causal, spread, 0.0)), 0.0)
    intersection = jnp.einsum("cin,cjn->cij", r_blocks, w_blocks, precision=PRECISE)
    mixing = intersection[:, None, :, :] * fading
    driven = step_blocks[..., None] * x_blocks
    to_end = jnp.exp(log_decay[:, -1:, :] - log_decay)
    stretch_state = jnp.einsum(
        "cjhp,cjn->chpn", to_end[..., None] * driven, w_blocks, precision=PRECISE
    )
    end_fade = jnp.exp(log_decay[:, -1, :])
    running = jnp.zeros(stretch_state.shape[1:], jnp.float32)
    entering = []
    entering.append(running)
    entering = jnp.stack(entering)
    from_start = jnp.exp(log_decay)
    carried_out = from_start[..., None] * jnp.einsum(
        "chpn,cin->cihp", entering, r_blocks, precision=PRECISE
    )
    inner_out = jnp.einsum("chij,cjhp->cihp", mixing, driven, precision=PRECISE)
    saved = (
        x_blocks,
        w_blocks,
        r_blocks,
        step_blocks,
        causal,
        fading,
        mixing,
        driven,
        to_end,
        entering,
        end_fade,
        from_start,
        carried_out,
    )
    return ((inner_out + carried_out).reshape(rows_all, heads * head_dim), saved)


def state_backward(saved, mixed_grad, decay_rate):
    (
        x_blocks,
        w_blocks,
        r_blocks,
        step_blocks,
        causal,
        fading,
        mixing,
        driven,
        to_end,
        entering,
        end_fade,
        from_start,
        carried_out,
    ) = saved
    stretches = x_blocks.shape[0]
    scaled = from_start[..., None] * mixed_grad
    readout_grad = jnp.einsum("cihp,chpn->cin", scaled, entering, precision=PRECISE)
    from_out = jnp.einsum("cihp,cin->chpn", scaled, r_blocks, precision=PRECISE)
    decay_grad = jnp.sum(carried_out * mixed_grad, axis=3)
    downstream = jnp.zeros(from_out.shape[1:], jnp.float32)
    passed = []
    end_grads = []
    for number in reversed(range(stretches)):
        handed = jnp.zeros_like(downstream)
        passed.append(handed)
        end_grads.append(jnp.sum(handed * entering[number], axis=(1, 2)))
        downstream = from_out[number] + end_fade[number][:, None, None] * handed
    passed = jnp.stack(passed[::-1])
    end_grads = jnp.stack(end_grads[::-1])
    pulled = jnp.einsum("chpn,cjn->cjhp", passed, w_blocks, precision=PRECISE)
    driven_grad = to_end[..., None] * pulled
    written_grad = jnp.einsum(
        "cjhp,chpn->cjn", to_end[..., None] * driven, passed, precision=PRECISE
    )
    tail_grad = jnp.sum(pulled * driven, axis=3) * to_end
    decay_grad = decay_grad - tail_grad
    last_extra = jnp.sum(tail_grad, axis=1) + end_grads * end_fade
    mixing_grad = jnp.where(
        causal, jnp.einsum("cihp,cjhp->chij", mixed_grad, driven, precision=PRECISE), 0.0
    )
    driven_grad = driven_grad + jnp.einsum("chij,cihp->cjhp", mixing, mixed_grad, precision=PRECISE)
    intersection_grad = jnp.sum(mixing_grad * fading, axis=1)
    readout_grad = readout_grad + jnp.einsum(
        "cij,cjn->cin", intersection_grad, w_blocks, precision=PRECISE
    )
    written_grad = written_grad + jnp.einsum(
        "cij,cin->cjn", intersection_grad, r_blocks, precision=PRECISE
    )
    product = mixing_grad * mixing
    decay_grad = decay_grad + jnp.transpose(
        jnp.sum(product, axis=3) - jnp.sum(product, axis=2), (0, 2, 1)
    )
    decay_grad = decay_grad.at[:, -1, :].add(last_extra)
    step_grad = jnp.sum(driven_grad * x_blocks, axis=3)
    x_state_grad = step_blocks[..., None] * driven_grad
    rate_grad = jnp.flip(jnp.cumsum(jnp.flip(decay_grad, axis=1), axis=1), axis=1)
    step_grad = step_grad + rate_grad * decay_rate[None, None, :]
    rate_total = jnp.sum(rate_grad * step_blocks, axis=(0, 1))
    return (x_state_grad, written_grad, readout_grad, step_grad, rate_total)


MESH = pl.DeviceIdType.MESH
BF = jnp.bfloat16
F32 = jnp.float32
NEG = -1e30


def dot_nn(a, b):
    return lax.dot_general(a, b, (((1,), (0,)), ((), ())), preferred_element_type=F32)


def dot_nt(a, b):
    return lax.dot_general(a, b, (((1,), (1,)), ((), ())), preferred_element_type=F32)


def dot_tn(a, b):
    return lax.dot_general(a, b, (((0,), (0,)), ((), ())), preferred_element_type=F32)


def iota(shape, axis):
    return lax.broadcasted_iota(jnp.int32, shape, axis)


def one_hot(cond):
    return jnp.where(cond, 1.0, 0.0).astype(BF)


def split3(v):
    high = v.astype(BF)
    rest = v - high.astype(F32)
    mid = rest.astype(BF)
    return high, mid, (rest - mid.astype(F32)).astype(BF)


def sigmoid(v):
    return 1.0 / (1.0 + jnp.exp(-v))


def rows_down(v, k):
    return jnp.where(iota(v.shape, 0) >= k, pltpu.roll(v, k, 0), 0.0)


def rows_up(v, k):
    n = v.shape[0]
    return jnp.where(iota(v.shape, 0) < n - k, pltpu.roll(v, n - k, 0), 0.0)


def pick(v, lane, index):
    return jnp.sum(jnp.where(lane == index, v, 0.0), axis=1, keepdims=True)


class Sizes:
    def __init__(self, dp, rows, half, inner, heads, state, capacity):
        self.dp, self.rows, self.half, self.inner = dp, rows, half, inner
        self.heads, self.state, self.cap = heads, state, capacity
        self.width = 2 * half
        self.nz = dp // 4
        self.share = self.width // dp
        self.quarter = self.nz * self.share
        self.slots = dp * capacity
        self.tiles = inner // 128
        self.extra = 2 * state + 128
        self.cols = 3 * inner + self.extra
        n = inner // 2
        sizes = [n // 3 * 2, n // 3 * 4, n, n, n, n // 2, n // 2, self.extra]
        self.chunks = [(sum(sizes[:k]), size) for k, size in enumerate(sizes)]
        self.levels = self.nz.bit_length() - 1


def targets_of(lines, sz):
    n = sz.rows // 128
    return jnp.concatenate([lines[pl.ds(k, sz.dp, stride=n), :] for k in range(n)], axis=1)


def send_table(targets, g, sz):
    strict = one_hot(iota((sz.rows, sz.rows), 0) < iota((sz.rows, sz.rows), 1))
    every = targets_of(targets, sz)
    own = jnp.sum(jnp.where(iota(every.shape, 0) == g, every, 0), axis=0, keepdims=True)
    group = lax.shift_right_logical(own, 8)
    hot = jnp.where(iota((sz.dp, sz.rows), 0) == group, 1.0, 0.0)
    before = dot_nn(hot.astype(BF), strict)
    rank = jnp.sum(hot * before, axis=0, keepdims=True)
    spot = group.astype(F32) * sz.cap + rank
    return one_hot(iota((sz.slots, sz.rows), 0).astype(F32) == spot)


def owner_table(targets, g, sz):
    strict = one_hot(iota((sz.rows, sz.rows), 0) < iota((sz.rows, sz.rows), 1))
    every = targets_of(targets, sz)
    mine = jnp.where(lax.shift_right_logical(every, 8) == g, 1.0, 0.0)
    rank = dot_nn(mine.astype(BF), strict)
    slot = mine * ((every & 255) + 1).astype(F32)
    lane = iota((sz.dp, 128), 1)
    found = jnp.zeros((sz.dp, 128), F32)
    for a in range(sz.cap):
        one = jnp.sum(jnp.where(rank == float(a), slot, 0.0), axis=1, keepdims=True)
        found = jnp.where(lane == a, one, found)
    place = iota((128, sz.slots), 1)
    spread = one_hot((place % sz.cap) == iota((128, sz.slots), 0))
    wide = dot_nn(found.astype(BF), spread)
    keep = (iota((sz.dp, sz.slots), 1) // sz.cap) == iota((sz.dp, sz.slots), 0)
    row = jnp.sum(jnp.where(keep, wide, 0.0), axis=0, keepdims=True) - 1.0
    return one_hot(iota((sz.rows, sz.slots), 0).astype(F32) == row)


def block_kernel(sz, *refs):
    (dest, back, length, rows_hbm, ct_hbm, win_hbm, wout_hbm, wst_hbm, wstep_in,
     tap_x, bias_x, gain_g, gain_n, skip_in, tap_s, bias_s, bias_step, log_rate,
     out_rows, out_grads, inner_out, proj_out, extra_out, small_out, gain_out,
     win, wout, wst, wstep, lines,
     pk_in, pk_ct, rc_in, rc_ct, gn_o, gn_g,
     p_own, q_in, q_bk,
     hid, cts, normed, lowct, perm, xA, xE, tA, tE,
     yb, pb, r0, r1, f_inner, f_proj, f_extra,
     inter, igrad, ptile,
     sraw, sslope, wr, dtv, lac, lar, sgr, rgr, stepsig, acc1, acc2, scale,
     stat_s, stat_r, half_s, half_r, raw_r, st_s, st_r,
     sms, smr, gall, gsum,
     a2a_s, a2a_r, fw_s, fw_r, quad_s, quad_r, xq_s, xq_r, z_s, z_r, y_s, y_r, gg_s, gg_r, sm_s, sm_r, w_s, own_s, relay_s, raw_sem, o_s, taken) = refs
    dp, R, H, C = sz.dp, sz.rows, sz.half, sz.inner
    W, NT_ = sz.width, sz.tiles
    g = lax.axis_index("dp")
    t = lax.axis_index("tensor")
    o = 1 - t
    c, x, z = g % 2, (g // 2) % 2, g // 4
    q = g % 4
    sib, xp = g + 1 - 2 * c, g + 2 - 4 * x
    diag = sib + 2 - 4 * x

    def rcopy(src, dst, ss, rs, peer, side=None):
        return pltpu.make_async_remote_copy(
            src_ref=src, dst_ref=dst, send_sem=ss, recv_sem=rs,
            device_id=(peer, t if side is None else side), device_id_type=MESH)

    sent = []

    def go(copy):
        copy.start()
        sent.append(copy)
        return copy

    loads = [pltpu.make_async_copy(a, b, w_s.at[i]) for i, (a, b) in enumerate(
        [(rows_hbm, lowct.at[:, pl.ds(0, H)]), (ct_hbm, lowct.at[:, pl.ds(H, H)]), (wst_hbm, wst), (wout_hbm, wout)])]
    for load in loads[:2]:
        load.start()

    barrier = pltpu.get_barrier_semaphore()
    for off in range(1, dp):
        pl.semaphore_signal(barrier, inc=1, device_id=((g + off) % dp, t), device_id_type=MESH)
    pl.semaphore_signal(barrier, inc=1, device_id=(g, o), device_id_type=MESH)

    side = z // 2
    zo, zi, fi, fo = 3 * side, 1 + side, 2 - side, 3 - 3 * side
    is_outer = (z + side + 1) % 2
    is_inner = 1 - is_outer
    far = [
        ((z + dz) % sz.nz) * 4 + ((x + dx) % 2) * 2 + (c + dc) % 2
        for dz in (2, 1, 3, 0) for dx in (1, 0) for dc in (1, 0) if dz + dx + dc]
    level = [z * 4 + ((x + dx) % 2) * 2 + (c + dc) % 2 for dx, dc in ((1, 1), (1, 0), (0, 1))]
    across = [zz * 4 + ((x + dx) % 2) * 2 + (c + dc) % 2 for zz in (fo, fi) for dx in (1, 0) for dc in (1, 0)]
    beside_z = is_outer * zi + (1 - is_outer) * zo
    beside = [beside_z * 4 + ((x + dx) % 2) * 2 + (c + dc) % 2 for dx, dc in ((1, 1), (1, 0), (0, 1))]
    partner = beside_z * 4 + q
    parts = [pl.ds(k * (H // 3), H // 3) for k in range(3)]

    def span(ref, n, ss, rs, at=slice(None)):
        return rcopy(ref.at[pl.ds(0, n), :, at], ref.at[pl.ds(0, n), :, at], ss, rs, partner)

    def exchange(i, source, target, at=slice(None)):
        for peer in far:
            rcopy(source.at[peer, :, at], target.at[g, :, at], a2a_s.at[i], a2a_r.at[i], peer).start()

    def settle(copies):
        for copy in copies:
            copy.wait_send()

    def arrived(i, target, at=slice(None)):
        span(target, dp - 1, a2a_s.at[i], a2a_r.at[i], at).wait_recv()

    def answer(table, value, dst):
        for k in range(2):
            n = sz.slots // 2
            part = dot_tn(table[:, k * n:(k + 1) * n], value).astype(BF)
            dst[k * (dp // 2):(k + 1) * (dp // 2)] = part.reshape(dp // 2, sz.cap, H)

    def block_to(i, source, target, peer, owner, sems):
        return rcopy(source.at[peer], target.at[owner], sems.at[i - 4], a2a_r.at[i + 2], peer)

    def raw_copy(i):
        return rcopy(lowct.at[:, pl.ds((i - 4) * H, H)], raw_r, raw_sem.at[0, i - 4], raw_sem.at[1, i - 4], partner)

    def near_x(peers, same):
        if len(peers) == 3:
            return peers[2:] if same else peers[:2]
        return [peer for k, peer in enumerate(peers) if (k % 4 >= 2) == same]

    def reply_send(i, packed, target, same):
        @pl.when(is_outer == 0)
        def _():
            for peer in near_x(across, same) + near_x(beside, same) + ([partner] if same else []):
                block_to(i, packed, target, peer, g, own_s).start()
        for peer in near_x(level, same):
            block_to(i, packed, target, peer, g, own_s).start()

    def reply(i, table, value, packed, target):
        answer(table, value, packed)
        target[pl.ds(g, 1)] = packed[pl.ds(g, 1)]

        @pl.when(is_outer == 1)
        def _():
            if i == 5:
                pl.semaphore_wait(taken, 1)
            lowct[:, (i - 4) * H:(i - 3) * H] = value
            raw_copy(i).start()

    def relay_send(i, packed, target, same):
        @pl.when(is_outer == 0)
        def _():
            for peer in near_x(across, same) + near_x(level, same):
                block_to(i, packed, target, peer, partner, relay_s).start()

    def relay(i, targets, packed, target):
        @pl.when(is_outer == 0)
        def _():
            raw_copy(i).wait_recv()
            answer(owner_table(targets, partner, sz), raw_r[...], packed)
            if i == 4:
                pl.semaphore_signal(taken, inc=1, device_id=(partner, t), device_id_type=MESH)
            target[pl.ds(partner, 1)] = packed[pl.ds(g, 1)]

    def replied(i, target):
        @pl.when(is_outer == 1)
        def _():
            span(target, dp - 1, own_s.at[i - 4], a2a_r.at[i + 2]).wait_recv()

        @pl.when(is_outer == 0)
        def _():
            span(target, dp - 2, own_s.at[i - 4], a2a_r.at[i + 2]).wait_recv()

    def reply_settle(i, packed):
        @pl.when(is_outer == 1)
        def _():
            span(packed, len(level), own_s.at[i - 4], a2a_r.at[i + 2]).wait_send()

        @pl.when(is_outer == 0)
        def _():
            span(packed, dp - 1, own_s.at[i - 4], a2a_r.at[i + 2]).wait_send()
            span(packed, len(across + level), relay_s.at[i - 4], a2a_r.at[i + 2]).wait_send()

    def pack(table, source, target):
        for k in range(2):
            n = sz.slots // 2
            part = dot_nn(table[k * n:(k + 1) * n, :], source[...]).astype(BF)
            target[k * (dp // 2):(k + 1) * (dp // 2)] = part.reshape(dp // 2, sz.cap, H)

    def unpack(i, table, source, full, part):
        at = parts[part]
        arrived(3 * i + part, source, at)
        n = at.size
        full[pl.ds(t, 1), :, at] = dot_nn(table[...], source[:, :, at].reshape(sz.slots, n)).astype(BF)[None]
        go(rcopy(full.at[t, :, at], full.at[t, :, at], fw_s.at[i, part], fw_r.at[i, part], g, o))

    def other_half(i, full):
        for part in range(3):
            at = parts[part]
            rcopy(full.at[o, :, at], full.at[o, :, at], fw_s.at[i, part], fw_r.at[i, part], g, o).wait_recv()

    def take_apart(stage, sems):
        n, held = W // 128, stage.shape[0]
        fetch = [
            pltpu.make_async_copy(win_hbm.at[pl.ds(k * 128, 128)], stage.at[k % held], sems.at[k % held]) for k in range(n)]
        for copy in fetch[:held] + loads[2:]:
            copy.start()
        p_own[...] = send_table(dest, g, sz)
        loads[0].wait()
        pack(p_own, lowct.at[:, pl.ds(0, H)], pk_in)
        pl.semaphore_wait(barrier, dp)
        for k in range(3):
            exchange(k, pk_in, rc_in, parts[k])
        rc_in[pl.ds(g, 1)] = pk_in[pl.ds(g, 1)]
        p_own[...] = send_table(back, g, sz)
        loads[1].wait()
        pack(p_own, lowct.at[:, pl.ds(H, H)], pk_ct)
        rc_ct[pl.ds(g, 1)] = pk_ct[pl.ds(g, 1)]
        q_in[...] = owner_table(dest, g, sz)
        q_bk[...] = owner_table(back, g, sz)
        place = iota((256, 256), 0)
        order = one_hot(iota((256, 256), 1) == jnp.where(place < 128, 2 * place, 2 * place - 255))
        for k in range(n):
            fetch[k].wait()
            for m in range(0, C, 256):
                pair = jnp.concatenate(
                    [stage[k % held, :, :, m + e:m + e + 128].reshape(256, 128) for e in (0, 128)], axis=1)
                both = dot_nn(order, pair).astype(BF)
                win[k * 128:(k + 1) * 128, m:m + 256] = both[:128]
                win[k * 128:(k + 1) * 128, C + m:C + m + 256] = both[128:]
            if k + held < n:
                fetch[k + held].start()

    pl.run_scoped(take_apart, pltpu.VMEM((10, 128, 2, C), BF), pltpu.SemaphoreType.DMA((10,)))
    for k in range(3):
        unpack(0, q_in, rc_in, hid, k)
    for k in range(3):
        exchange(3 + k, pk_ct, rc_ct, parts[k])
    other_half(0, hid)

    total = jnp.zeros((R, 128), F32)
    for k in range(W // 128):
        v = hid[k // (H // 128), :, (k % (H // 128)) * 128:(k % (H // 128)) * 128 + 128].astype(F32)
        total = total + v * v
    norm_scale = lax.rsqrt(jnp.sum(total, axis=1, keepdims=True) / W + EPSILON)
    scale[...] = jnp.broadcast_to(norm_scale, (R, 128))
    for k in range(W // 128):
        v = hid[k // (H // 128), :, (k % (H // 128)) * 128:(k % (H // 128)) * 128 + 128].astype(F32)
        normed[:, k * 128:(k + 1) * 128] = (v * scale[...] * gain_n[k:k + 1, :]).astype(BF)

    def quarters(source):
        for qq in range(4):
            perm[qq] = jnp.concatenate(
                [source[:, sz.share * (4 * zz + qq):sz.share * (4 * zz + qq + 1)] for zz in range(sz.nz)], axis=1)

    def send_quarter(i, dst):
        copies = [
            rcopy(perm.at[peer % 4], dst.at[rel], xq_s.at[i, rel - 1], xq_r.at[i, rel - 1], peer)
            for rel, peer in ((2, xp), (3, diag), (1, sib))]
        for copy in copies:
            copy.start()
        dst[0:1] = perm[pl.ds(q, 1)]
        return copies

    def turn_quarter(dst, turned):
        for rel, peer in ((1, sib), (2, xp), (3, diag)):
            rcopy(dst.at[rel], dst.at[rel], xq_s.at[0, rel - 1], xq_r.at[0, rel - 1], peer).wait_recv()
        for rel in range(4):
            turned[:, rel * R:(rel + 1) * R] = jnp.transpose(dst[rel].astype(F32)).astype(BF)

    def fold_half(which, place):
        value = cts[pl.ds(which, 1)][0]
        for qq in range(4):
            cut = jnp.concatenate(
                [value[:, sz.share * (4 * zz + qq):sz.share * (4 * zz + qq + 1)] for zz in range(sz.nz // 2)], axis=1)
            cut = jnp.where(iota(cut.shape, 0) < length[0, 0], cut.astype(F32), 0.0).astype(BF)
            perm[qq, place * (R // 2):(place + 1) * (R // 2)] = jnp.concatenate([cut[:R // 2], cut[R // 2:]], axis=1)

    def fold_copy(sem, quarter, place, half, rel, peer, to):
        return rcopy(perm.at[quarter, pl.ds(place * (R // 2), R // 2)], xE.at[half, rel], xq_s.at[1, sem], xq_r.at[1, sem], peer, to)

    def fold_pass(rel, half):
        return rcopy(xE.at[half, rel], xE.at[half, rel], xq_s.at[1, 2 + rel], xq_r.at[1, 2 + rel], g, o)

    def turn_folds():
        fold_copy(0, 0, 0, t, 1, sib, t).wait_recv()
        fold_copy(3, 0, 0, o, 1, sib, t).wait_recv()
        for rel in (2, 3):
            fold_pass(rel, o).wait_recv()
        n = sz.quarter // 2
        for half in range(2):
            for rel in range(4):
                flat = jnp.transpose(xE[half, rel].astype(F32)).astype(BF)
                tE[half * n:(half + 1) * n, rel * R:rel * R + R // 2] = flat[:n]
                tE[half * n:(half + 1) * n, rel * R + R // 2:(rel + 1) * R] = flat[n:]

    quarters(normed)
    quarter_away = send_quarter(0, xA)

    loads[2].wait()
    wstep[...] = jnp.zeros_like(wstep)
    wstep[:sz.heads] = wstep_in[...]
    lines[...] = jnp.zeros_like(lines)
    lines[0:1, :sz.heads] = bias_step[...]
    lines[1:2, :sz.heads] = log_rate[...]
    row = iota((R, 128), 0)
    lane = iota((R, 128), 1)
    live = jnp.where(row < length[0, 0], 1.0, 0.0)
    sraw[...] = dot_nn(normed[...], wst[...])
    step_in = dot_nt(normed[...], wstep[...]) + lines[0:1, :]
    S = sz.state
    for k in range(2):
        cut = slice(k * S, (k + 1) * S)
        raw = sraw[:, cut]
        conv = bias_s[:, cut] + tap_s[0:1, cut] * raw
        for tap in range(1, 4):
            conv = conv + tap_s[tap:tap + 1, cut] * rows_down(raw, tap)
        sg = sigmoid(conv)
        sslope[:, cut] = sg * (1.0 + conv * (1.0 - sg))
        wr[:, cut] = (conv * sg).astype(BF)
    written, readout = wr[:, :S], wr[:, S:]
    inter[...] = dot_nt(readout, written)
    stepsig[...] = sigmoid(step_in) * live
    heads_live = jnp.where(lane < sz.heads, live, 0.0)
    step = (jnp.maximum(step_in, 0.0) + jnp.log1p(jnp.exp(-jnp.abs(step_in)))) * heads_live
    rate = -jnp.exp(lines[1:2, :])
    dtv[...] = step
    lower = one_hot(iota((R, R), 0) >= iota((R, R), 1))
    log_decay = sum(dot_nn(lower, part) for part in split3(step * rate))
    lac[...] = log_decay
    lar[...] = jnp.transpose(log_decay)

    def cols_of(i):
        return pl.ds(sz.chunks[i][0], sz.chunks[i][1])

    def quad_send(i):
        at = cols_of(i)
        rcopy(yb.at[0, :, at], yb.at[2, :, at], quad_s.at[1], quad_r.at[i, 1], xp).start()
        rcopy(yb.at[0, :, at], yb.at[1, :, at], quad_s.at[0], quad_r.at[i, 0], sib).start()

    def quad_pass(i):
        at = cols_of(i)
        rcopy(yb.at[2, :, at], yb.at[2, :, at], quad_s.at[1], quad_r.at[i, 1], xp).wait_recv()
        rcopy(yb.at[2, :, at], yb.at[3, :, at], quad_s.at[2], quad_r.at[i, 2], sib).start()

    def z_copy(i, k):
        at = cols_of(i)
        column = g % 4
        if k < 3:
            block, slot, peer = (zi, fi, fo)[k], r0.at[k], zi
        elif k < 5:
            block, slot, peer = (fi, fo)[k - 3], r1.at[k - 3], fi
        else:
            block, slot, peer = zo, r0.at[0], zo
        return rcopy(pb.at[block, :, at], slot.at[:, at], z_s, z_r.at[i, k], peer * 4 + column)

    def z_wait(i, k):
        at = cols_of(i)
        slot = r0.at[k] if k < 3 else r1.at[k - 3] if k < 5 else r0.at[0]
        rcopy(slot.at[:, at], slot.at[:, at], z_s, z_r.at[i, k], g + 4 - 8 * (z // 3)).wait_recv()

    def each_tile(i, block, landed, keep):
        start, size = sz.chunks[i]
        for n in range(0, size, 128):
            cut = slice(start + n, start + n + 128)
            value = pb[pl.ds(block, 1), :, cut].astype(F32)[0] + landed[:, cut].astype(F32)
            if keep:
                pb[pl.ds(block, 1), :, cut] = value.astype(BF)[None]
            elif start + n < C:
                f_proj[:, cut] = value
            elif start + n < 3 * C:
                f_inner[:, start + n - C:start + n - C + 128] = value
            else:
                f_extra[:, start + n - 3 * C:start + n - 3 * C + 128] = value

    def z_first(i):
        @pl.when(is_outer == 1)
        def _():
            for k in range(3):
                z_copy(i, 2 - k).start()

    def z_second(i):
        @pl.when(is_outer == 0)
        def _():
            for k in (2, 1):
                z_wait(i, k)
                each_tile(i, (zi, fi, fo)[k], r0.at[k], True)
                z_copy(i, 2 + k).start()
            z_wait(i, 0)
            each_tile(i, zi, r0.at[0], True)

    def z_third(i):
        @pl.when(is_outer == 0)
        def _():
            z_wait(i, 4)
            each_tile(i, zo, r1.at[1], True)
            z_copy(i, 5).start()
            z_wait(i, 3)
            each_tile(i, zi, r1.at[0], False)

    def z_fourth(i):
        @pl.when(is_outer == 1)
        def _():
            z_wait(i, 5)
            each_tile(i, zo, r0.at[0], False)

    def write_out(i):
        start, size = sz.chunks[i]
        if i < 2:
            pairs = [(f_proj.at[:, pl.ds(start, size)], proj_out.at[:, pl.ds(start, size)])]
        elif i < 7:
            cut = pl.ds(start - C, size)
            pairs = [(f_inner.at[:, cut], inner_out.at[:, cut])]
        else:
            pairs = [(f_extra, extra_out)]
        copies = [pltpu.make_async_copy(a, b, o_s.at[i]) for a, b in pairs]
        for copy in copies:
            copy.start()
        return copies

    def settle_sums():
        for k in range(3):
            rcopy(yb.at[0], yb.at[0], quad_s.at[k], quad_r.at[0, k], sib).wait_send()
        rcopy(r0, r0, z_s, z_r.at[0, 0], partner).wait_send()

    def partial_sum(i, turned):
        at = cols_of(i)
        start, size = sz.chunks[i]
        rcopy(yb.at[1, :, at], yb.at[1, :, at], quad_s.at[0], quad_r.at[i, 0], sib).wait_recv()
        rcopy(yb.at[3, :, at], yb.at[3, :, at], quad_s.at[2], quad_r.at[i, 2], sib).wait_recv()
        n = 384 if size % 256 else 256

        def body(k, carry):
            at = pl.ds(pl.multiple_of(start + k * n, 128), n)
            part = dot_nn(turned[...], yb[:, :, at].reshape(4 * R, n))
            pb[:, :, at] = part.astype(BF).reshape(sz.nz, sz.share, n)
            return carry
        lax.fori_loop(0, size // n, body, 0)
        z_first(i)

    def remainder(gr, xr, xa, xs, mx, ng):
        def project(dst, base):
            def body(n, carry):
                at = pl.multiple_of(n * 256, 256)
                dst[:, pl.ds(at, 256)] = dot_nn(normed[...], win[:, pl.ds(pl.multiple_of(base + n * 256, 256), 256)])
                return carry
            lax.fori_loop(0, C // 256, body, 0)

        project(xr, C)
        project(gr, 0)

        unpack(1, q_bk, rc_ct, cts, 0)

        def lanes(p):
            return pl.ds(pl.multiple_of(p * 128, 128), 128)

        B = 64

        def head_line(v, p):
            first = iota((1, 128), 1) < 64
            spot = iota(v.shape, 1)
            return jnp.where(first, pick(v, spot, 2 * p), pick(v, spot, 2 * p + 1))

        def step_columns(p, lane):
            first = lane < 64
            return jnp.where(first, pick(dtv[...], lane, 2 * p), pick(dtv[...], lane, 2 * p + 1))

        acc1[...] = jnp.zeros_like(acc1)
        acc2[...] = jnp.zeros_like(acc2)

        def scan(p, carry):
            at = lanes(p)
            lane = iota((R, 128), 1)
            raw = xr[:, at]
            conv = bias_x[pl.ds(p, 1), :] + tap_x[0:1, at] * raw
            for tap in range(1, 4):
                conv = conv + tap_x[tap:tap + 1, at] * rows_down(raw, tap)
            sg = sigmoid(conv)
            act = conv * sg
            xa[:, at] = act
            xs[:, at] = (sg * (1.0 + conv * (1.0 - sg))).astype(BF)
            driven = act * step_columns(p, lane)
            parts = [jnp.where(lane < 64, driven, 0.0).astype(BF), jnp.where(lane >= 64, driven, 0.0).astype(BF)]
            cols = [pick(lac[...], lane, 2 * p + k) for k in range(2)]
            skip = head_line(skip_in[...], p)
            for b in range(R // B):
                reach = 128 * ((b * B) // 128 + 1)
                cut = slice(b * B, (b + 1) * B)
                causal = iota((B, reach), 0) + b * B >= iota((B, reach), 1)
                mixed = skip * act[cut]
                for k in range(2):
                    spread = cols[k][cut] - lar[pl.ds(2 * p + k, 1), :][:, :reach]
                    fading = jnp.exp(jnp.where(causal, spread, NEG))
                    mixing = (inter[cut, :reach] * fading).astype(BF)
                    mixed = mixed + dot_nn(mixing, parts[k][:reach])
                mx[cut, at] = mixed
                gate = gr[cut, at]
                gated = mixed * gate * sigmoid(gate)
                acc1[cut] += gated * gated
            return carry

        lax.fori_loop(0, NT_, scan, 0)

        whole = float(2 * C)

        def total_over_sides(i, value):
            stat_s[i] = jnp.transpose(jnp.where(lane == 0, jnp.sum(value, axis=1, keepdims=True), 0.0))[:8]
            return go(rcopy(stat_s.at[i], stat_r.at[i], y_s.at[i], y_r.at[i], g, o))

        def total_here(i):
            both = jnp.concatenate([stat_s[i] + stat_r[i], jnp.zeros((120, R), F32)], axis=0)
            return pick(jnp.transpose(both), lane, 0)

        squares = total_over_sides(0, acc1[...])
        unpack(1, q_bk, rc_ct, cts, 1)
        unpack(1, q_bk, rc_ct, cts, 2)
        turn_quarter(xA, tA)
        settle(quarter_away)
        fold_half(t, 0)
        for rel, peer in ((2, xp), (3, diag)):
            go(fold_copy(rel - 1, peer % 4, 0, t, rel, peer, t))
        squares.wait_recv()
        gate_scale = lax.rsqrt(total_here(0) / whole + EPSILON)
        acc1[...] = jnp.broadcast_to(gate_scale, (R, 128))

        def gate_forward(p, carry):
            at = lanes(p)
            gate = gr[:, at]
            yb[0, :, at] = (mx[:, at] * (gate * sigmoid(gate)) * acc1[...] * gain_g[pl.ds(p, 1), :]).astype(BF)
            return carry
        lax.fori_loop(0, NT_, gate_forward, 0)
        quad_send(0)

        other_half(1, cts)
        for k in range(W // 128):
            v = cts[k // (H // 128), :, (k % (H // 128)) * 128:(k % (H // 128)) * 128 + 128].astype(F32)
            lowct[:, k * 128:(k + 1) * 128] = (v * live).astype(BF)
        fold_half(o, 1)
        xE[t, 0] = perm[q, :R // 2]
        xE[o, 0] = perm[q, R // 2:]
        go(fold_copy(0, sib % 4, 0, t, 1, sib, t))
        go(fold_copy(3, sib % 4, 1, o, 1, sib, t))
        quad_send(1)
        loads[3].wait()

        def out_half(side, dst, cast):
            def body(n, carry):
                at = pl.ds(pl.multiple_of(side * H + n * 256, 256), 256)
                dst[:, pl.ds(pl.multiple_of(n * 256, 256), 256)] = dot_nn(yb[0, :, :C], wout[:, at]).astype(cast)
                return carry
            lax.fori_loop(0, H // 256, body, 0)

        def back_project(n, carry):
            at = pl.ds(pl.multiple_of(n * 256, 256), 256)
            ng[:, at] = dot_nt(lowct[...], wout[at, :])
            for k in range(2):
                here = pl.ds(pl.multiple_of(n * 256 + k * 128, 128), 128)
                gate = gr[:, here]
                acc2[...] += mx[:, here] * (gate * sigmoid(gate)) * (gain_g[pl.ds(2 * n + k, 1), :] * ng[:, here])
            return carry
        lax.fori_loop(0, C // 256, back_project, 0)
        crossed = total_over_sides(1, acc2[...])
        for rel in (2, 3):
            fold_copy(rel - 1, 0, 0, t, rel, xp, t).wait_recv()
            go(fold_pass(rel, t))
        out_half(o, half_s, BF)
        branch_away = rcopy(half_s, half_r, y_s.at[2], y_r.at[2], g, o)
        branch_away.start()
        crossed.wait_recv()
        acc2[...] = acc1[...] * acc1[...] * acc1[...] * (total_here(1) / whole)

        def gate_back(p, carry):
            at = lanes(p)
            gate, mixed, grad = gr[:, at], mx[:, at], ng[:, at]
            sg = sigmoid(gate)
            act = gate * sg
            gated = mixed * act
            gated_grad = acc1[...] * (gain_g[pl.ds(p, 1), :] * grad) - gated * acc2[...]
            sms[0, 5:6, at] = jnp.sum(grad * gated * acc1[...], axis=0, keepdims=True)
            mixed_grad = gated_grad * act
            ng[:, at] = mixed_grad
            sms[0, 6:7, at] = jnp.sum(mixed_grad * xa[:, at], axis=0, keepdims=True)
            yb[0, :, pl.ds(pl.multiple_of(C + p * 128, 128), 128)] = (
                gated_grad * mixed * (sg * (1.0 + gate * (1.0 - sg)))).astype(BF)
            return carry
        lax.fori_loop(0, NT_, gate_back, 0)
        quad_send(2)
        quad_send(3)
        out_half(t, gr, F32)
        quad_pass(0)
        turn_folds()
        partial_sum(0, tE)

        inter[...] = dot_nt(written, readout)
        igrad[...] = jnp.zeros_like(igrad)
        sgr[...] = jnp.zeros_like(sgr)
        rgr[...] = jnp.zeros_like(rgr)
        ptile[...] = jnp.zeros_like(ptile)

        def scan_back(p, carry):
            at = lanes(p)
            lane = iota((R, 128), 1)
            grad = ng[:, at]
            act = xa[:, at]
            stepw = step_columns(p, lane)
            driven = (act * stepw).astype(BF)
            parts = [jnp.where(lane < 64, grad, 0.0).astype(BF), jnp.where(lane >= 64, grad, 0.0).astype(BF)]
            cols = [pick(lac[...], lane, 2 * p + k) for k in range(2)]
            pieces = []
            for b in range(R // B):
                skip = 128 * ((b * B) // 128)
                cut = slice(b * B, (b + 1) * B)
                causal = iota((B, R - skip), 1) + skip >= iota((B, R - skip), 0) + b * B
                turned = inter[cut, skip:]
                piece = jnp.zeros((B, 128), F32)
                total = igrad[cut, skip:]
                for k in range(2):
                    spread = lar[pl.ds(2 * p + k, 1), :][:, skip:] - cols[k][cut]
                    fading = jnp.exp(jnp.where(causal, spread, NEG))
                    faded = dot_nt(driven[cut], parts[k][skip:]) * fading
                    total = total + faded
                    piece = piece + dot_nn((turned * fading).astype(BF), parts[k][skip:])
                    ptile[k, cut, skip:] = (faded * turned).astype(BF)
                igrad[cut, skip:] = total
                pieces.append(piece)
            strict = one_hot(iota((R, R), 0) > iota((R, R), 1))
            for k in range(2):
                found = []
                for b in range(R // B):
                    skip = 128 * ((b * B) // 128)
                    cut = slice(b * B, (b + 1) * B)
                    causal = iota((B, R - skip), 1) + skip >= iota((B, R - skip), 0) + b * B
                    sums = dot_nn(strict[cut], ptile[k, :, skip:])
                    found.append(jnp.sum(jnp.where(causal, sums, 0.0), axis=1, keepdims=True))
                rgr[...] = jnp.where(lane == 2 * p + k, jnp.concatenate(found, axis=0), rgr[...])
            driven_grad = jnp.concatenate(pieces, axis=0)
            pulled = driven_grad * act
            low = jnp.sum(jnp.where(lane < 64, pulled, 0.0), axis=1, keepdims=True)
            high = jnp.sum(jnp.where(lane >= 64, pulled, 0.0), axis=1, keepdims=True)
            sgr[...] = jnp.where(lane == 2 * p, low, jnp.where(lane == 2 * p + 1, high, sgr[...]))
            conv_grad = (head_line(skip_in[...], p) * grad + stepw * driven_grad) * xs[:, at].astype(F32)
            raw = xr[:, at]
            raw_grad = tap_x[0:1, at] * conv_grad
            sms[0, 0:1, at] = jnp.sum(conv_grad * raw, axis=0, keepdims=True)
            sms[0, 4:5, at] = jnp.sum(conv_grad, axis=0, keepdims=True)
            for tap in range(1, 4):
                up = rows_up(conv_grad, tap)
                raw_grad = raw_grad + tap_x[tap:tap + 1, at] * up
                sms[0, tap:tap + 1, at] = jnp.sum(up * raw, axis=0, keepdims=True)
            yb[0, :, pl.ds(pl.multiple_of(2 * C + p * 128, 128), 128)] = raw_grad.astype(BF)
            return carry

        lax.fori_loop(0, NT_ // 2, scan_back, 0)
        quad_send(4)

        rcopy(half_r, half_r, y_s.at[2], y_r.at[2], g, o).wait_recv()

        pieces = []
        mine = hid[pl.ds(t, 1)][0]
        for k in range(H // 128):
            cut = slice(k * 128, (k + 1) * 128)
            branch = gr[:, cut] + half_r[:, cut].astype(F32)
            pieces.append((mine[:, cut].astype(F32) + live * branch).astype(BF))
        for k in range(3):
            span(pk_in, dp - 1, a2a_s.at[k], a2a_r.at[k], parts[k]).wait_send()
        reply(4, q_bk, jnp.concatenate(pieces, axis=1), pk_in, gn_o)
        reply_send(4, pk_in, gn_o, True)

        quad_pass(1)
        lax.fori_loop(NT_ // 2, NT_ // 4 * 3, scan_back, 0)
        quad_send(5)
        lax.fori_loop(NT_ // 4 * 3, NT_, scan_back, 0)
        quad_send(6)

        ig = igrad[...].astype(BF)
        st_s[:, :S] = dot_nn(ig, wr[:, S:]).astype(BF)
        st_s[:, S:] = dot_tn(ig, wr[:, :S]).astype(BF)
        go(rcopy(st_s, st_r, y_s.at[3], y_r.at[3], g, o))
        step_grad = (sgr[...] + rgr[...] * rate) * stepsig[...]
        yb[0, :, 3 * C + 2 * S:] = step_grad.astype(BF)
        sms[0, 7:8, 10 * S:10 * S + 128] = jnp.sum(step_grad, axis=0, keepdims=True)
        sms[0, 7:8, 10 * S + 128:10 * S + 256] = jnp.sum(rgr[...] * dtv[...], axis=0, keepdims=True) * rate
        partial_sum(1, tE)
        z_second(0)
        rcopy(st_r, st_r, y_s.at[3], y_r.at[3], g, o).wait_recv()
        for k in range(2):
            cut = slice(k * S, (k + 1) * S)
            conv_grad = (st_s[:, cut].astype(F32) + st_r[:, cut].astype(F32)) * sslope[:, cut]
            raw = sraw[:, cut]
            raw_grad = tap_s[0:1, cut] * conv_grad
            sms[0, 7:8, cut] = jnp.sum(conv_grad * raw, axis=0, keepdims=True)
            sms[0, 7:8, 8 * S + k * S:8 * S + (k + 1) * S] = jnp.sum(conv_grad, axis=0, keepdims=True)
            for tap in range(1, 4):
                up = rows_up(conv_grad, tap)
                raw_grad = raw_grad + tap_s[tap:tap + 1, cut] * up
                sms[0, 7:8, tap * 2 * S + k * S:tap * 2 * S + (k + 1) * S] = jnp.sum(up * raw, axis=0, keepdims=True)
            yb[0, :, 3 * C + k * S:3 * C + (k + 1) * S] = raw_grad.astype(BF)
        quad_send(7)
        reply_send(4, pk_in, gn_o, False)

        hops = [2 ** k for k in range(2, dp.bit_length() - 1)] + [1, 2]

        def small_start(i):
            bit = (g // hops[i]) % 2
            go(rcopy(sms.at[i], smr.at[i], sm_s.at[i], sm_r.at[i], g + (1 - 2 * bit) * hops[i]))

        def small_end(i):
            bit = (g // hops[i]) % 2
            rcopy(sms.at[i], smr.at[i], sm_s.at[i], sm_r.at[i], g + (1 - 2 * bit) * hops[i]).wait_recv()
            if i + 1 < len(hops):
                sms[i + 1] = sms[i] + smr[i]
                small_start(i + 1)
            else:
                smr[0] = sms[i] + smr[i]
        small_start(0)

        acc1[...] = jnp.zeros_like(acc1)

        def normed_grad(side, dst, cast):
            def body(n, carry):
                at = pl.ds(pl.multiple_of(side * H + n * 256, 256), 256)
                value = dot_nt(yb[0, :, C:3 * C], win[at, :])
                mine_state = pl.ds(pl.multiple_of(t * S, 128), S)
                value = value + dot_nt(yb[0, :, pl.ds(pl.multiple_of(3 * C + t * S, 128), S)], wst[at, mine_state])
                value = value + dot_nn(yb[0, :, 3 * C + 2 * S:], wstep[:, at])
                for k in range(2):
                    cut = slice(k * 128, (k + 1) * 128)
                    here = pl.ds(pl.multiple_of(n * 256 + k * 128, 128), 128)
                    there = pl.ds(pl.multiple_of(side * H + n * 256 + k * 128, 128), 128)
                    acc1[...] += hid[pl.ds(side, 1), :, here][0].astype(F32) * (gain_n[pl.ds(side * (H // 128) + 2 * n + k, 1), :] * value[:, cut])
                dst[:, pl.ds(pl.multiple_of(n * 256, 256), 256)] = value.astype(cast)
                return carry
            lax.fori_loop(0, H // 256, body, 0)
        branch_away.wait_send()
        normed_grad(o, half_s, BF)
        go(rcopy(half_s, half_r, y_s.at[4], y_r.at[4], g, o))
        normed_grad(t, gr, F32)
        summed_rows = total_over_sides(2, acc1[...])
        relay(4, back, rc_ct, gn_o)
        relay_send(4, rc_ct, gn_o, True)
        relay_send(4, rc_ct, gn_o, False)
        quad_pass(2)
        partial_sum(2, tA)

        rcopy(half_r, half_r, y_s.at[4], y_r.at[4], g, o).wait_recv()
        summed_rows.wait_recv()
        pull = total_here(2) / W * (scale[...] * scale[...] * scale[...])
        pieces = []
        mine = hid[pl.ds(t, 1)][0]
        mine_ct = cts[pl.ds(t, 1)][0]
        gall[pl.ds(g, 1)] = jnp.zeros((1, 8, 128), F32)
        for k in range(H // 128):
            cut = slice(k * 128, (k + 1) * 128)
            there = pl.ds(pl.multiple_of(t * H + k * 128, 128), 128)
            value = gr[:, cut] + half_r[:, cut].astype(F32)
            rows_here = mine[:, cut].astype(F32)
            gall[pl.ds(g, 1), k:k + 1, :] = jnp.sum(value * rows_here * scale[...], axis=0, keepdims=True)[None]
            pieces.append((scale[...] * (gain_n[pl.ds(t * (H // 128) + k, 1), :] * value) - rows_here * pull
                           + mine_ct[:, cut].astype(F32)).astype(BF))
        for k in range(3):
            span(pk_ct, dp - 1, a2a_s.at[3 + k], a2a_r.at[3 + k], parts[k]).wait_send()
        reply(5, q_in, jnp.concatenate(pieces, axis=1), pk_ct, gn_g)
        reply_send(5, pk_ct, gn_g, True)
        reply_send(5, pk_ct, gn_g, False)
        for peer in far:
            rcopy(gall.at[g], gall.at[g], gg_s, gg_r, peer).start()

        small_end(0)
        z_second(1)
        quad_pass(3)
        partial_sum(3, tA)
        z_second(2)
        z_third(0)
        relay(5, dest, rc_in, gn_g)
        relay_send(5, rc_in, gn_g, True)
        relay_send(5, rc_in, gn_g, False)
        quad_pass(4)
        partial_sum(4, tA)
        z_third(1)
        quad_pass(5)
        partial_sum(5, tA)
        z_third(2)
        quad_pass(6)
        partial_sum(6, tA)
        z_second(3)
        quad_pass(7)
        partial_sum(7, tA)
        small_end(1)
        z_second(4)
        small_end(2)
        z_second(5)
        z_third(3)
        z_second(6)

        def give(i, value, dst):
            lowct[:, i * H:(i + 1) * H] = value.astype(BF)
            store = pltpu.make_async_copy(lowct.at[:, pl.ds(i * H, H)], dst, w_s.at[i])
            store.start()
            return store

        replied(4, gn_o)

        @pl.when(is_outer == 1)
        def _():
            raw_copy(4).wait_send()
            raw_copy(5).wait_send()
        stores = [give(0, dot_tn(p_own[...], gn_o[...].reshape(sz.slots, H)), out_rows)]
        p_own[...] = send_table(dest, g, sz)
        for i in range(4):
            z_fourth(i)
            stores += write_out(i)
        small_end(3)
        stores.append(pltpu.make_async_copy(smr.at[0], small_out, o_s.at[8]))
        stores[-1].start()
        span(gall, dp - 1, gg_s, gg_r).wait_recv()
        sent.append(span(gall, dp - 1, gg_s, gg_r))
        summed = gall[0]
        for d in range(1, dp):
            summed = summed + gall[d]
        gsum[pl.ds(t, 1)] = summed[None]
        go(rcopy(gsum.at[t], gsum.at[t], y_s.at[5], y_r.at[5], g, o))
        replied(5, gn_g)
        stores.append(give(1, dot_tn(p_own[...], gn_g[...].reshape(sz.slots, H)), out_grads))
        z_second(7)
        z_third(4)
        z_fourth(4)
        stores += write_out(4)
        for i in range(5, 8):
            z_third(i)
            z_fourth(i)
            stores += write_out(i)
        rcopy(gsum.at[o], gsum.at[o], y_s.at[5], y_r.at[5], g, o).wait_recv()
        stores.append(pltpu.make_async_copy(gsum, gain_out, o_s.at[9]))
        stores[-1].start()
        for copy in sent:
            copy.wait_send()
        settle_sums()
        reply_settle(4, pk_in)
        reply_settle(5, pk_ct)
        for store in stores:
            store.wait()

    big = pltpu.VMEM((R, C), F32)
    pl.run_scoped(remainder, big, big, big, pltpu.VMEM((R, C), BF), big, big)


def finish_kernel(sz, rows, grads, inner, proj, extra, small, gain, o_rows, o_grads, o_gain, o_inner, o_state, o_step,
                  o_tap_x, o_bias_x, o_tap_s, o_bias_s, o_bias_step, o_rate, o_skip, o_gate, o_proj):
    C, S = sz.inner, sz.state
    o_rows[...] = rows[...]
    o_grads[...] = grads[...]
    o_inner[:, 0, :] = inner[:, :C]
    o_inner[:, 1, :] = inner[:, C:]
    o_proj[...] = proj[...]
    o_state[...] = extra[:, :2 * S]
    o_step[...] = jnp.transpose(extra[:, 2 * S:])[:sz.heads]
    o_tap_x[...] = small[0:4, :]
    o_bias_x[...] = small[4, :]
    o_gate[...] = small[5, :]
    for k in range(4):
        o_tap_s[k:k + 1, :] = small[7:8, k * 2 * S:(k + 1) * 2 * S]
    o_bias_s[...] = small[7, 8 * S:10 * S]
    o_bias_step[...] = small[7, 10 * S:10 * S + sz.heads]
    o_rate[...] = small[7, 10 * S + 128:10 * S + 128 + sz.heads]
    shape = (C, sz.heads)
    member = one_hot(iota(shape, 0) // (C // sz.heads) == iota(shape, 1))
    skip = jnp.broadcast_to(small[6:7, :], (8, C))
    o_skip[...] = sum(dot_nn(part, member) for part in split3(skip))[0]
    flat = jnp.concatenate([gain[h, k:k + 1, :] for h in range(2) for k in range(sz.half // 128)], axis=1)
    start = lax.axis_index("dp") * sz.share
    moved = pltpu.roll(jnp.broadcast_to(flat, (8, sz.width)), lax.rem(sz.width - start, sz.width), 1)
    o_gain[...] = moved[0, :sz.share]


def fused(sz, block_in, cotangent, lengths, dest_slot, return_slot, norm_gain, inner_weight, state_weight,
          step_weight, conv_inner, conv_inner_bias, conv_state, conv_state_bias, step_bias, log_rate,
          skip_gain, gate_gain, out_weight):
    dp, R, H, C, S = sz.dp, sz.rows, sz.half, sz.inner, sz.state
    W = sz.width

    vm = pl.BlockSpec(memory_space=pltpu.VMEM)
    hb = pl.BlockSpec(memory_space=pl.ANY)
    sm = pl.BlockSpec(memory_space=pltpu.SMEM)
    V = pltpu.VMEM
    packed = V((dp, sz.cap, H), BF)
    D = pltpu.SemaphoreType.DMA
    nch = len(sz.chunks)
    scratch = [
        V((W, 2 * C), BF), V((C, W), BF), V((W, 2 * S), BF), V((128, W), BF), V((8, 128), F32),
        *[packed] * 6,
        V((sz.slots, R), BF), V((R, sz.slots), BF), V((R, sz.slots), BF),
        V((2, R, H), BF), V((2, R, H), BF), V((R, W), BF), V((R, W), BF),
        V((4, R, sz.quarter), BF), V((4, R, sz.quarter), BF), V((2, 4, R // 2, sz.quarter), BF),
        V((sz.quarter, 4 * R), BF), V((sz.quarter, 4 * R), BF),
        V((4, R, sz.cols), BF), V((sz.nz, sz.share, sz.cols), BF), V((3, sz.share, sz.cols), BF), V((2, sz.share, sz.cols), BF),
        V((sz.share, 2 * C), F32), V((sz.share, C), F32), V((sz.share, sz.extra), F32),
        V((R, R), F32), V((R, R), F32), V((2, R, R), BF),
        V((R, 2 * S), F32), V((R, 2 * S), F32), V((R, 2 * S), BF), V((R, 128), F32), V((R, 128), F32), V((128, R), F32),
        V((R, 128), F32), V((R, 128), F32), V((R, 128), F32), V((R, 128), F32), V((R, 128), F32), V((R, 128), F32),
        V((3, 8, R), F32), V((3, 8, R), F32), V((R, H), BF), V((R, H), BF), V((R, H), BF),
        V((R, 2 * S), BF), V((R, 2 * S), BF),
        V((4, 8, C), F32), V((4, 8, C), F32), V((dp, 8, 128), F32), V((2, 8, 128), F32),
        D((6,)), D((8,)), D((2, 3)), D((2, 3)), D((3,)), D((nch, 3)), D((2, 6)), D((2, 6)),
        D, D((nch, 6)), D((6,)), D((6,)), D, D, D((4,)), D((4,)), D((4,)), D((2,)), D((2,)), D((2, 2)), D((10,)),
        pltpu.SemaphoreType.REGULAR,
    ]
    out = jax.ShapeDtypeStruct
    rows_out, grads_out, inner_g, proj_g, extra_g, small, gain = pl.pallas_call(
        functools.partial(block_kernel, sz),
        out_shape=(out((R, H), BF), out((R, H), BF), out((sz.share, 2 * C), F32), out((sz.share, C), F32),
                   out((sz.share, sz.extra), F32), out((8, C), F32), out((2, 8, 128), F32)),
        in_specs=[vm, vm, sm, hb, hb, hb, hb, hb] + [vm] * 10,
        out_specs=(hb,) * 7,
        scratch_shapes=scratch,
        compiler_params=pltpu.CompilerParams(collective_id=0, has_side_effects=True, vmem_limit_bytes=66000000),
        name="block",
    )(dest_slot.reshape(-1, 128), return_slot.reshape(-1, 128), lengths, block_in, cotangent, inner_weight, out_weight,
      state_weight, step_weight.T, conv_inner, conv_inner_bias.reshape(-1, 128), gate_gain.reshape(-1, 128), norm_gain.reshape(-1, 128), skip_gain[None],
      conv_state, conv_state_bias[None], step_bias[None], log_rate[None])
    results = pl.pallas_call(
        functools.partial(finish_kernel, sz),
        out_shape=(out((R, H), BF), out((R, H), BF), out((sz.share,), F32), out((sz.share, 2, C), F32),
                   out((sz.share, 2 * S), F32), out((sz.heads, sz.share), F32), out((4, C), F32), out((C,), F32),
                   out((4, 2 * S), F32), out((2 * S,), F32), out((sz.heads,), F32), out((sz.heads,), F32),
                   out((sz.heads,), F32), out((C,), F32), out((sz.share, C), F32)),
        in_specs=[vm] * 7,
        out_specs=(vm,) * 15,
        name="finish",
    )(rows_out, grads_out, inner_g, proj_g, extra_g, small, gain)
    return results[:5] + (results[5].T,) + results[6:14] + (results[14].T,)


def with_collectives(
    block_in,
    cotangent,
    lengths,
    dest_slot,
    return_slot,
    norm_gain,
    inner_weight,
    state_weight,
    step_weight,
    conv_inner,
    conv_inner_bias,
    conv_state,
    conv_state_bias,
    step_bias,
    log_rate,
    skip_gain,
    gate_gain,
    out_weight,
):
    groups = lax.axis_size("dp")
    group_rows = block_in.shape[0]
    half_width = block_in.shape[1]
    capacity = 2 * group_rows // groups
    own_group = lax.axis_index("dp")
    own_dest = lax.dynamic_slice_in_dim(dest_slot, own_group * group_rows, group_rows)
    own_return = lax.dynamic_slice_in_dim(return_slot, own_group * group_rows, group_rows)
    send_spot = send_layout(own_dest, group_rows, capacity, groups)
    back_spot = send_layout(own_return, group_rows, capacity, groups)
    slots_in = arrivals(dest_slot, group_rows, capacity, groups, own_group)
    slots_back = arrivals(return_slot, group_rows, capacity, groups, own_group)
    blank_rows = jnp.zeros((groups * capacity, half_width), jnp.bfloat16)
    packed_rows = blank_rows.at[send_spot].set(block_in).reshape(groups, capacity, half_width)
    packed_grads = blank_rows.at[back_spot].set(cotangent).reshape(groups, capacity, half_width)
    came_rows, came_grads = (
        lax.all_to_all(packed_rows, "dp", split_axis=0, concat_axis=0, tiled=True),
        lax.all_to_all(packed_grads, "dp", split_axis=0, concat_axis=0, tiled=True),
    )
    empty_rows = jnp.zeros((group_rows, half_width), jnp.bfloat16)
    own_rows = empty_rows.at[slots_in].set(came_rows.reshape(-1, half_width), mode="drop")
    own_grads = empty_rows.at[slots_back].set(came_grads.reshape(-1, half_width), mode="drop")
    full_rows, full_grads = (
        lax.all_gather(own_rows, "tensor", axis=1, tiled=True),
        lax.all_gather(own_grads, "tensor", axis=1, tiled=True),
    )
    seq_pos, live_mask, keep_state = stretch_layout(lengths[0], STRETCH)
    live_col = live_mask[:, None]
    hidden = full_rows.astype(jnp.float32)
    norm_scale = lax.rsqrt(jnp.mean(hidden * hidden, axis=1, keepdims=True) + EPSILON)
    normed = (hidden * norm_scale * norm_gain).astype(jnp.bfloat16)
    inner_local = inner_weight.shape[2]
    zx_weight = inner_weight.reshape(inner_weight.shape[0], 2 * inner_local)
    projected = jnp.dot(normed, zx_weight, preferred_element_type=jnp.float32)
    gate_raw = projected[:, :inner_local]
    conv_in_x = projected[:, inner_local:]
    conv_in_state = jnp.dot(normed, state_weight, preferred_element_type=jnp.float32)
    step_raw = jnp.dot(normed, step_weight, preferred_element_type=jnp.float32)
    x_conv = conv_forward(conv_in_x, conv_inner, conv_inner_bias, seq_pos)
    state_conv = conv_forward(conv_in_state, conv_state, conv_state_bias, seq_pos)
    x_act = jax.nn.silu(x_conv)
    state_act = jax.nn.silu(state_conv)
    state_width = state_act.shape[1] // 2
    heads_local = step_weight.shape[1]
    head_dim = inner_local // heads_local
    stretches = group_rows // STRETCH
    step_input = step_raw + step_bias[None, :]
    step_size = jax.nn.softplus(step_input) * live_col
    decay_rate = -jnp.exp(log_rate)
    skip_wide = jnp.repeat(skip_gain, head_dim)[None, :]
    scanned, saved = state_forward(
        x_act.reshape(group_rows, heads_local, head_dim),
        state_act[:, :state_width],
        state_act[:, state_width:],
        step_size,
        decay_rate,
        STRETCH,
    )
    mixed = scanned + skip_wide * x_act
    gate_act = jax.nn.silu(gate_raw)
    gated = mixed * gate_act
    inner_total = inner_local * lax.axis_size("tensor")
    square_sum = lax.psum(jnp.sum(gated * gated, axis=1), "tensor")
    gate_scale = lax.rsqrt(square_sum / inner_total + EPSILON)[:, None]
    gate_normed = (gated * gate_scale * gate_gain).astype(jnp.bfloat16)
    partial_out = jnp.dot(gate_normed, out_weight, preferred_element_type=jnp.float32)
    branch_half = lax.psum_scatter(partial_out, "tensor", scatter_dimension=1, tiled=True)
    half_index = lax.axis_index("tensor")
    out_half = (own_rows.astype(jnp.float32) + live_col * branch_half).astype(jnp.bfloat16)
    zero_row = jnp.zeros((1, half_width), jnp.bfloat16)
    reply_rows = jnp.concatenate([out_half, zero_row], axis=0)[slots_back]
    returned = lax.all_to_all(
        reply_rows.reshape(groups, capacity, half_width),
        "dp",
        split_axis=0,
        concat_axis=0,
        tiled=True,
    )
    block_out = returned.reshape(-1, half_width)[back_spot]
    owner_ct = full_grads.astype(jnp.float32)
    out_grad = (owner_ct * live_col).astype(jnp.bfloat16)
    out_weight_grad = jnp.einsum(
        "ti,td->id", gate_normed, out_grad, preferred_element_type=jnp.float32
    )
    normed_out_grad = jnp.einsum(
        "td,id->ti", out_grad, out_weight, preferred_element_type=jnp.float32
    )
    gate_gain_grad = jnp.sum(normed_out_grad * gated * gate_scale, axis=0)
    scaled_grad = gate_gain * normed_out_grad
    cross = lax.psum(jnp.sum(gated * scaled_grad, axis=1), "tensor")[:, None]
    gated_grad = gate_scale * scaled_grad - gated * gate_scale**3 * cross / inner_total
    mixed_grad = gated_grad * gate_act
    gate_raw_grad = gated_grad * mixed * silu_slope(gate_raw)
    skip_gain_grad = jnp.sum(
        (mixed_grad * x_act).reshape(group_rows, heads_local, head_dim), axis=(0, 2)
    )
    x_state_grad, written_grad, readout_grad, step_grad, rate_total = state_backward(
        saved, mixed_grad.reshape(stretches, STRETCH, heads_local, head_dim), decay_rate
    )
    x_act_grad = x_state_grad.reshape(group_rows, inner_local) + skip_wide * mixed_grad
    state_grad = lax.psum(
        jnp.concatenate(
            [written_grad.reshape(group_rows, -1), readout_grad.reshape(group_rows, -1)], axis=1
        ),
        "tensor",
    )
    state_conv_grad = state_grad * silu_slope(state_conv)
    x_conv_grad = x_act_grad * silu_slope(x_conv)
    state_raw_grad, conv_state_grad, conv_state_bias_grad = conv_backward(
        conv_in_state, conv_state, seq_pos, state_conv_grad
    )
    x_raw_grad, conv_inner_grad, conv_inner_bias_grad = conv_backward(
        conv_in_x, conv_inner, seq_pos, x_conv_grad
    )
    step_raw_grad = (
        step_grad.reshape(group_rows, heads_local) * live_col * jax.nn.sigmoid(step_input)
    )
    step_bias_grad = jnp.sum(step_raw_grad, axis=0)
    log_rate_grad = rate_total * decay_rate
    zx_low = jnp.concatenate([gate_raw_grad, x_raw_grad], axis=1).astype(jnp.bfloat16)
    state_low = state_raw_grad.astype(jnp.bfloat16)
    step_low = step_raw_grad.astype(jnp.bfloat16)
    inner_weight_grad = jnp.einsum(
        "td,tk->dk", normed, zx_low, preferred_element_type=jnp.float32
    )
    state_weight_grad = jnp.einsum(
        "td,tk->dk", normed, state_low, preferred_element_type=jnp.float32
    )
    step_weight_grad = jnp.einsum("td,tk->dk", normed, step_low, preferred_element_type=jnp.float32)
    lead_share = (half_index == 0).astype(jnp.float32)
    normed_grad = jnp.einsum("tk,dk->td", zx_low, zx_weight, preferred_element_type=jnp.float32)
    normed_grad = normed_grad + jnp.einsum(
        "tk,dk->td", step_low, step_weight, preferred_element_type=jnp.float32
    )
    normed_grad = normed_grad + lead_share * jnp.einsum(
        "tk,dk->td", state_low, state_weight, preferred_element_type=jnp.float32
    )
    normed_grad = lax.psum(normed_grad, "tensor")
    norm_gain_grad = jnp.sum(normed_grad * hidden * norm_scale, axis=0)
    input_scaled = norm_gain * normed_grad
    hidden_grad = (
        norm_scale * input_scaled
        - hidden * norm_scale**3 * jnp.mean(hidden * input_scaled, axis=1, keepdims=True)
        + owner_ct
    )
    own_grad = lax.dynamic_slice_in_dim(hidden_grad, half_index * half_width, half_width, 1).astype(
        jnp.bfloat16
    )
    answer_rows = jnp.concatenate([own_grad, zero_row], axis=0)[slots_in]
    gone = lax.all_to_all(
        answer_rows.reshape(groups, capacity, half_width),
        "dp",
        split_axis=0,
        concat_axis=0,
        tiled=True,
    )
    input_grad = gone.reshape(-1, half_width)[send_spot]
    (
        conv_inner_grad,
        conv_inner_bias_grad,
        conv_state_grad,
        conv_state_bias_grad,
        step_bias_grad,
        log_rate_grad,
        skip_gain_grad,
        gate_gain_grad,
    ) = lax.psum(
        (
            conv_inner_grad,
            conv_inner_bias_grad,
            conv_state_grad,
            conv_state_bias_grad,
            step_bias_grad,
            log_rate_grad,
            skip_gain_grad,
            gate_gain_grad,
        ),
        "dp",
    )
    zx_share, state_share, step_share, gain_share, out_share = (
        lax.psum_scatter(inner_weight_grad.astype(jnp.bfloat16), "dp", scatter_dimension=0, tiled=True),
        lax.psum_scatter(state_weight_grad, "dp", scatter_dimension=0, tiled=True),
        lax.psum_scatter(step_weight_grad, "dp", scatter_dimension=0, tiled=True),
        lax.psum_scatter(norm_gain_grad, "dp", scatter_dimension=0, tiled=True),
        lax.psum_scatter(out_weight_grad.astype(jnp.bfloat16), "dp", scatter_dimension=1, tiled=True),
    )
    zx_share = zx_share.astype(jnp.float32).reshape((-1,) + inner_weight.shape[1:])
    out_share = out_share.astype(jnp.float32)
    return (
        block_out,
        input_grad,
        gain_share,
        zx_share,
        state_share,
        step_share,
        conv_inner_grad,
        conv_inner_bias_grad,
        conv_state_grad,
        conv_state_bias_grad,
        step_bias_grad,
        log_rate_grad,
        skip_gain_grad,
        gate_gain_grad,
        out_share,
    )


def on_device(*args):
    groups = lax.axis_size("dp")
    rows, half = args[0].shape
    inner, heads, state = args[6].shape[2], args[8].shape[1], args[7].shape[1] // 2
    capacity = 2 * rows // groups
    fits = (
        groups == 16 and capacity % 16 == 0 and (2 * half // groups) % 16 == 0
        and rows == STRETCH and args[2].shape[1] == 1 and inner == 64 * heads and inner == 2 * half
    )
    if fits:
        return fused(Sizes(groups, rows, half, inner, heads, state, capacity), *args)
    return with_collectives(*args)


def solution(mesh):
    placed = (
        P("dp", "tensor"),
        P("dp", "tensor"),
        P("dp", None),
        P(),
        P(),
        P(),
        P(None, None, "tensor"),
        P(),
        P(None, "tensor"),
        P(None, "tensor"),
        P("tensor"),
        P(),
        P(),
        P("tensor"),
        P("tensor"),
        P("tensor"),
        P("tensor"),
        P("tensor", None),
    )
    return jax.shard_map(
        on_device,
        mesh=mesh,
        in_specs=placed,
        out_specs=(
            P("dp", "tensor"),
            P("dp", "tensor"),
            P("dp"),
            P("dp", None, "tensor"),
            P("dp", None),
            P("dp", "tensor"),
            P(None, "tensor"),
            P("tensor"),
            P(),
            P(),
            P("tensor"),
            P("tensor"),
            P("tensor"),
            P("tensor"),
            P("tensor", "dp"),
        ),
        check_vma=False,
    )
```
